256 devices in a mesh: section: 4 (over x_hi, core), seq: 64 (over z, x_lo, y).
Axes of the slice: x: 4 (x_hi: 2, x_lo: 2; x = x_hi * 2 + x_lo), y: 4, z: 8, core: 2. Of those that a mesh axis runs over, the one named last changes fastest.
Arguments:
- x_in: bfloat16 [2, 64, 128, 2048], P(None, 'seq'), may hold values from -6 to 6
- x_tan: bfloat16 [2, 64, 128, 2048], P(None, 'seq'), may hold values from -6 to 6
- t_index: int32 [2], replicated, may hold values from 0 to 999
- w_qkv: bfloat16 [4, 2048, 3072], P('section', 'seq'), may hold values from -0.125 to 0.125
- w_out: bfloat16 [4, 1024, 2048], P('section', 'seq'), may hold values from -0.1875 to 0.1875
- qk_gain: float32 [4, 2, 128], P('section'), may hold values from 0.1 to 1.9
- mod_amp: float32 [4, 3, 2048], P('section'), may hold values from -1 to 1
- mod_freq: float32 [4, 3, 2048], P('section'), may hold values from 0.5 to 4
- mod_phase: float32 [4, 3, 2048], P('section'), may hold values from -3.140625 to 3.140625
Outputs:
- section_out: bfloat16 [4, 2, 64, 128, 2048], P('section', None, 'seq')
- section_tan: bfloat16 [4, 2, 64, 128, 2048], P('section', None, 'seq')
The draws below stay inside these ranges and needn't reach their ends.
All inputs are finite; a program needn't handle non-finite values.
Results may differ from the reference program's by a relative error of at most 0.018.
Values may be sent and summed in bfloat16 or wider, within the bound.
A program may use at most 192 MiB of HBM per device.

```python
import math
import jax
import jax.numpy as jnp
from jax import lax

D = 2048
HEADS = 8
HEAD = 128
HD = 1024
P_SIZE = 128
F = 64
MICRO = 2
T_STEPS = 1000
SECTIONS = 4


def shard_levels(rng, extent, shards, smallest, largest):
    def one(dim, shards_of):
        heights = jax.random.uniform(jax.random.fold_in(jax.random.fold_in(rng, 6), dim), (shards_of,), jnp.float32, smallest / len(shards), largest / len(shards))
        return jnp.repeat(jnp.exp(heights), extent[dim] // shards_of).reshape((-1,) + (1,) * (len(extent) - dim - 1))

    level = one(*shards[0])
    for cut in shards[1:]:
        level = level * one(*cut)
    return level


def scatter_about(key, extent, scale, bound, pieces=(), dtype=jnp.bfloat16):
    result = scale * jax.random.normal(key, extent, jnp.float32)
    if pieces:
        result = result * shard_levels(key, extent, pieces, -0.22, 0.18)
    return jnp.clip(result, -bound, bound).astype(dtype)


def setup_inputs(seed: int = 0) -> dict:
    key_list = jax.random.split(jax.random.key(seed), 10)
    x_in = scatter_about(key_list[0], (MICRO, F, P_SIZE, D), 1.0, 6.0, ((1, 64),))
    x_tan = scatter_about(key_list[1], (MICRO, F, P_SIZE, D), 1.0, 6.0, ((1, 64),))
    t_index = jax.random.randint(key_list[2], (MICRO,), 0, T_STEPS).astype(jnp.int32)
    w_qkv = scatter_about(key_list[3], (SECTIONS, D, 3 * HD), D ** -0.5, 0.125, ((0, 4), (1, 64)))
    w_out = scatter_about(key_list[4], (SECTIONS, HD, D), HD ** -0.5, 0.1875, ((0, 4), (1, 64)))
    qk_gain = jnp.clip(1.0 + 0.18 * jax.random.normal(key_list[5], (SECTIONS, 2, HEAD), jnp.float32), 0.1, 1.9)
    mod_amp = jnp.clip(jax.random.uniform(key_list[6], (SECTIONS, 3, D), jnp.float32, -1.0, 1.0) * shard_levels(key_list[6], (SECTIONS, 3, D), ((0, 4),), -0.4, 0.0), -1.0, 1.0)
    mod_freq = jnp.clip(jnp.exp(math.log(4.0) - 2.0794415 * jax.random.uniform(key_list[7], (SECTIONS, 3, D), jnp.float32) ** shard_levels(key_list[7], (SECTIONS, 3, D), ((0, 4),), -0.2, 0.2)), 0.5, 4.0)
    mod_phase = jnp.clip(jax.random.uniform(key_list[8], (SECTIONS, 3, D), jnp.float32, -3.140625, 3.140625), -3.140625, 3.140625)
    return dict(x_in=x_in, x_tan=x_tan, t_index=t_index, w_qkv=w_qkv, w_out=w_out, qk_gain=qk_gain, mod_amp=mod_amp, mod_freq=mod_freq, mod_phase=mod_phase)


def row_norm(values, tangents):
    square = lax.optimization_barrier(jnp.mean(values * values, axis=-1, keepdims=True)) + 1e-06
    inverse = lax.rsqrt(square)
    cross = lax.optimization_barrier(jnp.mean(values * tangents, axis=-1, keepdims=True))
    return (values * inverse, inverse * tangents - values * inverse ** 3 * cross)

def timing(amp, freq, phase, time_value):
    angle = freq * time_value + phase
    return (amp * jnp.sin(angle), amp * freq * jnp.cos(angle))

def project(modulated, dmodulated, wqkv, gains):
    leading = modulated.shape[:-1]
    flat = modulated.reshape(-1, D)
    dflat = dmodulated.reshape(-1, D)
    qkv = jnp.dot(flat, wqkv, preferred_element_type=jnp.float32).reshape(leading + (3, HEADS, HEAD))
    dqkv = jnp.dot(dflat, wqkv, preferred_element_type=jnp.float32).reshape(leading + (3, HEADS, HEAD))
    query, dquery = row_norm(qkv[..., 0, :, :], dqkv[..., 0, :, :])
    keys, dkeys = row_norm(qkv[..., 1, :, :], dqkv[..., 1, :, :])
    query = (query * gains[0]).astype(jnp.bfloat16)
    dquery = (dquery * gains[0]).astype(jnp.bfloat16)
    keys = (keys * gains[1]).astype(jnp.bfloat16)
    dkeys = (dkeys * gains[1]).astype(jnp.bfloat16)
    values = qkv[..., 2, :, :].astype(jnp.bfloat16)
    dvalues = dqkv[..., 2, :, :].astype(jnp.bfloat16)
    return (query, keys, values, dquery, dkeys, dvalues)

def attend(query, keys, values, dquery, dkeys, dvalues):
    factor = 1.0 / math.sqrt(HEAD)
    wide = jnp.float32
    score = jnp.einsum('fphe,gphe->phfg', query.astype(wide), keys.astype(wide)) * factor
    dscore = (jnp.einsum('fphe,gphe->phfg', dquery.astype(wide), keys.astype(wide)) + jnp.einsum('fphe,gphe->phfg', query.astype(wide), dkeys.astype(wide))) * factor
    expo = jnp.exp(score)
    prob = expo / lax.optimization_barrier(jnp.sum(expo, axis=-1, keepdims=True))
    growth = prob * dscore
    dprob = growth - prob * lax.optimization_barrier(jnp.sum(growth, axis=-1, keepdims=True))
    prob_low = prob.astype(jnp.bfloat16).astype(wide)
    dprob_low = dprob.astype(jnp.bfloat16).astype(wide)
    output = jnp.einsum('phfg,gphe->fphe', prob_low, values.astype(wide))
    doutput = jnp.einsum('phfg,gphe->fphe', prob_low, dvalues.astype(wide)) + jnp.einsum('phfg,gphe->fphe', dprob_low, values.astype(wide))
    return (output.astype(jnp.bfloat16), doutput.astype(jnp.bfloat16))

def block(hidden, tangent, wqkv, wout, gains, mods, dmods):
    frames, places = (hidden.shape[0], hidden.shape[1])
    hidden_f = hidden.astype(jnp.float32)
    tangent_f = tangent.astype(jnp.float32)
    normed, dnormed = row_norm(hidden_f, tangent_f)
    modulated = (normed * (1.0 + mods[1]) + mods[0]).astype(jnp.bfloat16)
    dmodulated = (dnormed * (1.0 + mods[1]) + normed * dmods[1] + dmods[0]).astype(jnp.bfloat16)
    parts = project(modulated, dmodulated, wqkv, gains)
    output, doutput = attend(*parts)
    output = output.reshape(-1, HEADS * HEAD)
    doutput = doutput.reshape(-1, HEADS * HEAD)
    proj = jnp.dot(output, wout, preferred_element_type=jnp.float32).reshape(frames, places, D)
    dproj = jnp.dot(doutput, wout, preferred_element_type=jnp.float32).reshape(frames, places, D)
    hidden_next = (hidden_f + mods[2] * proj).astype(jnp.bfloat16)
    tangent_next = (tangent_f + dmods[2] * proj + mods[2] * dproj).astype(jnp.bfloat16)
    return (hidden_next, tangent_next)

def reference(x_in, x_tan, t_index, w_qkv, w_out, qk_gain, mod_amp, mod_freq, mod_phase):
    section_rows = []
    tangent_rows = []
    for section_number in range(SECTIONS):
        section_rows.append([])
        tangent_rows.append([])
    for video in range(MICRO):
        time_value = (t_index[video].astype(jnp.float32) + 0.5) * (math.pi / (2.0 * T_STEPS))
        hidden = x_in[video]
        tangent = x_tan[video]
        for section_number in range(SECTIONS):
            mods, dmods = timing(mod_amp[section_number], mod_freq[section_number], mod_phase[section_number], time_value)
            hidden, tangent = block(hidden, tangent, w_qkv[section_number], w_out[section_number], qk_gain[section_number], mods, dmods)
            section_rows[section_number].append(hidden)
            tangent_rows[section_number].append(tangent)
    section_out = jnp.stack([jnp.stack(row) for row in section_rows])
    section_tan = jnp.stack([jnp.stack(row) for row in tangent_rows])
    return (section_out, section_tan)
```

```python
import functools
import math

import jax
import jax.numpy as jnp
from jax import lax
from jax.experimental import pallas as pl
from jax.experimental.pallas import tpu as pltpu
from jax.sharding import PartitionSpec as P

HEADS = 8
HEAD = 128
T_STEPS = 1000
D = 2048
KT = D // HEAD
HD = HEADS * HEAD
F = 64
NP = 2
VIDS = 2
ROWS = 2 * NP * F
HALF = ROWS // 2
EPS = 1e-06
F32 = jnp.float32
BF16 = jnp.bfloat16
MESH = pl.DeviceIdType.MESH


def timing(amp, freq, phase, time_value):
    angle = freq * time_value + phase
    return (amp * jnp.sin(angle), amp * freq * jnp.cos(angle))


class Gather:
    def __init__(self, sizes, section, coords, wq, wo, send, recv):
        self.sizes, self.section, self.coords = sizes, section, coords
        self.wq, self.wo, self.send, self.recv = wq, wo, send, recv
        self.live = []

    def peer(self, axis, by):
        z, xl, y = self.coords
        nz, nx, ny = self.sizes
        if axis == "z":
            z = lax.rem(z + by + nz, nz)
        elif axis == "y":
            y = lax.rem(y + by + ny, ny)
        else:
            xl = nx - 1 - xl
        return (self.section, (z * nx + xl) * ny + y)

    def parts(self, stream, z, xl, y):
        if stream == 0:
            return (
                self.wq.at[z, xl, y, pl.ds(0, 16), :],
                self.wo.at[z, xl, y, :, pl.ds(0, D // 2)],
            )
        return (
            self.wq.at[z, xl, y, pl.ds(16, 16), :],
            self.wo.at[z, xl, y, :, pl.ds(D // 2, D // 2)],
        )

    def block(self, stream, phase, index, half):
        z, _, y = self.coords
        xl = slice(None) if half is None else half
        if (stream, phase) == (0, 0):
            return self.parts(0, z, xl, index)
        if (stream, phase) == (0, 1):
            return self.parts(0, index, xl, slice(None))
        if (stream, phase) == (1, 0):
            return self.parts(1, index, xl, y)
        return self.parts(1, slice(None), xl, index)

    def ring(self, stream, phase):
        axis = "y" if (stream == 0) == (phase == 0) else "z"
        size = self.sizes[2] if axis == "y" else self.sizes[0]
        me = self.coords[2] if axis == "y" else self.coords[0]
        last = size // 2
        arriving = []
        for step in range(last):
            for way in (0, 1):
                by = 1 if way == 0 else -1
                index = lax.rem(me - by * step + size, size)
                half = None if step < last - 1 else way
                for array, ref in enumerate(self.block(stream, phase, index, half)):
                    sem = ((stream * 2 + phase) * 2 + way) * 2 + array
                    copy = pltpu.make_async_remote_copy(
                        src_ref=ref,
                        dst_ref=ref,
                        send_sem=self.send.at[sem, step],
                        recv_sem=self.recv.at[sem, step],
                        device_id=self.peer(axis, by),
                        device_id_type=MESH,
                    )
                    copy.start()
                    self.live.append(copy)
                came = lax.rem(me - by * (step + 1) + size, size)
                for array, ref in enumerate(self.block(stream, phase, came, half)):
                    sem = ((stream * 2 + phase) * 2 + way) * 2 + array
                    arriving.append(
                        pltpu.make_async_remote_copy(
                            src_ref=ref,
                            dst_ref=ref,
                            send_sem=self.send.at[sem, step],
                            recv_sem=self.recv.at[sem, step],
                            device_id=self.peer(axis, by),
                            device_id_type=MESH,
                        )
                    )
            yield
            for copy in arriving:
                copy.wait_recv()
            arriving = []

    def finish(self):
        for copy in self.live:
            copy.wait_send()


def run(generator, steps=None):
    while steps is None or steps > 0:
        if next(generator, "end") == "end":
            return
        steps = None if steps is None else steps - 1


def spread(source, tall, start):
    count = source.shape[0]
    for k in range(KT):
        tall[pl.ds(start + k, count, stride=KT), :] = source[:, k * HEAD : (k + 1) * HEAD].astype(
            F32
        )


def normalize(values, tangents, gain):
    inverse = lax.rsqrt(jnp.mean(values * values, axis=-1, keepdims=True) + EPS)
    cross = jnp.mean(values * tangents, axis=-1, keepdims=True)
    scaled = values * inverse
    return (
        (scaled * gain).astype(BF16),
        ((inverse * tangents - values * inverse**3 * cross) * gain).astype(BF16),
    )


def attend(q2, k2, v2, gains_ref):
    factor = 1.0 / math.sqrt(HEAD)
    qn, dqn = normalize(q2[:HALF], q2[HALF:], gains_ref[0:1, :])
    kn, dkn = normalize(k2[:HALF], k2[HALF:], gains_ref[1:2, :])
    queries = jnp.concatenate([qn, dqn], axis=0)
    keys = jnp.concatenate([kn, dkn], axis=0)
    scores = lax.dot_general(
        queries, keys, (((1,), (1,)), ((), ())), preferred_element_type=F32
    )
    score = scores[:HALF, :HALF] * factor
    dscore = (scores[HALF:, :HALF] + scores[:HALF, HALF:]) * factor
    same = (lax.broadcasted_iota(jnp.int32, (HALF, HALF), 0) < F) == (
        lax.broadcasted_iota(jnp.int32, (HALF, HALF), 1) < F
    )
    expo = jnp.where(same, jnp.exp(score), 0.0)
    prob = expo / jnp.sum(expo, axis=-1, keepdims=True)
    growth = prob * dscore
    dprob = growth - prob * jnp.sum(growth, axis=-1, keepdims=True)
    probs = jnp.concatenate([prob.astype(BF16), dprob.astype(BF16)], axis=0)
    values = jnp.concatenate([v2[:HALF].astype(BF16), v2[HALF:].astype(BF16)], axis=1)
    mixed = jnp.dot(probs, values, preferred_element_type=F32)
    return mixed[:HALF, :HEAD], mixed[:HALF, HEAD:] + mixed[HALF:, :HEAD]


def block_step(vid, entering, leaving, wq, wo, gains_ref, mods_ref, dmods_ref, tall, flat, att):
    group = 8
    groups = F // group

    @pl.loop(0, NP * groups)
    def _(i):
        pos = i // groups
        first = pl.multiple_of((i % groups) * group, group)
        hidden = entering[vid, pl.ds(first, group), 0, pos].astype(F32)
        tangent = entering[vid, pl.ds(first, group), 1, pos].astype(F32)

        def mean(values):
            return jnp.sum(
                jnp.sum(values, axis=1, keepdims=True), axis=2, keepdims=True
            ) * (1.0 / D)

        inverse = lax.rsqrt(mean(hidden * hidden) + EPS)
        cross = mean(hidden * tangent)
        normed = hidden * inverse
        dnormed = inverse * tangent - hidden * inverse**3 * cross
        scale = 1.0 + mods_ref[vid, 1][None]
        modulated = normed * scale + mods_ref[vid, 0][None]
        dmodulated = dnormed * scale + normed * dmods_ref[vid, 1][None] + dmods_ref[vid, 0][None]
        row = pl.multiple_of((pos * F + first) * KT, group * KT)
        tall[pl.ds(row, group * KT), :] = modulated.reshape(group * KT, HEAD)
        tall[pl.ds(row + HALF * KT, group * KT), :] = dmodulated.reshape(group * KT, HEAD)

    for k in range(KT):
        flat[:, k * HEAD : (k + 1) * HEAD] = tall[pl.ds(k, ROWS, stride=KT), :].astype(BF16)

    @pl.loop(0, HEADS // 2)
    def _(pair):
        def third(number):
            column = pl.multiple_of(number * HD + pair * 2 * HEAD, 2 * HEAD)
            weights = wq[:, :, :, :, pl.ds(column, 2 * HEAD)].reshape(D, 2 * HEAD)
            return jnp.dot(flat[...], weights, preferred_element_type=F32)

        q2, k2, v2 = third(0), third(1), third(2)
        for one in range(2):
            lanes = slice(one * HEAD, (one + 1) * HEAD)
            output, doutput = attend(q2[:, lanes], k2[:, lanes], v2[:, lanes], gains_ref)
            column = pl.multiple_of((pair * 2 + one) * HEAD, HEAD)
            att[:HALF, pl.ds(column, HEAD)] = output.astype(BF16)
            att[HALF:, pl.ds(column, HEAD)] = doutput.astype(BF16)

    @pl.loop(0, KT // 2)
    def _(n):
        column = pl.multiple_of(n * 2 * HEAD, 2 * HEAD)
        weights = wo[:, :, :, :, pl.ds(column, 2 * HEAD)].reshape(HD, 2 * HEAD)
        y = jnp.dot(att[...], weights, preferred_element_type=F32)
        tall[pl.ds(2 * n, ROWS, stride=KT), :] = y[:, :HEAD]
        tall[pl.ds(2 * n + 1, ROWS, stride=KT), :] = y[:, HEAD:]

    @pl.loop(0, NP * groups)
    def _(i):
        pos = i // groups
        first = pl.multiple_of((i % groups) * group, group)
        row = pl.multiple_of((pos * F + first) * KT, group * KT)
        y = tall[pl.ds(row, group * KT), :].reshape(group, KT, HEAD)
        dy = tall[pl.ds(row + HALF * KT, group * KT), :].reshape(group, KT, HEAD)
        hidden = entering[vid, pl.ds(first, group), 0, pos].astype(F32)
        tangent = entering[vid, pl.ds(first, group), 1, pos].astype(F32)
        gate = mods_ref[vid, 2][None]
        dgate = dmods_ref[vid, 2][None]
        leaving[vid, pl.ds(first, group), 0, pos] = (hidden + gate * y).astype(BF16)
        leaving[vid, pl.ds(first, group), 1, pos] = (tangent + dgate * y + gate * dy).astype(BF16)


def kernel(
    sizes,
    sections,
    x_ref,
    t_ref,
    wqkv_ref,
    wout_ref,
    gains_ref,
    mods_ref,
    dmods_ref,
    out_ref,
    tan_ref,
    wq,
    wo,
    plain,
    staged,
    entering,
    leaving,
    returned,
    tall,
    flat,
    att,
    load_sem,
    own_sem,
    swap_send,
    swap_recv,
    ring_send,
    ring_recv,
    x_send,
    x_recv,
    pass_send,
    pass_recv,
    out_send,
    out_recv,
    store_sem,
    turn_sem,
):
    nz, nx, ny = sizes
    count = nz * nx * ny
    section = lax.axis_index("section")
    me = lax.axis_index("seq")
    coords = (me // (nx * ny), (me // ny) % nx, me % ny)
    z, xl, y = coords
    other = nx - 1 - xl
    across = (section, (z * nx + other) * ny + y)
    neighbour = (section, lax.rem(me + 1, count))

    def exchange(vid, source, target, send, recv):
        pltpu.make_async_copy(source.at[vid, me], target.at[vid, me], recv.at[vid]).start()

        @pl.loop(1, count)
        def _(by):
            to = lax.rem(me + by, count)
            pltpu.make_async_remote_copy(
                src_ref=source.at[vid, to],
                dst_ref=target.at[vid, me],
                send_sem=send.at[vid],
                recv_sem=recv.at[vid],
                device_id=(section, to),
                device_id_type=MESH,
            ).start()

    def exchange_came(vid, source, target, recv):
        pltpu.make_async_copy(source.at[vid], target.at[vid], recv.at[vid]).wait()

    def exchange_sent(vid, source, target, send, recv):
        pltpu.make_async_remote_copy(
            src_ref=source.at[vid, pl.ds(0, count - 1)],
            dst_ref=target.at[vid, pl.ds(0, count - 1)],
            send_sem=send.at[vid],
            recv_sem=recv.at[vid],
            device_id=neighbour,
            device_id_type=MESH,
        ).wait_send()

    loads = [
        pltpu.make_async_copy(ref, plain.at[tan], load_sem.at[tan])
        for tan, ref in enumerate((x_ref, t_ref))
    ]

    @pl.when(section == 0)
    def _():
        for load in loads:
            load.start()

    @pl.when(lax.rem(section, 2) == 1)
    def _():
        pl.semaphore_wait(turn_sem, 1)

    own = [
        pltpu.make_async_copy(wqkv_ref, wq.at[z, xl, y], own_sem.at[0]),
        pltpu.make_async_copy(wout_ref, wo.at[z, xl, y], own_sem.at[1]),
    ]
    swaps = []
    for array, (ref, whole) in enumerate(((wqkv_ref, wq), (wout_ref, wo))):
        swaps.append(
            pltpu.make_async_remote_copy(
                src_ref=ref,
                dst_ref=whole.at[z, xl, y],
                send_sem=swap_send.at[array],
                recv_sem=swap_recv.at[array],
                device_id=across,
                device_id_type=MESH,
            )
        )
    for copy in own + swaps:
        copy.start()

    @pl.when(section == 0)
    def _():
        for load in loads:
            load.wait()
        group = 8

        @pl.loop(0, VIDS)
        def _(vid):
            for tan in range(2):
                spread(plain.at[tan, vid], tall, 0)

                @pl.loop(0, count // group)
                def _(i):
                    first = pl.multiple_of(i * group, group)
                    row = pl.multiple_of(first * NP * KT, group * NP * KT)
                    staged[vid, pl.ds(first, group), tan] = (
                        tall[pl.ds(row, group * NP * KT), :]
                        .astype(BF16)
                        .reshape(group, NP, KT, HEAD)
                    )

            exchange(vid, staged, entering, x_send, x_recv)

    for copy in own:
        copy.wait()
    for copy in swaps:
        copy.wait()

    gather = Gather(sizes, section, coords, wq, wo, ring_send, ring_recv)
    y_first, z_first = gather.ring(0, 0), gather.ring(1, 0)
    run(z_first, 1)
    run(y_first, 1)
    run(y_first, 1)
    run(z_first, 1)
    run(y_first)
    run(z_first)
    z_last, y_last = gather.ring(0, 1), gather.ring(1, 1)
    run(z_last, 1)
    run(y_last, 1)
    run(z_last, 1)
    run(z_last, 1)
    run(y_last, 1)
    run(z_last)
    run(y_last)
    gather.finish()

    @pl.when(lax.rem(section, 2) == 0)
    def _():
        pl.semaphore_signal(
            turn_sem, inc=1, device_id=(section + 1, me), device_id_type=MESH
        )

    def onward(vid):
        return pltpu.make_async_remote_copy(
            src_ref=leaving.at[vid],
            dst_ref=entering.at[vid],
            send_sem=pass_send.at[vid],
            recv_sem=pass_recv.at[vid],
            device_id=(lax.rem(section + 1, sections), me),
            device_id_type=MESH,
        )

    @pl.loop(0, VIDS)
    def _(vid):
        @pl.when(section == 0)
        def _():
            exchange_came(vid, staged, entering, x_recv)

        @pl.when(section > 0)
        def _():
            onward(vid).wait_recv()

        block_step(
            vid, entering, leaving, wq, wo, gains_ref, mods_ref, dmods_ref, tall, flat, att
        )

        @pl.when(section < sections - 1)
        def _():
            onward(vid).start()

        exchange(vid, leaving, returned, out_send, out_recv)

    group = 8

    def stores(vid):
        return [
            pltpu.make_async_copy(plain.at[tan, vid], ref.at[vid], store_sem.at[tan, vid])
            for tan, ref in enumerate((out_ref, tan_ref))
        ]

    @pl.loop(0, VIDS)
    def _(vid):
        exchange_came(vid, leaving, returned, out_recv)
        for tan, store in enumerate(stores(vid)):

            @pl.loop(0, count // group)
            def _(i):
                first = pl.multiple_of(i * group, group)
                row = pl.multiple_of(first * NP * KT, group * NP * KT)
                tall[pl.ds(row, group * NP * KT), :] = (
                    returned[vid, pl.ds(first, group), tan]
                    .reshape(group * NP * KT, HEAD)
                    .astype(F32)
                )

            for k in range(KT):
                plain[tan, vid, :, k * HEAD : (k + 1) * HEAD] = tall[
                    pl.ds(k, count * NP, stride=KT), :
                ].astype(BF16)
            store.start()

    for vid in range(VIDS):
        for store in stores(vid):
            store.wait()
        exchange_sent(vid, leaving, returned, out_send, out_recv)

        @pl.when(section == 0)
        def _():
            exchange_sent(vid, staged, entering, x_send, x_recv)

        @pl.when(section < sections - 1)
        def _():
            onward(vid).wait_send()


def shards(sizes, x_in, x_tan, t_index, w_qkv, w_out, qk_gain, mod_amp, mod_freq, mod_phase):
    nz, nx, ny = sizes
    count = nz * nx * ny
    sections = lax.axis_size("section")
    places = x_in.shape[2]
    time_value = (t_index.astype(F32) + 0.5) * (math.pi / (2.0 * T_STEPS))
    mods, dmods = timing(mod_amp, mod_freq, mod_phase, time_value[:, None, None])
    mods = mods.reshape(VIDS, 3, KT, HEAD)
    dmods = dmods.reshape(VIDS, 3, KT, HEAD)
    anywhere = pl.BlockSpec(memory_space=pl.ANY)
    inside = pl.BlockSpec(memory_space=pltpu.VMEM)
    result = jax.ShapeDtypeStruct((VIDS, places, D), BF16)
    unit = (VIDS, F, 2, NP, KT, HEAD)
    dma = pltpu.SemaphoreType.DMA
    out, tan = pl.pallas_call(
        functools.partial(kernel, sizes, sections),
        out_shape=(result, result),
        in_specs=[anywhere] * 4 + [inside] * 3,
        out_specs=(anywhere, anywhere),
        scratch_shapes=[
            pltpu.VMEM((nz, nx, ny, D // count, 3 * HD), BF16),
            pltpu.VMEM((nz, nx, ny, HD // count, D), BF16),
            pltpu.VMEM((2, VIDS, places, D), BF16),
            pltpu.VMEM(unit, BF16),
            pltpu.VMEM(unit, BF16),
            pltpu.VMEM(unit, BF16),
            pltpu.VMEM(unit, BF16),
            pltpu.VMEM((ROWS * KT, HEAD), F32),
            pltpu.VMEM((ROWS, D), BF16),
            pltpu.VMEM((ROWS, HD), BF16),
            dma((2,)),
            dma((2,)),
            dma((2,)),
            dma((2,)),
            dma((16, 4)),
            dma((16, 4)),
            dma((VIDS,)),
            dma((VIDS,)),
            dma((VIDS,)),
            dma((VIDS,)),
            dma((VIDS,)),
            dma((VIDS,)),
            dma((2, VIDS)),
            pltpu.SemaphoreType.REGULAR,
        ],
        compiler_params=pltpu.CompilerParams(
            has_side_effects=True, vmem_limit_bytes=48 * 1024 * 1024
        ),
        name="blocks",
    )(
        x_in.reshape(VIDS, places, D),
        x_tan.reshape(VIDS, places, D),
        w_qkv[0],
        w_out[0],
        qk_gain[0],
        mods,
        dmods,
    )
    return (out[None, :, None], tan[None, :, None])


def solution(mesh):
    count = mesh.shape["seq"]
    sizes = (count // 8, 2, 4)
    placed = (
        P(None, "seq", None, None),
        P(None, "seq", None, None),
        P(),
        P("section", "seq", None),
        P("section", "seq", None),
        P("section", None, None),
        P("section", None, None),
        P("section", None, None),
        P("section", None, None),
    )
    return jax.shard_map(
        functools.partial(shards, sizes),
        mesh=mesh,
        in_specs=placed,
        out_specs=(P("section", None, "seq", None, None), P("section", None, "seq", None, None)),
        check_vma=False,
    )
```

```python
import functools
import math

import jax
import jax.numpy as jnp
from jax import lax
from jax.experimental import pallas as pl
from jax.experimental.pallas import tpu as pltpu
from jax.sharding import PartitionSpec as P

HEADS = 8
HEAD = 128
T_STEPS = 1000
D = 2048
KT = D // HEAD
HD = HEADS * HEAD
F = 64
NP = 2
VIDS = 2
ROWS = 2 * NP * F
HALF = ROWS // 2
EPS = 1e-06
F32 = jnp.float32
BF16 = jnp.bfloat16
MESH = pl.DeviceIdType.MESH


def timing(amp, freq, phase, time_value):
    angle = freq * time_value + phase
    return (amp * jnp.sin(angle), amp * freq * jnp.cos(angle))


class Gather:
    def __init__(self, sizes, section, coords, wq, wo, send, recv):
        self.sizes, self.section, self.coords = sizes, section, coords
        self.wq, self.wo, self.send, self.recv = wq, wo, send, recv
        self.live = []

    def peer(self, axis, by):
        z, xl, y = self.coords
        nz, nx, ny = self.sizes
        if axis == "z":
            z = lax.rem(z + by + nz, nz)
        elif axis == "y":
            y = lax.rem(y + by + ny, ny)
        else:
            xl = nx - 1 - xl
        return (self.section, (z * nx + xl) * ny + y)

    def parts(self, stream, z, xl, y):
        if stream == 0:
            return (
                self.wq.at[z, xl, y, pl.ds(0, 16), :],
                self.wo.at[z, xl, y, :, pl.ds(0, D // 2)],
            )
        return (
            self.wq.at[z, xl, y, pl.ds(16, 16), :],
            self.wo.at[z, xl, y, :, pl.ds(D // 2, D // 2)],
        )

    def block(self, stream, phase, index, half):
        z, _, y = self.coords
        xl = slice(None) if half is None else half
        if (stream, phase) == (0, 0):
            return self.parts(0, z, xl, index)
        if (stream, phase) == (0, 1):
            return self.parts(0, index, xl, slice(None))
        if (stream, phase) == (1, 0):
            return self.parts(1, index, xl, y)
        return self.parts(1, slice(None), xl, index)

    def ring(self, stream, phase):
        axis = "y" if (stream == 0) == (phase == 0) else "z"
        size = self.sizes[2] if axis == "y" else self.sizes[0]
        me = self.coords[2] if axis == "y" else self.coords[0]
        last = size // 2
        arriving = []
        for step in range(last):
            for way in (0, 1):
                by = 1 if way == 0 else -1
                index = lax.rem(me - by * step + size, size)
                half = None if step < last - 1 else way
                for array, ref in enumerate(self.block(stream, phase, index, half)):
                    sem = ((stream * 2 + phase) * 2 + way) * 2 + array
                    copy = pltpu.make_async_remote_copy(
                        src_ref=ref,
                        dst_ref=ref,
                        send_sem=self.send.at[sem, step],
                        recv_sem=self.recv.at[sem, step],
                        device_id=self.peer(axis, by),
                        device_id_type=MESH,
                    )
                    copy.start()
                    self.live.append(copy)
                came = lax.rem(me - by * (step + 1) + size, size)
                for array, ref in enumerate(self.block(stream, phase, came, half)):
                    sem = ((stream * 2 + phase) * 2 + way) * 2 + array
                    arriving.append(
                        pltpu.make_async_remote_copy(
                            src_ref=ref,
                            dst_ref=ref,
                            send_sem=self.send.at[sem, step],
                            recv_sem=self.recv.at[sem, step],
                            device_id=self.peer(axis, by),
                            device_id_type=MESH,
                        )
                    )
            yield
            for copy in arriving:
                copy.wait_recv()
            arriving = []

    def finish(self):
        for copy in self.live:
            copy.wait_send()


def run(generator, steps=None):
    while steps is None or steps > 0:
        if next(generator, "end") == "end":
            return
        steps = None if steps is None else steps - 1


def spread(source, tall, start):
    count = source.shape[0]
    for k in range(KT):
        tall[pl.ds(start + k, count, stride=KT), :] = source[:, k * HEAD : (k + 1) * HEAD].astype(
            F32
        )


def normalize(values, tangents, gain):
    inverse = lax.rsqrt(jnp.mean(values * values, axis=-1, keepdims=True) + EPS)
    cross = jnp.mean(values * tangents, axis=-1, keepdims=True)
    scaled = values * inverse
    return (
        (scaled * gain).astype(BF16),
        ((inverse * tangents - values * inverse**3 * cross) * gain).astype(BF16),
    )


def attend(q2, k2, v2, gains_ref):
    factor = 1.0 / math.sqrt(HEAD)
    qn, dqn = normalize(q2[:HALF], q2[HALF:], gains_ref[0:1, :])
    kn, dkn = normalize(k2[:HALF], k2[HALF:], gains_ref[1:2, :])
    queries = jnp.concatenate([qn, dqn], axis=0)
    keys = jnp.concatenate([kn, dkn], axis=0)
    scores = lax.dot_general(
        queries, keys, (((1,), (1,)), ((), ())), preferred_element_type=F32
    )
    score = scores[:HALF, :HALF] * factor
    dscore = (scores[HALF:, :HALF] + scores[:HALF, HALF:]) * factor
    same = (lax.broadcasted_iota(jnp.int32, (HALF, HALF), 0) < F) == (
        lax.broadcasted_iota(jnp.int32, (HALF, HALF), 1) < F
    )
    expo = jnp.where(same, jnp.exp(score), 0.0)
    prob = expo / jnp.sum(expo, axis=-1, keepdims=True)
    growth = prob * dscore
    dprob = growth - prob * jnp.sum(growth, axis=-1, keepdims=True)
    probs = jnp.concatenate([prob.astype(BF16), dprob.astype(BF16)], axis=0)
    values = jnp.concatenate([v2[:HALF].astype(BF16), v2[HALF:].astype(BF16)], axis=1)
    mixed = jnp.dot(probs, values, preferred_element_type=F32)
    return mixed[:HALF, :HEAD], mixed[:HALF, HEAD:] + mixed[HALF:, :HEAD]


def block_step(vid, entering, leaving, wq, wo, gains_ref, mods_ref, dmods_ref, tall, flat, att):
    group = 8
    groups = F // group

    @pl.loop(0, NP * groups)
    def _(i):
        pos = i // groups
        first = pl.multiple_of((i % groups) * group, group)
        hidden = entering[vid, pl.ds(first, group), 0, pos].astype(F32)
        tangent = entering[vid, pl.ds(first, group), 1, pos].astype(F32)

        def mean(values):
            return jnp.sum(
                jnp.sum(values, axis=1, keepdims=True), axis=2, keepdims=True
            ) * (1.0 / D)

        inverse = lax.rsqrt(mean(hidden * hidden) + EPS)
        cross = mean(hidden * tangent)
        normed = hidden * inverse
        dnormed = inverse * tangent - hidden * inverse**3 * cross
        scale = 1.0 + mods_ref[vid, 1][None]
        modulated = normed * scale + mods_ref[vid, 0][None]
        dmodulated = dnormed * scale + normed * dmods_ref[vid, 1][None] + dmods_ref[vid, 0][None]
        row = pl.multiple_of((pos * F + first) * KT, group * KT)
        tall[pl.ds(row, group * KT), :] = modulated.reshape(group * KT, HEAD)
        tall[pl.ds(row + HALF * KT, group * KT), :] = dmodulated.reshape(group * KT, HEAD)

    for k in range(KT):
        flat[:, k * HEAD : (k + 1) * HEAD] = tall[pl.ds(k, ROWS, stride=KT), :].astype(BF16)

    @pl.loop(0, HEADS // 2)
    def _(pair):
        def third(number):
            column = pl.multiple_of(number * HD + pair * 2 * HEAD, 2 * HEAD)
            weights = wq[:, :, :, :, pl.ds(column, 2 * HEAD)].reshape(D, 2 * HEAD)
            return jnp.dot(flat[...], weights, preferred_element_type=F32)

        q2, k2, v2 = third(0), third(1), third(2)
        for one in range(2):
            lanes = slice(one * HEAD, (one + 1) * HEAD)
            output, doutput = attend(q2[:, lanes], k2[:, lanes], v2[:, lanes], gains_ref)
            column = pl.multiple_of((pair * 2 + one) * HEAD, HEAD)
            att[:HALF, pl.ds(column, HEAD)] = output.astype(BF16)
            att[HALF:, pl.ds(column, HEAD)] = doutput.astype(BF16)

    @pl.loop(0, KT // 2)
    def _(n):
        column = pl.multiple_of(n * 2 * HEAD, 2 * HEAD)
        weights = wo[:, :, :, :, pl.ds(column, 2 * HEAD)].reshape(HD, 2 * HEAD)
        y = jnp.dot(att[...], weights, preferred_element_type=F32)
        tall[pl.ds(2 * n, ROWS, stride=KT), :] = y[:, :HEAD]
        tall[pl.ds(2 * n + 1, ROWS, stride=KT), :] = y[:, HEAD:]

    @pl.loop(0, NP * groups)
    def _(i):
        pos = i // groups
        first = pl.multiple_of((i % groups) * group, group)
        row = pl.multiple_of((pos * F + first) * KT, group * KT)
        y = tall[pl.ds(row, group * KT), :].reshape(group, KT, HEAD)
        dy = tall[pl.ds(row + HALF * KT, group * KT), :].reshape(group, KT, HEAD)
        hidden = entering[vid, pl.ds(first, group), 0, pos].astype(F32)
        tangent = entering[vid, pl.ds(first, group), 1, pos].astype(F32)
        gate = mods_ref[vid, 2][None]
        dgate = dmods_ref[vid, 2][None]
        leaving[vid, pl.ds(first, group), 0, pos] = (hidden + gate * y).astype(BF16)
        leaving[vid, pl.ds(first, group), 1, pos] = (tangent + dgate * y + gate * dy).astype(BF16)


def kernel(
    sizes,
    sections,
    x_ref,
    t_ref,
    wqkv_ref,
    wout_ref,
    gains_ref,
    mods_ref,
    dmods_ref,
    out_ref,
    tan_ref,
    wq,
    wo,
    plain,
    staged,
    entering,
    leaving,
    returned,
    tall,
    flat,
    att,
    load_sem,
    own_sem,
    swap_send,
    swap_recv,
    ring_send,
    ring_recv,
    x_send,
    x_recv,
    pass_send,
    pass_recv,
    out_send,
    out_recv,
    store_sem,
):
    nz, nx, ny = sizes
    count = nz * nx * ny
    section = lax.axis_index("section")
    me = lax.axis_index("seq")
    coords = (me // (nx * ny), (me // ny) % nx, me % ny)
    z, xl, y = coords
    other = nx - 1 - xl
    across = (section, (z * nx + other) * ny + y)
    neighbour = (section, lax.rem(me + 1, count))

    def exchange(vid, source, target, send, recv):
        pltpu.make_async_copy(source.at[vid, me], target.at[vid, me], recv.at[vid]).start()

        @pl.loop(1, count)
        def _(by):
            to = lax.rem(me + by, count)
            pltpu.make_async_remote_copy(
                src_ref=source.at[vid, to],
                dst_ref=target.at[vid, me],
                send_sem=send.at[vid],
                recv_sem=recv.at[vid],
                device_id=(section, to),
                device_id_type=MESH,
            ).start()

    def exchange_came(vid, source, target, recv):
        pltpu.make_async_copy(source.at[vid], target.at[vid], recv.at[vid]).wait()

    def exchange_sent(vid, source, target, send, recv):
        pltpu.make_async_remote_copy(
            src_ref=source.at[vid, pl.ds(0, count - 1)],
            dst_ref=target.at[vid, pl.ds(0, count - 1)],
            send_sem=send.at[vid],
            recv_sem=recv.at[vid],
            device_id=neighbour,
            device_id_type=MESH,
        ).wait_send()

    loads = [
        pltpu.make_async_copy(ref, plain.at[tan], load_sem.at[tan])
        for tan, ref in enumerate((x_ref, t_ref))
    ]

    @pl.when(section == 0)
    def _():
        for load in loads:
            load.start()

    own = [
        pltpu.make_async_copy(wqkv_ref, wq.at[z, xl, y], own_sem.at[0]),
        pltpu.make_async_copy(wout_ref, wo.at[z, xl, y], own_sem.at[1]),
    ]
    swaps = []
    for array, (ref, whole) in enumerate(((wqkv_ref, wq), (wout_ref, wo))):
        swaps.append(
            pltpu.make_async_remote_copy(
                src_ref=ref,
                dst_ref=whole.at[z, xl, y],
                send_sem=swap_send.at[array],
                recv_sem=swap_recv.at[array],
                device_id=across,
                device_id_type=MESH,
            )
        )
    for copy in own + swaps:
        copy.start()

    @pl.when(section == 0)
    def _():
        for load in loads:
            load.wait()
        group = 8

        @pl.loop(0, VIDS)
        def _(vid):
            for tan in range(2):
                spread(plain.at[tan, vid], tall, 0)

                @pl.loop(0, count // group)
                def _(i):
                    first = pl.multiple_of(i * group, group)
                    row = pl.multiple_of(first * NP * KT, group * NP * KT)
                    staged[vid, pl.ds(first, group), tan] = (
                        tall[pl.ds(row, group * NP * KT), :]
                        .astype(BF16)
                        .reshape(group, NP, KT, HEAD)
                    )

            exchange(vid, staged, entering, x_send, x_recv)

    for copy in own:
        copy.wait()
    for copy in swaps:
        copy.wait()

    gather = Gather(sizes, section, coords, wq, wo, ring_send, ring_recv)
    y_first, z_first = gather.ring(0, 0), gather.ring(1, 0)
    run(z_first, 1)
    run(y_first, 1)
    run(y_first, 1)
    run(z_first, 1)
    run(y_first)
    run(z_first)
    z_last, y_last = gather.ring(0, 1), gather.ring(1, 1)
    run(z_last, 1)
    run(y_last, 1)
    run(z_last, 1)
    run(z_last, 1)
    run(y_last, 1)
    run(z_last)
    run(y_last)
    gather.finish()

    def onward(vid):
        return pltpu.make_async_remote_copy(
            src_ref=leaving.at[vid],
            dst_ref=entering.at[vid],
            send_sem=pass_send.at[vid],
            recv_sem=pass_recv.at[vid],
            device_id=(lax.rem(section + 1, sections), me),
            device_id_type=MESH,
        )

    @pl.loop(0, VIDS)
    def _(vid):
        @pl.when(section == 0)
        def _():
            exchange_came(vid, staged, entering, x_recv)

        @pl.when(section > 0)
        def _():
            onward(vid).wait_recv()

        block_step(
            vid, entering, leaving, wq, wo, gains_ref, mods_ref, dmods_ref, tall, flat, att
        )

        @pl.when(section < sections - 1)
        def _():
            onward(vid).start()

        exchange(vid, leaving, returned, out_send, out_recv)

    group = 8

    def stores(vid):
        return [
            pltpu.make_async_copy(plain.at[tan, vid], ref.at[vid], store_sem.at[tan, vid])
            for tan, ref in enumerate((out_ref, tan_ref))
        ]

    @pl.loop(0, VIDS)
    def _(vid):
        exchange_came(vid, leaving, returned, out_recv)
        for tan, store in enumerate(stores(vid)):

            @pl.loop(0, count // group)
            def _(i):
                first = pl.multiple_of(i * group, group)
                row = pl.multiple_of(first * NP * KT, group * NP * KT)
                tall[pl.ds(row, group * NP * KT), :] = (
                    returned[vid, pl.ds(first, group), tan]
                    .reshape(group * NP * KT, HEAD)
                    .astype(F32)
                )

            for k in range(KT):
                plain[tan, vid, :, k * HEAD : (k + 1) * HEAD] = tall[
                    pl.ds(k, count * NP, stride=KT), :
                ].astype(BF16)
            store.start()

    for vid in range(VIDS):
        for store in stores(vid):
            store.wait()
        exchange_sent(vid, leaving, returned, out_send, out_recv)

        @pl.when(section == 0)
        def _():
            exchange_sent(vid, staged, entering, x_send, x_recv)

        @pl.when(section < sections - 1)
        def _():
            onward(vid).wait_send()


def shards(sizes, x_in, x_tan, t_index, w_qkv, w_out, qk_gain, mod_amp, mod_freq, mod_phase):
    nz, nx, ny = sizes
    count = nz * nx * ny
    sections = lax.axis_size("section")
    places = x_in.shape[2]
    time_value = (t_index.astype(F32) + 0.5) * (math.pi / (2.0 * T_STEPS))
    mods, dmods = timing(mod_amp, mod_freq, mod_phase, time_value[:, None, None])
    mods = mods.reshape(VIDS, 3, KT, HEAD)
    dmods = dmods.reshape(VIDS, 3, KT, HEAD)
    anywhere = pl.BlockSpec(memory_space=pl.ANY)
    inside = pl.BlockSpec(memory_space=pltpu.VMEM)
    result = jax.ShapeDtypeStruct((VIDS, places, D), BF16)
    unit = (VIDS, F, 2, NP, KT, HEAD)
    dma = pltpu.SemaphoreType.DMA
    out, tan = pl.pallas_call(
        functools.partial(kernel, sizes, sections),
        out_shape=(result, result),
        in_specs=[anywhere] * 4 + [inside] * 3,
        out_specs=(anywhere, anywhere),
        scratch_shapes=[
            pltpu.VMEM((nz, nx, ny, D // count, 3 * HD), BF16),
            pltpu.VMEM((nz, nx, ny, HD // count, D), BF16),
            pltpu.VMEM((2, VIDS, places, D), BF16),
            pltpu.VMEM(unit, BF16),
            pltpu.VMEM(unit, BF16),
            pltpu.VMEM(unit, BF16),
            pltpu.VMEM(unit, BF16),
            pltpu.VMEM((ROWS * KT, HEAD), F32),
            pltpu.VMEM((ROWS, D), BF16),
            pltpu.VMEM((ROWS, HD), BF16),
            dma((2,)),
            dma((2,)),
            dma((2,)),
            dma((2,)),
            dma((16, 4)),
            dma((16, 4)),
            dma((VIDS,)),
            dma((VIDS,)),
            dma((VIDS,)),
            dma((VIDS,)),
            dma((VIDS,)),
            dma((VIDS,)),
            dma((2, VIDS)),
        ],
        compiler_params=pltpu.CompilerParams(
            has_side_effects=True, vmem_limit_bytes=48 * 1024 * 1024
        ),
        name="blocks",
    )(
        x_in.reshape(VIDS, places, D),
        x_tan.reshape(VIDS, places, D),
        w_qkv[0],
        w_out[0],
        qk_gain[0],
        mods,
        dmods,
    )
    return (out[None, :, None], tan[None, :, None])


def solution(mesh):
    count = mesh.shape["seq"]
    sizes = (count // 8, 2, 4)
    placed = (
        P(None, "seq", None, None),
        P(None, "seq", None, None),
        P(),
        P("section", "seq", None),
        P("section", "seq", None),
        P("section", None, None),
        P("section", None, None),
        P("section", None, None),
        P("section", None, None),
    )
    return jax.shard_map(
        functools.partial(shards, sizes),
        mesh=mesh,
        in_specs=placed,
        out_specs=(P("section", None, "seq", None, None), P("section", None, "seq", None, None)),
        check_vma=False,
    )
```

```python
import functools
import math

import jax
import jax.numpy as jnp
from jax import lax
from jax.experimental import pallas as pl
from jax.experimental.pallas import tpu as pltpu
from jax.sharding import PartitionSpec as P

HEADS = 8
HEAD = 128
T_STEPS = 1000
D = 2048
KT = D // HEAD
HD = HEADS * HEAD
F = 64
NP = 2
VIDS = 2
ROWS = 2 * NP * F
HALF = ROWS // 2
EPS = 1e-06
F32 = jnp.float32
BF16 = jnp.bfloat16
MESH = pl.DeviceIdType.MESH
ROWS_OUT = 16
PACKED = 2 * 3 * HD + D
SPLIT = 3456


def timing(amp, freq, phase, time_value):
    angle = freq * time_value + phase
    return (amp * jnp.sin(angle), amp * freq * jnp.cos(angle))


class Gather:
    def __init__(self, sizes, section, coords, weights, send, recv):
        self.sizes, self.section, self.coords = sizes, section, coords
        self.weights, self.send, self.recv = weights, send, recv
        self.live = []
        self.sems = 0
        self.rings = {}

    def peer(self, axis, by):
        z, xl, y = self.coords
        nz, nx, ny = self.sizes
        if axis == "z":
            z = lax.rem(z + by + nz, nz)
        else:
            y = lax.rem(y + by + ny, ny)
        return (self.section, (z * nx + xl) * ny + y)

    def ring(self, axis, columns, fixed):
        size = self.sizes[0] if axis == "z" else self.sizes[2]
        me = self.coords[0] if axis == "z" else self.coords[2]
        last = size // 2
        first_sem = self.sems
        self.sems += 2 * last

        def copy(way, step, index):
            half = slice(None) if step < last - 1 else way
            z, y = (index, fixed) if axis == "z" else (fixed, index)
            ref = self.weights.at[z, half, y, :, columns]
            sem = first_sem + 2 * step + way
            return pltpu.make_async_remote_copy(
                src_ref=ref,
                dst_ref=ref,
                send_sem=self.send.at[sem],
                recv_sem=self.recv.at[sem],
                device_id=self.peer(axis, 1 - 2 * way),
                device_id_type=MESH,
            )

        def at(way, step):
            return lax.rem(me - (1 - 2 * way) * step + size, size)

        for step in range(last):
            for way in (0, 1):
                sent = copy(way, step, at(way, step))
                sent.start()
                self.live.append(sent)
            yield
            for way in (0, 1):
                copy(way, step, at(way, step + 1)).wait_recv()

    def build(self):
        z, _, y = self.coords
        nz, _, ny = self.sizes
        early, late = pl.ds(0, SPLIT), pl.ds(SPLIT, PACKED - SPLIT)
        self.rings["a"] = self.ring("y", early, z)
        self.rings["b"] = self.ring("z", late, y)
        for by in range(ny):
            self.rings["az", by] = self.ring("z", early, lax.rem(y + by, ny))
        for by in range(nz):
            self.rings["by", by] = self.ring("y", late, lax.rem(z + by, nz))

    def go(self, *names):
        for name in names:
            next(self.rings[name], None)

    def finish(self):
        for copy in self.live:
            copy.wait_send()


def spread(source, tall, start):
    count = source.shape[0]
    for k in range(KT):
        tall[pl.ds(start + k, count, stride=KT), :] = source[:, k * HEAD : (k + 1) * HEAD].astype(
            F32
        )


def normalize(values, tangents, gain):
    inverse = lax.rsqrt(jnp.mean(values * values, axis=-1, keepdims=True) + EPS)
    cross = jnp.mean(values * tangents, axis=-1, keepdims=True)
    scaled = values * inverse
    return (
        (scaled * gain).astype(BF16),
        ((inverse * tangents - values * inverse**3 * cross) * gain).astype(BF16),
    )


def attend(q2, k2, v2, gains_ref):
    factor = 1.0 / math.sqrt(HEAD)
    qn, dqn = normalize(q2[:HALF], q2[HALF:], gains_ref[0:1, :])
    kn, dkn = normalize(k2[:HALF], k2[HALF:], gains_ref[1:2, :])
    queries = jnp.concatenate([qn, dqn], axis=0)
    keys = jnp.concatenate([kn, dkn], axis=0)
    scores = lax.dot_general(
        queries, keys, (((1,), (1,)), ((), ())), preferred_element_type=F32
    )
    score = scores[:HALF, :HALF] * factor
    dscore = (scores[HALF:, :HALF] + scores[:HALF, HALF:]) * factor
    same = (lax.broadcasted_iota(jnp.int32, (HALF, HALF), 0) < F) == (
        lax.broadcasted_iota(jnp.int32, (HALF, HALF), 1) < F
    )
    expo = jnp.where(same, jnp.exp(score), 0.0)
    prob = expo / jnp.sum(expo, axis=-1, keepdims=True)
    growth = prob * dscore
    dprob = growth - prob * jnp.sum(growth, axis=-1, keepdims=True)
    probs = jnp.concatenate([prob.astype(BF16), dprob.astype(BF16)], axis=0)
    values = jnp.concatenate([v2[:HALF].astype(BF16), v2[HALF:].astype(BF16)], axis=1)
    mixed = jnp.dot(probs, values, preferred_element_type=F32)
    return mixed[:HALF, :HEAD], mixed[:HALF, HEAD:] + mixed[HALF:, :HEAD]


def block_step(vid, entering, leaving, weights, gains_ref, mods_ref, dmods_ref, tall, flat, att):
    group = 8
    groups = F // group

    @pl.loop(0, NP * groups)
    def _(i):
        pos = i // groups
        first = pl.multiple_of((i % groups) * group, group)
        hidden = entering[vid, pl.ds(first, group), 0, pos].astype(F32)
        tangent = entering[vid, pl.ds(first, group), 1, pos].astype(F32)

        def mean(values):
            return jnp.sum(
                jnp.sum(values, axis=1, keepdims=True), axis=2, keepdims=True
            ) * (1.0 / D)

        inverse = lax.rsqrt(mean(hidden * hidden) + EPS)
        cross = mean(hidden * tangent)
        normed = hidden * inverse
        dnormed = inverse * tangent - hidden * inverse**3 * cross
        scale = 1.0 + mods_ref[vid, 1][None]
        modulated = normed * scale + mods_ref[vid, 0][None]
        dmodulated = dnormed * scale + normed * dmods_ref[vid, 1][None] + dmods_ref[vid, 0][None]
        row = pl.multiple_of((pos * F + first) * KT, group * KT)
        tall[pl.ds(row, group * KT), :] = modulated.reshape(group * KT, HEAD)
        tall[pl.ds(row + HALF * KT, group * KT), :] = dmodulated.reshape(group * KT, HEAD)

    for k in range(KT):
        flat[:, k * HEAD : (k + 1) * HEAD] = tall[pl.ds(k, ROWS, stride=KT), :].astype(BF16)

    @pl.loop(0, HEADS // 2)
    def _(pair):
        def third(number):
            column = pl.multiple_of(number * HD + pair * 2 * HEAD, 2 * HEAD)
            halves = [
                weights[:, :, :, :, pl.ds(column + lower * 3 * HD, 2 * HEAD)].reshape(
                    F, 1, ROWS_OUT, 2 * HEAD
                )
                for lower in range(2)
            ]
            matrix = jnp.concatenate(halves, axis=1).reshape(D, 2 * HEAD)
            return jnp.dot(flat[...], matrix, preferred_element_type=F32)

        q2, k2, v2 = third(0), third(1), third(2)
        for one in range(2):
            lanes = slice(one * HEAD, (one + 1) * HEAD)
            output, doutput = attend(q2[:, lanes], k2[:, lanes], v2[:, lanes], gains_ref)
            column = pl.multiple_of((pair * 2 + one) * HEAD, HEAD)
            att[:HALF, pl.ds(column, HEAD)] = output.astype(BF16)
            att[HALF:, pl.ds(column, HEAD)] = doutput.astype(BF16)

    @pl.loop(0, KT // 2)
    def _(n):
        column = pl.multiple_of(2 * 3 * HD + n * 2 * HEAD, 2 * HEAD)
        matrix = weights[:, :, :, :, pl.ds(column, 2 * HEAD)].reshape(HD, 2 * HEAD)
        y = jnp.dot(att[...], matrix, preferred_element_type=F32)
        tall[pl.ds(2 * n, ROWS, stride=KT), :] = y[:, :HEAD]
        tall[pl.ds(2 * n + 1, ROWS, stride=KT), :] = y[:, HEAD:]

    @pl.loop(0, NP * groups)
    def _(i):
        pos = i // groups
        first = pl.multiple_of((i % groups) * group, group)
        row = pl.multiple_of((pos * F + first) * KT, group * KT)
        y = tall[pl.ds(row, group * KT), :].reshape(group, KT, HEAD)
        dy = tall[pl.ds(row + HALF * KT, group * KT), :].reshape(group, KT, HEAD)
        hidden = entering[vid, pl.ds(first, group), 0, pos].astype(F32)
        tangent = entering[vid, pl.ds(first, group), 1, pos].astype(F32)
        gate = mods_ref[vid, 2][None]
        dgate = dmods_ref[vid, 2][None]
        leaving[vid, pl.ds(first, group), 0, pos] = (hidden + gate * y).astype(BF16)
        leaving[vid, pl.ds(first, group), 1, pos] = (tangent + dgate * y + gate * dy).astype(BF16)


def kernel(
    sizes,
    sections,
    x_ref,
    t_ref,
    wqkv_ref,
    wout_ref,
    gains_ref,
    mods_ref,
    dmods_ref,
    out_ref,
    tan_ref,
    weights,
    plain,
    staged,
    relay,
    entering,
    leaving,
    returned,
    tall,
    flat,
    att,
    load_sem,
    own_sem,
    swap_send,
    swap_recv,
    ring_send,
    ring_recv,
    x_send,
    x_recv,
    relay_send,
    relay_recv,
    pass_send,
    pass_recv,
    out_send,
    out_recv,
    store_sem,
    turn_sem,
):
    nz, nx, ny = sizes
    count = nz * nx * ny
    section = lax.axis_index("section")
    me = lax.axis_index("seq")
    coords = (me // (nx * ny), (me // ny) % nx, me % ny)
    z, xl, y = coords
    first_half = section < 2

    def flip(index):
        return index + ny - 2 * ny * ((index // ny) % nx)

    across = flip(me)
    slot = jnp.where(first_half, me, across)
    neighbour = (section, lax.rem(me + 1, count))
    group = 8

    def exchange(source, row_of, target, place, send, recv):
        pltpu.make_async_copy(source.at[row_of(me)], target.at[place], recv).start()

        @pl.loop(1, count)
        def _(by):
            to = lax.rem(me + by, count)
            pltpu.make_async_remote_copy(
                src_ref=source.at[row_of(to)],
                dst_ref=target.at[place],
                send_sem=send,
                recv_sem=recv,
                device_id=(section, to),
                device_id_type=MESH,
            ).start()

    def exchange_came(source, target, recv):
        pltpu.make_async_copy(source, target, recv).wait()

    def exchange_sent(source, target, send, recv):
        pltpu.make_async_remote_copy(
            src_ref=source.at[pl.ds(0, count - 1)],
            dst_ref=target.at[pl.ds(0, count - 1)],
            send_sem=send,
            recv_sem=recv,
            device_id=neighbour,
            device_id_type=MESH,
        ).wait_send()

    video = section // 2
    loads = [
        pltpu.make_async_copy(ref.at[video], plain.at[tan, 0], load_sem.at[tan])
        for tan, ref in enumerate((x_ref, t_ref))
    ]
    leads = lax.rem(section, 2) == 0

    @pl.when(leads)
    def _():
        for load in loads:
            load.start()

    @pl.when(jnp.logical_not(leads))
    def _():
        pl.semaphore_wait(turn_sem, 1)

    own, swaps = [], []
    for part, (ref, first, width) in enumerate(
        (
            (wqkv_ref.at[pl.ds(0, ROWS_OUT)], 0, 3 * HD),
            (wqkv_ref.at[pl.ds(ROWS_OUT, ROWS_OUT)], 3 * HD, 3 * HD),
            (wout_ref, 6 * HD, D),
        )
    ):
        home = weights.at[z, xl, y, :, pl.ds(first, width)]
        own.append(pltpu.make_async_copy(ref, home, own_sem.at[part]))
        swaps.append(
            pltpu.make_async_remote_copy(
                src_ref=ref,
                dst_ref=home,
                send_sem=swap_send.at[part],
                recv_sem=swap_recv.at[part],
                device_id=(section, across),
                device_id_type=MESH,
            )
        )
    for copy in swaps + own:
        copy.start()

    @pl.when(leads)
    def _():
        for load in loads:
            load.wait()
        for tan in range(2):
            spread(plain.at[tan, 0], tall, 0)

            @pl.loop(0, count // group)
            def _(i):
                first = pl.multiple_of(i * group, group)
                row = pl.multiple_of(first * NP * KT, group * NP * KT)
                staged[pl.ds(first, group), tan] = (
                    tall[pl.ds(row, group * NP * KT), :]
                    .astype(BF16)
                    .reshape(group, NP, KT, HEAD)
                )

        @pl.when(first_half)
        def _():
            exchange(staged, lambda f: f, entering.at[0], me, x_send, x_recv)

        @pl.when(jnp.logical_not(first_half))
        def _():
            exchange(staged, flip, relay, me, x_send, x_recv)

    for copy in own + swaps:
        copy.wait()

    def relayed():
        return pltpu.make_async_remote_copy(
            src_ref=relay,
            dst_ref=entering.at[1],
            send_sem=relay_send,
            recv_sem=relay_recv,
            device_id=(0, across),
            device_id_type=MESH,
        )

    gather = Gather(sizes, section, coords, weights, ring_send, ring_recv)
    gather.build()
    go = gather.go
    go("b", "a", ("by", 0), ("az", 0))
    go("a", ("az", 1), ("az", 3))
    go("b", ("by", 1), ("by", 7))
    go("a", ("az", 2))
    go(("az", 0), ("by", 0))
    go("b", ("by", 2), ("by", 6))
    go(("az", 1), ("az", 3), ("by", 1), ("by", 7), ("az", 2))
    go("b", ("by", 3), ("by", 5))
    go(("az", 0), ("by", 0), ("az", 1), ("az", 3))
    go("b", ("by", 4))

    @pl.when(section == 2)
    def _():
        exchange_came(staged, relay, x_recv)
        relayed().start()

    go(("by", 2), ("by", 6), ("az", 2), ("by", 1), ("by", 7), ("az", 0))
    go(("by", 3), ("by", 5), ("az", 1), ("az", 3), ("by", 4), ("az", 2))

    @pl.when(leads)
    def _():
        pl.semaphore_signal(
            turn_sem, inc=1, device_id=(section + 1, me), device_id_type=MESH
        )

    go(("by", 2), ("by", 6), ("az", 0), ("by", 3), ("by", 5))
    go(("az", 1), ("az", 3), ("by", 4), ("az", 2))
    gather.finish()

    def onward(vid):
        return pltpu.make_async_remote_copy(
            src_ref=leaving.at[vid],
            dst_ref=entering.at[vid],
            send_sem=pass_send.at[vid],
            recv_sem=pass_recv.at[vid],
            device_id=(
                lax.rem(section + 1, sections),
                jnp.where(section == 1, across, me),
            ),
            device_id_type=MESH,
        )

    @pl.loop(0, VIDS)
    def _(vid):
        @pl.when(jnp.logical_and(section == 0, vid == 0))
        def _():
            exchange_came(staged, entering.at[0], x_recv)

        @pl.when(jnp.logical_and(section == 0, vid == 1))
        def _():
            relayed().wait_recv()

        @pl.when(section > 0)
        def _():
            onward(vid).wait_recv()

        block_step(vid, entering, leaving, weights, gains_ref, mods_ref, dmods_ref, tall, flat, att)

        @pl.when(section < sections - 1)
        def _():
            onward(vid).start()

        exchange(
            leaving.at[vid],
            lambda f: f,
            returned.at[vid],
            slot,
            out_send.at[vid],
            out_recv.at[vid],
        )

    def stores(vid):
        return [
            pltpu.make_async_copy(plain.at[tan, vid], ref.at[vid], store_sem.at[tan, vid])
            for tan, ref in enumerate((out_ref, tan_ref))
        ]

    @pl.loop(0, VIDS)
    def _(vid):
        exchange_came(leaving.at[vid], returned.at[vid], out_recv.at[vid])
        for tan, store in enumerate(stores(vid)):

            @pl.loop(0, count // group)
            def _(i):
                first = pl.multiple_of(i * group, group)
                row = pl.multiple_of(first * NP * KT, group * NP * KT)
                tall[pl.ds(row, group * NP * KT), :] = (
                    returned[vid, pl.ds(first, group), tan]
                    .reshape(group * NP * KT, HEAD)
                    .astype(F32)
                )

            for k in range(KT):
                plain[tan, vid, :, k * HEAD : (k + 1) * HEAD] = tall[
                    pl.ds(k, count * NP, stride=KT), :
                ].astype(BF16)
            store.start()

    for vid in range(VIDS):
        for store in stores(vid):
            store.wait()
        exchange_sent(
            leaving.at[vid], returned.at[vid], out_send.at[vid], out_recv.at[vid]
        )

        @pl.when(section < sections - 1)
        def _():
            onward(vid).wait_send()

    @pl.when(leads)
    def _():
        exchange_sent(staged, relay, x_send, x_recv)

    @pl.when(section == 2)
    def _():
        relayed().wait_send()


def shards(sizes, x_in, x_tan, t_index, w_qkv, w_out, qk_gain, mod_amp, mod_freq, mod_phase):
    nz, nx, ny = sizes
    count = nz * nx * ny
    sections = lax.axis_size("section")
    places = x_in.shape[2]
    time_value = (t_index.astype(F32) + 0.5) * (math.pi / (2.0 * T_STEPS))
    mods, dmods = timing(mod_amp, mod_freq, mod_phase, time_value[:, None, None])
    mods = mods.reshape(VIDS, 3, KT, HEAD)
    dmods = dmods.reshape(VIDS, 3, KT, HEAD)
    anywhere = pl.BlockSpec(memory_space=pl.ANY)
    inside = pl.BlockSpec(memory_space=pltpu.VMEM)
    result = jax.ShapeDtypeStruct((VIDS, places, D), BF16)
    unit = (F, 2, NP, KT, HEAD)
    rings = 2 * (ny // 2) * (1 + nz) + 2 * (nz // 2) * (1 + ny)
    dma = pltpu.SemaphoreType.DMA
    out, tan = pl.pallas_call(
        functools.partial(kernel, sizes, sections),
        out_shape=(result, result),
        in_specs=[anywhere] * 4 + [inside] * 3,
        out_specs=(anywhere, anywhere),
        scratch_shapes=[
            pltpu.VMEM((nz, nx, ny, ROWS_OUT, PACKED), BF16),
            pltpu.VMEM((2, VIDS, places, D), BF16),
            pltpu.VMEM(unit, BF16),
            pltpu.VMEM(unit, BF16),
            pltpu.VMEM((VIDS,) + unit, BF16),
            pltpu.VMEM((VIDS,) + unit, BF16),
            pltpu.VMEM((VIDS,) + unit, BF16),
            pltpu.VMEM((ROWS * KT, HEAD), F32),
            pltpu.VMEM((ROWS, D), BF16),
            pltpu.VMEM((ROWS, HD), BF16),
            dma((2,)),
            dma((3,)),
            dma((3,)),
            dma((3,)),
            dma((rings,)),
            dma((rings,)),
            dma,
            dma,
            dma,
            dma,
            dma((VIDS,)),
            dma((VIDS,)),
            dma((VIDS,)),
            dma((VIDS,)),
            dma((2, VIDS)),
            pltpu.SemaphoreType.REGULAR,
        ],
        compiler_params=pltpu.CompilerParams(
            has_side_effects=True, vmem_limit_bytes=48 * 1024 * 1024
        ),
        name="blocks",
    )(
        x_in.reshape(VIDS, places, D),
        x_tan.reshape(VIDS, places, D),
        w_qkv[0],
        w_out[0],
        qk_gain[0],
        mods,
        dmods,
    )
    return (out[None, :, None], tan[None, :, None])


def solution(mesh):
    count = mesh.shape["seq"]
    sizes = (count // 8, 2, 4)
    placed = (
        P(None, "seq", None, None),
        P(None, "seq", None, None),
        P(),
        P("section", "seq", None),
        P("section", "seq", None),
        P("section", None, None),
        P("section", None, None),
        P("section", None, None),
        P("section", None, None),
    )
    return jax.shard_map(
        functools.partial(shards, sizes),
        mesh=mesh,
        in_specs=placed,
        out_specs=(P("section", None, "seq", None, None), P("section", None, "seq", None, None)),
        check_vma=False,
    )
```

```python
import functools
import math

import jax
import jax.numpy as jnp
from jax import lax
from jax.experimental import pallas as pl
from jax.experimental.pallas import tpu as pltpu
from jax.sharding import PartitionSpec as P

HEADS = 8
HEAD = 128
T_STEPS = 1000
D = 2048
KT = D // HEAD
HD = HEADS * HEAD
F = 64
NP = 2
VIDS = 2
ROWS = 2 * NP * F
HALF = ROWS // 2
EPS = 1e-06
F32 = jnp.float32
BF16 = jnp.bfloat16
MESH = pl.DeviceIdType.MESH
ROWS_OUT = 16
PACKED = 2 * 3 * HD + D
SPLIT = 3456


def timing(amp, freq, phase, time_value):
    angle = freq * time_value + phase
    return (amp * jnp.sin(angle), amp * freq * jnp.cos(angle))


class Gather:
    def __init__(self, sizes, section, coords, weights, send, recv):
        self.sizes, self.section, self.coords = sizes, section, coords
        self.weights, self.send, self.recv = weights, send, recv
        self.live = []
        self.sems = 0
        self.rings = {}

    def peer(self, axis, by):
        z, xl, y = self.coords
        nz, nx, ny = self.sizes
        if axis == "z":
            z = lax.rem(z + by + nz, nz)
        else:
            y = lax.rem(y + by + ny, ny)
        return (self.section, (z * nx + xl) * ny + y)

    def ring(self, axis, columns, fixed):
        size = self.sizes[0] if axis == "z" else self.sizes[2]
        me = self.coords[0] if axis == "z" else self.coords[2]
        last = size // 2
        first_sem = self.sems
        self.sems += 2 * last

        def copy(way, step, index):
            half = slice(None) if step < last - 1 else way
            z, y = (index, fixed) if axis == "z" else (fixed, index)
            ref = self.weights.at[z, half, y, :, columns]
            sem = first_sem + 2 * step + way
            return pltpu.make_async_remote_copy(
                src_ref=ref,
                dst_ref=ref,
                send_sem=self.send.at[sem],
                recv_sem=self.recv.at[sem],
                device_id=self.peer(axis, 1 - 2 * way),
                device_id_type=MESH,
            )

        def at(way, step):
            return lax.rem(me - (1 - 2 * way) * step + size, size)

        for step in range(last):
            for way in (0, 1):
                sent = copy(way, step, at(way, step))
                sent.start()
                self.live.append(sent)
            yield
            for way in (0, 1):
                copy(way, step, at(way, step + 1)).wait_recv()

    def build(self):
        z, _, y = self.coords
        nz, _, ny = self.sizes
        early, late = pl.ds(0, SPLIT), pl.ds(SPLIT, PACKED - SPLIT)
        self.rings["a"] = self.ring("y", early, z)
        self.rings["b"] = self.ring("z", late, y)
        for by in range(ny):
            self.rings["az", by] = self.ring("z", early, lax.rem(y + by, ny))
        for by in range(nz):
            self.rings["by", by] = self.ring("y", late, lax.rem(z + by, nz))

    def go(self, *names):
        for name in names:
            next(self.rings[name], None)

    def finish(self):
        for copy in self.live:
            copy.wait_send()


def spread(source, tall, start):
    count = source.shape[0]
    for k in range(KT):
        tall[pl.ds(start + k, count, stride=KT), :] = source[:, k * HEAD : (k + 1) * HEAD].astype(
            F32
        )


def normalize(values, tangents, gain):
    inverse = lax.rsqrt(jnp.mean(values * values, axis=-1, keepdims=True) + EPS)
    cross = jnp.mean(values * tangents, axis=-1, keepdims=True)
    scaled = values * inverse
    return (
        (scaled * gain).astype(BF16),
        ((inverse * tangents - values * inverse**3 * cross) * gain).astype(BF16),
    )


def attend(q2, k2, v2, gains_ref):
    factor = 1.0 / math.sqrt(HEAD)
    qn, dqn = normalize(q2[:HALF], q2[HALF:], gains_ref[0:1, :])
    kn, dkn = normalize(k2[:HALF], k2[HALF:], gains_ref[1:2, :])
    queries = jnp.concatenate([qn, dqn], axis=0)
    keys = jnp.concatenate([kn, dkn], axis=0)
    scores = lax.dot_general(
        queries, keys, (((1,), (1,)), ((), ())), preferred_element_type=F32
    )
    score = scores[:HALF, :HALF] * factor
    dscore = (scores[HALF:, :HALF] + scores[:HALF, HALF:]) * factor
    same = (lax.broadcasted_iota(jnp.int32, (HALF, HALF), 0) < F) == (
        lax.broadcasted_iota(jnp.int32, (HALF, HALF), 1) < F
    )
    expo = jnp.where(same, jnp.exp(score), 0.0)
    prob = expo * (1.0 / jnp.sum(expo, axis=-1, keepdims=True))
    growth = prob * dscore
    dprob = growth - prob * jnp.sum(growth, axis=-1, keepdims=True)
    probs = jnp.concatenate([prob.astype(BF16), dprob.astype(BF16)], axis=0)
    values = jnp.concatenate([v2[:HALF].astype(BF16), v2[HALF:].astype(BF16)], axis=1)
    mixed = jnp.dot(probs, values, preferred_element_type=F32)
    return mixed[:HALF, :HEAD], mixed[:HALF, HEAD:] + mixed[HALF:, :HEAD]


def block_step(vid, entering, leaving, weights, gains_ref, mods_ref, dmods_ref, tall, flat, att):
    group = 8
    groups = F // group

    @pl.loop(0, NP * groups, unroll=2)
    def _(i):
        pos = i // groups
        first = pl.multiple_of((i % groups) * group, group)
        hidden = entering[vid, pl.ds(first, group), 0, pos].astype(F32)
        tangent = entering[vid, pl.ds(first, group), 1, pos].astype(F32)

        def mean(values):
            return jnp.sum(
                jnp.sum(values, axis=1, keepdims=True), axis=2, keepdims=True
            ) * (1.0 / D)

        inverse = lax.rsqrt(mean(hidden * hidden) + EPS)
        cross = mean(hidden * tangent)
        normed = hidden * inverse
        dnormed = inverse * tangent - hidden * inverse**3 * cross
        scale = 1.0 + mods_ref[vid, 1][None]
        modulated = normed * scale + mods_ref[vid, 0][None]
        dmodulated = dnormed * scale + normed * dmods_ref[vid, 1][None] + dmods_ref[vid, 0][None]
        row = pl.multiple_of((pos * F + first) * KT, group * KT)
        tall[pl.ds(row, group * KT), :] = modulated.reshape(group * KT, HEAD)
        tall[pl.ds(row + HALF * KT, group * KT), :] = dmodulated.reshape(group * KT, HEAD)

    for k in range(KT):
        flat[:, k * HEAD : (k + 1) * HEAD] = tall[pl.ds(k, ROWS, stride=KT), :].astype(BF16)

    def third(number, pair):
        column = number * HD + pair * 2 * HEAD
        halves = [
            weights[
                :, :, :, :, column + lower * 3 * HD : column + lower * 3 * HD + 2 * HEAD
            ].reshape(F, 1, ROWS_OUT, 2 * HEAD)
            for lower in range(2)
        ]
        matrix = jnp.concatenate(halves, axis=1).reshape(D, 2 * HEAD)
        return jnp.dot(flat[...], matrix, preferred_element_type=F32)

    ahead = [third(number, 0) for number in range(3)]
    for pair in range(HEADS // 2):
        q2, k2, v2 = ahead
        if pair + 1 < HEADS // 2:
            ahead = [third(number, pair + 1) for number in range(3)]
        for one in range(2):
            lanes = slice(one * HEAD, (one + 1) * HEAD)
            output, doutput = attend(q2[:, lanes], k2[:, lanes], v2[:, lanes], gains_ref)
            column = (pair * 2 + one) * HEAD
            att[:HALF, column : column + HEAD] = output.astype(BF16)
            att[HALF:, column : column + HEAD] = doutput.astype(BF16)

    for n in range(KT // 2):
        column = 2 * 3 * HD + n * 2 * HEAD
        matrix = weights[:, :, :, :, column : column + 2 * HEAD].reshape(HD, 2 * HEAD)
        y = jnp.dot(att[...], matrix, preferred_element_type=F32)
        tall[pl.ds(2 * n, ROWS, stride=KT), :] = y[:, :HEAD]
        tall[pl.ds(2 * n + 1, ROWS, stride=KT), :] = y[:, HEAD:]

    @pl.loop(0, NP * groups, unroll=2)
    def _(i):
        pos = i // groups
        first = pl.multiple_of((i % groups) * group, group)
        row = pl.multiple_of((pos * F + first) * KT, group * KT)
        y = tall[pl.ds(row, group * KT), :].reshape(group, KT, HEAD)
        dy = tall[pl.ds(row + HALF * KT, group * KT), :].reshape(group, KT, HEAD)
        hidden = entering[vid, pl.ds(first, group), 0, pos].astype(F32)
        tangent = entering[vid, pl.ds(first, group), 1, pos].astype(F32)
        gate = mods_ref[vid, 2][None]
        dgate = dmods_ref[vid, 2][None]
        leaving[vid, pl.ds(first, group), 0, pos] = (hidden + gate * y).astype(BF16)
        leaving[vid, pl.ds(first, group), 1, pos] = (tangent + dgate * y + gate * dy).astype(BF16)


def kernel(
    sizes,
    sections,
    x_ref,
    t_ref,
    wqkv_ref,
    wout_ref,
    gains_ref,
    index_ref,
    amp_ref,
    freq_ref,
    phase_ref,
    out_ref,
    tan_ref,
    weights,
    mods_ref,
    dmods_ref,
    plain,
    staged,
    relay,
    entering,
    leaving,
    returned,
    tall,
    flat,
    att,
    load_sem,
    own_sem,
    swap_send,
    swap_recv,
    ring_send,
    ring_recv,
    x_send,
    x_recv,
    relay_send,
    relay_recv,
    pass_send,
    pass_recv,
    out_send,
    out_recv,
    turn_sem,
):
    nz, nx, ny = sizes
    count = nz * nx * ny
    section = lax.axis_index("section")
    me = lax.axis_index("seq")
    coords = (me // (nx * ny), (me // ny) % nx, me % ny)
    z, xl, y = coords
    first_half = section < 2

    def flip(index):
        return index + ny - 2 * ny * ((index // ny) % nx)

    across = flip(me)
    slot = jnp.where(first_half, me, across)
    neighbour = (section, lax.rem(me + 1, count))
    group = 8

    def exchange(source, row_of, target, place, send, recv):
        pltpu.make_async_copy(source.at[row_of(me)], target.at[place], recv).start()

        @pl.loop(1, count)
        def _(by):
            to = lax.rem(me + by, count)
            pltpu.make_async_remote_copy(
                src_ref=source.at[row_of(to)],
                dst_ref=target.at[place],
                send_sem=send,
                recv_sem=recv,
                device_id=(section, to),
                device_id_type=MESH,
            ).start()

    def exchange_came(source, target, recv):
        pltpu.make_async_copy(source, target, recv).wait()

    def exchange_sent(source, target, send, recv):
        pltpu.make_async_remote_copy(
            src_ref=source.at[pl.ds(0, count - 1)],
            dst_ref=target.at[pl.ds(0, count - 1)],
            send_sem=send,
            recv_sem=recv,
            device_id=neighbour,
            device_id_type=MESH,
        ).wait_send()

    video = section // 2
    loads = [
        pltpu.make_async_copy(ref.at[video], plain.at[tan], load_sem.at[tan])
        for tan, ref in enumerate((x_ref, t_ref))
    ]
    leads = lax.rem(section, 2) == 0

    @pl.when(leads)
    def _():
        for load in loads:
            load.start()

    @pl.when(jnp.logical_not(leads))
    def _():
        pl.semaphore_wait(turn_sem, 1)

    own, swaps = [], []
    for part, (ref, first, width) in enumerate(
        (
            (wqkv_ref.at[pl.ds(0, ROWS_OUT)], 0, 3 * HD),
            (wqkv_ref.at[pl.ds(ROWS_OUT, ROWS_OUT)], 3 * HD, 3 * HD),
            (wout_ref, 6 * HD, D),
        )
    ):
        home = weights.at[z, xl, y, :, pl.ds(first, width)]
        own.append(pltpu.make_async_copy(ref, home, own_sem.at[part]))
        swaps.append(
            pltpu.make_async_remote_copy(
                src_ref=ref,
                dst_ref=home,
                send_sem=swap_send.at[part],
                recv_sem=swap_recv.at[part],
                device_id=(section, across),
                device_id_type=MESH,
            )
        )
    for copy in swaps + own:
        copy.start()

    @pl.when(leads)
    def _():
        for load in loads:
            load.wait()
        for tan in range(2):
            spread(plain.at[tan], tall, 0)

            @pl.loop(0, count // group)
            def _(i):
                first = pl.multiple_of(i * group, group)
                row = pl.multiple_of(first * NP * KT, group * NP * KT)
                staged[pl.ds(first, group), tan] = (
                    tall[pl.ds(row, group * NP * KT), :]
                    .astype(BF16)
                    .reshape(group, NP, KT, HEAD)
                )

        @pl.when(first_half)
        def _():
            exchange(staged, lambda f: f, entering.at[0], me, x_send, x_recv)

        @pl.when(jnp.logical_not(first_half))
        def _():
            exchange(staged, flip, relay, me, x_send, x_recv)

    for vid in range(VIDS):
        time_value = (index_ref[vid].astype(F32) + 0.5) * (math.pi / (2.0 * T_STEPS))
        mods_ref[vid], dmods_ref[vid] = timing(
            amp_ref[...], freq_ref[...], phase_ref[...], time_value
        )

    for copy in own + swaps:
        copy.wait()

    def relayed():
        return pltpu.make_async_remote_copy(
            src_ref=relay,
            dst_ref=entering.at[1],
            send_sem=relay_send,
            recv_sem=relay_recv,
            device_id=(0, across),
            device_id_type=MESH,
        )

    gather = Gather(sizes, section, coords, weights, ring_send, ring_recv)
    gather.build()
    go = gather.go
    go("b", "a", ("by", 0), ("az", 0))
    go("a", ("az", 1), ("az", 3))
    go("b", ("by", 1), ("by", 7))
    go("a", ("az", 2))
    go(("az", 0), ("by", 0))
    go("b", ("by", 2), ("by", 6))
    go(("az", 1), ("az", 3), ("by", 1), ("by", 7), ("az", 2))
    go("b", ("by", 3), ("by", 5))
    go(("az", 0), ("by", 0), ("az", 1), ("az", 3))

    @pl.when(leads)
    def _():
        pl.semaphore_signal(
            turn_sem, inc=1, device_id=(section + 1, me), device_id_type=MESH
        )

    go("b", ("by", 4))

    @pl.when(section == 2)
    def _():
        exchange_came(staged, relay, x_recv)
        relayed().start()

    go(("by", 2), ("by", 6), ("az", 2), ("by", 1), ("by", 7), ("az", 0))
    go(("by", 3), ("by", 5), ("az", 1), ("az", 3), ("by", 4), ("az", 2))

    go(("by", 2), ("by", 6), ("az", 0), ("by", 3), ("by", 5))
    go(("az", 1), ("az", 3), ("by", 4), ("az", 2))
    gather.finish()

    def onward(vid):
        return pltpu.make_async_remote_copy(
            src_ref=leaving.at[vid],
            dst_ref=entering.at[vid],
            send_sem=pass_send.at[vid],
            recv_sem=pass_recv.at[vid],
            device_id=(
                lax.rem(section + 1, sections),
                jnp.where(section == 1, across, me),
            ),
            device_id_type=MESH,
        )

    def send_back(vid):
        exchange(
            leaving.at[vid],
            lambda f: f,
            returned.at[vid],
            slot,
            out_send.at[vid],
            out_recv.at[vid],
        )

    @pl.loop(0, VIDS)
    def _(vid):
        @pl.when(jnp.logical_and(section == 0, vid == 0))
        def _():
            exchange_came(staged, entering.at[0], x_recv)

        @pl.when(jnp.logical_and(section == 0, vid == 1))
        def _():
            relayed().wait_recv()

        @pl.when(section > 0)
        def _():
            onward(vid).wait_recv()

        block_step(vid, entering, leaving, weights, gains_ref, mods_ref, dmods_ref, tall, flat, att)

        @pl.when(section < sections - 1)
        def _():
            onward(vid).start()

        @pl.when(jnp.logical_and(section != 1, section < sections - 1))
        def _():
            onward(vid).wait_send()

        @pl.when(section != 1)
        def _():
            send_back(vid)

    @pl.when(section == 1)
    def _():
        for vid in range(VIDS):
            onward(vid).wait_send()
        for vid in range(VIDS):
            send_back(vid)

    @pl.loop(0, VIDS)
    def _(vid):
        exchange_came(leaving.at[vid], returned.at[vid], out_recv.at[vid])
        for tan, result in enumerate((out_ref, tan_ref)):

            @pl.loop(0, count // group)
            def _(i):
                first = pl.multiple_of(i * group, group)
                row = pl.multiple_of(first * NP * KT, group * NP * KT)
                tall[pl.ds(row, group * NP * KT), :] = (
                    returned[vid, pl.ds(first, group), tan]
                    .reshape(group * NP * KT, HEAD)
                    .astype(F32)
                )

            for k in range(KT):
                result[vid, :, k * HEAD : (k + 1) * HEAD] = tall[
                    pl.ds(k, count * NP, stride=KT), :
                ].astype(BF16)

    for vid in range(VIDS):
        exchange_sent(
            leaving.at[vid], returned.at[vid], out_send.at[vid], out_recv.at[vid]
        )

    @pl.when(leads)
    def _():
        exchange_sent(staged, relay, x_send, x_recv)

    @pl.when(section == 2)
    def _():
        relayed().wait_send()


def shards(sizes, x_in, x_tan, t_index, w_qkv, w_out, qk_gain, mod_amp, mod_freq, mod_phase):
    nz, nx, ny = sizes
    count = nz * nx * ny
    sections = lax.axis_size("section")
    places = x_in.shape[2]
    waves = [wave.reshape(3, KT, HEAD) for wave in (mod_amp, mod_freq, mod_phase)]
    anywhere = pl.BlockSpec(memory_space=pl.ANY)
    inside = pl.BlockSpec(memory_space=pltpu.VMEM)
    result = jax.ShapeDtypeStruct((VIDS, places, D), BF16)
    unit = (F, 2, NP, KT, HEAD)
    rings = 2 * (ny // 2) * (1 + nz) + 2 * (nz // 2) * (1 + ny)
    dma = pltpu.SemaphoreType.DMA
    out, tan = pl.pallas_call(
        functools.partial(kernel, sizes, sections),
        out_shape=(result, result),
        in_specs=[anywhere] * 4
        + [inside, pl.BlockSpec(memory_space=pltpu.SMEM)]
        + [inside] * 3,
        out_specs=(inside, inside),
        scratch_shapes=[
            pltpu.VMEM((nz, nx, ny, ROWS_OUT, PACKED), BF16),
            pltpu.VMEM((VIDS, 3, KT, HEAD), F32),
            pltpu.VMEM((VIDS, 3, KT, HEAD), F32),
            pltpu.VMEM((2, places, D), BF16),
            pltpu.VMEM(unit, BF16),
            pltpu.VMEM(unit, BF16),
            pltpu.VMEM((VIDS,) + unit, BF16),
            pltpu.VMEM((VIDS,) + unit, BF16),
            pltpu.VMEM((VIDS,) + unit, BF16),
            pltpu.VMEM((ROWS * KT, HEAD), F32),
            pltpu.VMEM((ROWS, D), BF16),
            pltpu.VMEM((ROWS, HD), BF16),
            dma((2,)),
            dma((3,)),
            dma((3,)),
            dma((3,)),
            dma((rings,)),
            dma((rings,)),
            dma,
            dma,
            dma,
            dma,
            dma((VIDS,)),
            dma((VIDS,)),
            dma((VIDS,)),
            dma((VIDS,)),
            pltpu.SemaphoreType.REGULAR,
        ],
        compiler_params=pltpu.CompilerParams(
            has_side_effects=True, vmem_limit_bytes=60 * 1024 * 1024
        ),
        name="blocks",
    )(
        x_in.reshape(VIDS, places, D),
        x_tan.reshape(VIDS, places, D),
        w_qkv[0],
        w_out[0],
        qk_gain[0],
        t_index,
        *waves,
    )
    return (out[None, :, None], tan[None, :, None])


def solution(mesh):
    count = mesh.shape["seq"]
    sizes = (count // 8, 2, 4)
    placed = (
        P(None, "seq", None, None),
        P(None, "seq", None, None),
        P(),
        P("section", "seq", None),
        P("section", "seq", None),
        P("section", None, None),
        P("section", None, None),
        P("section", None, None),
        P("section", None, None),
    )
    return jax.shard_map(
        functools.partial(shards, sizes),
        mesh=mesh,
        in_specs=placed,
        out_specs=(P("section", None, "seq", None, None), P("section", None, "seq", None, None)),
        check_vma=False,
    )
```

```python
import functools
import math

import jax
import jax.numpy as jnp
from jax import lax
from jax.experimental import pallas as pl
from jax.experimental.pallas import tpu as pltpu
from jax.sharding import PartitionSpec as P

HEADS = 8
HEAD = 128
T_STEPS = 1000
D = 2048
KT = D // HEAD
HD = HEADS * HEAD
F = 64
NP = 2
VIDS = 2
UNITS = VIDS * NP
ROWS = 2 * F
HALF = F
EPS = 1e-06
F32 = jnp.float32
BF16 = jnp.bfloat16
MESH = pl.DeviceIdType.MESH
ROWS_OUT = 16
PACKED = 2 * 3 * HD + D
Z_LAST, Y_LAST = 2560, 5632


def timing(amp, freq, phase, time_value):
    angle = freq * time_value + phase
    return (amp * jnp.sin(angle), amp * freq * jnp.cos(angle))


class Gather:
    def __init__(self, sizes, section, coords, weights, send, recv):
        self.sizes, self.section, self.coords = sizes, section, coords
        self.weights, self.send, self.recv = weights, send, recv
        self.live = []
        self.sems = 0
        self.rings = {}

    def peer(self, axis, by):
        z, xl, y = self.coords
        nz, nx, ny = self.sizes
        if axis == "z":
            z = lax.rem(z + by + nz, nz)
        elif axis == "y":
            y = lax.rem(y + by + ny, ny)
        else:
            xl = nx - 1 - xl
        return (self.section, (z * nx + xl) * ny + y)

    def copy(self, ref, sem, peer):
        return pltpu.make_async_remote_copy(
            src_ref=ref,
            dst_ref=ref,
            send_sem=self.send.at[sem],
            recv_sem=self.recv.at[sem],
            device_id=peer,
            device_id_type=MESH,
        )

    def start(self, copy):
        copy.start()
        self.live.append(copy)

    def ring(self, axis, first, stop, fixed, single=False):
        size = self.sizes[0] if axis == "z" else self.sizes[2]
        me = self.coords[0] if axis == "z" else self.coords[2]
        last = size // 2
        first_sem = self.sems
        self.sems += 2 * last

        def copy(way, step, index):
            z, y = (index, fixed) if axis == "z" else (fixed, index)
            begin, width = first, stop - first
            xl = self.coords[1] if single else slice(None)
            if step == last - 1:
                if single:
                    width = width // 2
                    begin = begin + way * width
                else:
                    xl = way
            ref = self.weights.at[z, xl, y, :, pl.ds(begin, width)]
            return self.copy(ref, first_sem + 2 * step + way, self.peer(axis, 1 - 2 * way))

        def at(way, step):
            return lax.rem(me - (1 - 2 * way) * step + size, size)

        for step in range(last):
            for way in (0, 1):
                self.start(copy(way, step, at(way, step)))
            yield
            for way in (0, 1):
                copy(way, step, at(way, step + 1)).wait_recv()

    def beside(self, fixed):
        sem = self.sems
        self.sems += 1
        columns = pl.ds(Y_LAST, PACKED - Y_LAST)
        _, xl, _ = self.coords
        nx = self.sizes[1]
        self.start(
            self.copy(self.weights.at[fixed, xl, :, :, columns], sem, self.peer("x", 0))
        )
        yield
        self.copy(
            self.weights.at[fixed, nx - 1 - xl, :, :, columns], sem, self.peer("x", 0)
        ).wait_recv()

    def build(self):
        z, _, y = self.coords
        nz, _, ny = self.sizes
        rings = self.rings
        rings["a"] = self.ring("y", 0, Z_LAST, z)
        rings["b"] = self.ring("z", Z_LAST, Y_LAST, y)
        rings["c"] = self.ring("z", Y_LAST, PACKED, y, True)
        for by in range(ny):
            rings["az", by] = self.ring("z", 0, Z_LAST, lax.rem(y + by, ny))
        for by in range(nz):
            there = lax.rem(z + by, nz)
            rings["by", by] = self.ring("y", Z_LAST, Y_LAST, there)
            rings["cy", by] = self.ring("y", Y_LAST, PACKED, there, True)
            rings["cx", by] = self.beside(there)

    def go(self, *names):
        for name in names:
            next(self.rings[name], None)

    def finish(self):
        for copy in self.live:
            copy.wait_send()


def spread(source, tall, start):
    count = source.shape[0]
    for k in range(KT):
        tall[pl.ds(start + k, count, stride=KT), :] = source[:, k * HEAD : (k + 1) * HEAD].astype(
            F32
        )


def normalize(values, tangents, gain):
    inverse = lax.rsqrt(jnp.mean(values * values, axis=-1, keepdims=True) + EPS)
    cross = jnp.mean(values * tangents, axis=-1, keepdims=True)
    scaled = values * inverse
    return (
        (scaled * gain).astype(BF16),
        ((inverse * tangents - values * inverse**3 * cross) * gain).astype(BF16),
    )


def attend(q2, k2, v2, gains_ref):
    factor = 1.0 / math.sqrt(HEAD)
    qn, dqn = normalize(q2[:HALF], q2[HALF:], gains_ref[0:1, :])
    kn, dkn = normalize(k2[:HALF], k2[HALF:], gains_ref[1:2, :])
    value, dvalue = v2[:HALF].astype(BF16), v2[HALF:].astype(BF16)

    def against(rows, columns):
        return lax.dot_general(
            rows, columns, (((1,), (1,)), ((), ())), preferred_element_type=F32
        )

    scores = against(jnp.concatenate([qn, dqn], axis=0), kn)
    score = scores[:HALF] * factor
    dscore = (scores[HALF:] + against(qn, dkn)) * factor
    expo = jnp.exp(score)
    prob = expo * (1.0 / jnp.sum(expo, axis=-1, keepdims=True))
    growth = prob * dscore
    dprob = growth - prob * jnp.sum(growth, axis=-1, keepdims=True)
    prob, dprob = prob.astype(BF16), dprob.astype(BF16)
    mixed = jnp.dot(
        jnp.concatenate([prob, dprob], axis=0), value, preferred_element_type=F32
    )
    return mixed[:HALF], mixed[HALF:] + jnp.dot(prob, dvalue, preferred_element_type=F32)


def block_step(
    unit, entering, leaving, weights, gains_ref, mods_ref, dmods_ref, tall, flat, att
):
    group = 8
    vid = unit // NP

    @pl.loop(0, F // group, unroll=2)
    def _(i):
        first = pl.multiple_of(i * group, group)
        hidden = entering[unit, pl.ds(first, group), 0].astype(F32)
        tangent = entering[unit, pl.ds(first, group), 1].astype(F32)

        def mean(values):
            return jnp.sum(
                jnp.sum(values, axis=1, keepdims=True), axis=2, keepdims=True
            ) * (1.0 / D)

        inverse = lax.rsqrt(mean(hidden * hidden) + EPS)
        cross = mean(hidden * tangent)
        normed = hidden * inverse
        dnormed = inverse * tangent - hidden * inverse**3 * cross
        scale = 1.0 + mods_ref[vid, 1][None]
        modulated = normed * scale + mods_ref[vid, 0][None]
        dmodulated = dnormed * scale + normed * dmods_ref[vid, 1][None] + dmods_ref[vid, 0][None]
        row = pl.multiple_of(first * KT, group * KT)
        tall[pl.ds(row, group * KT), :] = modulated.reshape(group * KT, HEAD)
        tall[pl.ds(row + HALF * KT, group * KT), :] = dmodulated.reshape(group * KT, HEAD)

    for k in range(KT):
        flat[:, k * HEAD : (k + 1) * HEAD] = tall[pl.ds(k, ROWS, stride=KT), :].astype(BF16)

    def third(number, pair):
        column = number * HD + pair * 2 * HEAD
        halves = [
            weights[
                :, :, :, :, column + lower * 3 * HD : column + lower * 3 * HD + 2 * HEAD
            ].reshape(F, 1, ROWS_OUT, 2 * HEAD)
            for lower in range(2)
        ]
        matrix = jnp.concatenate(halves, axis=1).reshape(D, 2 * HEAD)
        return jnp.dot(flat[...], matrix, preferred_element_type=F32)

    ahead = [third(number, 0) for number in range(3)]
    for pair in range(HEADS // 2):
        q2, k2, v2 = ahead
        if pair + 1 < HEADS // 2:
            ahead = [third(number, pair + 1) for number in range(3)]
        for one in range(2):
            lanes = slice(one * HEAD, (one + 1) * HEAD)
            output, doutput = attend(q2[:, lanes], k2[:, lanes], v2[:, lanes], gains_ref)
            column = (pair * 2 + one) * HEAD
            att[:HALF, column : column + HEAD] = output.astype(BF16)
            att[HALF:, column : column + HEAD] = doutput.astype(BF16)

    for n in range(KT // 2):
        column = 2 * 3 * HD + n * 2 * HEAD
        matrix = weights[:, :, :, :, column : column + 2 * HEAD].reshape(HD, 2 * HEAD)
        y = jnp.dot(att[...], matrix, preferred_element_type=F32)
        tall[pl.ds(2 * n, ROWS, stride=KT), :] = y[:, :HEAD]
        tall[pl.ds(2 * n + 1, ROWS, stride=KT), :] = y[:, HEAD:]

    @pl.loop(0, F // group, unroll=2)
    def _(i):
        first = pl.multiple_of(i * group, group)
        row = pl.multiple_of(first * KT, group * KT)
        y = tall[pl.ds(row, group * KT), :].reshape(group, KT, HEAD)
        dy = tall[pl.ds(row + HALF * KT, group * KT), :].reshape(group, KT, HEAD)
        hidden = entering[unit, pl.ds(first, group), 0].astype(F32)
        tangent = entering[unit, pl.ds(first, group), 1].astype(F32)
        gate = mods_ref[vid, 2][None]
        dgate = dmods_ref[vid, 2][None]
        leaving[unit, pl.ds(first, group), 0] = (hidden + gate * y).astype(BF16)
        leaving[unit, pl.ds(first, group), 1] = (tangent + dgate * y + gate * dy).astype(BF16)


def kernel(
    sizes,
    sections,
    x_ref,
    t_ref,
    wqkv_ref,
    wout_ref,
    gains_ref,
    index_ref,
    amp_ref,
    freq_ref,
    phase_ref,
    out_ref,
    tan_ref,
    weights,
    mods_ref,
    dmods_ref,
    plain,
    staged,
    relay,
    entering,
    leaving,
    returned,
    tall,
    flat,
    att,
    load_sem,
    own_sem,
    swap_send,
    swap_recv,
    ring_send,
    ring_recv,
    x_send,
    x_recv,
    relay_send,
    relay_recv,
    pass_send,
    pass_recv,
    out_send,
    out_recv,
    turn_sem,
):
    nz, nx, ny = sizes
    count = nz * nx * ny
    section = lax.axis_index("section")
    me = lax.axis_index("seq")
    coords = (me // (nx * ny), (me // ny) % nx, me % ny)
    z, xl, y = coords
    first_half = section < 2

    def flip(index):
        return index + ny - 2 * ny * ((index // ny) % nx)

    across = flip(me)
    slot = jnp.where(first_half, me, across)
    neighbour = (section, lax.rem(me + 1, count))
    group = 8

    def exchange(source, row_of, target, place, send, recv):
        pltpu.make_async_copy(source.at[row_of(me)], target.at[place], recv).start()

        @pl.loop(1, count)
        def _(by):
            to = lax.rem(me + by, count)
            pltpu.make_async_remote_copy(
                src_ref=source.at[row_of(to)],
                dst_ref=target.at[place],
                send_sem=send,
                recv_sem=recv,
                device_id=(section, to),
                device_id_type=MESH,
            ).start()

    def exchange_came(source, target, recv):
        pltpu.make_async_copy(source, target, recv).wait()

    def exchange_sent(source, target, send, recv):
        pltpu.make_async_remote_copy(
            src_ref=source.at[pl.ds(0, count - 1)],
            dst_ref=target.at[pl.ds(0, count - 1)],
            send_sem=send,
            recv_sem=recv,
            device_id=neighbour,
            device_id_type=MESH,
        ).wait_send()

    leads = lax.rem(section, 2) == 0
    loads = [
        pltpu.make_async_copy(ref, plain.at[tan], load_sem.at[tan])
        for tan, ref in enumerate((x_ref, t_ref))
    ]

    @pl.when(leads)
    def _():
        for load in loads:
            load.start()

    own = []
    for part, (ref, first, width) in enumerate(
        (
            (wqkv_ref.at[pl.ds(0, ROWS_OUT)], 0, 3 * HD),
            (wqkv_ref.at[pl.ds(ROWS_OUT, ROWS_OUT)], 3 * HD, 3 * HD),
            (wout_ref, 6 * HD, D),
        )
    ):
        home = weights.at[z, xl, y, :, pl.ds(first, width)]
        own.append(pltpu.make_async_copy(ref, home, own_sem.at[part]))
        own[-1].start()
    for copy in own:
        copy.wait()

    @pl.when(jnp.logical_not(leads))
    def _():
        pl.semaphore_wait(turn_sem, 1)

    gather = Gather(sizes, section, coords, weights, ring_send, ring_recv)
    gather.build()
    go = gather.go
    mine = weights.at[z, xl, y, :, pl.ds(0, Y_LAST)]
    swap = pltpu.make_async_remote_copy(
        src_ref=mine,
        dst_ref=mine,
        send_sem=swap_send,
        recv_sem=swap_recv,
        device_id=(section, across),
        device_id_type=MESH,
    )
    theirs = weights.at[z, nx - 1 - xl, y, :, pl.ds(0, Y_LAST)]
    swapped = pltpu.make_async_remote_copy(
        src_ref=theirs,
        dst_ref=theirs,
        send_sem=swap_send,
        recv_sem=swap_recv,
        device_id=(section, across),
        device_id_type=MESH,
    )
    swap.start()
    go("c", ("cy", 0))

    def prepare(vid):
        for tan in range(2):
            spread(plain.at[tan, vid], tall, 0)

            @pl.loop(0, count // group)
            def _(i):
                first = pl.multiple_of(i * group, group)
                row = pl.multiple_of(first * NP * KT, group * NP * KT)
                tiles = (
                    tall[pl.ds(row, group * NP * KT), :]
                    .astype(BF16)
                    .reshape(group, NP, KT, HEAD)
                )
                for pos in range(NP):
                    staged[vid * NP + pos, pl.ds(first, group), tan] = tiles[:, pos]

    @pl.when(leads)
    def _():
        for load in loads:
            load.wait()
        prepare(0)

    @pl.when(section == 0)
    def _():
        exchange(
            staged.at[0], lambda f: f, entering.at[0], me, x_send.at[0], x_recv.at[0]
        )

    def second_round(unit):
        exchange(
            staged.at[unit], flip, relay.at[unit], me, x_send.at[unit], x_recv.at[unit]
        )

    @pl.when(section == 2)
    def _():
        second_round(1)
        prepare(1)
        second_round(2)
        second_round(3)

    def relayed(unit):
        return pltpu.make_async_remote_copy(
            src_ref=relay.at[unit],
            dst_ref=entering.at[unit],
            send_sem=relay_send.at[unit],
            recv_sem=relay_recv.at[unit],
            device_id=(0, across),
            device_id_type=MESH,
        )

    def pass_to_first(unit):
        @pl.when(section == 2)
        def _():
            exchange_came(staged.at[unit], relay.at[unit], x_recv.at[unit])
            relayed(unit).start()

    for vid in range(VIDS):
        time_value = (index_ref[vid].astype(F32) + 0.5) * (math.pi / (2.0 * T_STEPS))
        mods_ref[vid], dmods_ref[vid] = timing(
            amp_ref[...], freq_ref[...], phase_ref[...], time_value
        )

    swapped.wait_recv()
    go("b", "a", ("by", 0), ("az", 0))
    go("c", ("cy", 1), ("cy", 7))
    go("a", ("az", 1), ("az", 3))
    go(("cy", 0),)
    go("b", ("by", 1), ("by", 7))
    go("c", ("cy", 2), ("cy", 6))
    go("a", ("az", 2))
    go(("cy", 0), ("cx", 0), ("cy", 1), ("cy", 7))
    go(("az", 0), ("by", 0))
    go("c", ("cy", 3), ("cy", 5))
    go(("cy", 1), ("cx", 1), ("cy", 7), ("cx", 7), ("cy", 2), ("cy", 6))
    go("b", ("by", 2), ("by", 6))
    go("c", ("cy", 4))
    pass_to_first(1)
    go(("az", 1), ("az", 3), ("by", 1), ("by", 7), ("az", 2))
    go(("cy", 2), ("cx", 2), ("cy", 6), ("cx", 6), ("cy", 3), ("cy", 5), ("cy", 4))
    go("b", ("by", 3), ("by", 5))
    go(("az", 0), ("by", 0), ("az", 1), ("az", 3))
    go(("cy", 3), ("cx", 3), ("cy", 5), ("cx", 5), ("cy", 4), ("cx", 4))
    pass_to_first(2)

    @pl.when(leads)
    def _():
        pl.semaphore_signal(
            turn_sem, inc=1, device_id=(section + 1, me), device_id_type=MESH
        )

    go("b", ("by", 4))
    go(("by", 2), ("by", 6), ("az", 2), ("by", 1), ("by", 7), ("az", 0))
    pass_to_first(3)
    go(("by", 3), ("by", 5), ("az", 1), ("az", 3), ("by", 4), ("az", 2))
    go(("by", 2), ("by", 6), ("az", 0), ("by", 3), ("by", 5))
    go(("az", 1), ("az", 3), ("by", 4), ("az", 2))
    go(*(("cx", by) for by in range(nz)))
    gather.finish()
    swap.wait_send()

    def onward(unit):
        return pltpu.make_async_remote_copy(
            src_ref=leaving.at[unit],
            dst_ref=entering.at[unit],
            send_sem=pass_send.at[unit],
            recv_sem=pass_recv.at[unit],
            device_id=(
                lax.rem(section + 1, sections),
                jnp.where(section == 1, across, me),
            ),
            device_id_type=MESH,
        )

    @pl.loop(0, UNITS)
    def _(unit):
        @pl.when(jnp.logical_and(section == 0, unit == 0))
        def _():
            exchange_came(staged.at[0], entering.at[0], x_recv.at[0])

        @pl.when(jnp.logical_and(section == 0, unit > 0))
        def _():
            relayed(unit).wait_recv()

        @pl.when(section > 0)
        def _():
            onward(unit).wait_recv()

        block_step(
            unit, entering, leaving, weights, gains_ref, mods_ref, dmods_ref, tall, flat, att
        )

        @pl.when(section < sections - 1)
        def _():
            onward(unit).start()

        exchange(
            leaving.at[unit],
            lambda f: f,
            returned.at[unit],
            slot,
            out_send.at[unit],
            out_recv.at[unit],
        )

    @pl.loop(0, VIDS)
    def _(vid):
        for pos in range(NP):
            unit = vid * NP + pos
            exchange_came(leaving.at[unit], returned.at[unit], out_recv.at[unit])

            @pl.loop(0, count // group)
            def _(i):
                first = pl.multiple_of(i * group, group)
                for tan in range(2):
                    tiles = returned[unit, pl.ds(first, group), tan].astype(F32)
                    for one in range(group):
                        row = pl.multiple_of(
                            ((tan * count + first + one) * NP + pos) * KT, KT
                        )
                        tall[pl.ds(row, KT), :] = tiles[one]

        for tan, result in enumerate((out_ref, tan_ref)):
            for k in range(KT):
                result[vid, :, k * HEAD : (k + 1) * HEAD] = tall[
                    pl.ds(tan * count * NP * KT + k, count * NP, stride=KT), :
                ].astype(BF16)

    @pl.loop(0, UNITS)
    def _(unit):
        exchange_sent(
            leaving.at[unit], returned.at[unit], out_send.at[unit], out_recv.at[unit]
        )

        @pl.when(section < sections - 1)
        def _():
            onward(unit).wait_send()

        @pl.when(
            jnp.logical_or(
                jnp.logical_and(section == 0, unit == 0),
                jnp.logical_and(section == 2, unit > 0),
            )
        )
        def _():
            exchange_sent(
                staged.at[unit], relay.at[unit], x_send.at[unit], x_recv.at[unit]
            )

        @pl.when(jnp.logical_and(section == 2, unit > 0))
        def _():
            relayed(unit).wait_send()


def shards(sizes, x_in, x_tan, t_index, w_qkv, w_out, qk_gain, mod_amp, mod_freq, mod_phase):
    nz, nx, ny = sizes
    count = nz * nx * ny
    sections = lax.axis_size("section")
    places = x_in.shape[2]
    waves = [wave.reshape(3, KT, HEAD) for wave in (mod_amp, mod_freq, mod_phase)]
    anywhere = pl.BlockSpec(memory_space=pl.ANY)
    inside = pl.BlockSpec(memory_space=pltpu.VMEM)
    result = jax.ShapeDtypeStruct((VIDS, places, D), BF16)
    units = (UNITS, F, 2, KT, HEAD)
    rings = 2 * (ny // 2) * (1 + 2 * nz) + 2 * (nz // 2) * (2 + ny) + nz
    dma = pltpu.SemaphoreType.DMA
    out, tan = pl.pallas_call(
        functools.partial(kernel, sizes, sections),
        out_shape=(result, result),
        in_specs=[anywhere] * 4
        + [inside, pl.BlockSpec(memory_space=pltpu.SMEM)]
        + [inside] * 3,
        out_specs=(inside, inside),
        scratch_shapes=[
            pltpu.VMEM((nz, nx, ny, ROWS_OUT, PACKED), BF16),
            pltpu.VMEM((VIDS, 3, KT, HEAD), F32),
            pltpu.VMEM((VIDS, 3, KT, HEAD), F32),
            pltpu.VMEM((2, VIDS, places, D), BF16),
            pltpu.VMEM(units, BF16),
            pltpu.VMEM(units, BF16),
            pltpu.VMEM(units, BF16),
            pltpu.VMEM(units, BF16),
            pltpu.VMEM(units, BF16),
            pltpu.VMEM((2 * places * KT, HEAD), F32),
            pltpu.VMEM((ROWS, D), BF16),
            pltpu.VMEM((ROWS, HD), BF16),
            dma((2,)),
            dma((3,)),
            dma,
            dma,
            dma((rings,)),
            dma((rings,)),
            dma((UNITS,)),
            dma((UNITS,)),
            dma((UNITS,)),
            dma((UNITS,)),
            dma((UNITS,)),
            dma((UNITS,)),
            dma((UNITS,)),
            dma((UNITS,)),
            pltpu.SemaphoreType.REGULAR,
        ],
        compiler_params=pltpu.CompilerParams(
            has_side_effects=True, vmem_limit_bytes=60 * 1024 * 1024
        ),
        name="blocks",
    )(
        x_in.reshape(VIDS, places, D),
        x_tan.reshape(VIDS, places, D),
        w_qkv[0],
        w_out[0],
        qk_gain[0],
        t_index,
        *waves,
    )
    return (out[None, :, None], tan[None, :, None])


def solution(mesh):
    count = mesh.shape["seq"]
    sizes = (count // 8, 2, 4)
    placed = (
        P(None, "seq", None, None),
        P(None, "seq", None, None),
        P(),
        P("section", "seq", None),
        P("section", "seq", None),
        P("section", None, None),
        P("section", None, None),
        P("section", None, None),
        P("section", None, None),
    )
    return jax.shard_map(
        functools.partial(shards, sizes),
        mesh=mesh,
        in_specs=placed,
        out_specs=(P("section", None, "seq", None, None), P("section", None, "seq", None, None)),
        check_vma=False,
    )
```

```python
import functools
import math

import jax
import jax.numpy as jnp
from jax import lax
from jax.experimental import pallas as pl
from jax.experimental.pallas import tpu as pltpu
from jax.sharding import PartitionSpec as P

HEADS = 8
HEAD = 128
T_STEPS = 1000
D = 2048
KT = D // HEAD
HD = HEADS * HEAD
F = 64
NP = 2
VIDS = 2
UNITS = VIDS * NP
ROWS = 2 * F
HALF = F
HOP_PARTS = 4
EPS = 1e-06
F32 = jnp.float32
BF16 = jnp.bfloat16
MESH = pl.DeviceIdType.MESH
ROWS_OUT = 16
PACKED = 2 * 3 * HD + D
Z_LAST, Y_LAST = 2560, 5632


def timing(amp, freq, phase, time_value):
    angle = freq * time_value + phase
    return (amp * jnp.sin(angle), amp * freq * jnp.cos(angle))


class Gather:
    def __init__(self, sizes, section, coords, weights, send, recv):
        self.sizes, self.section, self.coords = sizes, section, coords
        self.weights, self.send, self.recv = weights, send, recv
        self.live = []
        self.sems = 0
        self.rings = {}

    def peer(self, axis, by):
        z, xl, y = self.coords
        nz, nx, ny = self.sizes
        if axis == "z":
            z = lax.rem(z + by + nz, nz)
        elif axis == "y":
            y = lax.rem(y + by + ny, ny)
        else:
            xl = nx - 1 - xl
        return (self.section, (z * nx + xl) * ny + y)

    def copy(self, ref, sem, peer):
        return pltpu.make_async_remote_copy(
            src_ref=ref,
            dst_ref=ref,
            send_sem=self.send.at[sem],
            recv_sem=self.recv.at[sem],
            device_id=peer,
            device_id_type=MESH,
        )

    def start(self, copy):
        copy.start()
        self.live.append(copy)

    def ring(self, axis, first, stop, fixed, single=False):
        size = self.sizes[0] if axis == "z" else self.sizes[2]
        me = self.coords[0] if axis == "z" else self.coords[2]
        last = size // 2
        first_sem = self.sems
        self.sems += 2 * last

        def copy(way, step, index):
            z, y = (index, fixed) if axis == "z" else (fixed, index)
            begin, width = first, stop - first
            xl = self.coords[1] if single else slice(None)
            if step == last - 1:
                if single:
                    width = width // 2
                    begin = begin + way * width
                else:
                    xl = way
            ref = self.weights.at[z, xl, y, :, pl.ds(begin, width)]
            return self.copy(ref, first_sem + 2 * step + way, self.peer(axis, 1 - 2 * way))

        def at(way, step):
            return lax.rem(me - (1 - 2 * way) * step + size, size)

        for step in range(last):
            for way in (0, 1):
                self.start(copy(way, step, at(way, step)))
            yield
            for way in (0, 1):
                copy(way, step, at(way, step + 1)).wait_recv()

    def beside(self, fixed):
        sem = self.sems
        self.sems += 1
        columns = pl.ds(Y_LAST, PACKED - Y_LAST)
        _, xl, _ = self.coords
        nx = self.sizes[1]
        self.start(
            self.copy(self.weights.at[fixed, xl, :, :, columns], sem, self.peer("x", 0))
        )
        yield
        self.copy(
            self.weights.at[fixed, nx - 1 - xl, :, :, columns], sem, self.peer("x", 0)
        ).wait_recv()

    def build(self):
        z, _, y = self.coords
        nz, _, ny = self.sizes
        rings = self.rings
        rings["a"] = self.ring("y", 0, Z_LAST, z)
        rings["b"] = self.ring("z", Z_LAST, Y_LAST, y)
        rings["c"] = self.ring("z", Y_LAST, PACKED, y, True)
        for by in range(ny):
            rings["az", by] = self.ring("z", 0, Z_LAST, lax.rem(y + by, ny))
        for by in range(nz):
            there = lax.rem(z + by, nz)
            rings["by", by] = self.ring("y", Z_LAST, Y_LAST, there)
            rings["cy", by] = self.ring("y", Y_LAST, PACKED, there, True)
            rings["cx", by] = self.beside(there)

    def go(self, *names):
        for name in names:
            next(self.rings[name], None)

    def finish(self):
        for copy in self.live:
            copy.wait_send()


def spread(source, tall, start):
    count = source.shape[0]
    for k in range(KT):
        tall[pl.ds(start + k, count, stride=KT), :] = source[:, k * HEAD : (k + 1) * HEAD].astype(
            F32
        )


def normalize(values, tangents, gain):
    inverse = lax.rsqrt(jnp.mean(values * values, axis=-1, keepdims=True) + EPS)
    cross = jnp.mean(values * tangents, axis=-1, keepdims=True)
    scaled = values * inverse
    return (
        (scaled * gain).astype(BF16),
        ((inverse * tangents - values * inverse**3 * cross) * gain).astype(BF16),
    )


def attend(q2, k2, v2, gains_ref):
    factor = 1.0 / math.sqrt(HEAD)
    qn, dqn = normalize(q2[:HALF], q2[HALF:], gains_ref[0:1, :])
    kn, dkn = normalize(k2[:HALF], k2[HALF:], gains_ref[1:2, :])
    value, dvalue = v2[:HALF].astype(BF16), v2[HALF:].astype(BF16)

    def against(rows, columns):
        return lax.dot_general(
            rows, columns, (((1,), (1,)), ((), ())), preferred_element_type=F32
        )

    scores = against(jnp.concatenate([qn, dqn], axis=0), kn)
    score = scores[:HALF] * factor
    dscore = (scores[HALF:] + against(qn, dkn)) * factor
    expo = jnp.exp(score)
    prob = expo * (1.0 / jnp.sum(expo, axis=-1, keepdims=True))
    growth = prob * dscore
    dprob = growth - prob * jnp.sum(growth, axis=-1, keepdims=True)
    prob, dprob = prob.astype(BF16), dprob.astype(BF16)
    mixed = jnp.dot(
        jnp.concatenate([prob, dprob], axis=0), value, preferred_element_type=F32
    )
    return mixed[:HALF], mixed[HALF:] + jnp.dot(prob, dvalue, preferred_element_type=F32)


def block_step(
    unit, entering, leaving, weights, gains_ref, mods_ref, dmods_ref, tall, flat, att
):
    group = 8
    vid = unit // NP

    @pl.loop(0, F // group, unroll=2)
    def _(i):
        first = pl.multiple_of(i * group, group)
        hidden = entering[unit, pl.ds(first, group), 0].astype(F32)
        tangent = entering[unit, pl.ds(first, group), 1].astype(F32)

        def mean(values):
            return jnp.sum(
                jnp.sum(values, axis=1, keepdims=True), axis=2, keepdims=True
            ) * (1.0 / D)

        inverse = lax.rsqrt(mean(hidden * hidden) + EPS)
        cross = mean(hidden * tangent)
        normed = hidden * inverse
        dnormed = inverse * tangent - hidden * inverse**3 * cross
        scale = 1.0 + mods_ref[vid, 1][None]
        modulated = normed * scale + mods_ref[vid, 0][None]
        dmodulated = dnormed * scale + normed * dmods_ref[vid, 1][None] + dmods_ref[vid, 0][None]
        row = pl.multiple_of(first * KT, group * KT)
        tall[pl.ds(row, group * KT), :] = modulated.reshape(group * KT, HEAD)
        tall[pl.ds(row + HALF * KT, group * KT), :] = dmodulated.reshape(group * KT, HEAD)

    for k in range(KT):
        flat[:, k * HEAD : (k + 1) * HEAD] = tall[pl.ds(k, ROWS, stride=KT), :].astype(BF16)

    def third(number, pair):
        column = number * HD + pair * 2 * HEAD
        halves = [
            weights[
                :, :, :, :, column + lower * 3 * HD : column + lower * 3 * HD + 2 * HEAD
            ].reshape(F, 1, ROWS_OUT, 2 * HEAD)
            for lower in range(2)
        ]
        matrix = jnp.concatenate(halves, axis=1).reshape(D, 2 * HEAD)
        return jnp.dot(flat[...], matrix, preferred_element_type=F32)

    ahead = [third(number, 0) for number in range(3)]
    for pair in range(HEADS // 2):
        q2, k2, v2 = ahead
        if pair + 1 < HEADS // 2:
            ahead = [third(number, pair + 1) for number in range(3)]
        for one in range(2):
            lanes = slice(one * HEAD, (one + 1) * HEAD)
            output, doutput = attend(q2[:, lanes], k2[:, lanes], v2[:, lanes], gains_ref)
            column = (pair * 2 + one) * HEAD
            att[:HALF, column : column + HEAD] = output.astype(BF16)
            att[HALF:, column : column + HEAD] = doutput.astype(BF16)

    for n in range(KT // 2):
        column = 2 * 3 * HD + n * 2 * HEAD
        matrix = weights[:, :, :, :, column : column + 2 * HEAD].reshape(HD, 2 * HEAD)
        y = jnp.dot(att[...], matrix, preferred_element_type=F32)
        tall[pl.ds(2 * n, ROWS, stride=KT), :] = y[:, :HEAD]
        tall[pl.ds(2 * n + 1, ROWS, stride=KT), :] = y[:, HEAD:]

    @pl.loop(0, F // group, unroll=2)
    def _(i):
        first = pl.multiple_of(i * group, group)
        row = pl.multiple_of(first * KT, group * KT)
        y = tall[pl.ds(row, group * KT), :].reshape(group, KT, HEAD)
        dy = tall[pl.ds(row + HALF * KT, group * KT), :].reshape(group, KT, HEAD)
        hidden = entering[unit, pl.ds(first, group), 0].astype(F32)
        tangent = entering[unit, pl.ds(first, group), 1].astype(F32)
        gate = mods_ref[vid, 2][None]
        dgate = dmods_ref[vid, 2][None]
        leaving[unit, pl.ds(first, group), 0] = (hidden + gate * y).astype(BF16)
        leaving[unit, pl.ds(first, group), 1] = (tangent + dgate * y + gate * dy).astype(BF16)


def kernel(
    sizes,
    sections,
    x_ref,
    t_ref,
    wqkv_ref,
    wout_ref,
    gains_ref,
    index_ref,
    amp_ref,
    freq_ref,
    phase_ref,
    out_ref,
    tan_ref,
    weights,
    mods_ref,
    dmods_ref,
    plain,
    staged,
    relay,
    entering,
    leaving,
    returned,
    tall,
    flat,
    att,
    load_sem,
    own_sem,
    swap_send,
    swap_recv,
    ring_send,
    ring_recv,
    x_send,
    x_recv,
    relay_send,
    relay_recv,
    pass_send,
    pass_recv,
    out_send,
    out_recv,
    turn_sem,
):
    nz, nx, ny = sizes
    count = nz * nx * ny
    section = lax.axis_index("section")
    me = lax.axis_index("seq")
    coords = (me // (nx * ny), (me // ny) % nx, me % ny)
    z, xl, y = coords
    first_half = section < 2

    def flip(index):
        return index + ny - 2 * ny * ((index // ny) % nx)

    across = flip(me)
    slot = jnp.where(first_half, me, across)
    neighbour = (section, lax.rem(me + 1, count))
    group = 8

    def exchange(source, row_of, target, place, send, recv):
        pltpu.make_async_copy(source.at[row_of(me)], target.at[place], recv).start()

        @pl.loop(1, count)
        def _(by):
            to = lax.rem(me + by, count)
            pltpu.make_async_remote_copy(
                src_ref=source.at[row_of(to)],
                dst_ref=target.at[place],
                send_sem=send,
                recv_sem=recv,
                device_id=(section, to),
                device_id_type=MESH,
            ).start()

    def exchange_came(source, target, recv):
        pltpu.make_async_copy(source, target, recv).wait()

    def exchange_sent(source, target, send, recv):
        pltpu.make_async_remote_copy(
            src_ref=source.at[pl.ds(0, count - 1)],
            dst_ref=target.at[pl.ds(0, count - 1)],
            send_sem=send,
            recv_sem=recv,
            device_id=neighbour,
            device_id_type=MESH,
        ).wait_send()

    leads = lax.rem(section, 2) == 0
    loads = [
        pltpu.make_async_copy(ref, plain.at[tan], load_sem.at[tan])
        for tan, ref in enumerate((x_ref, t_ref))
    ]

    @pl.when(leads)
    def _():
        for load in loads:
            load.start()

    own = []
    for part, (ref, first, width) in enumerate(
        (
            (wqkv_ref.at[pl.ds(0, ROWS_OUT)], 0, 3 * HD),
            (wqkv_ref.at[pl.ds(ROWS_OUT, ROWS_OUT)], 3 * HD, 3 * HD),
            (wout_ref, 6 * HD, D),
        )
    ):
        home = weights.at[z, xl, y, :, pl.ds(first, width)]
        own.append(pltpu.make_async_copy(ref, home, own_sem.at[part]))
        own[-1].start()
    for copy in own:
        copy.wait()

    @pl.when(jnp.logical_not(leads))
    def _():
        pl.semaphore_wait(turn_sem, 1)

    gather = Gather(sizes, section, coords, weights, ring_send, ring_recv)
    gather.build()
    go = gather.go
    mine = weights.at[z, xl, y, :, pl.ds(0, Y_LAST)]
    swap = pltpu.make_async_remote_copy(
        src_ref=mine,
        dst_ref=mine,
        send_sem=swap_send,
        recv_sem=swap_recv,
        device_id=(section, across),
        device_id_type=MESH,
    )
    theirs = weights.at[z, nx - 1 - xl, y, :, pl.ds(0, Y_LAST)]
    swapped = pltpu.make_async_remote_copy(
        src_ref=theirs,
        dst_ref=theirs,
        send_sem=swap_send,
        recv_sem=swap_recv,
        device_id=(section, across),
        device_id_type=MESH,
    )
    swap.start()
    go("c", ("cy", 0))

    def prepare(vid):
        for tan in range(2):
            spread(plain.at[tan, vid], tall, 0)

            @pl.loop(0, count // group)
            def _(i):
                first = pl.multiple_of(i * group, group)
                row = pl.multiple_of(first * NP * KT, group * NP * KT)
                tiles = (
                    tall[pl.ds(row, group * NP * KT), :]
                    .astype(BF16)
                    .reshape(group, NP, KT, HEAD)
                )
                for pos in range(NP):
                    staged[vid * NP + pos, pl.ds(first, group), tan] = tiles[:, pos]

    @pl.when(leads)
    def _():
        for load in loads:
            load.wait()
        prepare(0)

    @pl.when(section == 0)
    def _():
        exchange(
            staged.at[0], lambda f: f, entering.at[0], me, x_send.at[0], x_recv.at[0]
        )

    def second_round(unit):
        exchange(
            staged.at[unit], flip, relay.at[unit], me, x_send.at[unit], x_recv.at[unit]
        )

    @pl.when(section == 2)
    def _():
        second_round(1)
        prepare(1)
        second_round(2)
        second_round(3)

    def relayed(unit):
        return pltpu.make_async_remote_copy(
            src_ref=relay.at[unit],
            dst_ref=entering.at[unit],
            send_sem=relay_send.at[unit],
            recv_sem=relay_recv.at[unit],
            device_id=(0, across),
            device_id_type=MESH,
        )

    def pass_to_first(unit):
        @pl.when(section == 2)
        def _():
            exchange_came(staged.at[unit], relay.at[unit], x_recv.at[unit])
            relayed(unit).start()

    for vid in range(VIDS):
        time_value = (index_ref[vid].astype(F32) + 0.5) * (math.pi / (2.0 * T_STEPS))
        mods_ref[vid], dmods_ref[vid] = timing(
            amp_ref[...], freq_ref[...], phase_ref[...], time_value
        )

    swapped.wait_recv()
    go("b", "a", ("by", 0), ("az", 0))
    go("c", ("cy", 1), ("cy", 7))
    go("a", ("az", 1), ("az", 3))
    go(("cy", 0),)
    go("b", ("by", 1), ("by", 7))
    go("c", ("cy", 2), ("cy", 6))
    go("a", ("az", 2))
    go(("cy", 0), ("cx", 0), ("cy", 1), ("cy", 7))
    go(("az", 0), ("by", 0))
    go("c", ("cy", 3), ("cy", 5))
    go(("cy", 1), ("cx", 1), ("cy", 7), ("cx", 7), ("cy", 2), ("cy", 6))
    go("b", ("by", 2), ("by", 6))
    go("c", ("cy", 4))
    pass_to_first(1)
    go(("az", 1), ("az", 3), ("by", 1), ("by", 7), ("az", 2))
    go(("cy", 2), ("cx", 2), ("cy", 6), ("cx", 6), ("cy", 3), ("cy", 5), ("cy", 4))
    go("b", ("by", 3), ("by", 5))
    go(("az", 0), ("by", 0), ("az", 1), ("az", 3))
    go(("cy", 3), ("cx", 3), ("cy", 5), ("cx", 5), ("cy", 4), ("cx", 4))
    pass_to_first(2)

    @pl.when(leads)
    def _():
        pl.semaphore_signal(
            turn_sem, inc=1, device_id=(section + 1, me), device_id_type=MESH
        )

    go("b", ("by", 4))
    go(("by", 2), ("by", 6), ("az", 2), ("by", 1), ("by", 7), ("az", 0))
    pass_to_first(3)
    go(("by", 3), ("by", 5), ("az", 1), ("az", 3), ("by", 4), ("az", 2))
    go(("by", 2), ("by", 6), ("az", 0), ("by", 3), ("by", 5))
    go(("az", 1), ("az", 3), ("by", 4), ("az", 2))
    go(*(("cx", by) for by in range(nz)))

    @pl.when(section == 1)
    def _():
        pl.semaphore_signal(turn_sem, inc=1, device_id=(0, me), device_id_type=MESH)

    def onward(unit, first=0, frames=F):
        return pltpu.make_async_remote_copy(
            src_ref=leaving.at[unit, pl.ds(first, frames)],
            dst_ref=entering.at[unit, pl.ds(first, frames)],
            send_sem=pass_send.at[unit],
            recv_sem=pass_recv.at[unit],
            device_id=(
                lax.rem(section + 1, sections),
                jnp.where(section == 1, across, me),
            ),
            device_id_type=MESH,
        )

    def send_back(unit):
        exchange(
            leaving.at[unit],
            lambda f: f,
            returned.at[unit],
            slot,
            out_send.at[unit],
            out_recv.at[unit],
        )

    @pl.loop(0, UNITS)
    def _(unit):
        @pl.when(jnp.logical_and(section == 0, unit == 0))
        def _():
            exchange_came(staged.at[0], entering.at[0], x_recv.at[0])

        @pl.when(jnp.logical_and(section == 0, unit > 0))
        def _():
            relayed(unit).wait_recv()

        @pl.when(section > 0)
        def _():
            onward(unit).wait_recv()

        block_step(
            unit, entering, leaving, weights, gains_ref, mods_ref, dmods_ref, tall, flat, att
        )

        @pl.when(section < sections - 1)
        def _():
            for part in range(HOP_PARTS):
                onward(unit, part * (F // HOP_PARTS), F // HOP_PARTS).start()

        @pl.when(section > 0)
        def _():
            send_back(unit)

    @pl.when(section == 0)
    def _():
        pl.semaphore_wait(turn_sem, 1)

        @pl.loop(0, UNITS)
        def _(unit):
            send_back(unit)

    @pl.loop(0, VIDS)
    def _(vid):
        for pos in range(NP):
            unit = vid * NP + pos
            exchange_came(leaving.at[unit], returned.at[unit], out_recv.at[unit])

            @pl.loop(0, count // group)
            def _(i):
                first = pl.multiple_of(i * group, group)
                for tan in range(2):
                    tiles = returned[unit, pl.ds(first, group), tan].astype(F32)
                    for one in range(group):
                        row = pl.multiple_of(
                            ((tan * count + first + one) * NP + pos) * KT, KT
                        )
                        tall[pl.ds(row, KT), :] = tiles[one]

        for tan, result in enumerate((out_ref, tan_ref)):
            for k in range(KT):
                result[vid, :, k * HEAD : (k + 1) * HEAD] = tall[
                    pl.ds(tan * count * NP * KT + k, count * NP, stride=KT), :
                ].astype(BF16)

    gather.finish()
    swap.wait_send()

    @pl.loop(0, UNITS)
    def _(unit):
        exchange_sent(
            leaving.at[unit], returned.at[unit], out_send.at[unit], out_recv.at[unit]
        )

        @pl.when(section < sections - 1)
        def _():
            onward(unit).wait_send()

        @pl.when(
            jnp.logical_or(
                jnp.logical_and(section == 0, unit == 0),
                jnp.logical_and(section == 2, unit > 0),
            )
        )
        def _():
            exchange_sent(
                staged.at[unit], relay.at[unit], x_send.at[unit], x_recv.at[unit]
            )

        @pl.when(jnp.logical_and(section == 2, unit > 0))
        def _():
            relayed(unit).wait_send()


def shards(sizes, x_in, x_tan, t_index, w_qkv, w_out, qk_gain, mod_amp, mod_freq, mod_phase):
    nz, nx, ny = sizes
    count = nz * nx * ny
    sections = lax.axis_size("section")
    places = x_in.shape[2]
    waves = [wave.reshape(3, KT, HEAD) for wave in (mod_amp, mod_freq, mod_phase)]
    outside = pl.BlockSpec(memory_space=pl.ANY)
    inside = pl.BlockSpec(memory_space=pltpu.VMEM)
    result = jax.ShapeDtypeStruct((VIDS, places, D), BF16)
    units = (UNITS, F, 2, KT, HEAD)
    rings = 2 * (ny // 2) * (1 + 2 * nz) + 2 * (nz // 2) * (2 + ny) + nz
    dma = pltpu.SemaphoreType.DMA
    out, tan = pl.pallas_call(
        functools.partial(kernel, sizes, sections),
        out_shape=(result, result),
        in_specs=[outside] * 4
        + [inside, pl.BlockSpec(memory_space=pltpu.SMEM)]
        + [inside] * 3,
        out_specs=(inside, inside),
        scratch_shapes=[
            pltpu.VMEM((nz, nx, ny, ROWS_OUT, PACKED), BF16),
            pltpu.VMEM((VIDS, 3, KT, HEAD), F32),
            pltpu.VMEM((VIDS, 3, KT, HEAD), F32),
            pltpu.VMEM((2, VIDS, places, D), BF16),
            pltpu.VMEM(units, BF16),
            pltpu.VMEM(units, BF16),
            pltpu.VMEM(units, BF16),
            pltpu.VMEM(units, BF16),
            pltpu.VMEM(units, BF16),
            pltpu.VMEM((2 * places * KT, HEAD), F32),
            pltpu.VMEM((ROWS, D), BF16),
            pltpu.VMEM((ROWS, HD), BF16),
            dma((2,)),
            dma((3,)),
            dma,
            dma,
            dma((rings,)),
            dma((rings,)),
            dma((UNITS,)),
            dma((UNITS,)),
            dma((UNITS,)),
            dma((UNITS,)),
            dma((UNITS,)),
            dma((UNITS,)),
            dma((UNITS,)),
            dma((UNITS,)),
            pltpu.SemaphoreType.REGULAR,
        ],
        compiler_params=pltpu.CompilerParams(
            has_side_effects=True, vmem_limit_bytes=60 * 1024 * 1024
        ),
        name="blocks",
    )(
        x_in.reshape(VIDS, places, D),
        x_tan.reshape(VIDS, places, D),
        w_qkv[0],
        w_out[0],
        qk_gain[0],
        t_index,
        *waves,
    )
    return (out[None, :, None], tan[None, :, None])


def solution(mesh):
    count = mesh.shape["seq"]
    sizes = (count // 8, 2, 4)
    placed = (
        P(None, "seq", None, None),
        P(None, "seq", None, None),
        P(),
        P("section", "seq", None),
        P("section", "seq", None),
        P("section", None, None),
        P("section", None, None),
        P("section", None, None),
        P("section", None, None),
    )
    return jax.shard_map(
        functools.partial(shards, sizes),
        mesh=mesh,
        in_specs=placed,
        out_specs=(P("section", None, "seq", None, None), P("section", None, "seq", None, None)),
        check_vma=False,
    )
```

```python
import functools
import math

import jax
import jax.numpy as jnp
from jax import lax
from jax.experimental import pallas as pl
from jax.experimental.pallas import tpu as pltpu
from jax.sharding import PartitionSpec as P

HEADS = 8
HEAD = 128
T_STEPS = 1000
D = 2048
KT = D // HEAD
HD = HEADS * HEAD
F = 64
NP = 2
VIDS = 2
UNITS = VIDS * NP
ROWS = 2 * F
HALF = F
HOP_PARTS = 4
STRIDE = 27
EPS = 1e-06
F32 = jnp.float32
BF16 = jnp.bfloat16
MESH = pl.DeviceIdType.MESH
ROWS_OUT = 16
PACKED = 2 * 3 * HD + D
Z_LAST, Y_LAST = 2560, 5632


def timing(amp, freq, phase, time_value):
    angle = freq * time_value + phase
    return (amp * jnp.sin(angle), amp * freq * jnp.cos(angle))


class Gather:
    def __init__(self, sizes, section, coords, weights, send, recv):
        self.sizes, self.section, self.coords = sizes, section, coords
        self.weights, self.send, self.recv = weights, send, recv
        self.live = []
        self.sems = 0
        self.rings = {}

    def peer(self, axis, by):
        z, xl, y = self.coords
        nz, nx, ny = self.sizes
        if axis == "z":
            z = lax.rem(z + by + nz, nz)
        elif axis == "y":
            y = lax.rem(y + by + ny, ny)
        else:
            xl = nx - 1 - xl
        return (self.section, (z * nx + xl) * ny + y)

    def copy(self, ref, sem, peer):
        return pltpu.make_async_remote_copy(
            src_ref=ref,
            dst_ref=ref,
            send_sem=self.send.at[sem],
            recv_sem=self.recv.at[sem],
            device_id=peer,
            device_id_type=MESH,
        )

    def start(self, copy):
        copy.start()
        self.live.append(copy)

    def ring(self, axis, first, stop, fixed, single=False):
        size = self.sizes[0] if axis == "z" else self.sizes[2]
        me = self.coords[0] if axis == "z" else self.coords[2]
        last = size // 2
        first_sem = self.sems
        self.sems += 2 * last

        def copy(way, step, index):
            z, y = (index, fixed) if axis == "z" else (fixed, index)
            begin, width = first, stop - first
            xl = self.coords[1] if single else slice(None)
            if step == last - 1:
                if single:
                    width = width // 2
                    begin = begin + way * width
                else:
                    xl = way
            ref = self.weights.at[z, xl, y, :, pl.ds(begin, width)]
            return self.copy(ref, first_sem + 2 * step + way, self.peer(axis, 1 - 2 * way))

        def at(way, step):
            return lax.rem(me - (1 - 2 * way) * step + size, size)

        for step in range(last):
            for way in (0, 1):
                self.start(copy(way, step, at(way, step)))
            yield
            for way in (0, 1):
                copy(way, step, at(way, step + 1)).wait_recv()

    def beside(self, fixed):
        sem = self.sems
        self.sems += 1
        columns = pl.ds(Y_LAST, PACKED - Y_LAST)
        _, xl, _ = self.coords
        nx = self.sizes[1]
        self.start(
            self.copy(self.weights.at[fixed, xl, :, :, columns], sem, self.peer("x", 0))
        )
        yield
        self.copy(
            self.weights.at[fixed, nx - 1 - xl, :, :, columns], sem, self.peer("x", 0)
        ).wait_recv()

    def build(self):
        z, _, y = self.coords
        nz, _, ny = self.sizes
        rings = self.rings
        rings["a"] = self.ring("y", 0, Z_LAST, z)
        rings["b"] = self.ring("z", Z_LAST, Y_LAST, y)
        rings["c"] = self.ring("z", Y_LAST, PACKED, y, True)
        for by in range(ny):
            rings["az", by] = self.ring("z", 0, Z_LAST, lax.rem(y + by, ny))
        for by in range(nz):
            there = lax.rem(z + by, nz)
            rings["by", by] = self.ring("y", Z_LAST, Y_LAST, there)
            rings["cy", by] = self.ring("y", Y_LAST, PACKED, there, True)
            rings["cx", by] = self.beside(there)

    def go(self, *names):
        for name in names:
            next(self.rings[name], None)

    def finish(self):
        for copy in self.live:
            copy.wait_send()


def spread(source, tall, start):
    count = source.shape[0]
    for k in range(KT):
        tall[pl.ds(start + k, count, stride=KT), :] = source[:, k * HEAD : (k + 1) * HEAD].astype(
            F32
        )


def normalize(values, tangents, gain):
    inverse = lax.rsqrt(jnp.mean(values * values, axis=-1, keepdims=True) + EPS)
    cross = jnp.mean(values * tangents, axis=-1, keepdims=True)
    scaled = values * inverse
    return (
        (scaled * gain).astype(BF16),
        ((inverse * tangents - values * inverse**3 * cross) * gain).astype(BF16),
    )


def attend(q2, k2, v2, gains_ref):
    factor = 1.0 / math.sqrt(HEAD)
    qn, dqn = normalize(q2[:HALF], q2[HALF:], gains_ref[0:1, :])
    kn, dkn = normalize(k2[:HALF], k2[HALF:], gains_ref[1:2, :])
    value, dvalue = v2[:HALF].astype(BF16), v2[HALF:].astype(BF16)

    def against(rows, columns):
        return lax.dot_general(
            rows, columns, (((1,), (1,)), ((), ())), preferred_element_type=F32
        )

    scores = against(jnp.concatenate([qn, dqn], axis=0), kn)
    score = scores[:HALF] * factor
    dscore = (scores[HALF:] + against(qn, dkn)) * factor
    expo = jnp.exp(score)
    prob = expo * (1.0 / jnp.sum(expo, axis=-1, keepdims=True))
    growth = prob * dscore
    dprob = growth - prob * jnp.sum(growth, axis=-1, keepdims=True)
    prob, dprob = prob.astype(BF16), dprob.astype(BF16)
    mixed = jnp.dot(
        jnp.concatenate([prob, dprob], axis=0), value, preferred_element_type=F32
    )
    return mixed[:HALF], mixed[HALF:] + jnp.dot(prob, dvalue, preferred_element_type=F32)


def block_step(
    unit, entering, leaving, weights, gains_ref, mods_ref, dmods_ref, tall, flat, att
):
    group = 8
    vid = unit // NP

    @pl.loop(0, F // group, unroll=2)
    def _(i):
        first = pl.multiple_of(i * group, group)
        hidden = entering[unit, pl.ds(first, group), 0].astype(F32)
        tangent = entering[unit, pl.ds(first, group), 1].astype(F32)

        def mean(values):
            return jnp.sum(
                jnp.sum(values, axis=1, keepdims=True), axis=2, keepdims=True
            ) * (1.0 / D)

        inverse = lax.rsqrt(mean(hidden * hidden) + EPS)
        cross = mean(hidden * tangent)
        normed = hidden * inverse
        dnormed = inverse * tangent - hidden * inverse**3 * cross
        scale = 1.0 + mods_ref[vid, 1][None]
        modulated = normed * scale + mods_ref[vid, 0][None]
        dmodulated = dnormed * scale + normed * dmods_ref[vid, 1][None] + dmods_ref[vid, 0][None]
        row = pl.multiple_of(first * KT, group * KT)
        tall[pl.ds(row, group * KT), :] = modulated.reshape(group * KT, HEAD)
        tall[pl.ds(row + HALF * KT, group * KT), :] = dmodulated.reshape(group * KT, HEAD)

    for k in range(KT):
        flat[:, k * HEAD : (k + 1) * HEAD] = tall[pl.ds(k, ROWS, stride=KT), :].astype(BF16)

    def third(number, pair):
        column = number * HD + pair * 2 * HEAD
        halves = [
            weights[
                :, :, :, :, column + lower * 3 * HD : column + lower * 3 * HD + 2 * HEAD
            ].reshape(F, 1, ROWS_OUT, 2 * HEAD)
            for lower in range(2)
        ]
        matrix = jnp.concatenate(halves, axis=1).reshape(D, 2 * HEAD)
        return jnp.dot(flat[...], matrix, preferred_element_type=F32)

    ahead = [third(number, 0) for number in range(3)]
    for pair in range(HEADS // 2):
        q2, k2, v2 = ahead
        if pair + 1 < HEADS // 2:
            ahead = [third(number, pair + 1) for number in range(3)]
        for one in range(2):
            lanes = slice(one * HEAD, (one + 1) * HEAD)
            output, doutput = attend(q2[:, lanes], k2[:, lanes], v2[:, lanes], gains_ref)
            column = (pair * 2 + one) * HEAD
            att[:HALF, column : column + HEAD] = output.astype(BF16)
            att[HALF:, column : column + HEAD] = doutput.astype(BF16)

    for n in range(KT // 2):
        column = 2 * 3 * HD + n * 2 * HEAD
        matrix = weights[:, :, :, :, column : column + 2 * HEAD].reshape(HD, 2 * HEAD)
        y = jnp.dot(att[...], matrix, preferred_element_type=F32)
        tall[pl.ds(2 * n, ROWS, stride=KT), :] = y[:, :HEAD]
        tall[pl.ds(2 * n + 1, ROWS, stride=KT), :] = y[:, HEAD:]

    @pl.loop(0, F // group, unroll=2)
    def _(i):
        first = pl.multiple_of(i * group, group)
        row = pl.multiple_of(first * KT, group * KT)
        y = tall[pl.ds(row, group * KT), :].reshape(group, KT, HEAD)
        dy = tall[pl.ds(row + HALF * KT, group * KT), :].reshape(group, KT, HEAD)
        hidden = entering[unit, pl.ds(first, group), 0].astype(F32)
        tangent = entering[unit, pl.ds(first, group), 1].astype(F32)
        gate = mods_ref[vid, 2][None]
        dgate = dmods_ref[vid, 2][None]
        leaving[unit, pl.ds(first, group), 0] = (hidden + gate * y).astype(BF16)
        leaving[unit, pl.ds(first, group), 1] = (tangent + dgate * y + gate * dy).astype(BF16)


def kernel(
    sizes,
    sections,
    x_ref,
    t_ref,
    wqkv_ref,
    wout_ref,
    gains_ref,
    index_ref,
    amp_ref,
    freq_ref,
    phase_ref,
    out_ref,
    tan_ref,
    weights,
    mods_ref,
    dmods_ref,
    plain,
    staged,
    relay,
    entering,
    leaving,
    returned,
    tall,
    flat,
    att,
    load_sem,
    own_sem,
    swap_send,
    swap_recv,
    ring_send,
    ring_recv,
    x_send,
    x_recv,
    relay_send,
    relay_recv,
    pass_send,
    pass_recv,
    out_send,
    out_recv,
    turn_sem,
):
    nz, nx, ny = sizes
    count = nz * nx * ny
    section = lax.axis_index("section")
    me = lax.axis_index("seq")
    coords = (me // (nx * ny), (me // ny) % nx, me % ny)
    z, xl, y = coords
    first_half = section < 2

    def flip(index):
        return index + ny - 2 * ny * ((index // ny) % nx)

    across = flip(me)
    slot = jnp.where(first_half, me, across)
    neighbour = (section, lax.rem(me + 1, count))
    group = 8

    def exchange(source, row_of, target, place, send, recv):
        pltpu.make_async_copy(source.at[row_of(me)], target.at[place], recv).start()

        @pl.loop(1, count, unroll=7)
        def _(by):
            to = lax.rem(me + by * STRIDE, count)
            pltpu.make_async_remote_copy(
                src_ref=source.at[row_of(to)],
                dst_ref=target.at[place],
                send_sem=send,
                recv_sem=recv,
                device_id=(section, to),
                device_id_type=MESH,
            ).start()

    def exchange_came(source, target, recv):
        pltpu.make_async_copy(source, target, recv).wait()

    def exchange_sent(source, target, send, recv):
        pltpu.make_async_remote_copy(
            src_ref=source.at[pl.ds(0, count - 1)],
            dst_ref=target.at[pl.ds(0, count - 1)],
            send_sem=send,
            recv_sem=recv,
            device_id=neighbour,
            device_id_type=MESH,
        ).wait_send()

    leads = lax.rem(section, 2) == 0
    loads = [
        pltpu.make_async_copy(ref, plain.at[tan], load_sem.at[tan])
        for tan, ref in enumerate((x_ref, t_ref))
    ]

    @pl.when(leads)
    def _():
        for load in loads:
            load.start()

    own = []
    for part, (ref, first, width) in enumerate(
        (
            (wqkv_ref.at[pl.ds(0, ROWS_OUT)], 0, 3 * HD),
            (wqkv_ref.at[pl.ds(ROWS_OUT, ROWS_OUT)], 3 * HD, 3 * HD),
            (wout_ref, 6 * HD, D),
        )
    ):
        home = weights.at[z, xl, y, :, pl.ds(first, width)]
        own.append(pltpu.make_async_copy(ref, home, own_sem.at[part]))
        own[-1].start()
    for copy in own:
        copy.wait()

    @pl.when(jnp.logical_not(leads))
    def _():
        pl.semaphore_wait(turn_sem, 1)

    gather = Gather(sizes, section, coords, weights, ring_send, ring_recv)
    gather.build()
    go = gather.go
    mine = weights.at[z, xl, y, :, pl.ds(0, Y_LAST)]
    swap = pltpu.make_async_remote_copy(
        src_ref=mine,
        dst_ref=mine,
        send_sem=swap_send,
        recv_sem=swap_recv,
        device_id=(section, across),
        device_id_type=MESH,
    )
    theirs = weights.at[z, nx - 1 - xl, y, :, pl.ds(0, Y_LAST)]
    swapped = pltpu.make_async_remote_copy(
        src_ref=theirs,
        dst_ref=theirs,
        send_sem=swap_send,
        recv_sem=swap_recv,
        device_id=(section, across),
        device_id_type=MESH,
    )
    swap.start()
    go("c", ("cy", 0))

    def prepare(vid):
        for tan in range(2):
            spread(plain.at[tan, vid], tall, 0)

            @pl.loop(0, count // group)
            def _(i):
                first = pl.multiple_of(i * group, group)
                row = pl.multiple_of(first * NP * KT, group * NP * KT)
                tiles = (
                    tall[pl.ds(row, group * NP * KT), :]
                    .astype(BF16)
                    .reshape(group, NP, KT, HEAD)
                )
                for pos in range(NP):
                    staged[vid * NP + pos, pl.ds(first, group), tan] = tiles[:, pos]

    @pl.when(leads)
    def _():
        for load in loads:
            load.wait()
        prepare(0)

    @pl.when(section == 0)
    def _():
        exchange(
            staged.at[0], lambda f: f, entering.at[0], me, x_send.at[0], x_recv.at[0]
        )

    def second_round(unit):
        exchange(
            staged.at[unit], flip, relay.at[unit], me, x_send.at[unit], x_recv.at[unit]
        )

    @pl.when(section == 2)
    def _():
        second_round(1)
        prepare(1)
        second_round(2)
        second_round(3)

    def relayed(unit):
        return pltpu.make_async_remote_copy(
            src_ref=relay.at[unit],
            dst_ref=entering.at[unit],
            send_sem=relay_send.at[unit],
            recv_sem=relay_recv.at[unit],
            device_id=(0, across),
            device_id_type=MESH,
        )

    def pass_to_first(unit):
        @pl.when(section == 2)
        def _():
            exchange_came(staged.at[unit], relay.at[unit], x_recv.at[unit])
            relayed(unit).start()

    for vid in range(VIDS):
        time_value = (index_ref[vid].astype(F32) + 0.5) * (math.pi / (2.0 * T_STEPS))
        mods_ref[vid], dmods_ref[vid] = timing(
            amp_ref[...], freq_ref[...], phase_ref[...], time_value
        )

    swapped.wait_recv()
    go("b", "a", ("by", 0), ("az", 0))
    go("c", ("cy", 1), ("cy", 7))
    go("a", ("az", 1), ("az", 3))
    go(("cy", 0),)
    go("b", ("by", 1), ("by", 7))
    go("c", ("cy", 2), ("cy", 6))

    @pl.when(leads)
    def _():
        pl.semaphore_signal(
            turn_sem, inc=1, device_id=(section + 1, me), device_id_type=MESH
        )

    go("a", ("az", 2))
    go(("cy", 0), ("cx", 0), ("cy", 1), ("cy", 7))
    go(("az", 0), ("by", 0))
    go("c", ("cy", 3), ("cy", 5))
    go(("cy", 1), ("cx", 1), ("cy", 7), ("cx", 7), ("cy", 2), ("cy", 6))
    go("b", ("by", 2), ("by", 6))
    go("c", ("cy", 4))
    pass_to_first(1)
    go(("az", 1), ("az", 3), ("by", 1), ("by", 7), ("az", 2))
    go(("cy", 2), ("cx", 2), ("cy", 6), ("cx", 6), ("cy", 3), ("cy", 5), ("cy", 4))
    go("b", ("by", 3), ("by", 5))
    go(("az", 0), ("by", 0), ("az", 1), ("az", 3))
    go(("cy", 3), ("cx", 3), ("cy", 5), ("cx", 5), ("cy", 4), ("cx", 4))
    pass_to_first(2)

    go("b", ("by", 4))
    go(("by", 2), ("by", 6), ("az", 2), ("by", 1), ("by", 7), ("az", 0))
    pass_to_first(3)
    go(("by", 3), ("by", 5), ("az", 1), ("az", 3), ("by", 4), ("az", 2))
    go(("by", 2), ("by", 6), ("az", 0), ("by", 3), ("by", 5))
    go(("az", 1), ("az", 3), ("by", 4), ("az", 2))
    go(*(("cx", by) for by in range(nz)))

    @pl.when(section == 1)
    def _():
        pl.semaphore_signal(turn_sem, inc=1, device_id=(0, me), device_id_type=MESH)

    def onward(unit, first=0, frames=F):
        return pltpu.make_async_remote_copy(
            src_ref=leaving.at[unit, pl.ds(first, frames)],
            dst_ref=entering.at[unit, pl.ds(first, frames)],
            send_sem=pass_send.at[unit],
            recv_sem=pass_recv.at[unit],
            device_id=(
                lax.rem(section + 1, sections),
                jnp.where(section == 1, across, me),
            ),
            device_id_type=MESH,
        )

    def send_back(unit):
        exchange(
            leaving.at[unit],
            lambda f: f,
            returned.at[unit],
            slot,
            out_send.at[unit],
            out_recv.at[unit],
        )

    @pl.loop(0, UNITS)
    def _(unit):
        @pl.when(jnp.logical_and(section == 0, unit == 0))
        def _():
            exchange_came(staged.at[0], entering.at[0], x_recv.at[0])

        @pl.when(jnp.logical_and(section == 0, unit > 0))
        def _():
            relayed(unit).wait_recv()

        @pl.when(section > 0)
        def _():
            onward(unit).wait_recv()

        block_step(
            unit, entering, leaving, weights, gains_ref, mods_ref, dmods_ref, tall, flat, att
        )

        @pl.when(section < sections - 1)
        def _():
            for part in range(HOP_PARTS):
                onward(unit, part * (F // HOP_PARTS), F // HOP_PARTS).start()

        @pl.when(section > 0)
        def _():
            send_back(unit)

    @pl.when(section == 0)
    def _():
        pl.semaphore_wait(turn_sem, 1)

        @pl.loop(0, UNITS)
        def _(unit):
            send_back(unit)

    @pl.loop(0, VIDS)
    def _(vid):
        for pos in range(NP):
            unit = vid * NP + pos
            exchange_came(leaving.at[unit], returned.at[unit], out_recv.at[unit])

            @pl.loop(0, count // group)
            def _(i):
                first = pl.multiple_of(i * group, group)
                for tan in range(2):
                    tiles = returned[unit, pl.ds(first, group), tan].astype(F32)
                    for one in range(group):
                        row = pl.multiple_of(
                            ((tan * count + first + one) * NP + pos) * KT, KT
                        )
                        tall[pl.ds(row, KT), :] = tiles[one]

        for tan, result in enumerate((out_ref, tan_ref)):
            for k in range(KT):
                result[vid, :, k * HEAD : (k + 1) * HEAD] = tall[
                    pl.ds(tan * count * NP * KT + k, count * NP, stride=KT), :
                ].astype(BF16)

    gather.finish()
    swap.wait_send()

    @pl.loop(0, UNITS)
    def _(unit):
        exchange_sent(
            leaving.at[unit], returned.at[unit], out_send.at[unit], out_recv.at[unit]
        )

        @pl.when(section < sections - 1)
        def _():
            onward(unit).wait_send()

        @pl.when(
            jnp.logical_or(
                jnp.logical_and(section == 0, unit == 0),
                jnp.logical_and(section == 2, unit > 0),
            )
        )
        def _():
            exchange_sent(
                staged.at[unit], relay.at[unit], x_send.at[unit], x_recv.at[unit]
            )

        @pl.when(jnp.logical_and(section == 2, unit > 0))
        def _():
            relayed(unit).wait_send()


def shards(sizes, x_in, x_tan, t_index, w_qkv, w_out, qk_gain, mod_amp, mod_freq, mod_phase):
    nz, nx, ny = sizes
    count = nz * nx * ny
    sections = lax.axis_size("section")
    places = x_in.shape[2]
    waves = [wave.reshape(3, KT, HEAD) for wave in (mod_amp, mod_freq, mod_phase)]
    outside = pl.BlockSpec(memory_space=pl.ANY)
    inside = pl.BlockSpec(memory_space=pltpu.VMEM)
    result = jax.ShapeDtypeStruct((VIDS, places, D), BF16)
    units = (UNITS, F, 2, KT, HEAD)
    rings = 2 * (ny // 2) * (1 + 2 * nz) + 2 * (nz // 2) * (2 + ny) + nz
    dma = pltpu.SemaphoreType.DMA
    out, tan = pl.pallas_call(
        functools.partial(kernel, sizes, sections),
        out_shape=(result, result),
        in_specs=[outside] * 4
        + [inside, pl.BlockSpec(memory_space=pltpu.SMEM)]
        + [inside] * 3,
        out_specs=(inside, inside),
        scratch_shapes=[
            pltpu.VMEM((nz, nx, ny, ROWS_OUT, PACKED), BF16),
            pltpu.VMEM((VIDS, 3, KT, HEAD), F32),
            pltpu.VMEM((VIDS, 3, KT, HEAD), F32),
            pltpu.VMEM((2, VIDS, places, D), BF16),
            pltpu.VMEM(units, BF16),
            pltpu.VMEM(units, BF16),
            pltpu.VMEM(units, BF16),
            pltpu.VMEM(units, BF16),
            pltpu.VMEM(units, BF16),
            pltpu.VMEM((2 * places * KT, HEAD), F32),
            pltpu.VMEM((ROWS, D), BF16),
            pltpu.VMEM((ROWS, HD), BF16),
            dma((2,)),
            dma((3,)),
            dma,
            dma,
            dma((rings,)),
            dma((rings,)),
            dma((UNITS,)),
            dma((UNITS,)),
            dma((UNITS,)),
            dma((UNITS,)),
            dma((UNITS,)),
            dma((UNITS,)),
            dma((UNITS,)),
            dma((UNITS,)),
            pltpu.SemaphoreType.REGULAR,
        ],
        compiler_params=pltpu.CompilerParams(
            has_side_effects=True, vmem_limit_bytes=60 * 1024 * 1024
        ),
        name="blocks",
    )(
        x_in.reshape(VIDS, places, D),
        x_tan.reshape(VIDS, places, D),
        w_qkv[0],
        w_out[0],
        qk_gain[0],
        t_index,
        *waves,
    )
    return (out[None, :, None], tan[None, :, None])


def solution(mesh):
    count = mesh.shape["seq"]
    sizes = (count // 8, 2, 4)
    placed = (
        P(None, "seq", None, None),
        P(None, "seq", None, None),
        P(),
        P("section", "seq", None),
        P("section", "seq", None),
        P("section", None, None),
        P("section", None, None),
        P("section", None, None),
        P("section", None, None),
    )
    return jax.shard_map(
        functools.partial(shards, sizes),
        mesh=mesh,
        in_specs=placed,
        out_specs=(P("section", None, "seq", None, None), P("section", None, "seq", None, None)),
        check_vma=False,
    )
```

```python
import functools
import math

import jax
import jax.numpy as jnp
from jax import lax
from jax.experimental import pallas as pl
from jax.experimental.pallas import tpu as pltpu
from jax.sharding import PartitionSpec as P

HEADS = 8
HEAD = 128
T_STEPS = 1000
D = 2048
KT = D // HEAD
HD = HEADS * HEAD
F = 64
NP = 2
VIDS = 2
UNITS = VIDS * NP
ROWS = 2 * F
HALF = F
HOP_PARTS = 4
STRIDE = 27
EPS = 1e-06
F32 = jnp.float32
BF16 = jnp.bfloat16
MESH = pl.DeviceIdType.MESH
ROWS_OUT = 16
PACKED = 2 * 3 * HD + D
Z_LAST, Y_LAST = 2816, 5632


def timing(amp, freq, phase, time_value):
    angle = freq * time_value + phase
    return (amp * jnp.sin(angle), amp * freq * jnp.cos(angle))


class Gather:
    def __init__(self, sizes, section, coords, weights, send, recv):
        self.sizes, self.section, self.coords = sizes, section, coords
        self.weights, self.send, self.recv = weights, send, recv
        self.live = []
        self.sems = 0
        self.rings = {}

    def peer(self, axis, by):
        z, xl, y = self.coords
        nz, nx, ny = self.sizes
        if axis == "z":
            z = lax.rem(z + by + nz, nz)
        elif axis == "y":
            y = lax.rem(y + by + ny, ny)
        else:
            xl = nx - 1 - xl
        return (self.section, (z * nx + xl) * ny + y)

    def copy(self, ref, sem, peer):
        return pltpu.make_async_remote_copy(
            src_ref=ref,
            dst_ref=ref,
            send_sem=self.send.at[sem],
            recv_sem=self.recv.at[sem],
            device_id=peer,
            device_id_type=MESH,
        )

    def start(self, piece, begin, width, sem, peer):
        for part in range(2):
            columns = pl.ds(begin + part * (width // 2), width // 2)
            self.copy(piece(columns), sem, peer).start()
        self.live.append(self.copy(piece(pl.ds(begin, width)), sem, peer))

    def ring(self, axis, first, stop, fixed, single=False):
        size = self.sizes[0] if axis == "z" else self.sizes[2]
        me = self.coords[0] if axis == "z" else self.coords[2]
        last = size // 2
        first_sem = self.sems
        self.sems += 2 * last

        def arguments(way, step, index):
            z, y = (index, fixed) if axis == "z" else (fixed, index)
            begin, width = first, stop - first
            xl = self.coords[1] if single else slice(None)
            if step == last - 1:
                if single:
                    width = width // 2
                    begin = begin + way * width
                else:
                    xl = way

            def piece(columns):
                return self.weights.at[z, xl, y, :, columns]

            return piece, begin, width, first_sem + 2 * step + way, self.peer(axis, 1 - 2 * way)

        def at(way, step):
            return lax.rem(me - (1 - 2 * way) * step + size, size)

        for step in range(last):
            for way in (0, 1):
                self.start(*arguments(way, step, at(way, step)))
            yield
            for way in (0, 1):
                piece, begin, width, sem, peer = arguments(way, step, at(way, step + 1))
                self.copy(piece(pl.ds(begin, width)), sem, peer).wait_recv()

    def beside(self, fixed):
        sem = self.sems
        self.sems += 1
        _, xl, _ = self.coords
        nx = self.sizes[1]
        peer = self.peer("x", 0)
        self.start(
            lambda columns: self.weights.at[fixed, xl, :, :, columns],
            Y_LAST,
            PACKED - Y_LAST,
            sem,
            peer,
        )
        yield
        columns = pl.ds(Y_LAST, PACKED - Y_LAST)
        self.copy(self.weights.at[fixed, nx - 1 - xl, :, :, columns], sem, peer).wait_recv()

    def build(self):
        z, _, y = self.coords
        nz, _, ny = self.sizes
        rings = self.rings
        rings["a"] = self.ring("y", 0, Z_LAST, z)
        rings["b"] = self.ring("z", Z_LAST, Y_LAST, y)
        rings["c"] = self.ring("z", Y_LAST, PACKED, y, True)
        for by in range(ny):
            rings["az", by] = self.ring("z", 0, Z_LAST, lax.rem(y + by, ny))
        for by in range(nz):
            there = lax.rem(z + by, nz)
            rings["by", by] = self.ring("y", Z_LAST, Y_LAST, there)
            rings["cy", by] = self.ring("y", Y_LAST, PACKED, there, True)
            rings["cx", by] = self.beside(there)

    def go(self, *names):
        for name in names:
            next(self.rings[name], None)

    def finish(self):
        for copy in self.live:
            copy.wait_send()


def spread(source, tall, start):
    count = source.shape[0]
    for k in range(KT):
        tall[pl.ds(start + k, count, stride=KT), :] = source[:, k * HEAD : (k + 1) * HEAD].astype(
            F32
        )


def normalize(values, tangents, gain):
    inverse = lax.rsqrt(jnp.mean(values * values, axis=-1, keepdims=True) + EPS)
    cross = jnp.mean(values * tangents, axis=-1, keepdims=True)
    scaled = values * inverse
    return (
        (scaled * gain).astype(BF16),
        ((inverse * tangents - values * inverse**3 * cross) * gain).astype(BF16),
    )


def attend(q2, k2, v2, gains_ref):
    factor = 1.0 / math.sqrt(HEAD)
    qn, dqn = normalize(q2[:HALF], q2[HALF:], gains_ref[0:1, :])
    kn, dkn = normalize(k2[:HALF], k2[HALF:], gains_ref[1:2, :])
    value, dvalue = v2[:HALF].astype(BF16), v2[HALF:].astype(BF16)

    def against(rows, columns):
        return lax.dot_general(
            rows, columns, (((1,), (1,)), ((), ())), preferred_element_type=F32
        )

    scores = against(jnp.concatenate([qn, dqn], axis=0), kn)
    score = scores[:HALF] * factor
    dscore = (scores[HALF:] + against(qn, dkn)) * factor
    expo = jnp.exp(score)
    prob = expo * (1.0 / jnp.sum(expo, axis=-1, keepdims=True))
    growth = prob * dscore
    dprob = growth - prob * jnp.sum(growth, axis=-1, keepdims=True)
    prob, dprob = prob.astype(BF16), dprob.astype(BF16)
    mixed = jnp.dot(
        jnp.concatenate([prob, dprob], axis=0), value, preferred_element_type=F32
    )
    return mixed[:HALF], mixed[HALF:] + jnp.dot(prob, dvalue, preferred_element_type=F32)


def block_step(
    unit, entering, leaving, weights, gains_ref, mods_ref, dmods_ref, tall, flat, att
):
    group = 8
    vid = unit // NP

    @pl.loop(0, F // group, unroll=4)
    def _(i):
        first = pl.multiple_of(i * group, group)
        hidden = entering[unit, pl.ds(first, group), 0].astype(F32)
        tangent = entering[unit, pl.ds(first, group), 1].astype(F32)

        def mean(values):
            return jnp.sum(
                jnp.sum(values, axis=1, keepdims=True), axis=2, keepdims=True
            ) * (1.0 / D)

        inverse = lax.rsqrt(mean(hidden * hidden) + EPS)
        cross = mean(hidden * tangent)
        normed = hidden * inverse
        dnormed = inverse * tangent - hidden * inverse**3 * cross
        scale = 1.0 + mods_ref[vid, 1][None]
        modulated = normed * scale + mods_ref[vid, 0][None]
        dmodulated = dnormed * scale + normed * dmods_ref[vid, 1][None] + dmods_ref[vid, 0][None]
        row = pl.multiple_of(first * KT, group * KT)
        tall[pl.ds(row, group * KT), :] = modulated.reshape(group * KT, HEAD)
        tall[pl.ds(row + HALF * KT, group * KT), :] = dmodulated.reshape(group * KT, HEAD)

    for k in range(KT):
        flat[:, k * HEAD : (k + 1) * HEAD] = tall[pl.ds(k, ROWS, stride=KT), :].astype(BF16)

    def third(number, pair):
        column = number * HD + pair * 2 * HEAD
        halves = [
            weights[
                :, :, :, :, column + lower * 3 * HD : column + lower * 3 * HD + 2 * HEAD
            ].reshape(F, 1, ROWS_OUT, 2 * HEAD)
            for lower in range(2)
        ]
        matrix = jnp.concatenate(halves, axis=1).reshape(D, 2 * HEAD)
        return jnp.dot(flat[...], matrix, preferred_element_type=F32)

    ahead = [third(number, 0) for number in range(3)]
    for pair in range(HEADS // 2):
        q2, k2, v2 = ahead
        if pair + 1 < HEADS // 2:
            ahead = [third(number, pair + 1) for number in range(3)]
        for one in range(2):
            lanes = slice(one * HEAD, (one + 1) * HEAD)
            output, doutput = attend(q2[:, lanes], k2[:, lanes], v2[:, lanes], gains_ref)
            column = (pair * 2 + one) * HEAD
            att[:HALF, column : column + HEAD] = output.astype(BF16)
            att[HALF:, column : column + HEAD] = doutput.astype(BF16)

    for n in range(KT // 2):
        column = 2 * 3 * HD + n * 2 * HEAD
        matrix = weights[:, :, :, :, column : column + 2 * HEAD].reshape(HD, 2 * HEAD)
        y = jnp.dot(att[...], matrix, preferred_element_type=F32)
        tall[pl.ds(2 * n, ROWS, stride=KT), :] = y[:, :HEAD]
        tall[pl.ds(2 * n + 1, ROWS, stride=KT), :] = y[:, HEAD:]

    @pl.loop(0, F // group, unroll=4)
    def _(i):
        first = pl.multiple_of(i * group, group)
        row = pl.multiple_of(first * KT, group * KT)
        y = tall[pl.ds(row, group * KT), :].reshape(group, KT, HEAD)
        dy = tall[pl.ds(row + HALF * KT, group * KT), :].reshape(group, KT, HEAD)
        hidden = entering[unit, pl.ds(first, group), 0].astype(F32)
        tangent = entering[unit, pl.ds(first, group), 1].astype(F32)
        gate = mods_ref[vid, 2][None]
        dgate = dmods_ref[vid, 2][None]
        leaving[unit, pl.ds(first, group), 0] = (hidden + gate * y).astype(BF16)
        leaving[unit, pl.ds(first, group), 1] = (tangent + dgate * y + gate * dy).astype(BF16)


def kernel(
    sizes,
    sections,
    x_ref,
    t_ref,
    wqkv_ref,
    wout_ref,
    gains_ref,
    index_ref,
    amp_ref,
    freq_ref,
    phase_ref,
    out_ref,
    tan_ref,
    weights,
    mods_ref,
    dmods_ref,
    plain,
    staged,
    relay,
    entering,
    leaving,
    returned,
    tall,
    flat,
    att,
    load_sem,
    own_sem,
    swap_send,
    swap_recv,
    ring_send,
    ring_recv,
    x_send,
    x_recv,
    relay_send,
    relay_recv,
    pass_send,
    pass_recv,
    out_send,
    out_recv,
    turn_sem,
):
    nz, nx, ny = sizes
    count = nz * nx * ny
    section = lax.axis_index("section")
    me = lax.axis_index("seq")
    coords = (me // (nx * ny), (me // ny) % nx, me % ny)
    z, xl, y = coords
    first_half = section < 2

    def flip(index):
        return index + ny - 2 * ny * ((index // ny) % nx)

    across = flip(me)
    slot = jnp.where(first_half, me, across)
    neighbour = (section, lax.rem(me + 1, count))
    group = 8

    def exchange(source, row_of, target, place, send, recv):
        pltpu.make_async_copy(source.at[row_of(me)], target.at[place], recv).start()

        @pl.loop(1, count, unroll=21)
        def _(by):
            to = lax.rem(me + by * STRIDE, count)
            pltpu.make_async_remote_copy(
                src_ref=source.at[row_of(to)],
                dst_ref=target.at[place],
                send_sem=send,
                recv_sem=recv,
                device_id=(section, to),
                device_id_type=MESH,
            ).start()

    def exchange_came(source, target, recv):
        pltpu.make_async_copy(source, target, recv).wait()

    def exchange_sent(source, target, send, recv):
        pltpu.make_async_remote_copy(
            src_ref=source.at[pl.ds(0, count - 1)],
            dst_ref=target.at[pl.ds(0, count - 1)],
            send_sem=send,
            recv_sem=recv,
            device_id=neighbour,
            device_id_type=MESH,
        ).wait_send()

    leads = lax.rem(section, 2) == 0
    loads = [
        pltpu.make_async_copy(ref, plain.at[tan], load_sem.at[tan])
        for tan, ref in enumerate((x_ref, t_ref))
    ]

    @pl.when(leads)
    def _():
        for load in loads:
            load.start()

    own = []
    for part, (ref, first, width) in enumerate(
        (
            (wqkv_ref.at[pl.ds(0, ROWS_OUT)], 0, 3 * HD),
            (wqkv_ref.at[pl.ds(ROWS_OUT, ROWS_OUT)], 3 * HD, 3 * HD),
            (wout_ref, 6 * HD, D),
        )
    ):
        home = weights.at[z, xl, y, :, pl.ds(first, width)]
        own.append(pltpu.make_async_copy(ref, home, own_sem.at[part]))
        own[-1].start()
    for copy in own:
        copy.wait()

    @pl.when(jnp.logical_not(leads))
    def _():
        pl.semaphore_wait(turn_sem, 1)

    gather = Gather(sizes, section, coords, weights, ring_send, ring_recv)
    gather.build()
    go = gather.go
    mine = weights.at[z, xl, y, :, pl.ds(0, Y_LAST)]
    swap = pltpu.make_async_remote_copy(
        src_ref=mine,
        dst_ref=mine,
        send_sem=swap_send,
        recv_sem=swap_recv,
        device_id=(section, across),
        device_id_type=MESH,
    )
    theirs = weights.at[z, nx - 1 - xl, y, :, pl.ds(0, Y_LAST)]
    swapped = pltpu.make_async_remote_copy(
        src_ref=theirs,
        dst_ref=theirs,
        send_sem=swap_send,
        recv_sem=swap_recv,
        device_id=(section, across),
        device_id_type=MESH,
    )
    swap.start()
    go("c", ("cy", 0))

    def prepare(vid):
        for tan in range(2):
            spread(plain.at[tan, vid], tall, 0)

            @pl.loop(0, count // group)
            def _(i):
                first = pl.multiple_of(i * group, group)
                row = pl.multiple_of(first * NP * KT, group * NP * KT)
                tiles = (
                    tall[pl.ds(row, group * NP * KT), :]
                    .astype(BF16)
                    .reshape(group, NP, KT, HEAD)
                )
                for pos in range(NP):
                    staged[vid * NP + pos, pl.ds(first, group), tan] = tiles[:, pos]

    @pl.when(leads)
    def _():
        for load in loads:
            load.wait()
        prepare(0)

    @pl.when(section == 0)
    def _():
        exchange(
            staged.at[0], lambda f: f, entering.at[0], me, x_send.at[0], x_recv.at[0]
        )

    def second_round(unit):
        exchange(
            staged.at[unit], flip, relay.at[unit], me, x_send.at[unit], x_recv.at[unit]
        )

    @pl.when(section == 2)
    def _():
        second_round(1)
        prepare(1)
        second_round(2)
        second_round(3)

    def relayed(unit):
        return pltpu.make_async_remote_copy(
            src_ref=relay.at[unit],
            dst_ref=entering.at[unit],
            send_sem=relay_send.at[unit],
            recv_sem=relay_recv.at[unit],
            device_id=(0, across),
            device_id_type=MESH,
        )

    def pass_to_first(unit):
        @pl.when(section == 2)
        def _():
            exchange_came(staged.at[unit], relay.at[unit], x_recv.at[unit])
            relayed(unit).start()

    for vid in range(VIDS):
        time_value = (index_ref[vid].astype(F32) + 0.5) * (math.pi / (2.0 * T_STEPS))
        mods_ref[vid], dmods_ref[vid] = timing(
            amp_ref[...], freq_ref[...], phase_ref[...], time_value
        )

    swapped.wait_recv()
    go("b", "a", ("by", 0), ("az", 0))
    go("c", ("cy", 1), ("cy", 7))
    go("a", ("az", 1), ("az", 3))
    go(("cy", 0),)
    go("b", ("by", 1), ("by", 7))
    go("c", ("cy", 2), ("cy", 6))

    @pl.when(leads)
    def _():
        pl.semaphore_signal(
            turn_sem, inc=1, device_id=(section + 1, me), device_id_type=MESH
        )

    go("a", ("az", 2))
    go(("cy", 0), ("cx", 0), ("cy", 1), ("cy", 7))
    go(("az", 0), ("by", 0))
    go("c", ("cy", 3), ("cy", 5))
    go(("cy", 1), ("cx", 1), ("cy", 7), ("cx", 7), ("cy", 2), ("cy", 6))
    go("b", ("by", 2), ("by", 6))
    go("c", ("cy", 4))
    pass_to_first(1)
    go(("az", 1), ("az", 3), ("by", 1), ("by", 7), ("az", 2))
    go(("cy", 2), ("cx", 2), ("cy", 6), ("cx", 6), ("cy", 3), ("cy", 5), ("cy", 4))
    go("b", ("by", 3), ("by", 5))
    go(("az", 0), ("by", 0), ("az", 1), ("az", 3))
    go(("cy", 3), ("cx", 3), ("cy", 5), ("cx", 5), ("cy", 4), ("cx", 4))
    pass_to_first(2)

    go("b", ("by", 4))
    go(("by", 2), ("by", 6), ("az", 2), ("by", 1), ("by", 7), ("az", 0))
    pass_to_first(3)
    go(("by", 3), ("by", 5), ("az", 1), ("az", 3), ("by", 4), ("az", 2))
    go(("by", 2), ("by", 6), ("az", 0), ("by", 3), ("by", 5))
    go(("az", 1), ("az", 3), ("by", 4), ("az", 2))
    go(*(("cx", by) for by in range(nz)))

    @pl.when(section == 1)
    def _():
        pl.semaphore_signal(turn_sem, inc=1, device_id=(0, me), device_id_type=MESH)

    def onward(unit, first=0, frames=F):
        return pltpu.make_async_remote_copy(
            src_ref=leaving.at[unit, pl.ds(first, frames)],
            dst_ref=entering.at[unit, pl.ds(first, frames)],
            send_sem=pass_send.at[unit],
            recv_sem=pass_recv.at[unit],
            device_id=(
                lax.rem(section + 1, sections),
                jnp.where(section == 1, across, me),
            ),
            device_id_type=MESH,
        )

    def send_back(unit):
        exchange(
            leaving.at[unit],
            lambda f: f,
            returned.at[unit],
            slot,
            out_send.at[unit],
            out_recv.at[unit],
        )

    @pl.loop(0, UNITS)
    def _(unit):
        @pl.when(jnp.logical_and(section == 0, unit == 0))
        def _():
            exchange_came(staged.at[0], entering.at[0], x_recv.at[0])

        @pl.when(jnp.logical_and(section == 0, unit > 0))
        def _():
            relayed(unit).wait_recv()

        @pl.when(section > 0)
        def _():
            onward(unit).wait_recv()

        block_step(
            unit, entering, leaving, weights, gains_ref, mods_ref, dmods_ref, tall, flat, att
        )

        @pl.when(section < sections - 1)
        def _():
            for part in range(HOP_PARTS):
                onward(unit, part * (F // HOP_PARTS), F // HOP_PARTS).start()

        @pl.when(section > 0)
        def _():
            send_back(unit)

    @pl.when(section == 0)
    def _():
        pl.semaphore_wait(turn_sem, 1)

        @pl.loop(0, UNITS)
        def _(unit):
            send_back(unit)

    gather.finish()
    swap.wait_send()

    @pl.loop(0, VIDS)
    def _(vid):
        for pos in range(NP):
            unit = vid * NP + pos
            exchange_came(leaving.at[unit], returned.at[unit], out_recv.at[unit])

            @pl.loop(0, count // group)
            def _(i):
                first = pl.multiple_of(i * group, group)
                for tan in range(2):
                    tiles = returned[unit, pl.ds(first, group), tan].astype(F32)
                    for one in range(group):
                        row = pl.multiple_of(
                            ((tan * count + first + one) * NP + pos) * KT, KT
                        )
                        tall[pl.ds(row, KT), :] = tiles[one]

        for tan, result in enumerate((out_ref, tan_ref)):
            for k in range(KT):
                result[vid, :, k * HEAD : (k + 1) * HEAD] = tall[
                    pl.ds(tan * count * NP * KT + k, count * NP, stride=KT), :
                ].astype(BF16)

    @pl.loop(0, UNITS)
    def _(unit):
        exchange_sent(
            leaving.at[unit], returned.at[unit], out_send.at[unit], out_recv.at[unit]
        )

        @pl.when(section < sections - 1)
        def _():
            onward(unit).wait_send()

        @pl.when(
            jnp.logical_or(
                jnp.logical_and(section == 0, unit == 0),
                jnp.logical_and(section == 2, unit > 0),
            )
        )
        def _():
            exchange_sent(
                staged.at[unit], relay.at[unit], x_send.at[unit], x_recv.at[unit]
            )

        @pl.when(jnp.logical_and(section == 2, unit > 0))
        def _():
            relayed(unit).wait_send()


def shards(sizes, x_in, x_tan, t_index, w_qkv, w_out, qk_gain, mod_amp, mod_freq, mod_phase):
    nz, nx, ny = sizes
    count = nz * nx * ny
    sections = lax.axis_size("section")
    places = x_in.shape[2]
    waves = [wave.reshape(3, KT, HEAD) for wave in (mod_amp, mod_freq, mod_phase)]
    outside = pl.BlockSpec(memory_space=pl.ANY)
    inside = pl.BlockSpec(memory_space=pltpu.VMEM)
    result = jax.ShapeDtypeStruct((VIDS, places, D), BF16)
    units = (UNITS, F, 2, KT, HEAD)
    rings = 2 * (ny // 2) * (1 + 2 * nz) + 2 * (nz // 2) * (2 + ny) + nz
    dma = pltpu.SemaphoreType.DMA
    out, tan = pl.pallas_call(
        functools.partial(kernel, sizes, sections),
        out_shape=(result, result),
        in_specs=[outside] * 4
        + [inside, pl.BlockSpec(memory_space=pltpu.SMEM)]
        + [inside] * 3,
        out_specs=(inside, inside),
        scratch_shapes=[
            pltpu.VMEM((nz, nx, ny, ROWS_OUT, PACKED), BF16),
            pltpu.VMEM((VIDS, 3, KT, HEAD), F32),
            pltpu.VMEM((VIDS, 3, KT, HEAD), F32),
            pltpu.VMEM((2, VIDS, places, D), BF16),
            pltpu.VMEM(units, BF16),
            pltpu.VMEM(units, BF16),
            pltpu.VMEM(units, BF16),
            pltpu.VMEM(units, BF16),
            pltpu.VMEM(units, BF16),
            pltpu.VMEM((2 * places * KT, HEAD), F32),
            pltpu.VMEM((ROWS, D), BF16),
            pltpu.VMEM((ROWS, HD), BF16),
            dma((2,)),
            dma((3,)),
            dma,
            dma,
            dma((rings,)),
            dma((rings,)),
            dma((UNITS,)),
            dma((UNITS,)),
            dma((UNITS,)),
            dma((UNITS,)),
            dma((UNITS,)),
            dma((UNITS,)),
            dma((UNITS,)),
            dma((UNITS,)),
            pltpu.SemaphoreType.REGULAR,
        ],
        compiler_params=pltpu.CompilerParams(
            has_side_effects=True, vmem_limit_bytes=60 * 1024 * 1024
        ),
        name="blocks",
    )(
        x_in.reshape(VIDS, places, D),
        x_tan.reshape(VIDS, places, D),
        w_qkv[0],
        w_out[0],
        qk_gain[0],
        t_index,
        *waves,
    )
    return (out[None, :, None], tan[None, :, None])


def solution(mesh):
    count = mesh.shape["seq"]
    sizes = (count // 8, 2, 4)
    placed = (
        P(None, "seq", None, None),
        P(None, "seq", None, None),
        P(),
        P("section", "seq", None),
        P("section", "seq", None),
        P("section", None, None),
        P("section", None, None),
        P("section", None, None),
        P("section", None, None),
    )
    return jax.shard_map(
        functools.partial(shards, sizes),
        mesh=mesh,
        in_specs=placed,
        out_specs=(P("section", None, "seq", None, None), P("section", None, "seq", None, None)),
        check_vma=False,
    )
```

```python
import functools
import math

import jax
import jax.numpy as jnp
from jax import lax
from jax.experimental import pallas as pl
from jax.experimental.pallas import tpu as pltpu
from jax.sharding import PartitionSpec as P

HEADS = 8
HEAD = 128
T_STEPS = 1000
D = 2048
KT = D // HEAD
HD = HEADS * HEAD
F = 64
NP = 2
VIDS = 2
UNITS = VIDS * NP
ROWS = 2 * F
HALF = F
HOP_PARTS = 4
STRIDE = 27
EPS = 1e-06
F32 = jnp.float32
BF16 = jnp.bfloat16
MESH = pl.DeviceIdType.MESH
ROWS_OUT = 16
PACKED = 2 * 3 * HD + D
Z_LAST, Y_LAST = 2816, 5632


def timing(amp, freq, phase, time_value):
    angle = freq * time_value + phase
    return (amp * jnp.sin(angle), amp * freq * jnp.cos(angle))


class Gather:
    def __init__(self, sizes, section, coords, weights, send, recv):
        self.sizes, self.section, self.coords = sizes, section, coords
        self.weights, self.send, self.recv = weights, send, recv
        self.live = []
        self.sems = 0
        self.rings = {}

    def peer(self, axis, by):
        z, xl, y = self.coords
        nz, nx, ny = self.sizes
        if axis == "z":
            z = lax.rem(z + by + nz, nz)
        elif axis == "y":
            y = lax.rem(y + by + ny, ny)
        else:
            xl = nx - 1 - xl
        return (self.section, (z * nx + xl) * ny + y)

    def copy(self, ref, sem, peer):
        return pltpu.make_async_remote_copy(
            src_ref=ref,
            dst_ref=ref,
            send_sem=self.send.at[sem],
            recv_sem=self.recv.at[sem],
            device_id=peer,
            device_id_type=MESH,
        )

    def start(self, piece, begin, width, sem, peer):
        for part in range(2):
            columns = pl.ds(begin + part * (width // 2), width // 2)
            self.copy(piece(columns), sem, peer).start()
        self.live.append(self.copy(piece(pl.ds(begin, width)), sem, peer))

    def ring(self, axis, first, stop, fixed, single=False):
        size = self.sizes[0] if axis == "z" else self.sizes[2]
        me = self.coords[0] if axis == "z" else self.coords[2]
        last = size // 2
        first_sem = self.sems
        self.sems += 2 * last

        def arguments(way, step, index):
            z, y = (index, fixed) if axis == "z" else (fixed, index)
            begin, width = first, stop - first
            xl = self.coords[1] if single else slice(None)
            if step == last - 1:
                if single:
                    width = width // 2
                    begin = begin + way * width
                else:
                    xl = way

            def piece(columns):
                return self.weights.at[z, xl, y, :, columns]

            return piece, begin, width, first_sem + 2 * step + way, self.peer(axis, 1 - 2 * way)

        def at(way, step):
            return lax.rem(me - (1 - 2 * way) * step + size, size)

        for step in range(last):
            for way in (0, 1):
                self.start(*arguments(way, step, at(way, step)))
            yield
            for way in (0, 1):
                piece, begin, width, sem, peer = arguments(way, step, at(way, step + 1))
                self.copy(piece(pl.ds(begin, width)), sem, peer).wait_recv()

    def beside(self, fixed):
        sem = self.sems
        self.sems += 1
        _, xl, _ = self.coords
        nx = self.sizes[1]
        peer = self.peer("x", 0)
        self.start(
            lambda columns: self.weights.at[fixed, xl, :, :, columns],
            Y_LAST,
            PACKED - Y_LAST,
            sem,
            peer,
        )
        yield
        columns = pl.ds(Y_LAST, PACKED - Y_LAST)
        self.copy(self.weights.at[fixed, nx - 1 - xl, :, :, columns], sem, peer).wait_recv()

    def build(self):
        z, _, y = self.coords
        nz, _, ny = self.sizes
        rings = self.rings
        rings["a"] = self.ring("y", 0, Z_LAST, z)
        rings["b"] = self.ring("z", Z_LAST, Y_LAST, y)
        rings["c"] = self.ring("z", Y_LAST, PACKED, y, True)
        for by in range(ny):
            rings["az", by] = self.ring("z", 0, Z_LAST, lax.rem(y + by, ny))
        for by in range(nz):
            there = lax.rem(z + by, nz)
            rings["by", by] = self.ring("y", Z_LAST, Y_LAST, there)
            rings["cy", by] = self.ring("y", Y_LAST, PACKED, there, True)
            rings["cx", by] = self.beside(there)

    def go(self, *names):
        for name in names:
            next(self.rings[name], None)

    def finish(self):
        for copy in self.live:
            copy.wait_send()


def spread(source, tall, start):
    count = source.shape[0]
    for k in range(KT):
        tall[pl.ds(start + k, count, stride=KT), :] = source[:, k * HEAD : (k + 1) * HEAD].astype(
            F32
        )


def normalize(values, tangents, gain):
    inverse = lax.rsqrt(jnp.mean(values * values, axis=-1, keepdims=True) + EPS)
    cross = jnp.mean(values * tangents, axis=-1, keepdims=True)
    scaled = values * inverse
    return (
        (scaled * gain).astype(BF16),
        ((inverse * tangents - values * inverse**3 * cross) * gain).astype(BF16),
    )


def attend(q2, k2, v2, gains_ref):
    factor = 1.0 / math.sqrt(HEAD)
    qn, dqn = normalize(q2[:HALF], q2[HALF:], gains_ref[0:1, :])
    kn, dkn = normalize(k2[:HALF], k2[HALF:], gains_ref[1:2, :])
    value, dvalue = v2[:HALF].astype(BF16), v2[HALF:].astype(BF16)

    def against(rows, columns):
        return lax.dot_general(
            rows, columns, (((1,), (1,)), ((), ())), preferred_element_type=F32
        )

    scores = against(jnp.concatenate([qn, dqn], axis=0), kn)
    score = scores[:HALF] * factor
    dscore = (scores[HALF:] + against(qn, dkn)) * factor
    expo = jnp.exp(score)
    prob = expo * (1.0 / jnp.sum(expo, axis=-1, keepdims=True))
    growth = prob * dscore
    dprob = growth - prob * jnp.sum(growth, axis=-1, keepdims=True)
    prob, dprob = prob.astype(BF16), dprob.astype(BF16)
    mixed = jnp.dot(
        jnp.concatenate([prob, dprob], axis=0), value, preferred_element_type=F32
    )
    return mixed[:HALF], mixed[HALF:] + jnp.dot(prob, dvalue, preferred_element_type=F32)


def block_step(
    unit, entering, leaving, weights, gains_ref, mods_ref, dmods_ref, tall, flat, att
):
    group = 8
    vid = unit // NP

    @pl.loop(0, F // group, unroll=4)
    def _(i):
        first = pl.multiple_of(i * group, group)
        hidden = entering[unit, pl.ds(first, group), 0].astype(F32)
        tangent = entering[unit, pl.ds(first, group), 1].astype(F32)

        def mean(values):
            return jnp.sum(
                jnp.sum(values, axis=1, keepdims=True), axis=2, keepdims=True
            ) * (1.0 / D)

        inverse = lax.rsqrt(mean(hidden * hidden) + EPS)
        cross = mean(hidden * tangent)
        normed = hidden * inverse
        dnormed = inverse * tangent - hidden * inverse**3 * cross
        scale = 1.0 + mods_ref[vid, 1][None]
        modulated = normed * scale + mods_ref[vid, 0][None]
        dmodulated = dnormed * scale + normed * dmods_ref[vid, 1][None] + dmods_ref[vid, 0][None]
        row = pl.multiple_of(first * KT, group * KT)
        tall[pl.ds(row, group * KT), :] = modulated.reshape(group * KT, HEAD)
        tall[pl.ds(row + HALF * KT, group * KT), :] = dmodulated.reshape(group * KT, HEAD)

    for k in range(KT):
        flat[:, k * HEAD : (k + 1) * HEAD] = tall[pl.ds(k, ROWS, stride=KT), :].astype(BF16)

    def third(number, pair):
        column = number * HD + pair * 2 * HEAD
        halves = [
            weights[
                :, :, :, :, column + lower * 3 * HD : column + lower * 3 * HD + 2 * HEAD
            ].reshape(F, 1, ROWS_OUT, 2 * HEAD)
            for lower in range(2)
        ]
        matrix = jnp.concatenate(halves, axis=1).reshape(D, 2 * HEAD)
        return jnp.dot(flat[...], matrix, preferred_element_type=F32)

    ahead = [third(number, 0) for number in range(3)]
    for pair in range(HEADS // 2):
        q2, k2, v2 = ahead
        if pair + 1 < HEADS // 2:
            ahead = [third(number, pair + 1) for number in range(3)]
        for one in range(2):
            lanes = slice(one * HEAD, (one + 1) * HEAD)
            output, doutput = attend(q2[:, lanes], k2[:, lanes], v2[:, lanes], gains_ref)
            column = (pair * 2 + one) * HEAD
            att[:HALF, column : column + HEAD] = output.astype(BF16)
            att[HALF:, column : column + HEAD] = doutput.astype(BF16)

    for n in range(KT // 2):
        column = 2 * 3 * HD + n * 2 * HEAD
        matrix = weights[:, :, :, :, column : column + 2 * HEAD].reshape(HD, 2 * HEAD)
        y = jnp.dot(att[...], matrix, preferred_element_type=F32)
        tall[pl.ds(2 * n, ROWS, stride=KT), :] = y[:, :HEAD]
        tall[pl.ds(2 * n + 1, ROWS, stride=KT), :] = y[:, HEAD:]

    @pl.loop(0, F // group, unroll=4)
    def _(i):
        first = pl.multiple_of(i * group, group)
        row = pl.multiple_of(first * KT, group * KT)
        y = tall[pl.ds(row, group * KT), :].reshape(group, KT, HEAD)
        dy = tall[pl.ds(row + HALF * KT, group * KT), :].reshape(group, KT, HEAD)
        hidden = entering[unit, pl.ds(first, group), 0].astype(F32)
        tangent = entering[unit, pl.ds(first, group), 1].astype(F32)
        gate = mods_ref[vid, 2][None]
        dgate = dmods_ref[vid, 2][None]
        leaving[unit, pl.ds(first, group), 0] = (hidden + gate * y).astype(BF16)
        leaving[unit, pl.ds(first, group), 1] = (tangent + dgate * y + gate * dy).astype(BF16)


def kernel(
    sizes,
    sections,
    x_ref,
    t_ref,
    wqkv_ref,
    wout_ref,
    gains_ref,
    index_ref,
    amp_ref,
    freq_ref,
    phase_ref,
    out_ref,
    tan_ref,
    weights,
    mods_ref,
    dmods_ref,
    plain,
    staged,
    relay,
    entering,
    leaving,
    returned,
    tall,
    flat,
    att,
    load_sem,
    own_sem,
    swap_send,
    swap_recv,
    ring_send,
    ring_recv,
    x_send,
    x_recv,
    relay_send,
    relay_recv,
    pass_send,
    pass_recv,
    out_send,
    out_recv,
    turn_sem,
):
    nz, nx, ny = sizes
    count = nz * nx * ny
    section = lax.axis_index("section")
    me = lax.axis_index("seq")
    coords = (me // (nx * ny), (me // ny) % nx, me % ny)
    z, xl, y = coords
    first_half = section < 2

    def flip(index):
        return index + ny - 2 * ny * ((index // ny) % nx)

    across = flip(me)
    slot = jnp.where(first_half, me, across)
    neighbour = (section, lax.rem(me + 1, count))
    group = 8

    def exchange(source, row_of, target, place, send, recv):
        pltpu.make_async_copy(source.at[row_of(me)], target.at[place], recv).start()

        @pl.loop(1, count, unroll=21)
        def _(by):
            to = lax.rem(me + by * STRIDE, count)
            pltpu.make_async_remote_copy(
                src_ref=source.at[row_of(to)],
                dst_ref=target.at[place],
                send_sem=send,
                recv_sem=recv,
                device_id=(section, to),
                device_id_type=MESH,
            ).start()

    def exchange_came(source, target, recv):
        pltpu.make_async_copy(source, target, recv).wait()

    def exchange_sent(source, target, send, recv):
        pltpu.make_async_remote_copy(
            src_ref=source.at[pl.ds(0, count - 1)],
            dst_ref=target.at[pl.ds(0, count - 1)],
            send_sem=send,
            recv_sem=recv,
            device_id=neighbour,
            device_id_type=MESH,
        ).wait_send()

    leads = lax.rem(section, 2) == 0
    video = section // 2
    loads = [
        pltpu.make_async_copy(ref.at[video], plain.at[tan], load_sem.at[tan])
        for tan, ref in enumerate((x_ref, t_ref))
    ]

    @pl.when(leads)
    def _():
        for load in loads:
            load.start()

    own = []
    for part, (ref, first, width) in enumerate(
        (
            (wqkv_ref.at[pl.ds(0, ROWS_OUT)], 0, 3 * HD),
            (wqkv_ref.at[pl.ds(ROWS_OUT, ROWS_OUT)], 3 * HD, 3 * HD),
            (wout_ref, 6 * HD, D),
        )
    ):
        home = weights.at[z, xl, y, :, pl.ds(first, width)]
        own.append(pltpu.make_async_copy(ref, home, own_sem.at[part]))
        own[-1].start()
    for copy in own:
        copy.wait()

    @pl.when(jnp.logical_not(leads))
    def _():
        pl.semaphore_wait(turn_sem, 1)

    gather = Gather(sizes, section, coords, weights, ring_send, ring_recv)
    gather.build()
    go = gather.go
    mine = weights.at[z, xl, y, :, pl.ds(0, Y_LAST)]
    swap = pltpu.make_async_remote_copy(
        src_ref=mine,
        dst_ref=mine,
        send_sem=swap_send,
        recv_sem=swap_recv,
        device_id=(section, across),
        device_id_type=MESH,
    )
    theirs = weights.at[z, nx - 1 - xl, y, :, pl.ds(0, Y_LAST)]
    swapped = pltpu.make_async_remote_copy(
        src_ref=theirs,
        dst_ref=theirs,
        send_sem=swap_send,
        recv_sem=swap_recv,
        device_id=(section, across),
        device_id_type=MESH,
    )
    swap.start()
    go("c", ("cy", 0))

    @pl.when(leads)
    def _():
        for load in loads:
            load.wait()
        for tan in range(2):
            spread(plain.at[tan], tall, 0)

            @pl.loop(0, count // group)
            def _(i):
                first = pl.multiple_of(i * group, group)
                row = pl.multiple_of(first * NP * KT, group * NP * KT)
                tiles = (
                    tall[pl.ds(row, group * NP * KT), :]
                    .astype(BF16)
                    .reshape(group, NP, KT, HEAD)
                )
                for pos in range(NP):
                    staged[pos, pl.ds(first, group), tan] = tiles[:, pos]

    @pl.when(section == 0)
    def _():
        for pos in range(NP):
            exchange(
                staged.at[pos],
                lambda f: f,
                entering.at[pos],
                me,
                x_send.at[pos],
                x_recv.at[pos],
            )

    @pl.when(section == 2)
    def _():
        for pos in range(NP):
            exchange(
                staged.at[pos], flip, relay.at[pos], me, x_send.at[pos], x_recv.at[pos]
            )

    def relayed(pos):
        return pltpu.make_async_remote_copy(
            src_ref=relay.at[pos],
            dst_ref=entering.at[NP + pos],
            send_sem=relay_send.at[pos],
            recv_sem=relay_recv.at[pos],
            device_id=(0, across),
            device_id_type=MESH,
        )

    def pass_to_first(pos):
        @pl.when(section == 2)
        def _():
            exchange_came(staged.at[pos], relay.at[pos], x_recv.at[pos])
            relayed(pos).start()

    for vid in range(VIDS):
        time_value = (index_ref[vid].astype(F32) + 0.5) * (math.pi / (2.0 * T_STEPS))
        mods_ref[vid], dmods_ref[vid] = timing(
            amp_ref[...], freq_ref[...], phase_ref[...], time_value
        )

    swapped.wait_recv()
    go("b", "a", ("by", 0), ("az", 0))
    go("c", ("cy", 1), ("cy", 7))
    go("a", ("az", 1), ("az", 3))
    go(("cy", 0),)
    go("b", ("by", 1), ("by", 7))
    go("c", ("cy", 2), ("cy", 6))

    @pl.when(leads)
    def _():
        pl.semaphore_signal(
            turn_sem, inc=1, device_id=(section + 1, me), device_id_type=MESH
        )

    go("a", ("az", 2))
    go(("cy", 0), ("cx", 0), ("cy", 1), ("cy", 7))
    go(("az", 0), ("by", 0))
    go("c", ("cy", 3), ("cy", 5))
    go(("cy", 1), ("cx", 1), ("cy", 7), ("cx", 7), ("cy", 2), ("cy", 6))
    go("b", ("by", 2), ("by", 6))
    go("c", ("cy", 4))
    pass_to_first(0)
    go(("az", 1), ("az", 3), ("by", 1), ("by", 7), ("az", 2))
    go(("cy", 2), ("cx", 2), ("cy", 6), ("cx", 6), ("cy", 3), ("cy", 5), ("cy", 4))
    go("b", ("by", 3), ("by", 5))
    go(("az", 0), ("by", 0), ("az", 1), ("az", 3))
    go(("cy", 3), ("cx", 3), ("cy", 5), ("cx", 5), ("cy", 4), ("cx", 4))
    pass_to_first(1)

    go("b", ("by", 4))
    go(("by", 2), ("by", 6), ("az", 2), ("by", 1), ("by", 7), ("az", 0))
    go(("by", 3), ("by", 5), ("az", 1), ("az", 3), ("by", 4), ("az", 2))
    go(("by", 2), ("by", 6), ("az", 0), ("by", 3), ("by", 5))
    go(("az", 1), ("az", 3), ("by", 4), ("az", 2))
    go(*(("cx", by) for by in range(nz)))

    @pl.when(section == 1)
    def _():
        pl.semaphore_signal(turn_sem, inc=1, device_id=(0, me), device_id_type=MESH)

    def onward(unit, first=0, frames=F):
        return pltpu.make_async_remote_copy(
            src_ref=leaving.at[unit, pl.ds(first, frames)],
            dst_ref=entering.at[unit, pl.ds(first, frames)],
            send_sem=pass_send.at[unit],
            recv_sem=pass_recv.at[unit],
            device_id=(
                lax.rem(section + 1, sections),
                jnp.where(section == 1, across, me),
            ),
            device_id_type=MESH,
        )

    def send_back(unit):
        exchange(
            leaving.at[unit],
            lambda f: f,
            returned.at[unit],
            slot,
            out_send.at[unit],
            out_recv.at[unit],
        )

    @pl.loop(0, UNITS)
    def _(unit):
        pos = unit % NP

        @pl.when(jnp.logical_and(section == 0, unit < NP))
        def _():
            exchange_came(staged.at[pos], entering.at[pos], x_recv.at[pos])

        @pl.when(jnp.logical_and(section == 0, unit >= NP))
        def _():
            relayed(pos).wait_recv()

        @pl.when(section > 0)
        def _():
            onward(unit).wait_recv()

        block_step(
            unit, entering, leaving, weights, gains_ref, mods_ref, dmods_ref, tall, flat, att
        )

        @pl.when(section < sections - 1)
        def _():
            for part in range(HOP_PARTS):
                onward(unit, part * (F // HOP_PARTS), F // HOP_PARTS).start()

        @pl.when(section > 0)
        def _():
            send_back(unit)

    @pl.when(section == 0)
    def _():
        pl.semaphore_wait(turn_sem, 1)

        @pl.loop(0, UNITS)
        def _(unit):
            send_back(unit)

    gather.finish()
    swap.wait_send()

    @pl.loop(0, VIDS)
    def _(vid):
        for pos in range(NP):
            unit = vid * NP + pos
            exchange_came(leaving.at[unit], returned.at[unit], out_recv.at[unit])

            @pl.loop(0, count // group)
            def _(i):
                first = pl.multiple_of(i * group, group)
                for tan in range(2):
                    tiles = returned[unit, pl.ds(first, group), tan].astype(F32)
                    for one in range(group):
                        row = pl.multiple_of(
                            ((tan * count + first + one) * NP + pos) * KT, KT
                        )
                        tall[pl.ds(row, KT), :] = tiles[one]

        for tan, result in enumerate((out_ref, tan_ref)):
            for k in range(KT):
                result[vid, :, k * HEAD : (k + 1) * HEAD] = tall[
                    pl.ds(tan * count * NP * KT + k, count * NP, stride=KT), :
                ].astype(BF16)

    @pl.loop(0, UNITS)
    def _(unit):
        exchange_sent(
            leaving.at[unit], returned.at[unit], out_send.at[unit], out_recv.at[unit]
        )

        @pl.when(section < sections - 1)
        def _():
            onward(unit).wait_send()

    @pl.when(leads)
    def _():
        for pos in range(NP):
            exchange_sent(staged.at[pos], relay.at[pos], x_send.at[pos], x_recv.at[pos])

    @pl.when(section == 2)
    def _():
        for pos in range(NP):
            relayed(pos).wait_send()


def shards(sizes, x_in, x_tan, t_index, w_qkv, w_out, qk_gain, mod_amp, mod_freq, mod_phase):
    nz, nx, ny = sizes
    count = nz * nx * ny
    sections = lax.axis_size("section")
    places = x_in.shape[2]
    waves = [wave.reshape(3, KT, HEAD) for wave in (mod_amp, mod_freq, mod_phase)]
    outside = pl.BlockSpec(memory_space=pl.ANY)
    inside = pl.BlockSpec(memory_space=pltpu.VMEM)
    result = jax.ShapeDtypeStruct((VIDS, places, D), BF16)
    units = (UNITS, F, 2, KT, HEAD)
    rings = 2 * (ny // 2) * (1 + 2 * nz) + 2 * (nz // 2) * (2 + ny) + nz
    dma = pltpu.SemaphoreType.DMA
    out, tan = pl.pallas_call(
        functools.partial(kernel, sizes, sections),
        out_shape=(result, result),
        in_specs=[outside] * 4
        + [inside, pl.BlockSpec(memory_space=pltpu.SMEM)]
        + [inside] * 3,
        out_specs=(inside, inside),
        scratch_shapes=[
            pltpu.VMEM((nz, nx, ny, ROWS_OUT, PACKED), BF16),
            pltpu.VMEM((VIDS, 3, KT, HEAD), F32),
            pltpu.VMEM((VIDS, 3, KT, HEAD), F32),
            pltpu.VMEM((2, places, D), BF16),
            pltpu.VMEM((NP,) + units[1:], BF16),
            pltpu.VMEM((NP,) + units[1:], BF16),
            pltpu.VMEM(units, BF16),
            pltpu.VMEM(units, BF16),
            pltpu.VMEM(units, BF16),
            pltpu.VMEM((2 * places * KT, HEAD), F32),
            pltpu.VMEM((ROWS, D), BF16),
            pltpu.VMEM((ROWS, HD), BF16),
            dma((2,)),
            dma((3,)),
            dma,
            dma,
            dma((rings,)),
            dma((rings,)),
            dma((NP,)),
            dma((NP,)),
            dma((NP,)),
            dma((NP,)),
            dma((UNITS,)),
            dma((UNITS,)),
            dma((UNITS,)),
            dma((UNITS,)),
            pltpu.SemaphoreType.REGULAR,
        ],
        compiler_params=pltpu.CompilerParams(
            has_side_effects=True, vmem_limit_bytes=60 * 1024 * 1024
        ),
        name="blocks",
    )(
        x_in.reshape(VIDS, places, D),
        x_tan.reshape(VIDS, places, D),
        w_qkv[0],
        w_out[0],
        qk_gain[0],
        t_index,
        *waves,
    )
    return (out[None, :, None], tan[None, :, None])


def solution(mesh):
    count = mesh.shape["seq"]
    sizes = (count // 8, 2, 4)
    placed = (
        P(None, "seq", None, None),
        P(None, "seq", None, None),
        P(),
        P("section", "seq", None),
        P("section", "seq", None),
        P("section", None, None),
        P("section", None, None),
        P("section", None, None),
        P("section", None, None),
    )
    return jax.shard_map(
        functools.partial(shards, sizes),
        mesh=mesh,
        in_specs=placed,
        out_specs=(P("section", None, "seq", None, None), P("section", None, "seq", None, None)),
        check_vma=False,
    )
```

```python
import functools
import math

import jax
import jax.numpy as jnp
from jax import lax
from jax.experimental import pallas as pl
from jax.experimental.pallas import tpu as pltpu
from jax.sharding import PartitionSpec as P

HEADS = 8
HEAD = 128
T_STEPS = 1000
D = 2048
KT = D // HEAD
HD = HEADS * HEAD
F = 64
NP = 2
VIDS = 2
UNITS = VIDS * NP
ROWS = 2 * F
HALF = F
HOP_PARTS = 4
STRIDE = 27
EPS = 1e-06
F32 = jnp.float32
BF16 = jnp.bfloat16
MESH = pl.DeviceIdType.MESH
ROWS_OUT = 16
PACKED = 2 * 3 * HD + D
Z_LAST, Y_LAST = 2304, 5376


def timing(amp, freq, phase, time_value):
    angle = freq * time_value + phase
    return (amp * jnp.sin(angle), amp * freq * jnp.cos(angle))


class Gather:
    def __init__(self, sizes, section, coords, weights, send, recv):
        self.sizes, self.section, self.coords = sizes, section, coords
        self.weights, self.send, self.recv = weights, send, recv
        self.live = []
        self.sems = 0
        self.rings = {}

    def peer(self, axis, by):
        z, xl, y = self.coords
        nz, nx, ny = self.sizes
        if axis == "z":
            z = lax.rem(z + by + nz, nz)
        elif axis == "y":
            y = lax.rem(y + by + ny, ny)
        else:
            xl = nx - 1 - xl
        return (self.section, (z * nx + xl) * ny + y)

    def copy(self, ref, sem, peer):
        return pltpu.make_async_remote_copy(
            src_ref=ref,
            dst_ref=ref,
            send_sem=self.send.at[sem],
            recv_sem=self.recv.at[sem],
            device_id=peer,
            device_id_type=MESH,
        )

    def start(self, piece, begin, width, sem, peer):
        copy = self.copy(piece(pl.ds(begin, width)), sem, peer)
        copy.start()
        self.live.append(copy)

    def ring(self, axis, first, stop, fixed, single=False):
        size = self.sizes[0] if axis == "z" else self.sizes[2]
        me = self.coords[0] if axis == "z" else self.coords[2]
        last = size // 2
        first_sem = self.sems
        self.sems += 2 * last

        def arguments(way, step, index):
            z, y = (index, fixed) if axis == "z" else (fixed, index)
            begin, width = first, stop - first
            xl = self.coords[1] if single else slice(None)
            if step == last - 1:
                if single:
                    width = width // 2
                    begin = begin + way * width
                else:
                    xl = way

            def piece(columns):
                return self.weights.at[z, xl, y, :, columns]

            return piece, begin, width, first_sem + 2 * step + way, self.peer(axis, 1 - 2 * way)

        def at(way, step):
            return lax.rem(me - (1 - 2 * way) * step + size, size)

        for step in range(last):
            for way in (0, 1):
                self.start(*arguments(way, step, at(way, step)))
            yield
            for way in (0, 1):
                piece, begin, width, sem, peer = arguments(way, step, at(way, step + 1))
                self.copy(piece(pl.ds(begin, width)), sem, peer).wait_recv()

    def beside(self, fixed):
        sem = self.sems
        self.sems += 1
        _, xl, _ = self.coords
        nx = self.sizes[1]
        peer = self.peer("x", 0)
        self.start(
            lambda columns: self.weights.at[fixed, xl, :, :, columns],
            Y_LAST,
            PACKED - Y_LAST,
            sem,
            peer,
        )
        yield
        columns = pl.ds(Y_LAST, PACKED - Y_LAST)
        self.copy(self.weights.at[fixed, nx - 1 - xl, :, :, columns], sem, peer).wait_recv()

    def build(self):
        z, _, y = self.coords
        nz, _, ny = self.sizes
        rings = self.rings
        rings["a"] = self.ring("y", 0, Z_LAST, z)
        rings["b"] = self.ring("z", Z_LAST, Y_LAST, y)
        rings["c"] = self.ring("z", Y_LAST, PACKED, y, True)
        for by in range(ny):
            rings["az", by] = self.ring("z", 0, Z_LAST, lax.rem(y + by, ny))
        for by in range(nz):
            there = lax.rem(z + by, nz)
            rings["by", by] = self.ring("y", Z_LAST, Y_LAST, there)
            rings["cy", by] = self.ring("y", Y_LAST, PACKED, there, True)
            rings["cx", by] = self.beside(there)

    def go(self, *names):
        for name in names:
            next(self.rings[name], None)

    def finish(self):
        for copy in self.live:
            copy.wait_send()


def spread(source, tall, start):
    count = source.shape[0]
    for k in range(KT):
        tall[pl.ds(start + k, count, stride=KT), :] = source[:, k * HEAD : (k + 1) * HEAD].astype(
            F32
        )


def normalize(values, tangents, gain):
    inverse = lax.rsqrt(jnp.mean(values * values, axis=-1, keepdims=True) + EPS)
    cross = jnp.mean(values * tangents, axis=-1, keepdims=True)
    scaled = values * inverse
    return (
        (scaled * gain).astype(BF16),
        ((inverse * tangents - values * inverse**3 * cross) * gain).astype(BF16),
    )


def attend(q2, k2, v2, gains_ref):
    factor = 1.0 / math.sqrt(HEAD)
    qn, dqn = normalize(q2[:HALF], q2[HALF:], gains_ref[0:1, :])
    kn, dkn = normalize(k2[:HALF], k2[HALF:], gains_ref[1:2, :])
    value, dvalue = v2[:HALF].astype(BF16), v2[HALF:].astype(BF16)

    def against(rows, columns):
        return lax.dot_general(
            rows, columns, (((1,), (1,)), ((), ())), preferred_element_type=F32
        )

    scores = against(jnp.concatenate([qn, dqn], axis=0), kn)
    score = scores[:HALF] * factor
    dscore = (scores[HALF:] + against(qn, dkn)) * factor
    expo = jnp.exp(score)
    prob = expo * (1.0 / jnp.sum(expo, axis=-1, keepdims=True))
    growth = prob * dscore
    dprob = growth - prob * jnp.sum(growth, axis=-1, keepdims=True)
    prob, dprob = prob.astype(BF16), dprob.astype(BF16)
    mixed = jnp.dot(
        jnp.concatenate([prob, dprob], axis=0), value, preferred_element_type=F32
    )
    return mixed[:HALF], mixed[HALF:] + jnp.dot(prob, dvalue, preferred_element_type=F32)


def block_step(
    unit, entering, leaving, weights, gains_ref, mods_ref, dmods_ref, tall, flat, att
):
    group = 8
    vid = unit // NP

    @pl.loop(0, F // group, unroll=4)
    def _(i):
        first = pl.multiple_of(i * group, group)
        hidden = entering[unit, pl.ds(first, group), 0].astype(F32)
        tangent = entering[unit, pl.ds(first, group), 1].astype(F32)

        def mean(values):
            return jnp.sum(
                jnp.sum(values, axis=1, keepdims=True), axis=2, keepdims=True
            ) * (1.0 / D)

        inverse = lax.rsqrt(mean(hidden * hidden) + EPS)
        cross = mean(hidden * tangent)
        normed = hidden * inverse
        dnormed = inverse * tangent - hidden * inverse**3 * cross
        scale = 1.0 + mods_ref[vid, 1][None]
        modulated = normed * scale + mods_ref[vid, 0][None]
        dmodulated = dnormed * scale + normed * dmods_ref[vid, 1][None] + dmods_ref[vid, 0][None]
        row = pl.multiple_of(first * KT, group * KT)
        tall[pl.ds(row, group * KT), :] = modulated.reshape(group * KT, HEAD)
        tall[pl.ds(row + HALF * KT, group * KT), :] = dmodulated.reshape(group * KT, HEAD)

    for k in range(KT):
        flat[:, k * HEAD : (k + 1) * HEAD] = tall[pl.ds(k, ROWS, stride=KT), :].astype(BF16)

    def third(number, pair):
        column = number * HD + pair * 2 * HEAD
        halves = [
            weights[
                :, :, :, :, column + lower * 3 * HD : column + lower * 3 * HD + 2 * HEAD
            ].reshape(F, 1, ROWS_OUT, 2 * HEAD)
            for lower in range(2)
        ]
        matrix = jnp.concatenate(halves, axis=1).reshape(D, 2 * HEAD)
        return jnp.dot(flat[...], matrix, preferred_element_type=F32)

    ahead = [third(number, 0) for number in range(3)]
    for pair in range(HEADS // 2):
        q2, k2, v2 = ahead
        if pair + 1 < HEADS // 2:
            ahead = [third(number, pair + 1) for number in range(3)]
        for one in range(2):
            lanes = slice(one * HEAD, (one + 1) * HEAD)
            output, doutput = attend(q2[:, lanes], k2[:, lanes], v2[:, lanes], gains_ref)
            column = (pair * 2 + one) * HEAD
            att[:HALF, column : column + HEAD] = output.astype(BF16)
            att[HALF:, column : column + HEAD] = doutput.astype(BF16)

    for n in range(KT // 2):
        column = 2 * 3 * HD + n * 2 * HEAD
        matrix = weights[:, :, :, :, column : column + 2 * HEAD].reshape(HD, 2 * HEAD)
        y = jnp.dot(att[...], matrix, preferred_element_type=F32)
        tall[pl.ds(2 * n, ROWS, stride=KT), :] = y[:, :HEAD]
        tall[pl.ds(2 * n + 1, ROWS, stride=KT), :] = y[:, HEAD:]

    @pl.loop(0, F // group, unroll=4)
    def _(i):
        first = pl.multiple_of(i * group, group)
        row = pl.multiple_of(first * KT, group * KT)
        y = tall[pl.ds(row, group * KT), :].reshape(group, KT, HEAD)
        dy = tall[pl.ds(row + HALF * KT, group * KT), :].reshape(group, KT, HEAD)
        hidden = entering[unit, pl.ds(first, group), 0].astype(F32)
        tangent = entering[unit, pl.ds(first, group), 1].astype(F32)
        gate = mods_ref[vid, 2][None]
        dgate = dmods_ref[vid, 2][None]
        leaving[unit, pl.ds(first, group), 0] = (hidden + gate * y).astype(BF16)
        leaving[unit, pl.ds(first, group), 1] = (tangent + dgate * y + gate * dy).astype(BF16)


def kernel(
    sizes,
    sections,
    x_ref,
    t_ref,
    wqkv_ref,
    wout_ref,
    gains_ref,
    index_ref,
    amp_ref,
    freq_ref,
    phase_ref,
    out_ref,
    tan_ref,
    weights,
    mods_ref,
    dmods_ref,
    plain,
    staged,
    relay,
    entering,
    leaving,
    returned,
    tall,
    flat,
    att,
    load_sem,
    own_sem,
    swap_send,
    swap_recv,
    ring_send,
    ring_recv,
    x_send,
    x_recv,
    relay_send,
    relay_recv,
    pass_send,
    pass_recv,
    out_send,
    out_recv,
    turn_sem,
):
    nz, nx, ny = sizes
    count = nz * nx * ny
    section = lax.axis_index("section")
    me = lax.axis_index("seq")
    coords = (me // (nx * ny), (me // ny) % nx, me % ny)
    z, xl, y = coords
    first_half = section < 2

    def flip(index):
        return index + ny - 2 * ny * ((index // ny) % nx)

    across = flip(me)
    slot = jnp.where(first_half, me, across)
    neighbour = (section, lax.rem(me + 1, count))
    group = 8

    def exchange(source, row_of, target, place, send, recv):
        pltpu.make_async_copy(source.at[row_of(me)], target.at[place], recv).start()

        @pl.loop(1, count, unroll=21)
        def _(by):
            to = lax.rem(me + by * STRIDE, count)
            pltpu.make_async_remote_copy(
                src_ref=source.at[row_of(to)],
                dst_ref=target.at[place],
                send_sem=send,
                recv_sem=recv,
                device_id=(section, to),
                device_id_type=MESH,
            ).start()

    def exchange_came(source, target, recv):
        pltpu.make_async_copy(source, target, recv).wait()

    def exchange_sent(source, target, send, recv):
        pltpu.make_async_remote_copy(
            src_ref=source.at[pl.ds(0, count - 1)],
            dst_ref=target.at[pl.ds(0, count - 1)],
            send_sem=send,
            recv_sem=recv,
            device_id=neighbour,
            device_id_type=MESH,
        ).wait_send()

    leads = lax.rem(section, 2) == 0
    loads = [
        pltpu.make_async_copy(ref, plain.at[tan], load_sem.at[tan])
        for tan, ref in enumerate((x_ref, t_ref))
    ]

    @pl.when(leads)
    def _():
        for load in loads:
            load.start()

    own = []
    for part, (ref, first, width) in enumerate(
        (
            (wqkv_ref.at[pl.ds(0, ROWS_OUT)], 0, 3 * HD),
            (wqkv_ref.at[pl.ds(ROWS_OUT, ROWS_OUT)], 3 * HD, 3 * HD),
            (wout_ref, 6 * HD, D),
        )
    ):
        home = weights.at[z, xl, y, :, pl.ds(first, width)]
        own.append(pltpu.make_async_copy(ref, home, own_sem.at[part]))
        own[-1].start()
    for copy in own:
        copy.wait()

    @pl.when(jnp.logical_not(leads))
    def _():
        pl.semaphore_wait(turn_sem, 1)

    gather = Gather(sizes, section, coords, weights, ring_send, ring_recv)
    gather.build()
    go = gather.go
    mine = weights.at[z, xl, y, :, pl.ds(0, Y_LAST)]
    swap = pltpu.make_async_remote_copy(
        src_ref=mine,
        dst_ref=mine,
        send_sem=swap_send,
        recv_sem=swap_recv,
        device_id=(section, across),
        device_id_type=MESH,
    )
    theirs = weights.at[z, nx - 1 - xl, y, :, pl.ds(0, Y_LAST)]
    swapped = pltpu.make_async_remote_copy(
        src_ref=theirs,
        dst_ref=theirs,
        send_sem=swap_send,
        recv_sem=swap_recv,
        device_id=(section, across),
        device_id_type=MESH,
    )
    swap.start()
    go("c", ("cy", 0))

    def prepare(vid):
        for tan in range(2):
            spread(plain.at[tan, vid], tall, 0)

            @pl.loop(0, count // group)
            def _(i):
                first = pl.multiple_of(i * group, group)
                row = pl.multiple_of(first * NP * KT, group * NP * KT)
                tiles = (
                    tall[pl.ds(row, group * NP * KT), :]
                    .astype(BF16)
                    .reshape(group, NP, KT, HEAD)
                )
                for pos in range(NP):
                    staged[vid * NP + pos, pl.ds(first, group), tan] = tiles[:, pos]

    @pl.when(leads)
    def _():
        for load in loads:
            load.wait()
        prepare(0)

    @pl.when(section == 0)
    def _():
        exchange(
            staged.at[0], lambda f: f, entering.at[0], me, x_send.at[0], x_recv.at[0]
        )

    def second_round(unit):
        exchange(
            staged.at[unit], flip, relay.at[unit], me, x_send.at[unit], x_recv.at[unit]
        )

    @pl.when(section == 2)
    def _():
        second_round(1)
        prepare(1)
        second_round(2)
        second_round(3)

    def relayed(unit):
        return pltpu.make_async_remote_copy(
            src_ref=relay.at[unit],
            dst_ref=entering.at[unit],
            send_sem=relay_send.at[unit],
            recv_sem=relay_recv.at[unit],
            device_id=(0, across),
            device_id_type=MESH,
        )

    def pass_to_first(unit):
        @pl.when(section == 2)
        def _():
            exchange_came(staged.at[unit], relay.at[unit], x_recv.at[unit])
            relayed(unit).start()

    for vid in range(VIDS):
        time_value = (index_ref[vid].astype(F32) + 0.5) * (math.pi / (2.0 * T_STEPS))
        mods_ref[vid], dmods_ref[vid] = timing(
            amp_ref[...], freq_ref[...], phase_ref[...], time_value
        )

    swapped.wait_recv()
    go("b", "a", ("by", 0), ("az", 0))
    go("c", ("cy", 1), ("cy", 7))
    go("a", ("az", 1), ("az", 3))
    go(("cy", 0),)
    go("b", ("by", 1), ("by", 7))
    go("c", ("cy", 2), ("cy", 6))

    @pl.when(leads)
    def _():
        pl.semaphore_signal(
            turn_sem, inc=1, device_id=(section + 1, me), device_id_type=MESH
        )

    go("a", ("az", 2))
    go(("cy", 0), ("cx", 0), ("cy", 1), ("cy", 7))
    go(("az", 0), ("by", 0))
    go("c", ("cy", 3), ("cy", 5))
    go(("cy", 1), ("cx", 1), ("cy", 7), ("cx", 7), ("cy", 2), ("cy", 6))
    go("b", ("by", 2), ("by", 6))
    go("c", ("cy", 4))
    pass_to_first(1)
    go(("az", 1), ("az", 3), ("by", 1), ("by", 7), ("az", 2))
    go(("cy", 2), ("cx", 2), ("cy", 6), ("cx", 6), ("cy", 3), ("cy", 5), ("cy", 4))
    go("b", ("by", 3), ("by", 5))
    go(("az", 0), ("by", 0), ("az", 1), ("az", 3))
    go(("cy", 3), ("cx", 3), ("cy", 5), ("cx", 5), ("cy", 4), ("cx", 4))
    pass_to_first(2)

    go("b", ("by", 4))
    go(("by", 2), ("by", 6), ("az", 2), ("by", 1), ("by", 7), ("az", 0))
    pass_to_first(3)
    go(("by", 3), ("by", 5), ("az", 1), ("az", 3), ("by", 4), ("az", 2))
    go(("by", 2), ("by", 6), ("az", 0), ("by", 3), ("by", 5))
    go(("az", 1), ("az", 3), ("by", 4), ("az", 2))
    go(*(("cx", by) for by in range(nz)))

    @pl.when(section == 1)
    def _():
        pl.semaphore_signal(turn_sem, inc=1, device_id=(0, me), device_id_type=MESH)

    def onward(unit, first=0, frames=F):
        return pltpu.make_async_remote_copy(
            src_ref=leaving.at[unit, pl.ds(first, frames)],
            dst_ref=entering.at[unit, pl.ds(first, frames)],
            send_sem=pass_send.at[unit],
            recv_sem=pass_recv.at[unit],
            device_id=(
                lax.rem(section + 1, sections),
                jnp.where(section == 1, across, me),
            ),
            device_id_type=MESH,
        )

    def send_back(unit):
        exchange(
            leaving.at[unit],
            lambda f: f,
            returned.at[unit],
            slot,
            out_send.at[unit],
            out_recv.at[unit],
        )

    @pl.loop(0, UNITS)
    def _(unit):
        @pl.when(jnp.logical_and(section == 0, unit == 0))
        def _():
            exchange_came(staged.at[0], entering.at[0], x_recv.at[0])

        @pl.when(jnp.logical_and(section == 0, unit > 0))
        def _():
            relayed(unit).wait_recv()

        @pl.when(section > 0)
        def _():
            onward(unit).wait_recv()

        block_step(
            unit, entering, leaving, weights, gains_ref, mods_ref, dmods_ref, tall, flat, att
        )

        @pl.when(section < sections - 1)
        def _():
            for part in range(HOP_PARTS):
                onward(unit, part * (F // HOP_PARTS), F // HOP_PARTS).start()

        @pl.when(section > 0)
        def _():
            send_back(unit)

    @pl.when(section == 0)
    def _():
        pl.semaphore_wait(turn_sem, 1)

        @pl.loop(0, UNITS)
        def _(unit):
            send_back(unit)

    gather.finish()
    swap.wait_send()

    @pl.loop(0, VIDS)
    def _(vid):
        for pos in range(NP):
            unit = vid * NP + pos
            exchange_came(leaving.at[unit], returned.at[unit], out_recv.at[unit])

            @pl.loop(0, count // group)
            def _(i):
                first = pl.multiple_of(i * group, group)
                for tan in range(2):
                    tiles = returned[unit, pl.ds(first, group), tan].astype(F32)
                    for one in range(group):
                        row = pl.multiple_of(
                            ((tan * count + first + one) * NP + pos) * KT, KT
                        )
                        tall[pl.ds(row, KT), :] = tiles[one]

        for tan, result in enumerate((out_ref, tan_ref)):
            for k in range(KT):
                result[vid, :, k * HEAD : (k + 1) * HEAD] = tall[
                    pl.ds(tan * count * NP * KT + k, count * NP, stride=KT), :
                ].astype(BF16)

    @pl.loop(0, UNITS)
    def _(unit):
        exchange_sent(
            leaving.at[unit], returned.at[unit], out_send.at[unit], out_recv.at[unit]
        )

        @pl.when(section < sections - 1)
        def _():
            onward(unit).wait_send()

        @pl.when(
            jnp.logical_or(
                jnp.logical_and(section == 0, unit == 0),
                jnp.logical_and(section == 2, unit > 0),
            )
        )
        def _():
            exchange_sent(
                staged.at[unit], relay.at[unit], x_send.at[unit], x_recv.at[unit]
            )

        @pl.when(jnp.logical_and(section == 2, unit > 0))
        def _():
            relayed(unit).wait_send()


def shards(sizes, x_in, x_tan, t_index, w_qkv, w_out, qk_gain, mod_amp, mod_freq, mod_phase):
    nz, nx, ny = sizes
    count = nz * nx * ny
    sections = lax.axis_size("section")
    places = x_in.shape[2]
    waves = [wave.reshape(3, KT, HEAD) for wave in (mod_amp, mod_freq, mod_phase)]
    outside = pl.BlockSpec(memory_space=pl.ANY)
    inside = pl.BlockSpec(memory_space=pltpu.VMEM)
    result = jax.ShapeDtypeStruct((VIDS, places, D), BF16)
    units = (UNITS, F, 2, KT, HEAD)
    rings = 2 * (ny // 2) * (1 + 2 * nz) + 2 * (nz // 2) * (2 + ny) + nz
    dma = pltpu.SemaphoreType.DMA
    out, tan = pl.pallas_call(
        functools.partial(kernel, sizes, sections),
        out_shape=(result, result),
        in_specs=[outside] * 4
        + [inside, pl.BlockSpec(memory_space=pltpu.SMEM)]
        + [inside] * 3,
        out_specs=(inside, inside),
        scratch_shapes=[
            pltpu.VMEM((nz, nx, ny, ROWS_OUT, PACKED), BF16),
            pltpu.VMEM((VIDS, 3, KT, HEAD), F32),
            pltpu.VMEM((VIDS, 3, KT, HEAD), F32),
            pltpu.VMEM((2, VIDS, places, D), BF16),
            pltpu.VMEM(units, BF16),
            pltpu.VMEM(units, BF16),
            pltpu.VMEM(units, BF16),
            pltpu.VMEM(units, BF16),
            pltpu.VMEM(units, BF16),
            pltpu.VMEM((2 * places * KT, HEAD), F32),
            pltpu.VMEM((ROWS, D), BF16),
            pltpu.VMEM((ROWS, HD), BF16),
            dma((2,)),
            dma((3,)),
            dma,
            dma,
            dma((rings,)),
            dma((rings,)),
            dma((UNITS,)),
            dma((UNITS,)),
            dma((UNITS,)),
            dma((UNITS,)),
            dma((UNITS,)),
            dma((UNITS,)),
            dma((UNITS,)),
            dma((UNITS,)),
            pltpu.SemaphoreType.REGULAR,
        ],
        compiler_params=pltpu.CompilerParams(
            has_side_effects=True, vmem_limit_bytes=60 * 1024 * 1024
        ),
        name="blocks",
    )(
        x_in.reshape(VIDS, places, D),
        x_tan.reshape(VIDS, places, D),
        w_qkv[0],
        w_out[0],
        qk_gain[0],
        t_index,
        *waves,
    )
    return (out[None, :, None], tan[None, :, None])


def solution(mesh):
    count = mesh.shape["seq"]
    sizes = (count // 8, 2, 4)
    placed = (
        P(None, "seq", None, None),
        P(None, "seq", None, None),
        P(),
        P("section", "seq", None),
        P("section", "seq", None),
        P("section", None, None),
        P("section", None, None),
        P("section", None, None),
        P("section", None, None),
    )
    return jax.shard_map(
        functools.partial(shards, sizes),
        mesh=mesh,
        in_specs=placed,
        out_specs=(P("section", None, "seq", None, None), P("section", None, "seq", None, None)),
        check_vma=False,
    )
```

```python
import functools
import math

import jax
import jax.numpy as jnp
from jax import lax
from jax.experimental import pallas as pl
from jax.experimental.pallas import tpu as pltpu
from jax.sharding import PartitionSpec as P

HEADS = 8
HEAD = 128
T_STEPS = 1000
D = 2048
KT = D // HEAD
HD = HEADS * HEAD
F = 64
NP = 2
VIDS = 2
UNITS = VIDS * NP
ROWS = 2 * F
HALF = F
HOP_PARTS = 4
STRIDE = 27
EPS = 1e-06
F32 = jnp.float32
BF16 = jnp.bfloat16
MESH = pl.DeviceIdType.MESH
ROWS_OUT = 16
PACKED = 2 * 3 * HD + D
Z_LAST, Y_LAST = 2816, 5632


def timing(amp, freq, phase, time_value):
    angle = freq * time_value + phase
    return (amp * jnp.sin(angle), amp * freq * jnp.cos(angle))


class Gather:
    def __init__(self, sizes, section, coords, weights, send, recv):
        self.sizes, self.section, self.coords = sizes, section, coords
        self.weights, self.send, self.recv = weights, send, recv
        self.live = []
        self.sems = 0
        self.rings = {}

    def peer(self, axis, by):
        z, xl, y = self.coords
        nz, nx, ny = self.sizes
        if axis == "z":
            z = lax.rem(z + by + nz, nz)
        elif axis == "y":
            y = lax.rem(y + by + ny, ny)
        else:
            xl = nx - 1 - xl
        return (self.section, (z * nx + xl) * ny + y)

    def copy(self, ref, sem, peer):
        return pltpu.make_async_remote_copy(
            src_ref=ref,
            dst_ref=ref,
            send_sem=self.send.at[sem],
            recv_sem=self.recv.at[sem],
            device_id=peer,
            device_id_type=MESH,
        )

    def start(self, piece, begin, width, sem, peer):
        copy = self.copy(piece(pl.ds(begin, width)), sem, peer)
        copy.start()
        self.live.append(copy)

    def ring(self, axis, first, stop, fixed, single=False):
        size = self.sizes[0] if axis == "z" else self.sizes[2]
        me = self.coords[0] if axis == "z" else self.coords[2]
        last = size // 2
        first_sem = self.sems
        self.sems += 2 * last

        def arguments(way, step, index):
            z, y = (index, fixed) if axis == "z" else (fixed, index)
            begin, width = first, stop - first
            xl = self.coords[1] if single else slice(None)
            if step == last - 1:
                if single:
                    width = width // 2
                    begin = begin + way * width
                else:
                    xl = way

            def piece(columns):
                return self.weights.at[z, xl, y, :, columns]

            return piece, begin, width, first_sem + 2 * step + way, self.peer(axis, 1 - 2 * way)

        def at(way, step):
            return lax.rem(me - (1 - 2 * way) * step + size, size)

        for step in range(last):
            for way in (0, 1):
                self.start(*arguments(way, step, at(way, step)))
            yield
            for way in (0, 1):
                piece, begin, width, sem, peer = arguments(way, step, at(way, step + 1))
                self.copy(piece(pl.ds(begin, width)), sem, peer).wait_recv()

    def beside(self, fixed):
        sem = self.sems
        self.sems += 1
        _, xl, _ = self.coords
        nx = self.sizes[1]
        peer = self.peer("x", 0)
        self.start(
            lambda columns: self.weights.at[fixed, xl, :, :, columns],
            Y_LAST,
            PACKED - Y_LAST,
            sem,
            peer,
        )
        yield
        columns = pl.ds(Y_LAST, PACKED - Y_LAST)
        self.copy(self.weights.at[fixed, nx - 1 - xl, :, :, columns], sem, peer).wait_recv()

    def build(self):
        z, _, y = self.coords
        nz, _, ny = self.sizes
        rings = self.rings
        rings["a"] = self.ring("y", 0, Z_LAST, z)
        rings["b"] = self.ring("z", Z_LAST, Y_LAST, y)
        rings["c"] = self.ring("z", Y_LAST, PACKED, y, True)
        for by in range(ny):
            rings["az", by] = self.ring("z", 0, Z_LAST, lax.rem(y + by, ny))
        for by in range(nz):
            there = lax.rem(z + by, nz)
            rings["by", by] = self.ring("y", Z_LAST, Y_LAST, there)
            rings["cy", by] = self.ring("y", Y_LAST, PACKED, there, True)
            rings["cx", by] = self.beside(there)

    def go(self, *names):
        for name in names:
            next(self.rings[name], None)

    def finish(self):
        for copy in self.live:
            copy.wait_send()


def spread(source, tall, start):
    count = source.shape[0]
    for k in range(KT):
        tall[pl.ds(start + k, count, stride=KT), :] = source[:, k * HEAD : (k + 1) * HEAD].astype(
            F32
        )


def normalize(values, tangents, gain):
    inverse = lax.rsqrt(jnp.mean(values * values, axis=-1, keepdims=True) + EPS)
    cross = jnp.mean(values * tangents, axis=-1, keepdims=True)
    scaled = values * inverse
    return (
        (scaled * gain).astype(BF16),
        ((inverse * tangents - values * inverse**3 * cross) * gain).astype(BF16),
    )


def attend(q2, k2, v2, gains_ref):
    factor = 1.0 / math.sqrt(HEAD)
    qn, dqn = normalize(q2[:HALF], q2[HALF:], gains_ref[0:1, :])
    kn, dkn = normalize(k2[:HALF], k2[HALF:], gains_ref[1:2, :])
    value, dvalue = v2[:HALF].astype(BF16), v2[HALF:].astype(BF16)

    def against(rows, columns):
        return lax.dot_general(
            rows, columns, (((1,), (1,)), ((), ())), preferred_element_type=F32
        )

    scores = against(jnp.concatenate([qn, dqn], axis=0), kn)
    score = scores[:HALF] * factor
    dscore = (scores[HALF:] + against(qn, dkn)) * factor
    expo = jnp.exp(score)
    prob = expo * (1.0 / jnp.sum(expo, axis=-1, keepdims=True))
    growth = prob * dscore
    dprob = growth - prob * jnp.sum(growth, axis=-1, keepdims=True)
    prob, dprob = prob.astype(BF16), dprob.astype(BF16)
    mixed = jnp.dot(
        jnp.concatenate([prob, dprob], axis=0), value, preferred_element_type=F32
    )
    return mixed[:HALF], mixed[HALF:] + jnp.dot(prob, dvalue, preferred_element_type=F32)


def block_step(
    unit, entering, leaving, weights, gains_ref, mods_ref, dmods_ref, tall, flat, att
):
    group = 8
    vid = unit // NP

    @pl.loop(0, F // group, unroll=4)
    def _(i):
        first = pl.multiple_of(i * group, group)
        hidden = entering[unit, pl.ds(first, group), 0].astype(F32)
        tangent = entering[unit, pl.ds(first, group), 1].astype(F32)

        def mean(values):
            return jnp.sum(
                jnp.sum(values, axis=1, keepdims=True), axis=2, keepdims=True
            ) * (1.0 / D)

        inverse = lax.rsqrt(mean(hidden * hidden) + EPS)
        cross = mean(hidden * tangent)
        normed = hidden * inverse
        dnormed = inverse * tangent - hidden * inverse**3 * cross
        scale = 1.0 + mods_ref[vid, 1][None]
        modulated = normed * scale + mods_ref[vid, 0][None]
        dmodulated = dnormed * scale + normed * dmods_ref[vid, 1][None] + dmods_ref[vid, 0][None]
        row = pl.multiple_of(first * KT, group * KT)
        tall[pl.ds(row, group * KT), :] = modulated.reshape(group * KT, HEAD)
        tall[pl.ds(row + HALF * KT, group * KT), :] = dmodulated.reshape(group * KT, HEAD)

    for k in range(KT):
        flat[:, k * HEAD : (k + 1) * HEAD] = tall[pl.ds(k, ROWS, stride=KT), :].astype(BF16)

    def third(number, pair):
        column = number * HD + pair * 2 * HEAD
        halves = [
            weights[
                :, :, :, :, column + lower * 3 * HD : column + lower * 3 * HD + 2 * HEAD
            ].reshape(F, 1, ROWS_OUT, 2 * HEAD)
            for lower in range(2)
        ]
        matrix = jnp.concatenate(halves, axis=1).reshape(D, 2 * HEAD)
        return jnp.dot(flat[...], matrix, preferred_element_type=F32)

    ahead = [third(number, 0) for number in range(3)]
    for pair in range(HEADS // 2):
        q2, k2, v2 = ahead
        if pair + 1 < HEADS // 2:
            ahead = [third(number, pair + 1) for number in range(3)]
        for one in range(2):
            lanes = slice(one * HEAD, (one + 1) * HEAD)
            output, doutput = attend(q2[:, lanes], k2[:, lanes], v2[:, lanes], gains_ref)
            column = (pair * 2 + one) * HEAD
            att[:HALF, column : column + HEAD] = output.astype(BF16)
            att[HALF:, column : column + HEAD] = doutput.astype(BF16)

    for n in range(KT // 2):
        column = 2 * 3 * HD + n * 2 * HEAD
        matrix = weights[:, :, :, :, column : column + 2 * HEAD].reshape(HD, 2 * HEAD)
        y = jnp.dot(att[...], matrix, preferred_element_type=F32)
        tall[pl.ds(2 * n, ROWS, stride=KT), :] = y[:, :HEAD]
        tall[pl.ds(2 * n + 1, ROWS, stride=KT), :] = y[:, HEAD:]

    @pl.loop(0, F // group, unroll=4)
    def _(i):
        first = pl.multiple_of(i * group, group)
        row = pl.multiple_of(first * KT, group * KT)
        y = tall[pl.ds(row, group * KT), :].reshape(group, KT, HEAD)
        dy = tall[pl.ds(row + HALF * KT, group * KT), :].reshape(group, KT, HEAD)
        hidden = entering[unit, pl.ds(first, group), 0].astype(F32)
        tangent = entering[unit, pl.ds(first, group), 1].astype(F32)
        gate = mods_ref[vid, 2][None]
        dgate = dmods_ref[vid, 2][None]
        leaving[unit, pl.ds(first, group), 0] = (hidden + gate * y).astype(BF16)
        leaving[unit, pl.ds(first, group), 1] = (tangent + dgate * y + gate * dy).astype(BF16)


def kernel(
    sizes,
    sections,
    x_ref,
    t_ref,
    wqkv_ref,
    wout_ref,
    gains_ref,
    index_ref,
    amp_ref,
    freq_ref,
    phase_ref,
    out_ref,
    tan_ref,
    weights,
    mods_ref,
    dmods_ref,
    plain,
    staged,
    relay,
    entering,
    leaving,
    returned,
    tall,
    flat,
    att,
    load_sem,
    own_sem,
    swap_send,
    swap_recv,
    ring_send,
    ring_recv,
    x_send,
    x_recv,
    relay_send,
    relay_recv,
    pass_send,
    pass_recv,
    out_send,
    out_recv,
    turn_sem,
):
    nz, nx, ny = sizes
    count = nz * nx * ny
    section = lax.axis_index("section")
    me = lax.axis_index("seq")
    coords = (me // (nx * ny), (me // ny) % nx, me % ny)
    z, xl, y = coords
    first_half = section < 2

    def flip(index):
        return index + ny - 2 * ny * ((index // ny) % nx)

    across = flip(me)
    slot = jnp.where(first_half, me, across)
    neighbour = (section, lax.rem(me + 1, count))
    group = 8

    def exchange(source, row_of, target, place, send, recv):
        pltpu.make_async_copy(source.at[row_of(me)], target.at[place], recv).start()

        @pl.loop(1, count, unroll=21)
        def _(by):
            to = lax.rem(me + by * STRIDE, count)
            pltpu.make_async_remote_copy(
                src_ref=source.at[row_of(to)],
                dst_ref=target.at[place],
                send_sem=send,
                recv_sem=recv,
                device_id=(section, to),
                device_id_type=MESH,
            ).start()

    def exchange_came(source, target, recv):
        pltpu.make_async_copy(source, target, recv).wait()

    def exchange_sent(source, target, send, recv):
        pltpu.make_async_remote_copy(
            src_ref=source.at[pl.ds(0, count - 1)],
            dst_ref=target.at[pl.ds(0, count - 1)],
            send_sem=send,
            recv_sem=recv,
            device_id=neighbour,
            device_id_type=MESH,
        ).wait_send()

    leads = lax.rem(section, 2) == 0
    loads = [
        pltpu.make_async_copy(ref, plain.at[tan], load_sem.at[tan])
        for tan, ref in enumerate((x_ref, t_ref))
    ]

    @pl.when(leads)
    def _():
        for load in loads:
            load.start()

    own = []
    for part, (ref, first, width) in enumerate(
        (
            (wqkv_ref.at[pl.ds(0, ROWS_OUT)], 0, 3 * HD),
            (wqkv_ref.at[pl.ds(ROWS_OUT, ROWS_OUT)], 3 * HD, 3 * HD),
            (wout_ref, 6 * HD, D),
        )
    ):
        home = weights.at[z, xl, y, :, pl.ds(first, width)]
        own.append(pltpu.make_async_copy(ref, home, own_sem.at[part]))
        own[-1].start()
    for copy in own:
        copy.wait()

    @pl.when(jnp.logical_not(leads))
    def _():
        pl.semaphore_wait(turn_sem, 1)

    gather = Gather(sizes, section, coords, weights, ring_send, ring_recv)
    gather.build()
    go = gather.go
    mine = weights.at[z, xl, y, :, pl.ds(0, Y_LAST)]
    swap = pltpu.make_async_remote_copy(
        src_ref=mine,
        dst_ref=mine,
        send_sem=swap_send,
        recv_sem=swap_recv,
        device_id=(section, across),
        device_id_type=MESH,
    )
    theirs = weights.at[z, nx - 1 - xl, y, :, pl.ds(0, Y_LAST)]
    swapped = pltpu.make_async_remote_copy(
        src_ref=theirs,
        dst_ref=theirs,
        send_sem=swap_send,
        recv_sem=swap_recv,
        device_id=(section, across),
        device_id_type=MESH,
    )
    swap.start()
    go("c", ("cy", 0))

    def prepare(vid):
        for tan in range(2):
            spread(plain.at[tan, vid], tall, 0)

            @pl.loop(0, count // group)
            def _(i):
                first = pl.multiple_of(i * group, group)
                row = pl.multiple_of(first * NP * KT, group * NP * KT)
                tiles = (
                    tall[pl.ds(row, group * NP * KT), :]
                    .astype(BF16)
                    .reshape(group, NP, KT, HEAD)
                )
                for pos in range(NP):
                    staged[vid * NP + pos, pl.ds(first, group), tan] = tiles[:, pos]

    @pl.when(leads)
    def _():
        for load in loads:
            load.wait()
        prepare(0)

    @pl.when(section == 0)
    def _():
        exchange(
            staged.at[0], lambda f: f, entering.at[0], me, x_send.at[0], x_recv.at[0]
        )

    def second_round(unit):
        exchange(
            staged.at[unit], flip, relay.at[unit], me, x_send.at[unit], x_recv.at[unit]
        )

    @pl.when(section == 2)
    def _():
        second_round(1)
        prepare(1)
        second_round(2)
        second_round(3)

    def relayed(unit):
        return pltpu.make_async_remote_copy(
            src_ref=relay.at[unit],
            dst_ref=entering.at[unit],
            send_sem=relay_send.at[unit],
            recv_sem=relay_recv.at[unit],
            device_id=(0, across),
            device_id_type=MESH,
        )

    def pass_to_first(unit):
        @pl.when(section == 2)
        def _():
            exchange_came(staged.at[unit], relay.at[unit], x_recv.at[unit])
            relayed(unit).start()

    for vid in range(VIDS):
        time_value = (index_ref[vid].astype(F32) + 0.5) * (math.pi / (2.0 * T_STEPS))
        mods_ref[vid], dmods_ref[vid] = timing(
            amp_ref[...], freq_ref[...], phase_ref[...], time_value
        )

    swapped.wait_recv()
    go("b", "a", ("by", 0), ("az", 0))
    go("c", ("cy", 1), ("cy", 7))
    go("a", ("az", 1), ("az", 3))
    go(("cy", 0),)
    go("b", ("by", 1), ("by", 7))
    go("c", ("cy", 2), ("cy", 6))

    @pl.when(leads)
    def _():
        pl.semaphore_signal(
            turn_sem, inc=1, device_id=(section + 1, me), device_id_type=MESH
        )

    go("a", ("az", 2))
    go(("cy", 0), ("cx", 0), ("cy", 1), ("cy", 7))
    go(("az", 0), ("by", 0))
    go("c", ("cy", 3), ("cy", 5))
    go(("cy", 1), ("cx", 1), ("cy", 7), ("cx", 7), ("cy", 2), ("cy", 6))
    go("b", ("by", 2), ("by", 6))
    go("c", ("cy", 4))
    pass_to_first(1)
    go(("az", 1), ("az", 3), ("by", 1), ("by", 7), ("az", 2))
    go(("cy", 2), ("cx", 2), ("cy", 6), ("cx", 6), ("cy", 3), ("cy", 5), ("cy", 4))
    go("b", ("by", 3), ("by", 5))
    go(("az", 0), ("by", 0), ("az", 1), ("az", 3))
    go(("cy", 3), ("cx", 3), ("cy", 5), ("cx", 5), ("cy", 4), ("cx", 4))
    pass_to_first(2)

    go("b", ("by", 4))
    go(("by", 2), ("by", 6), ("az", 2), ("by", 1), ("by", 7), ("az", 0))
    pass_to_first(3)
    go(("by", 3), ("by", 5), ("az", 1), ("az", 3), ("by", 4), ("az", 2))
    go(("by", 2), ("by", 6), ("az", 0), ("by", 3), ("by", 5))
    go(("az", 1), ("az", 3), ("by", 4), ("az", 2))
    go(*(("cx", by) for by in range(nz)))

    @pl.when(section == 1)
    def _():
        pl.semaphore_signal(turn_sem, inc=1, device_id=(0, me), device_id_type=MESH)

    def onward(unit, first=0, frames=F):
        return pltpu.make_async_remote_copy(
            src_ref=leaving.at[unit, pl.ds(first, frames)],
            dst_ref=entering.at[unit, pl.ds(first, frames)],
            send_sem=pass_send.at[unit],
            recv_sem=pass_recv.at[unit],
            device_id=(
                lax.rem(section + 1, sections),
                jnp.where(section == 1, across, me),
            ),
            device_id_type=MESH,
        )

    def send_back(unit):
        exchange(
            leaving.at[unit],
            lambda f: f,
            returned.at[unit],
            slot,
            out_send.at[unit],
            out_recv.at[unit],
        )

    @pl.loop(0, UNITS)
    def _(unit):
        @pl.when(jnp.logical_and(section == 0, unit == 0))
        def _():
            exchange_came(staged.at[0], entering.at[0], x_recv.at[0])

        @pl.when(jnp.logical_and(section == 0, unit > 0))
        def _():
            relayed(unit).wait_recv()

        @pl.when(section > 0)
        def _():
            onward(unit).wait_recv()

        block_step(
            unit, entering, leaving, weights, gains_ref, mods_ref, dmods_ref, tall, flat, att
        )

        @pl.when(section < sections - 1)
        def _():
            for part in range(HOP_PARTS):
                onward(unit, part * (F // HOP_PARTS), F // HOP_PARTS).start()

        @pl.when(section > 1)
        def _():
            send_back(unit)

    @pl.when(section == 0)
    def _():
        pl.semaphore_wait(turn_sem, 1)

    @pl.when(section < 2)
    def _():
        @pl.loop(0, UNITS)
        def _(unit):
            send_back(unit)

    gather.finish()
    swap.wait_send()

    @pl.loop(0, VIDS)
    def _(vid):
        for pos in range(NP):
            unit = vid * NP + pos
            exchange_came(leaving.at[unit], returned.at[unit], out_recv.at[unit])

            @pl.loop(0, count // group)
            def _(i):
                first = pl.multiple_of(i * group, group)
                for tan in range(2):
                    tiles = returned[unit, pl.ds(first, group), tan].astype(F32)
                    for one in range(group):
                        row = pl.multiple_of(
                            ((tan * count + first + one) * NP + pos) * KT, KT
                        )
                        tall[pl.ds(row, KT), :] = tiles[one]

        for tan, result in enumerate((out_ref, tan_ref)):
            for k in range(KT):
                result[vid, :, k * HEAD : (k + 1) * HEAD] = tall[
                    pl.ds(tan * count * NP * KT + k, count * NP, stride=KT), :
                ].astype(BF16)

    @pl.loop(0, UNITS)
    def _(unit):
        exchange_sent(
            leaving.at[unit], returned.at[unit], out_send.at[unit], out_recv.at[unit]
        )

        @pl.when(section < sections - 1)
        def _():
            onward(unit).wait_send()

        @pl.when(
            jnp.logical_or(
                jnp.logical_and(section == 0, unit == 0),
                jnp.logical_and(section == 2, unit > 0),
            )
        )
        def _():
            exchange_sent(
                staged.at[unit], relay.at[unit], x_send.at[unit], x_recv.at[unit]
            )

        @pl.when(jnp.logical_and(section == 2, unit > 0))
        def _():
            relayed(unit).wait_send()


def shards(sizes, x_in, x_tan, t_index, w_qkv, w_out, qk_gain, mod_amp, mod_freq, mod_phase):
    nz, nx, ny = sizes
    count = nz * nx * ny
    sections = lax.axis_size("section")
    places = x_in.shape[2]
    waves = [wave.reshape(3, KT, HEAD) for wave in (mod_amp, mod_freq, mod_phase)]
    outside = pl.BlockSpec(memory_space=pl.ANY)
    inside = pl.BlockSpec(memory_space=pltpu.VMEM)
    result = jax.ShapeDtypeStruct((VIDS, places, D), BF16)
    units = (UNITS, F, 2, KT, HEAD)
    rings = 2 * (ny // 2) * (1 + 2 * nz) + 2 * (nz // 2) * (2 + ny) + nz
    dma = pltpu.SemaphoreType.DMA
    out, tan = pl.pallas_call(
        functools.partial(kernel, sizes, sections),
        out_shape=(result, result),
        in_specs=[outside] * 4
        + [inside, pl.BlockSpec(memory_space=pltpu.SMEM)]
        + [inside] * 3,
        out_specs=(inside, inside),
        scratch_shapes=[
            pltpu.VMEM((nz, nx, ny, ROWS_OUT, PACKED), BF16),
            pltpu.VMEM((VIDS, 3, KT, HEAD), F32),
            pltpu.VMEM((VIDS, 3, KT, HEAD), F32),
            pltpu.VMEM((2, VIDS, places, D), BF16),
            pltpu.VMEM(units, BF16),
            pltpu.VMEM(units, BF16),
            pltpu.VMEM(units, BF16),
            pltpu.VMEM(units, BF16),
            pltpu.VMEM(units, BF16),
            pltpu.VMEM((2 * places * KT, HEAD), F32),
            pltpu.VMEM((ROWS, D), BF16),
            pltpu.VMEM((ROWS, HD), BF16),
            dma((2,)),
            dma((3,)),
            dma,
            dma,
            dma((rings,)),
            dma((rings,)),
            dma((UNITS,)),
            dma((UNITS,)),
            dma((UNITS,)),
            dma((UNITS,)),
            dma((UNITS,)),
            dma((UNITS,)),
            dma((UNITS,)),
            dma((UNITS,)),
            pltpu.SemaphoreType.REGULAR,
        ],
        compiler_params=pltpu.CompilerParams(
            has_side_effects=True, vmem_limit_bytes=60 * 1024 * 1024
        ),
        name="blocks",
    )(
        x_in.reshape(VIDS, places, D),
        x_tan.reshape(VIDS, places, D),
        w_qkv[0],
        w_out[0],
        qk_gain[0],
        t_index,
        *waves,
    )
    return (out[None, :, None], tan[None, :, None])


def solution(mesh):
    count = mesh.shape["seq"]
    sizes = (count // 8, 2, 4)
    placed = (
        P(None, "seq", None, None),
        P(None, "seq", None, None),
        P(),
        P("section", "seq", None),
        P("section", "seq", None),
        P("section", None, None),
        P("section", None, None),
        P("section", None, None),
        P("section", None, None),
    )
    return jax.shard_map(
        functools.partial(shards, sizes),
        mesh=mesh,
        in_specs=placed,
        out_specs=(P("section", None, "seq", None, None), P("section", None, "seq", None, None)),
        check_vma=False,
    )
```

```python
import functools
import math

import jax
import jax.numpy as jnp
from jax import lax
from jax.experimental import pallas as pl
from jax.experimental.pallas import tpu as pltpu
from jax.sharding import PartitionSpec as P

HEADS = 8
HEAD = 128
T_STEPS = 1000
D = 2048
KT = D // HEAD
HD = HEADS * HEAD
F = 64
NP = 2
VIDS = 2
UNITS = VIDS * NP
ROWS = 2 * F
HALF = F
HOP_PARTS = 4
EPS = 1e-06
F32 = jnp.float32
BF16 = jnp.bfloat16
MESH = pl.DeviceIdType.MESH
ROWS_OUT = 16
PACKED = 2 * 3 * HD + D
Z_LAST, Y_LAST = 2816, 5632


def timing(amp, freq, phase, time_value):
    angle = freq * time_value + phase
    return (amp * jnp.sin(angle), amp * freq * jnp.cos(angle))


class Gather:
    def __init__(self, sizes, section, coords, weights, send, recv):
        self.sizes, self.section, self.coords = sizes, section, coords
        self.weights, self.send, self.recv = weights, send, recv
        self.live = []
        self.sems = 0
        self.rings = {}

    def peer(self, axis, by):
        z, xl, y = self.coords
        nz, nx, ny = self.sizes
        if axis == "z":
            z = lax.rem(z + by + nz, nz)
        elif axis == "y":
            y = lax.rem(y + by + ny, ny)
        else:
            xl = nx - 1 - xl
        return (self.section, (z * nx + xl) * ny + y)

    def copy(self, ref, sem, peer):
        return pltpu.make_async_remote_copy(
            src_ref=ref,
            dst_ref=ref,
            send_sem=self.send.at[sem],
            recv_sem=self.recv.at[sem],
            device_id=peer,
            device_id_type=MESH,
        )

    def start(self, piece, begin, width, sem, peer):
        copy = self.copy(piece(pl.ds(begin, width)), sem, peer)
        copy.start()
        self.live.append(copy)

    def ring(self, axis, first, stop, fixed, single=False):
        size = self.sizes[0] if axis == "z" else self.sizes[2]
        me = self.coords[0] if axis == "z" else self.coords[2]
        last = size // 2
        first_sem = self.sems
        self.sems += 2 * last

        def arguments(way, step, index):
            z, y = (index, fixed) if axis == "z" else (fixed, index)
            begin, width = first, stop - first
            xl = self.coords[1] if single else slice(None)
            if step == last - 1:
                if single:
                    width = width // 2
                    begin = begin + way * width
                else:
                    xl = way

            def piece(columns):
                return self.weights.at[z, xl, y, :, columns]

            return piece, begin, width, first_sem + 2 * step + way, self.peer(axis, 1 - 2 * way)

        def at(way, step):
            return lax.rem(me - (1 - 2 * way) * step + size, size)

        for step in range(last):
            for way in (0, 1):
                self.start(*arguments(way, step, at(way, step)))
            yield
            for way in (0, 1):
                piece, begin, width, sem, peer = arguments(way, step, at(way, step + 1))
                self.copy(piece(pl.ds(begin, width)), sem, peer).wait_recv()

    def beside(self, fixed):
        sem = self.sems
        self.sems += 1
        _, xl, _ = self.coords
        nx = self.sizes[1]
        peer = self.peer("x", 0)
        self.start(
            lambda columns: self.weights.at[fixed, xl, :, :, columns],
            Y_LAST,
            PACKED - Y_LAST,
            sem,
            peer,
        )
        yield
        columns = pl.ds(Y_LAST, PACKED - Y_LAST)
        self.copy(self.weights.at[fixed, nx - 1 - xl, :, :, columns], sem, peer).wait_recv()

    def build(self):
        z, _, y = self.coords
        nz, _, ny = self.sizes
        rings = self.rings
        rings["a"] = self.ring("y", 0, Z_LAST, z)
        rings["b"] = self.ring("z", Z_LAST, Y_LAST, y)
        rings["c"] = self.ring("z", Y_LAST, PACKED, y, True)
        for by in range(ny):
            rings["az", by] = self.ring("z", 0, Z_LAST, lax.rem(y + by, ny))
        for by in range(nz):
            there = lax.rem(z + by, nz)
            rings["by", by] = self.ring("y", Z_LAST, Y_LAST, there)
            rings["cy", by] = self.ring("y", Y_LAST, PACKED, there, True)
            rings["cx", by] = self.beside(there)

    def go(self, *names):
        for name in names:
            next(self.rings[name], None)

    def finish(self):
        for copy in self.live:
            copy.wait_send()


def spread(source, tall, start):
    count = source.shape[0]
    for k in range(KT):
        tall[pl.ds(start + k, count, stride=KT), :] = source[:, k * HEAD : (k + 1) * HEAD].astype(
            F32
        )


def normalize(values, tangents, gain):
    inverse = lax.rsqrt(jnp.mean(values * values, axis=-1, keepdims=True) + EPS)
    cross = jnp.mean(values * tangents, axis=-1, keepdims=True)
    scaled = values * inverse
    return (
        (scaled * gain).astype(BF16),
        ((inverse * tangents - values * inverse**3 * cross) * gain).astype(BF16),
    )


def attend(q2, k2, v2, gains_ref):
    factor = 1.0 / math.sqrt(HEAD)
    qn, dqn = normalize(q2[:HALF], q2[HALF:], gains_ref[0:1, :])
    kn, dkn = normalize(k2[:HALF], k2[HALF:], gains_ref[1:2, :])
    value, dvalue = v2[:HALF].astype(BF16), v2[HALF:].astype(BF16)

    def against(rows, columns):
        return lax.dot_general(
            rows, columns, (((1,), (1,)), ((), ())), preferred_element_type=F32
        )

    scores = against(jnp.concatenate([qn, dqn], axis=0), kn)
    score = scores[:HALF] * factor
    dscore = (scores[HALF:] + against(qn, dkn)) * factor
    expo = jnp.exp(score)
    prob = expo * (1.0 / jnp.sum(expo, axis=-1, keepdims=True))
    growth = prob * dscore
    dprob = growth - prob * jnp.sum(growth, axis=-1, keepdims=True)
    prob, dprob = prob.astype(BF16), dprob.astype(BF16)
    mixed = jnp.dot(
        jnp.concatenate([prob, dprob], axis=0), value, preferred_element_type=F32
    )
    return mixed[:HALF], mixed[HALF:] + jnp.dot(prob, dvalue, preferred_element_type=F32)


def block_step(
    unit, entering, leaving, weights, gains_ref, mods_ref, dmods_ref, tall, flat, att
):
    group = 8
    vid = unit // NP

    @pl.loop(0, F // group, unroll=4)
    def _(i):
        first = pl.multiple_of(i * group, group)
        hidden = entering[unit, pl.ds(first, group), 0].astype(F32)
        tangent = entering[unit, pl.ds(first, group), 1].astype(F32)

        def mean(values):
            return jnp.sum(
                jnp.sum(values, axis=1, keepdims=True), axis=2, keepdims=True
            ) * (1.0 / D)

        inverse = lax.rsqrt(mean(hidden * hidden) + EPS)
        cross = mean(hidden * tangent)
        normed = hidden * inverse
        dnormed = inverse * tangent - hidden * inverse**3 * cross
        scale = 1.0 + mods_ref[vid, 1][None]
        modulated = normed * scale + mods_ref[vid, 0][None]
        dmodulated = dnormed * scale + normed * dmods_ref[vid, 1][None] + dmods_ref[vid, 0][None]
        row = pl.multiple_of(first * KT, group * KT)
        tall[pl.ds(row, group * KT), :] = modulated.reshape(group * KT, HEAD)
        tall[pl.ds(row + HALF * KT, group * KT), :] = dmodulated.reshape(group * KT, HEAD)

    for k in range(KT):
        flat[:, k * HEAD : (k + 1) * HEAD] = tall[pl.ds(k, ROWS, stride=KT), :].astype(BF16)

    def third(number, pair):
        column = number * HD + pair * 2 * HEAD
        halves = [
            weights[
                :, :, :, :, column + lower * 3 * HD : column + lower * 3 * HD + 2 * HEAD
            ].reshape(F, 1, ROWS_OUT, 2 * HEAD)
            for lower in range(2)
        ]
        matrix = jnp.concatenate(halves, axis=1).reshape(D, 2 * HEAD)
        return jnp.dot(flat[...], matrix, preferred_element_type=F32)

    ahead = [third(number, 0) for number in range(3)]
    for pair in range(HEADS // 2):
        q2, k2, v2 = ahead
        if pair + 1 < HEADS // 2:
            ahead = [third(number, pair + 1) for number in range(3)]
        for one in range(2):
            lanes = slice(one * HEAD, (one + 1) * HEAD)
            output, doutput = attend(q2[:, lanes], k2[:, lanes], v2[:, lanes], gains_ref)
            column = (pair * 2 + one) * HEAD
            att[:HALF, column : column + HEAD] = output.astype(BF16)
            att[HALF:, column : column + HEAD] = doutput.astype(BF16)

    for n in range(KT // 2):
        column = 2 * 3 * HD + n * 2 * HEAD
        matrix = weights[:, :, :, :, column : column + 2 * HEAD].reshape(HD, 2 * HEAD)
        y = jnp.dot(att[...], matrix, preferred_element_type=F32)
        tall[pl.ds(2 * n, ROWS, stride=KT), :] = y[:, :HEAD]
        tall[pl.ds(2 * n + 1, ROWS, stride=KT), :] = y[:, HEAD:]

    @pl.loop(0, F // group, unroll=4)
    def _(i):
        first = pl.multiple_of(i * group, group)
        row = pl.multiple_of(first * KT, group * KT)
        y = tall[pl.ds(row, group * KT), :].reshape(group, KT, HEAD)
        dy = tall[pl.ds(row + HALF * KT, group * KT), :].reshape(group, KT, HEAD)
        hidden = entering[unit, pl.ds(first, group), 0].astype(F32)
        tangent = entering[unit, pl.ds(first, group), 1].astype(F32)
        gate = mods_ref[vid, 2][None]
        dgate = dmods_ref[vid, 2][None]
        leaving[unit, pl.ds(first, group), 0] = (hidden + gate * y).astype(BF16)
        leaving[unit, pl.ds(first, group), 1] = (tangent + dgate * y + gate * dy).astype(BF16)


def kernel(
    sizes,
    sections,
    x_ref,
    t_ref,
    wqkv_ref,
    wout_ref,
    gains_ref,
    index_ref,
    amp_ref,
    freq_ref,
    phase_ref,
    out_ref,
    tan_ref,
    weights,
    mods_ref,
    dmods_ref,
    plain,
    staged,
    relay,
    entering,
    leaving,
    returned,
    carry,
    tall,
    flat,
    att,
    load_sem,
    own_sem,
    swap_send,
    swap_recv,
    ring_send,
    ring_recv,
    x_send,
    x_recv,
    relay_send,
    relay_recv,
    pass_send,
    pass_recv,
    out_send,
    out_recv,
    carry_send,
    carry_recv,
    turn_sem,
):
    nz, nx, ny = sizes
    count = nz * nx * ny
    section = lax.axis_index("section")
    me = lax.axis_index("seq")
    coords = (me // (nx * ny), (me // ny) % nx, me % ny)
    z, xl, y = coords
    first_half = section < 2

    def flip(index):
        return index + ny - 2 * ny * ((index // ny) % nx)

    across = flip(me)
    slot = jnp.where(first_half, me, across)
    neighbour = (section, lax.rem(me + 1, count))
    group = 8

    plane = nx * ny
    low = lax.rem(me, plane)
    far = nz // 2

    def exchange(source, row_of, target, place, send, recv, distances):
        def one(distance, by):
            to = lax.rem(z + distance + nz, nz) * plane + lax.rem(low + by, plane)
            pltpu.make_async_remote_copy(
                src_ref=source.at[row_of(to)],
                dst_ref=target.at[place],
                send_sem=send,
                recv_sem=recv,
                device_id=(section, to),
                device_id_type=MESH,
            ).start()

        pltpu.make_async_copy(source.at[row_of(me)], target.at[place], recv).start()

        @pl.loop(0, plane)
        def _(by):
            for distance in distances:
                one(distance, by)

        @pl.loop(1, plane)
        def _(by):
            one(0, by)

    near = [sign * distance for distance in range(1, far) for sign in (1, -1)]

    def carried(unit, way, ref):
        to = lax.rem(z + (2 * way - 1) + nz, nz) * plane + low
        return pltpu.make_async_remote_copy(
            src_ref=ref,
            dst_ref=carry.at[unit, way],
            send_sem=out_send.at[unit],
            recv_sem=carry_recv.at[unit, way],
            device_id=(section, to),
            device_id_type=MESH,
        )

    def send_back(unit):
        for way in range(2):
            row = lax.rem(z + far, nz) * plane + way * ny
            carried(unit, way, leaving.at[unit, pl.ds(row, ny)]).start()
        exchange(
            leaving.at[unit],
            lambda f: f,
            returned.at[unit],
            slot,
            out_send.at[unit],
            out_recv.at[unit],
            near,
        )

    def carry_on(unit):
        for way in range(2):
            carried(unit, way, carry.at[unit, way]).wait_recv()
            begun = lax.rem(z - (2 * way - 1) + nz, nz)
            end = lax.rem(begun + far, nz)
            for to_y in range(ny):
                pltpu.make_async_remote_copy(
                    src_ref=carry.at[unit, way, to_y],
                    dst_ref=returned.at[unit, slot + (begun - z) * plane],
                    send_sem=carry_send.at[unit],
                    recv_sem=out_recv.at[unit],
                    device_id=(section, end * plane + way * ny + to_y),
                    device_id_type=MESH,
                ).start()

    def carried_on(unit):
        pltpu.make_async_remote_copy(
            src_ref=carry.at[unit],
            dst_ref=carry.at[unit],
            send_sem=carry_send.at[unit],
            recv_sem=carry_recv.at[unit, 0],
            device_id=neighbour,
            device_id_type=MESH,
        ).wait_send()

    def exchange_came(source, target, recv):
        pltpu.make_async_copy(source, target, recv).wait()

    def exchange_sent(source, target, send, recv):
        pltpu.make_async_remote_copy(
            src_ref=source.at[pl.ds(0, count - 1)],
            dst_ref=target.at[pl.ds(0, count - 1)],
            send_sem=send,
            recv_sem=recv,
            device_id=neighbour,
            device_id_type=MESH,
        ).wait_send()

    leads = lax.rem(section, 2) == 0
    loads = [
        pltpu.make_async_copy(ref, plain.at[tan], load_sem.at[tan])
        for tan, ref in enumerate((x_ref, t_ref))
    ]

    @pl.when(leads)
    def _():
        for load in loads:
            load.start()

    own = []
    for part, (ref, first, width) in enumerate(
        (
            (wqkv_ref.at[pl.ds(0, ROWS_OUT)], 0, 3 * HD),
            (wqkv_ref.at[pl.ds(ROWS_OUT, ROWS_OUT)], 3 * HD, 3 * HD),
            (wout_ref, 6 * HD, D),
        )
    ):
        home = weights.at[z, xl, y, :, pl.ds(first, width)]
        own.append(pltpu.make_async_copy(ref, home, own_sem.at[part]))
        own[-1].start()
    for copy in own:
        copy.wait()

    @pl.when(jnp.logical_not(leads))
    def _():
        pl.semaphore_wait(turn_sem, 1)

    gather = Gather(sizes, section, coords, weights, ring_send, ring_recv)
    gather.build()
    go = gather.go
    mine = weights.at[z, xl, y, :, pl.ds(0, Y_LAST)]
    swap = pltpu.make_async_remote_copy(
        src_ref=mine,
        dst_ref=mine,
        send_sem=swap_send,
        recv_sem=swap_recv,
        device_id=(section, across),
        device_id_type=MESH,
    )
    theirs = weights.at[z, nx - 1 - xl, y, :, pl.ds(0, Y_LAST)]
    swapped = pltpu.make_async_remote_copy(
        src_ref=theirs,
        dst_ref=theirs,
        send_sem=swap_send,
        recv_sem=swap_recv,
        device_id=(section, across),
        device_id_type=MESH,
    )
    swap.start()
    go("c", ("cy", 0))

    def prepare(vid):
        for tan in range(2):
            spread(plain.at[tan, vid], tall, 0)

            @pl.loop(0, count // group)
            def _(i):
                first = pl.multiple_of(i * group, group)
                row = pl.multiple_of(first * NP * KT, group * NP * KT)
                tiles = (
                    tall[pl.ds(row, group * NP * KT), :]
                    .astype(BF16)
                    .reshape(group, NP, KT, HEAD)
                )
                for pos in range(NP):
                    staged[vid * NP + pos, pl.ds(first, group), tan] = tiles[:, pos]

    @pl.when(leads)
    def _():
        for load in loads:
            load.wait()
        prepare(0)

    @pl.when(section == 0)
    def _():
        exchange(
            staged.at[0],
            lambda f: f,
            entering.at[0],
            me,
            x_send.at[0],
            x_recv.at[0],
            near + [far],
        )

    def second_round(unit):
        exchange(
            staged.at[unit],
            flip,
            relay.at[unit],
            me,
            x_send.at[unit],
            x_recv.at[unit],
            near + [far],
        )

    @pl.when(section == 2)
    def _():
        second_round(1)
        prepare(1)
        second_round(2)
        second_round(3)

    def relayed(unit):
        return pltpu.make_async_remote_copy(
            src_ref=relay.at[unit],
            dst_ref=entering.at[unit],
            send_sem=relay_send.at[unit],
            recv_sem=relay_recv.at[unit],
            device_id=(0, across),
            device_id_type=MESH,
        )

    def pass_to_first(unit):
        @pl.when(section == 2)
        def _():
            exchange_came(staged.at[unit], relay.at[unit], x_recv.at[unit])
            relayed(unit).start()

    for vid in range(VIDS):
        time_value = (index_ref[vid].astype(F32) + 0.5) * (math.pi / (2.0 * T_STEPS))
        mods_ref[vid], dmods_ref[vid] = timing(
            amp_ref[...], freq_ref[...], phase_ref[...], time_value
        )

    swapped.wait_recv()
    go("b", "a", ("by", 0), ("az", 0))
    go("c", ("cy", 1), ("cy", 7))
    go("a", ("az", 1), ("az", 3))
    go(("cy", 0),)
    go("b", ("by", 1), ("by", 7))
    go("c", ("cy", 2), ("cy", 6))

    @pl.when(leads)
    def _():
        pl.semaphore_signal(
            turn_sem, inc=1, device_id=(section + 1, me), device_id_type=MESH
        )

    go("a", ("az", 2))
    go(("cy", 0), ("cx", 0), ("cy", 1), ("cy", 7))
    go(("az", 0), ("by", 0))
    go("c", ("cy", 3), ("cy", 5))
    go(("cy", 1), ("cx", 1), ("cy", 7), ("cx", 7), ("cy", 2), ("cy", 6))
    go("b", ("by", 2), ("by", 6))
    go("c", ("cy", 4))
    pass_to_first(1)
    go(("az", 1), ("az", 3), ("by", 1), ("by", 7), ("az", 2))
    go(("cy", 2), ("cx", 2), ("cy", 6), ("cx", 6), ("cy", 3), ("cy", 5), ("cy", 4))
    go("b", ("by", 3), ("by", 5))
    go(("az", 0), ("by", 0), ("az", 1), ("az", 3))
    go(("cy", 3), ("cx", 3), ("cy", 5), ("cx", 5), ("cy", 4), ("cx", 4))
    pass_to_first(2)

    go("b", ("by", 4))
    go(("by", 2), ("by", 6), ("az", 2), ("by", 1), ("by", 7), ("az", 0))
    pass_to_first(3)
    go(("by", 3), ("by", 5), ("az", 1), ("az", 3), ("by", 4), ("az", 2))
    go(("by", 2), ("by", 6), ("az", 0), ("by", 3), ("by", 5))
    go(("az", 1), ("az", 3), ("by", 4), ("az", 2))
    go(*(("cx", by) for by in range(nz)))

    @pl.when(section == 1)
    def _():
        pl.semaphore_signal(turn_sem, inc=1, device_id=(0, me), device_id_type=MESH)

    def onward(unit, first=0, frames=F):
        return pltpu.make_async_remote_copy(
            src_ref=leaving.at[unit, pl.ds(first, frames)],
            dst_ref=entering.at[unit, pl.ds(first, frames)],
            send_sem=pass_send.at[unit],
            recv_sem=pass_recv.at[unit],
            device_id=(
                lax.rem(section + 1, sections),
                jnp.where(section == 1, across, me),
            ),
            device_id_type=MESH,
        )

    @pl.loop(0, UNITS)
    def _(unit):
        @pl.when(jnp.logical_and(section == 0, unit == 0))
        def _():
            exchange_came(staged.at[0], entering.at[0], x_recv.at[0])

        @pl.when(jnp.logical_and(section == 0, unit > 0))
        def _():
            relayed(unit).wait_recv()

        @pl.when(section > 0)
        def _():
            onward(unit).wait_recv()

        block_step(
            unit, entering, leaving, weights, gains_ref, mods_ref, dmods_ref, tall, flat, att
        )

        @pl.when(section < sections - 1)
        def _():
            for part in range(HOP_PARTS):
                onward(unit, part * (F // HOP_PARTS), F // HOP_PARTS).start()

        @pl.when(section > 1)
        def _():
            send_back(unit)

        @pl.when(jnp.logical_and(section > 1, unit > 0))
        def _():
            carry_on(unit - 1)

    @pl.when(section == 0)
    def _():
        pl.semaphore_wait(turn_sem, 1)

    @pl.when(section < 2)
    def _():
        @pl.loop(0, UNITS)
        def _(unit):
            send_back(unit)

        @pl.loop(0, UNITS - 1)
        def _(unit):
            carry_on(unit)

    carry_on(UNITS - 1)

    gather.finish()
    swap.wait_send()

    @pl.loop(0, VIDS)
    def _(vid):
        for pos in range(NP):
            unit = vid * NP + pos
            exchange_came(leaving.at[unit], returned.at[unit], out_recv.at[unit])

            @pl.loop(0, count // group)
            def _(i):
                first = pl.multiple_of(i * group, group)
                for tan in range(2):
                    tiles = returned[unit, pl.ds(first, group), tan].astype(F32)
                    for one in range(group):
                        row = pl.multiple_of(
                            ((tan * count + first + one) * NP + pos) * KT, KT
                        )
                        tall[pl.ds(row, KT), :] = tiles[one]

        for tan, result in enumerate((out_ref, tan_ref)):
            for k in range(KT):
                result[vid, :, k * HEAD : (k + 1) * HEAD] = tall[
                    pl.ds(tan * count * NP * KT + k, count * NP, stride=KT), :
                ].astype(BF16)

    @pl.loop(0, UNITS)
    def _(unit):
        exchange_sent(
            leaving.at[unit], returned.at[unit], out_send.at[unit], out_recv.at[unit]
        )
        carried_on(unit)

        @pl.when(section < sections - 1)
        def _():
            onward(unit).wait_send()

        @pl.when(
            jnp.logical_or(
                jnp.logical_and(section == 0, unit == 0),
                jnp.logical_and(section == 2, unit > 0),
            )
        )
        def _():
            exchange_sent(
                staged.at[unit], relay.at[unit], x_send.at[unit], x_recv.at[unit]
            )

        @pl.when(jnp.logical_and(section == 2, unit > 0))
        def _():
            relayed(unit).wait_send()


def shards(sizes, x_in, x_tan, t_index, w_qkv, w_out, qk_gain, mod_amp, mod_freq, mod_phase):
    nz, nx, ny = sizes
    count = nz * nx * ny
    sections = lax.axis_size("section")
    places = x_in.shape[2]
    waves = [wave.reshape(3, KT, HEAD) for wave in (mod_amp, mod_freq, mod_phase)]
    outside = pl.BlockSpec(memory_space=pl.ANY)
    inside = pl.BlockSpec(memory_space=pltpu.VMEM)
    result = jax.ShapeDtypeStruct((VIDS, places, D), BF16)
    units = (UNITS, F, 2, KT, HEAD)
    rings = 2 * (ny // 2) * (1 + 2 * nz) + 2 * (nz // 2) * (2 + ny) + nz
    dma = pltpu.SemaphoreType.DMA
    out, tan = pl.pallas_call(
        functools.partial(kernel, sizes, sections),
        out_shape=(result, result),
        in_specs=[outside] * 4
        + [inside, pl.BlockSpec(memory_space=pltpu.SMEM)]
        + [inside] * 3,
        out_specs=(inside, inside),
        scratch_shapes=[
            pltpu.VMEM((nz, nx, ny, ROWS_OUT, PACKED), BF16),
            pltpu.VMEM((VIDS, 3, KT, HEAD), F32),
            pltpu.VMEM((VIDS, 3, KT, HEAD), F32),
            pltpu.VMEM((2, VIDS, places, D), BF16),
            pltpu.VMEM(units, BF16),
            pltpu.VMEM(units, BF16),
            pltpu.VMEM(units, BF16),
            pltpu.VMEM(units, BF16),
            pltpu.VMEM(units, BF16),
            pltpu.VMEM((UNITS, 2, ny, 2, KT, HEAD), BF16),
            pltpu.VMEM((2 * places * KT, HEAD), F32),
            pltpu.VMEM((ROWS, D), BF16),
            pltpu.VMEM((ROWS, HD), BF16),
            dma((2,)),
            dma((3,)),
            dma,
            dma,
            dma((rings,)),
            dma((rings,)),
            dma((UNITS,)),
            dma((UNITS,)),
            dma((UNITS,)),
            dma((UNITS,)),
            dma((UNITS,)),
            dma((UNITS,)),
            dma((UNITS,)),
            dma((UNITS,)),
            dma((UNITS,)),
            dma((UNITS, 2)),
            pltpu.SemaphoreType.REGULAR,
        ],
        compiler_params=pltpu.CompilerParams(
            has_side_effects=True, vmem_limit_bytes=60 * 1024 * 1024
        ),
        name="blocks",
    )(
        x_in.reshape(VIDS, places, D),
        x_tan.reshape(VIDS, places, D),
        w_qkv[0],
        w_out[0],
        qk_gain[0],
        t_index,
        *waves,
    )
    return (out[None, :, None], tan[None, :, None])


def solution(mesh):
    count = mesh.shape["seq"]
    sizes = (count // 8, 2, 4)
    placed = (
        P(None, "seq", None, None),
        P(None, "seq", None, None),
        P(),
        P("section", "seq", None),
        P("section", "seq", None),
        P("section", None, None),
        P("section", None, None),
        P("section", None, None),
        P("section", None, None),
    )
    return jax.shard_map(
        functools.partial(shards, sizes),
        mesh=mesh,
        in_specs=placed,
        out_specs=(P("section", None, "seq", None, None), P("section", None, "seq", None, None)),
        check_vma=False,
    )
```

```python
import functools
import math

import jax
import jax.numpy as jnp
from jax import lax
from jax.experimental import pallas as pl
from jax.experimental.pallas import tpu as pltpu
from jax.sharding import PartitionSpec as P

HEADS = 8
HEAD = 128
T_STEPS = 1000
D = 2048
KT = D // HEAD
HD = HEADS * HEAD
F = 64
NP = 2
VIDS = 2
UNITS = VIDS * NP
ROWS = 2 * F
HALF = F
HOP_PARTS = 4
STRIDE = 27
EPS = 1e-06
F32 = jnp.float32
BF16 = jnp.bfloat16
MESH = pl.DeviceIdType.MESH
ROWS_OUT = 16
PACKED = 2 * 3 * HD + D
Z_LAST, Y_LAST = 2816, 5632


def timing(amp, freq, phase, time_value):
    angle = freq * time_value + phase
    return (amp * jnp.sin(angle), amp * freq * jnp.cos(angle))


class Gather:
    def __init__(self, sizes, section, coords, weights, send, recv):
        self.sizes, self.section, self.coords = sizes, section, coords
        self.weights, self.send, self.recv = weights, send, recv
        self.live = []
        self.sems = 0
        self.rings = {}

    def peer(self, axis, by):
        z, xl, y = self.coords
        nz, nx, ny = self.sizes
        if axis == "z":
            z = lax.rem(z + by + nz, nz)
        elif axis == "y":
            y = lax.rem(y + by + ny, ny)
        else:
            xl = nx - 1 - xl
        return (self.section, (z * nx + xl) * ny + y)

    def copy(self, ref, sem, peer):
        return pltpu.make_async_remote_copy(
            src_ref=ref,
            dst_ref=ref,
            send_sem=self.send.at[sem],
            recv_sem=self.recv.at[sem],
            device_id=peer,
            device_id_type=MESH,
        )

    def start(self, piece, begin, width, sem, peer):
        copy = self.copy(piece(pl.ds(begin, width)), sem, peer)
        copy.start()
        self.live.append(copy)

    def ring(self, axis, first, stop, fixed, single=False):
        size = self.sizes[0] if axis == "z" else self.sizes[2]
        me = self.coords[0] if axis == "z" else self.coords[2]
        last = size // 2
        first_sem = self.sems
        self.sems += 2 * last

        def arguments(way, step, index):
            z, y = (index, fixed) if axis == "z" else (fixed, index)
            begin, width = first, stop - first
            xl = self.coords[1] if single else slice(None)
            if step == last - 1:
                if single:
                    width = width // 2
                    begin = begin + way * width
                else:
                    xl = way

            def piece(columns):
                return self.weights.at[z, xl, y, :, columns]

            return piece, begin, width, first_sem + 2 * step + way, self.peer(axis, 1 - 2 * way)

        def at(way, step):
            return lax.rem(me - (1 - 2 * way) * step + size, size)

        for step in range(last):
            for way in (0, 1):
                self.start(*arguments(way, step, at(way, step)))
            yield
            for way in (0, 1):
                piece, begin, width, sem, peer = arguments(way, step, at(way, step + 1))
                self.copy(piece(pl.ds(begin, width)), sem, peer).wait_recv()

    def beside(self, fixed):
        sem = self.sems
        self.sems += 1
        _, xl, _ = self.coords
        nx = self.sizes[1]
        peer = self.peer("x", 0)
        self.start(
            lambda columns: self.weights.at[fixed, xl, :, :, columns],
            Y_LAST,
            PACKED - Y_LAST,
            sem,
            peer,
        )
        yield
        columns = pl.ds(Y_LAST, PACKED - Y_LAST)
        self.copy(self.weights.at[fixed, nx - 1 - xl, :, :, columns], sem, peer).wait_recv()

    def build(self):
        z, _, y = self.coords
        nz, _, ny = self.sizes
        rings = self.rings
        rings["a"] = self.ring("y", 0, Z_LAST, z)
        rings["b"] = self.ring("z", Z_LAST, Y_LAST, y)
        rings["c"] = self.ring("z", Y_LAST, PACKED, y, True)
        for by in range(ny):
            rings["az", by] = self.ring("z", 0, Z_LAST, lax.rem(y + by, ny))
        for by in range(nz):
            there = lax.rem(z + by, nz)
            rings["by", by] = self.ring("y", Z_LAST, Y_LAST, there)
            rings["cy", by] = self.ring("y", Y_LAST, PACKED, there, True)
            rings["cx", by] = self.beside(there)

    def go(self, *names):
        for name in names:
            next(self.rings[name], None)

    def finish(self):
        for copy in self.live:
            copy.wait_send()


def spread(source, tall, start):
    count = source.shape[0]
    for k in range(KT):
        tall[pl.ds(start + k, count, stride=KT), :] = source[:, k * HEAD : (k + 1) * HEAD].astype(
            F32
        )


def normalize(values, tangents, gain):
    inverse = lax.rsqrt(jnp.mean(values * values, axis=-1, keepdims=True) + EPS)
    cross = jnp.mean(values * tangents, axis=-1, keepdims=True)
    scaled = values * inverse
    return (
        (scaled * gain).astype(BF16),
        ((inverse * tangents - values * inverse**3 * cross) * gain).astype(BF16),
    )


def attend(q2, k2, v2, gains_ref):
    factor = 1.0 / math.sqrt(HEAD)
    qn, dqn = normalize(q2[:HALF], q2[HALF:], gains_ref[0:1, :])
    kn, dkn = normalize(k2[:HALF], k2[HALF:], gains_ref[1:2, :])
    value, dvalue = v2[:HALF].astype(BF16), v2[HALF:].astype(BF16)

    def against(rows, columns):
        return lax.dot_general(
            rows, columns, (((1,), (1,)), ((), ())), preferred_element_type=F32
        )

    scores = against(jnp.concatenate([qn, dqn], axis=0), kn)
    score = scores[:HALF] * factor
    dscore = (scores[HALF:] + against(qn, dkn)) * factor
    expo = jnp.exp(score)
    prob = expo * (1.0 / jnp.sum(expo, axis=-1, keepdims=True))
    growth = prob * dscore
    dprob = growth - prob * jnp.sum(growth, axis=-1, keepdims=True)
    prob, dprob = prob.astype(BF16), dprob.astype(BF16)
    mixed = jnp.dot(
        jnp.concatenate([prob, dprob], axis=0), value, preferred_element_type=F32
    )
    return mixed[:HALF], mixed[HALF:] + jnp.dot(prob, dvalue, preferred_element_type=F32)


def modulate(unit, entering, mods_ref, dmods_ref, tall, flat):
    group = 8
    vid = unit // NP

    @pl.loop(0, F // group, unroll=4)
    def _(i):
        first = pl.multiple_of(i * group, group)
        hidden = entering[unit, pl.ds(first, group), 0].astype(F32)
        tangent = entering[unit, pl.ds(first, group), 1].astype(F32)

        def mean(values):
            return jnp.sum(
                jnp.sum(values, axis=1, keepdims=True), axis=2, keepdims=True
            ) * (1.0 / D)

        inverse = lax.rsqrt(mean(hidden * hidden) + EPS)
        cross = mean(hidden * tangent)
        normed = hidden * inverse
        dnormed = inverse * tangent - hidden * inverse**3 * cross
        scale = 1.0 + mods_ref[vid, 1][None]
        modulated = normed * scale + mods_ref[vid, 0][None]
        dmodulated = dnormed * scale + normed * dmods_ref[vid, 1][None] + dmods_ref[vid, 0][None]
        row = pl.multiple_of(first * KT, group * KT)
        tall[pl.ds(row, group * KT), :] = modulated.reshape(group * KT, HEAD)
        tall[pl.ds(row + HALF * KT, group * KT), :] = dmodulated.reshape(group * KT, HEAD)

    for k in range(KT):
        flat[:, k * HEAD : (k + 1) * HEAD] = tall[pl.ds(k, ROWS, stride=KT), :].astype(BF16)


def block_step(
    unit, entering, leaving, weights, gains_ref, mods_ref, dmods_ref, tall, flat, att
):
    group = 8
    vid = unit // NP

    def third(number, pair):
        column = number * HD + pair * 2 * HEAD
        halves = [
            weights[
                :, :, :, :, column + lower * 3 * HD : column + lower * 3 * HD + 2 * HEAD
            ].reshape(F, 1, ROWS_OUT, 2 * HEAD)
            for lower in range(2)
        ]
        matrix = jnp.concatenate(halves, axis=1).reshape(D, 2 * HEAD)
        return jnp.dot(flat[...], matrix, preferred_element_type=F32)

    ahead = [third(number, 0) for number in range(3)]
    for pair in range(HEADS // 2):
        q2, k2, v2 = ahead
        if pair + 1 < HEADS // 2:
            ahead = [third(number, pair + 1) for number in range(3)]
        for one in range(2):
            lanes = slice(one * HEAD, (one + 1) * HEAD)
            output, doutput = attend(q2[:, lanes], k2[:, lanes], v2[:, lanes], gains_ref)
            column = (pair * 2 + one) * HEAD
            att[:HALF, column : column + HEAD] = output.astype(BF16)
            att[HALF:, column : column + HEAD] = doutput.astype(BF16)

    for n in range(KT // 2):
        column = 2 * 3 * HD + n * 2 * HEAD
        matrix = weights[:, :, :, :, column : column + 2 * HEAD].reshape(HD, 2 * HEAD)
        y = jnp.dot(att[...], matrix, preferred_element_type=F32)
        tall[pl.ds(2 * n, ROWS, stride=KT), :] = y[:, :HEAD]
        tall[pl.ds(2 * n + 1, ROWS, stride=KT), :] = y[:, HEAD:]

    @pl.loop(0, F // group, unroll=4)
    def _(i):
        first = pl.multiple_of(i * group, group)
        row = pl.multiple_of(first * KT, group * KT)
        y = tall[pl.ds(row, group * KT), :].reshape(group, KT, HEAD)
        dy = tall[pl.ds(row + HALF * KT, group * KT), :].reshape(group, KT, HEAD)
        hidden = entering[unit, pl.ds(first, group), 0].astype(F32)
        tangent = entering[unit, pl.ds(first, group), 1].astype(F32)
        gate = mods_ref[vid, 2][None]
        dgate = dmods_ref[vid, 2][None]
        leaving[unit, pl.ds(first, group), 0] = (hidden + gate * y).astype(BF16)
        leaving[unit, pl.ds(first, group), 1] = (tangent + dgate * y + gate * dy).astype(BF16)


def kernel(
    sizes,
    sections,
    x_ref,
    t_ref,
    wqkv_ref,
    wout_ref,
    gains_ref,
    index_ref,
    amp_ref,
    freq_ref,
    phase_ref,
    out_ref,
    tan_ref,
    weights,
    mods_ref,
    dmods_ref,
    plain,
    staged,
    relay,
    entering,
    leaving,
    returned,
    tall,
    flat,
    att,
    load_sem,
    own_sem,
    swap_send,
    swap_recv,
    ring_send,
    ring_recv,
    x_send,
    x_recv,
    relay_send,
    relay_recv,
    pass_send,
    pass_recv,
    out_send,
    out_recv,
    turn_sem,
):
    nz, nx, ny = sizes
    count = nz * nx * ny
    section = lax.axis_index("section")
    me = lax.axis_index("seq")
    coords = (me // (nx * ny), (me // ny) % nx, me % ny)
    z, xl, y = coords
    first_half = section < 2

    def flip(index):
        return index + ny - 2 * ny * ((index // ny) % nx)

    across = flip(me)
    slot = jnp.where(first_half, me, across)
    neighbour = (section, lax.rem(me + 1, count))
    group = 8

    def exchange(source, row_of, target, place, send, recv):
        pltpu.make_async_copy(source.at[row_of(me)], target.at[place], recv).start()

        @pl.loop(1, count, unroll=21)
        def _(by):
            to = lax.rem(me + by * STRIDE, count)
            pltpu.make_async_remote_copy(
                src_ref=source.at[row_of(to)],
                dst_ref=target.at[place],
                send_sem=send,
                recv_sem=recv,
                device_id=(section, to),
                device_id_type=MESH,
            ).start()

    def exchange_came(source, target, recv):
        pltpu.make_async_copy(source, target, recv).wait()

    def exchange_sent(source, target, send, recv):
        pltpu.make_async_remote_copy(
            src_ref=source.at[pl.ds(0, count - 1)],
            dst_ref=target.at[pl.ds(0, count - 1)],
            send_sem=send,
            recv_sem=recv,
            device_id=neighbour,
            device_id_type=MESH,
        ).wait_send()

    leads = lax.rem(section, 2) == 0
    loads = [
        pltpu.make_async_copy(ref, plain.at[tan], load_sem.at[tan])
        for tan, ref in enumerate((x_ref, t_ref))
    ]

    @pl.when(leads)
    def _():
        for load in loads:
            load.start()

    own = []
    for part, (ref, first, width) in enumerate(
        (
            (wqkv_ref.at[pl.ds(0, ROWS_OUT)], 0, 3 * HD),
            (wqkv_ref.at[pl.ds(ROWS_OUT, ROWS_OUT)], 3 * HD, 3 * HD),
            (wout_ref, 6 * HD, D),
        )
    ):
        home = weights.at[z, xl, y, :, pl.ds(first, width)]
        own.append(pltpu.make_async_copy(ref, home, own_sem.at[part]))
        own[-1].start()
    for copy in own:
        copy.wait()

    @pl.when(jnp.logical_not(leads))
    def _():
        pl.semaphore_wait(turn_sem, 1)

    gather = Gather(sizes, section, coords, weights, ring_send, ring_recv)
    gather.build()
    go = gather.go
    mine = weights.at[z, xl, y, :, pl.ds(0, Y_LAST)]
    swap = pltpu.make_async_remote_copy(
        src_ref=mine,
        dst_ref=mine,
        send_sem=swap_send,
        recv_sem=swap_recv,
        device_id=(section, across),
        device_id_type=MESH,
    )
    theirs = weights.at[z, nx - 1 - xl, y, :, pl.ds(0, Y_LAST)]
    swapped = pltpu.make_async_remote_copy(
        src_ref=theirs,
        dst_ref=theirs,
        send_sem=swap_send,
        recv_sem=swap_recv,
        device_id=(section, across),
        device_id_type=MESH,
    )
    swap.start()
    go("c", ("cy", 0))
    swapped.wait_recv()
    go("b", "a", ("by", 0), ("az", 0))

    def prepare(vid):
        for tan in range(2):
            spread(plain.at[tan, vid], tall, 0)

            @pl.loop(0, count // group)
            def _(i):
                first = pl.multiple_of(i * group, group)
                row = pl.multiple_of(first * NP * KT, group * NP * KT)
                tiles = (
                    tall[pl.ds(row, group * NP * KT), :]
                    .astype(BF16)
                    .reshape(group, NP, KT, HEAD)
                )
                for pos in range(NP):
                    staged[vid * NP + pos, pl.ds(first, group), tan] = tiles[:, pos]

    @pl.when(leads)
    def _():
        for load in loads:
            load.wait()
        prepare(0)

    @pl.when(section == 0)
    def _():
        exchange(
            staged.at[0], lambda f: f, entering.at[0], me, x_send.at[0], x_recv.at[0]
        )

    def second_round(unit):
        exchange(
            staged.at[unit], flip, relay.at[unit], me, x_send.at[unit], x_recv.at[unit]
        )

    @pl.when(section == 2)
    def _():
        second_round(1)
        prepare(1)
        second_round(2)
        second_round(3)

    def relayed(unit):
        return pltpu.make_async_remote_copy(
            src_ref=relay.at[unit],
            dst_ref=entering.at[unit],
            send_sem=relay_send.at[unit],
            recv_sem=relay_recv.at[unit],
            device_id=(0, across),
            device_id_type=MESH,
        )

    def pass_to_first(unit):
        @pl.when(section == 2)
        def _():
            exchange_came(staged.at[unit], relay.at[unit], x_recv.at[unit])
            relayed(unit).start()

    for vid in range(VIDS):
        time_value = (index_ref[vid].astype(F32) + 0.5) * (math.pi / (2.0 * T_STEPS))
        mods_ref[vid], dmods_ref[vid] = timing(
            amp_ref[...], freq_ref[...], phase_ref[...], time_value
        )

    go("c", ("cy", 1), ("cy", 7))
    go("a", ("az", 1), ("az", 3))
    go(("cy", 0),)
    go("b", ("by", 1), ("by", 7))
    go("c", ("cy", 2), ("cy", 6))

    @pl.when(leads)
    def _():
        pl.semaphore_signal(
            turn_sem, inc=1, device_id=(section + 1, me), device_id_type=MESH
        )

    go("a", ("az", 2))
    go(("cy", 0), ("cx", 0), ("cy", 1), ("cy", 7))
    go(("az", 0), ("by", 0))
    go("c", ("cy", 3), ("cy", 5))
    go(("cy", 1), ("cx", 1), ("cy", 7), ("cx", 7), ("cy", 2), ("cy", 6))
    go("b", ("by", 2), ("by", 6))
    go("c", ("cy", 4))
    pass_to_first(1)
    go(("az", 1), ("az", 3), ("by", 1), ("by", 7), ("az", 2))
    go(("cy", 2), ("cx", 2), ("cy", 6), ("cx", 6), ("cy", 3), ("cy", 5), ("cy", 4))
    go("b", ("by", 3), ("by", 5))
    go(("az", 0), ("by", 0), ("az", 1), ("az", 3))
    go(("cy", 3), ("cx", 3), ("cy", 5), ("cx", 5), ("cy", 4), ("cx", 4))
    pass_to_first(2)

    go("b", ("by", 4))
    go(("by", 2), ("by", 6), ("az", 2), ("by", 1), ("by", 7), ("az", 0))
    pass_to_first(3)
    go(("by", 3), ("by", 5), ("az", 1), ("az", 3), ("by", 4), ("az", 2))
    def onward(unit, first=0, frames=F):
        return pltpu.make_async_remote_copy(
            src_ref=leaving.at[unit, pl.ds(first, frames)],
            dst_ref=entering.at[unit, pl.ds(first, frames)],
            send_sem=pass_send.at[unit],
            recv_sem=pass_recv.at[unit],
            device_id=(
                lax.rem(section + 1, sections),
                jnp.where(section == 1, across, me),
            ),
            device_id_type=MESH,
        )

    def take_in(unit):
        @pl.when(jnp.logical_and(section == 0, unit == 0))
        def _():
            exchange_came(staged.at[0], entering.at[0], x_recv.at[0])

        @pl.when(jnp.logical_and(section == 0, unit > 0))
        def _():
            relayed(unit).wait_recv()

        @pl.when(section > 0)
        def _():
            onward(unit).wait_recv()

        modulate(unit, entering, mods_ref, dmods_ref, tall, flat)

    @pl.when(first_half)
    def _():
        take_in(0)

    go(("by", 2), ("by", 6), ("az", 0), ("by", 3), ("by", 5))
    go(("az", 1), ("az", 3), ("by", 4), ("az", 2))
    go(*(("cx", by) for by in range(nz)))

    @pl.when(section == 1)
    def _():
        pl.semaphore_signal(turn_sem, inc=1, device_id=(0, me), device_id_type=MESH)

    def send_back(unit):
        exchange(
            leaving.at[unit],
            lambda f: f,
            returned.at[unit],
            slot,
            out_send.at[unit],
            out_recv.at[unit],
        )

    @pl.loop(0, UNITS)
    def _(unit):
        @pl.when(jnp.logical_or(jnp.logical_not(first_half), unit > 0))
        def _():
            take_in(unit)

        block_step(
            unit, entering, leaving, weights, gains_ref, mods_ref, dmods_ref, tall, flat, att
        )

        @pl.when(section < sections - 1)
        def _():
            for part in range(HOP_PARTS):
                onward(unit, part * (F // HOP_PARTS), F // HOP_PARTS).start()

        @pl.when(section > 1)
        def _():
            send_back(unit)

    @pl.when(section == 0)
    def _():
        pl.semaphore_wait(turn_sem, 1)

    @pl.when(section < 2)
    def _():
        @pl.loop(0, UNITS)
        def _(unit):
            send_back(unit)

    gather.finish()
    swap.wait_send()

    @pl.loop(0, VIDS)
    def _(vid):
        for pos in range(NP):
            unit = vid * NP + pos
            exchange_came(leaving.at[unit], returned.at[unit], out_recv.at[unit])

            @pl.loop(0, count // group)
            def _(i):
                first = pl.multiple_of(i * group, group)
                for tan in range(2):
                    tiles = returned[unit, pl.ds(first, group), tan].astype(F32)
                    for one in range(group):
                        row = pl.multiple_of(
                            ((tan * count + first + one) * NP + pos) * KT, KT
                        )
                        tall[pl.ds(row, KT), :] = tiles[one]

        for tan, result in enumerate((out_ref, tan_ref)):
            for k in range(KT):
                result[vid, :, k * HEAD : (k + 1) * HEAD] = tall[
                    pl.ds(tan * count * NP * KT + k, count * NP, stride=KT), :
                ].astype(BF16)

    @pl.loop(0, UNITS)
    def _(unit):
        exchange_sent(
            leaving.at[unit], returned.at[unit], out_send.at[unit], out_recv.at[unit]
        )

        @pl.when(section < sections - 1)
        def _():
            onward(unit).wait_send()

        @pl.when(
            jnp.logical_or(
                jnp.logical_and(section == 0, unit == 0),
                jnp.logical_and(section == 2, unit > 0),
            )
        )
        def _():
            exchange_sent(
                staged.at[unit], relay.at[unit], x_send.at[unit], x_recv.at[unit]
            )

        @pl.when(jnp.logical_and(section == 2, unit > 0))
        def _():
            relayed(unit).wait_send()


def shards(sizes, x_in, x_tan, t_index, w_qkv, w_out, qk_gain, mod_amp, mod_freq, mod_phase):
    nz, nx, ny = sizes
    count = nz * nx * ny
    sections = lax.axis_size("section")
    places = x_in.shape[2]
    waves = [wave.reshape(3, KT, HEAD) for wave in (mod_amp, mod_freq, mod_phase)]
    outside = pl.BlockSpec(memory_space=pl.ANY)
    inside = pl.BlockSpec(memory_space=pltpu.VMEM)
    result = jax.ShapeDtypeStruct((VIDS, places, D), BF16)
    units = (UNITS, F, 2, KT, HEAD)
    rings = 2 * (ny // 2) * (1 + 2 * nz) + 2 * (nz // 2) * (2 + ny) + nz
    dma = pltpu.SemaphoreType.DMA
    out, tan = pl.pallas_call(
        functools.partial(kernel, sizes, sections),
        out_shape=(result, result),
        in_specs=[outside] * 4
        + [inside, pl.BlockSpec(memory_space=pltpu.SMEM)]
        + [inside] * 3,
        out_specs=(inside, inside),
        scratch_shapes=[
            pltpu.VMEM((nz, nx, ny, ROWS_OUT, PACKED), BF16),
            pltpu.VMEM((VIDS, 3, KT, HEAD), F32),
            pltpu.VMEM((VIDS, 3, KT, HEAD), F32),
            pltpu.VMEM((2, VIDS, places, D), BF16),
            pltpu.VMEM(units, BF16),
            pltpu.VMEM(units, BF16),
            pltpu.VMEM(units, BF16),
            pltpu.VMEM(units, BF16),
            pltpu.VMEM(units, BF16),
            pltpu.VMEM((2 * places * KT, HEAD), F32),
            pltpu.VMEM((ROWS, D), BF16),
            pltpu.VMEM((ROWS, HD), BF16),
            dma((2,)),
            dma((3,)),
            dma,
            dma,
            dma((rings,)),
            dma((rings,)),
            dma((UNITS,)),
            dma((UNITS,)),
            dma((UNITS,)),
            dma((UNITS,)),
            dma((UNITS,)),
            dma((UNITS,)),
            dma((UNITS,)),
            dma((UNITS,)),
            pltpu.SemaphoreType.REGULAR,
        ],
        compiler_params=pltpu.CompilerParams(
            has_side_effects=True, vmem_limit_bytes=60 * 1024 * 1024
        ),
        name="blocks",
    )(
        x_in.reshape(VIDS, places, D),
        x_tan.reshape(VIDS, places, D),
        w_qkv[0],
        w_out[0],
        qk_gain[0],
        t_index,
        *waves,
    )
    return (out[None, :, None], tan[None, :, None])


def solution(mesh):
    count = mesh.shape["seq"]
    sizes = (count // 8, 2, 4)
    placed = (
        P(None, "seq", None, None),
        P(None, "seq", None, None),
        P(),
        P("section", "seq", None),
        P("section", "seq", None),
        P("section", None, None),
        P("section", None, None),
        P("section", None, None),
        P("section", None, None),
    )
    return jax.shard_map(
        functools.partial(shards, sizes),
        mesh=mesh,
        in_specs=placed,
        out_specs=(P("section", None, "seq", None, None), P("section", None, "seq", None, None)),
        check_vma=False,
    )
```

```python
import functools
import math

import jax
import jax.numpy as jnp
from jax import lax
from jax.experimental import pallas as pl
from jax.experimental.pallas import tpu as pltpu
from jax.sharding import PartitionSpec as P

HEADS = 8
HEAD = 128
T_STEPS = 1000
D = 2048
KT = D // HEAD
HD = HEADS * HEAD
F = 64
NP = 2
VIDS = 2
UNITS = VIDS * NP
ROWS = 2 * F
HALF = F
HOP_PARTS = 16
STRIDE = 27
EPS = 1e-06
F32 = jnp.float32
BF16 = jnp.bfloat16
MESH = pl.DeviceIdType.MESH
ROWS_OUT = 16
PACKED = 2 * 3 * HD + D
Z_LAST, Y_LAST = 2816, 5632


def timing(amp, freq, phase, time_value):
    angle = freq * time_value + phase
    return (amp * jnp.sin(angle), amp * freq * jnp.cos(angle))


class Gather:
    def __init__(self, sizes, section, coords, weights, send, recv):
        self.sizes, self.section, self.coords = sizes, section, coords
        self.weights, self.send, self.recv = weights, send, recv
        self.live = []
        self.sems = 0
        self.rings = {}

    def peer(self, axis, by):
        z, xl, y = self.coords
        nz, nx, ny = self.sizes
        if axis == "z":
            z = lax.rem(z + by + nz, nz)
        elif axis == "y":
            y = lax.rem(y + by + ny, ny)
        else:
            xl = nx - 1 - xl
        return (self.section, (z * nx + xl) * ny + y)

    def copy(self, ref, sem, peer):
        return pltpu.make_async_remote_copy(
            src_ref=ref,
            dst_ref=ref,
            send_sem=self.send.at[sem],
            recv_sem=self.recv.at[sem],
            device_id=peer,
            device_id_type=MESH,
        )

    def start(self, piece, begin, width, sem, peer):
        copy = self.copy(piece(pl.ds(begin, width)), sem, peer)
        copy.start()
        self.live.append(copy)

    def ring(self, axis, first, stop, fixed, single=False):
        size = self.sizes[0] if axis == "z" else self.sizes[2]
        me = self.coords[0] if axis == "z" else self.coords[2]
        last = size // 2
        first_sem = self.sems
        self.sems += 2 * last

        def arguments(way, step, index):
            z, y = (index, fixed) if axis == "z" else (fixed, index)
            begin, width = first, stop - first
            xl = self.coords[1] if single else slice(None)
            if step == last - 1:
                if single:
                    width = width // 2
                    begin = begin + way * width
                else:
                    xl = way

            def piece(columns):
                return self.weights.at[z, xl, y, :, columns]

            return piece, begin, width, first_sem + 2 * step + way, self.peer(axis, 1 - 2 * way)

        def at(way, step):
            return lax.rem(me - (1 - 2 * way) * step + size, size)

        for step in range(last):
            for way in (0, 1):
                self.start(*arguments(way, step, at(way, step)))
            yield
            for way in (0, 1):
                piece, begin, width, sem, peer = arguments(way, step, at(way, step + 1))
                self.copy(piece(pl.ds(begin, width)), sem, peer).wait_recv()

    def beside(self, fixed):
        sem = self.sems
        self.sems += 1
        _, xl, _ = self.coords
        nx = self.sizes[1]
        peer = self.peer("x", 0)
        self.start(
            lambda columns: self.weights.at[fixed, xl, :, :, columns],
            Y_LAST,
            PACKED - Y_LAST,
            sem,
            peer,
        )
        yield
        columns = pl.ds(Y_LAST, PACKED - Y_LAST)
        self.copy(self.weights.at[fixed, nx - 1 - xl, :, :, columns], sem, peer).wait_recv()

    def build(self):
        z, _, y = self.coords
        nz, _, ny = self.sizes
        rings = self.rings
        rings["a"] = self.ring("y", 0, Z_LAST, z)
        rings["b"] = self.ring("z", Z_LAST, Y_LAST, y)
        rings["c"] = self.ring("z", Y_LAST, PACKED, y, True)
        for by in range(ny):
            rings["az", by] = self.ring("z", 0, Z_LAST, lax.rem(y + by, ny))
        for by in range(nz):
            there = lax.rem(z + by, nz)
            rings["by", by] = self.ring("y", Z_LAST, Y_LAST, there)
            rings["cy", by] = self.ring("y", Y_LAST, PACKED, there, True)
            rings["cx", by] = self.beside(there)

    def go(self, *names):
        for name in names:
            next(self.rings[name], None)

    def finish(self):
        for copy in self.live:
            copy.wait_send()


def spread(source, tall, start):
    count = source.shape[0]
    for k in range(KT):
        tall[pl.ds(start + k, count, stride=KT), :] = source[:, k * HEAD : (k + 1) * HEAD].astype(
            F32
        )


def normalize(values, tangents, gain):
    inverse = lax.rsqrt(jnp.mean(values * values, axis=-1, keepdims=True) + EPS)
    cross = jnp.mean(values * tangents, axis=-1, keepdims=True)
    scaled = values * inverse
    return (
        (scaled * gain).astype(BF16),
        ((inverse * tangents - values * inverse**3 * cross) * gain).astype(BF16),
    )


def attend(q2, k2, v2, gains_ref):
    factor = 1.0 / math.sqrt(HEAD)
    qn, dqn = normalize(q2[:HALF], q2[HALF:], gains_ref[0:1, :])
    kn, dkn = normalize(k2[:HALF], k2[HALF:], gains_ref[1:2, :])
    value, dvalue = v2[:HALF].astype(BF16), v2[HALF:].astype(BF16)

    def against(rows, columns):
        return lax.dot_general(
            rows, columns, (((1,), (1,)), ((), ())), preferred_element_type=F32
        )

    scores = against(jnp.concatenate([qn, dqn], axis=0), kn)
    score = scores[:HALF] * factor
    dscore = (scores[HALF:] + against(qn, dkn)) * factor
    expo = jnp.exp(score)
    prob = expo * (1.0 / jnp.sum(expo, axis=-1, keepdims=True))
    growth = prob * dscore
    dprob = growth - prob * jnp.sum(growth, axis=-1, keepdims=True)
    prob, dprob = prob.astype(BF16), dprob.astype(BF16)
    mixed = jnp.dot(
        jnp.concatenate([prob, dprob], axis=0), value, preferred_element_type=F32
    )
    return mixed[:HALF], mixed[HALF:] + jnp.dot(prob, dvalue, preferred_element_type=F32)


def block_step(
    unit, entering, leaving, weights, gains_ref, mods_ref, dmods_ref, tall, flat, att
):
    group = 8
    vid = unit // NP

    @pl.loop(0, F // group, unroll=4)
    def _(i):
        first = pl.multiple_of(i * group, group)
        hidden = entering[unit, pl.ds(first, group), 0].astype(F32)
        tangent = entering[unit, pl.ds(first, group), 1].astype(F32)

        def mean(values):
            return jnp.sum(
                jnp.sum(values, axis=1, keepdims=True), axis=2, keepdims=True
            ) * (1.0 / D)

        inverse = lax.rsqrt(mean(hidden * hidden) + EPS)
        cross = mean(hidden * tangent)
        normed = hidden * inverse
        dnormed = inverse * tangent - hidden * inverse**3 * cross
        scale = 1.0 + mods_ref[vid, 1][None]
        modulated = normed * scale + mods_ref[vid, 0][None]
        dmodulated = dnormed * scale + normed * dmods_ref[vid, 1][None] + dmods_ref[vid, 0][None]
        row = pl.multiple_of(first * KT, group * KT)
        tall[pl.ds(row, group * KT), :] = modulated.reshape(group * KT, HEAD)
        tall[pl.ds(row + HALF * KT, group * KT), :] = dmodulated.reshape(group * KT, HEAD)

    for k in range(KT):
        flat[:, k * HEAD : (k + 1) * HEAD] = tall[pl.ds(k, ROWS, stride=KT), :].astype(BF16)

    def third(number, pair):
        column = number * HD + pair * 2 * HEAD
        halves = [
            weights[
                :, :, :, :, column + lower * 3 * HD : column + lower * 3 * HD + 2 * HEAD
            ].reshape(F, 1, ROWS_OUT, 2 * HEAD)
            for lower in range(2)
        ]
        matrix = jnp.concatenate(halves, axis=1).reshape(D, 2 * HEAD)
        return jnp.dot(flat[...], matrix, preferred_element_type=F32)

    ahead = [third(number, 0) for number in range(3)]
    for pair in range(HEADS // 2):
        q2, k2, v2 = ahead
        if pair + 1 < HEADS // 2:
            ahead = [third(number, pair + 1) for number in range(3)]
        for one in range(2):
            lanes = slice(one * HEAD, (one + 1) * HEAD)
            output, doutput = attend(q2[:, lanes], k2[:, lanes], v2[:, lanes], gains_ref)
            column = (pair * 2 + one) * HEAD
            att[:HALF, column : column + HEAD] = output.astype(BF16)
            att[HALF:, column : column + HEAD] = doutput.astype(BF16)

    for n in range(KT // 2):
        column = 2 * 3 * HD + n * 2 * HEAD
        matrix = weights[:, :, :, :, column : column + 2 * HEAD].reshape(HD, 2 * HEAD)
        y = jnp.dot(att[...], matrix, preferred_element_type=F32)
        tall[pl.ds(2 * n, ROWS, stride=KT), :] = y[:, :HEAD]
        tall[pl.ds(2 * n + 1, ROWS, stride=KT), :] = y[:, HEAD:]

    @pl.loop(0, F // group, unroll=4)
    def _(i):
        first = pl.multiple_of(i * group, group)
        row = pl.multiple_of(first * KT, group * KT)
        y = tall[pl.ds(row, group * KT), :].reshape(group, KT, HEAD)
        dy = tall[pl.ds(row + HALF * KT, group * KT), :].reshape(group, KT, HEAD)
        hidden = entering[unit, pl.ds(first, group), 0].astype(F32)
        tangent = entering[unit, pl.ds(first, group), 1].astype(F32)
        gate = mods_ref[vid, 2][None]
        dgate = dmods_ref[vid, 2][None]
        leaving[unit, pl.ds(first, group), 0] = (hidden + gate * y).astype(BF16)
        leaving[unit, pl.ds(first, group), 1] = (tangent + dgate * y + gate * dy).astype(BF16)


def kernel(
    sizes,
    sections,
    x_ref,
    t_ref,
    wqkv_ref,
    wout_ref,
    gains_ref,
    index_ref,
    amp_ref,
    freq_ref,
    phase_ref,
    out_ref,
    tan_ref,
    weights,
    mods_ref,
    dmods_ref,
    plain,
    staged,
    relay,
    entering,
    leaving,
    returned,
    tall,
    flat,
    att,
    load_sem,
    own_sem,
    swap_send,
    swap_recv,
    ring_send,
    ring_recv,
    x_send,
    x_recv,
    relay_send,
    relay_recv,
    pass_send,
    pass_recv,
    out_send,
    out_recv,
    turn_sem,
):
    nz, nx, ny = sizes
    count = nz * nx * ny
    section = lax.axis_index("section")
    me = lax.axis_index("seq")
    coords = (me // (nx * ny), (me // ny) % nx, me % ny)
    z, xl, y = coords
    first_half = section < 2

    def flip(index):
        return index + ny - 2 * ny * ((index // ny) % nx)

    across = flip(me)
    slot = jnp.where(first_half, me, across)
    neighbour = (section, lax.rem(me + 1, count))
    group = 8

    def exchange(source, row_of, target, place, send, recv):
        pltpu.make_async_copy(source.at[row_of(me)], target.at[place], recv).start()

        @pl.loop(1, count, unroll=21)
        def _(by):
            to = lax.rem(me + by * STRIDE, count)
            pltpu.make_async_remote_copy(
                src_ref=source.at[row_of(to)],
                dst_ref=target.at[place],
                send_sem=send,
                recv_sem=recv,
                device_id=(section, to),
                device_id_type=MESH,
            ).start()

    def exchange_came(source, target, recv):
        pltpu.make_async_copy(source, target, recv).wait()

    def exchange_sent(source, target, send, recv):
        pltpu.make_async_remote_copy(
            src_ref=source.at[pl.ds(0, count - 1)],
            dst_ref=target.at[pl.ds(0, count - 1)],
            send_sem=send,
            recv_sem=recv,
            device_id=neighbour,
            device_id_type=MESH,
        ).wait_send()

    leads = lax.rem(section, 2) == 0
    loads = [
        pltpu.make_async_copy(ref, plain.at[tan], load_sem.at[tan])
        for tan, ref in enumerate((x_ref, t_ref))
    ]

    @pl.when(leads)
    def _():
        for load in loads:
            load.start()

    own = []
    for part, (ref, first, width) in enumerate(
        (
            (wqkv_ref.at[pl.ds(0, ROWS_OUT)], 0, 3 * HD),
            (wqkv_ref.at[pl.ds(ROWS_OUT, ROWS_OUT)], 3 * HD, 3 * HD),
            (wout_ref, 6 * HD, D),
        )
    ):
        home = weights.at[z, xl, y, :, pl.ds(first, width)]
        own.append(pltpu.make_async_copy(ref, home, own_sem.at[part]))
        own[-1].start()
    for copy in own:
        copy.wait()

    @pl.when(jnp.logical_not(leads))
    def _():
        pl.semaphore_wait(turn_sem, 1)

    gather = Gather(sizes, section, coords, weights, ring_send, ring_recv)
    gather.build()
    go = gather.go
    mine = weights.at[z, xl, y, :, pl.ds(0, Y_LAST)]
    swap = pltpu.make_async_remote_copy(
        src_ref=mine,
        dst_ref=mine,
        send_sem=swap_send,
        recv_sem=swap_recv,
        device_id=(section, across),
        device_id_type=MESH,
    )
    theirs = weights.at[z, nx - 1 - xl, y, :, pl.ds(0, Y_LAST)]
    swapped = pltpu.make_async_remote_copy(
        src_ref=theirs,
        dst_ref=theirs,
        send_sem=swap_send,
        recv_sem=swap_recv,
        device_id=(section, across),
        device_id_type=MESH,
    )
    swap.start()
    go("c", ("cy", 0))

    def prepare(vid):
        for tan in range(2):
            spread(plain.at[tan, vid], tall, 0)

            @pl.loop(0, count // group)
            def _(i):
                first = pl.multiple_of(i * group, group)
                row = pl.multiple_of(first * NP * KT, group * NP * KT)
                tiles = (
                    tall[pl.ds(row, group * NP * KT), :]
                    .astype(BF16)
                    .reshape(group, NP, KT, HEAD)
                )
                for pos in range(NP):
                    staged[vid * NP + pos, pl.ds(first, group), tan] = tiles[:, pos]

    @pl.when(leads)
    def _():
        for load in loads:
            load.wait()
        prepare(0)

    @pl.when(section == 0)
    def _():
        exchange(
            staged.at[0], lambda f: f, entering.at[0], me, x_send.at[0], x_recv.at[0]
        )

    def second_round(unit):
        exchange(
            staged.at[unit], flip, relay.at[unit], me, x_send.at[unit], x_recv.at[unit]
        )

    @pl.when(section == 2)
    def _():
        second_round(1)
        prepare(1)
        second_round(2)
        second_round(3)

    def relayed(unit):
        return pltpu.make_async_remote_copy(
            src_ref=relay.at[unit],
            dst_ref=entering.at[unit],
            send_sem=relay_send.at[unit],
            recv_sem=relay_recv.at[unit],
            device_id=(0, across),
            device_id_type=MESH,
        )

    def pass_to_first(unit):
        @pl.when(section == 2)
        def _():
            exchange_came(staged.at[unit], relay.at[unit], x_recv.at[unit])
            relayed(unit).start()

    for vid in range(VIDS):
        time_value = (index_ref[vid].astype(F32) + 0.5) * (math.pi / (2.0 * T_STEPS))
        mods_ref[vid], dmods_ref[vid] = timing(
            amp_ref[...], freq_ref[...], phase_ref[...], time_value
        )

    swapped.wait_recv()
    go("b", "a", ("by", 0), ("az", 0))
    go("c", ("cy", 1), ("cy", 7))
    go("a", ("az", 1), ("az", 3))
    go(("cy", 0),)
    go("b", ("by", 1), ("by", 7))
    go("c", ("cy", 2), ("cy", 6))

    @pl.when(leads)
    def _():
        pl.semaphore_signal(
            turn_sem, inc=1, device_id=(section + 1, me), device_id_type=MESH
        )

    go("a", ("az", 2))
    go(("cy", 0), ("cx", 0), ("cy", 1), ("cy", 7))
    go(("az", 0), ("by", 0))
    go("c", ("cy", 3), ("cy", 5))
    go(("cy", 1), ("cx", 1), ("cy", 7), ("cx", 7), ("cy", 2), ("cy", 6))
    go("b", ("by", 2), ("by", 6))
    go("c", ("cy", 4))
    pass_to_first(1)
    go(("az", 1), ("az", 3), ("by", 1), ("by", 7), ("az", 2))
    go(("cy", 2), ("cx", 2), ("cy", 6), ("cx", 6), ("cy", 3), ("cy", 5), ("cy", 4))
    go("b", ("by", 3), ("by", 5))
    go(("az", 0), ("by", 0), ("az", 1), ("az", 3))
    go(("cy", 3), ("cx", 3), ("cy", 5), ("cx", 5), ("cy", 4), ("cx", 4))
    pass_to_first(2)

    go("b", ("by", 4))
    go(("by", 2), ("by", 6), ("az", 2), ("by", 1), ("by", 7), ("az", 0))
    pass_to_first(3)
    go(("by", 3), ("by", 5), ("az", 1), ("az", 3), ("by", 4), ("az", 2))
    go(("by", 2), ("by", 6), ("az", 0), ("by", 3), ("by", 5))
    go(("az", 1), ("az", 3), ("by", 4), ("az", 2))
    go(*(("cx", by) for by in range(nz)))

    @pl.when(section == 1)
    def _():
        pl.semaphore_signal(turn_sem, inc=1, device_id=(0, me), device_id_type=MESH)

    def onward(unit, first=0, frames=F):
        return pltpu.make_async_remote_copy(
            src_ref=leaving.at[unit, pl.ds(first, frames)],
            dst_ref=entering.at[unit, pl.ds(first, frames)],
            send_sem=pass_send.at[unit],
            recv_sem=pass_recv.at[unit],
            device_id=(
                lax.rem(section + 1, sections),
                jnp.where(section == 1, across, me),
            ),
            device_id_type=MESH,
        )

    def send_back(unit):
        exchange(
            leaving.at[unit],
            lambda f: f,
            returned.at[unit],
            slot,
            out_send.at[unit],
            out_recv.at[unit],
        )

    @pl.loop(0, UNITS)
    def _(unit):
        @pl.when(jnp.logical_and(section == 0, unit == 0))
        def _():
            exchange_came(staged.at[0], entering.at[0], x_recv.at[0])

        @pl.when(jnp.logical_and(section == 0, unit > 0))
        def _():
            relayed(unit).wait_recv()

        @pl.when(section > 0)
        def _():
            onward(unit).wait_recv()

        block_step(
            unit, entering, leaving, weights, gains_ref, mods_ref, dmods_ref, tall, flat, att
        )

        @pl.when(section < sections - 1)
        def _():
            for part in range(HOP_PARTS):
                onward(unit, part * (F // HOP_PARTS), F // HOP_PARTS).start()

        @pl.when(section > 1)
        def _():
            send_back(unit)

    @pl.when(section == 0)
    def _():
        pl.semaphore_wait(turn_sem, 1)

    @pl.when(section < 2)
    def _():
        @pl.loop(0, UNITS)
        def _(unit):
            send_back(unit)

    gather.finish()
    swap.wait_send()

    @pl.loop(0, VIDS)
    def _(vid):
        for pos in range(NP):
            unit = vid * NP + pos
            exchange_came(leaving.at[unit], returned.at[unit], out_recv.at[unit])

            @pl.loop(0, count // group)
            def _(i):
                first = pl.multiple_of(i * group, group)
                for tan in range(2):
                    tiles = returned[unit, pl.ds(first, group), tan].astype(F32)
                    for one in range(group):
                        row = pl.multiple_of(
                            ((tan * count + first + one) * NP + pos) * KT, KT
                        )
                        tall[pl.ds(row, KT), :] = tiles[one]

        for tan, result in enumerate((out_ref, tan_ref)):
            for k in range(KT):
                result[vid, :, k * HEAD : (k + 1) * HEAD] = tall[
                    pl.ds(tan * count * NP * KT + k, count * NP, stride=KT), :
                ].astype(BF16)

    @pl.loop(0, UNITS)
    def _(unit):
        exchange_sent(
            leaving.at[unit], returned.at[unit], out_send.at[unit], out_recv.at[unit]
        )

        @pl.when(section < sections - 1)
        def _():
            onward(unit).wait_send()

        @pl.when(
            jnp.logical_or(
                jnp.logical_and(section == 0, unit == 0),
                jnp.logical_and(section == 2, unit > 0),
            )
        )
        def _():
            exchange_sent(
                staged.at[unit], relay.at[unit], x_send.at[unit], x_recv.at[unit]
            )

        @pl.when(jnp.logical_and(section == 2, unit > 0))
        def _():
            relayed(unit).wait_send()


def shards(sizes, x_in, x_tan, t_index, w_qkv, w_out, qk_gain, mod_amp, mod_freq, mod_phase):
    nz, nx, ny = sizes
    count = nz * nx * ny
    sections = lax.axis_size("section")
    places = x_in.shape[2]
    waves = [wave.reshape(3, KT, HEAD) for wave in (mod_amp, mod_freq, mod_phase)]
    outside = pl.BlockSpec(memory_space=pl.ANY)
    inside = pl.BlockSpec(memory_space=pltpu.VMEM)
    result = jax.ShapeDtypeStruct((VIDS, places, D), BF16)
    units = (UNITS, F, 2, KT, HEAD)
    rings = 2 * (ny // 2) * (1 + 2 * nz) + 2 * (nz // 2) * (2 + ny) + nz
    dma = pltpu.SemaphoreType.DMA
    out, tan = pl.pallas_call(
        functools.partial(kernel, sizes, sections),
        out_shape=(result, result),
        in_specs=[outside] * 4
        + [inside, pl.BlockSpec(memory_space=pltpu.SMEM)]
        + [inside] * 3,
        out_specs=(inside, inside),
        scratch_shapes=[
            pltpu.VMEM((nz, nx, ny, ROWS_OUT, PACKED), BF16),
            pltpu.VMEM((VIDS, 3, KT, HEAD), F32),
            pltpu.VMEM((VIDS, 3, KT, HEAD), F32),
            pltpu.VMEM((2, VIDS, places, D), BF16),
            pltpu.VMEM(units, BF16),
            pltpu.VMEM(units, BF16),
            pltpu.VMEM(units, BF16),
            pltpu.VMEM(units, BF16),
            pltpu.VMEM(units, BF16),
            pltpu.VMEM((2 * places * KT, HEAD), F32),
            pltpu.VMEM((ROWS, D), BF16),
            pltpu.VMEM((ROWS, HD), BF16),
            dma((2,)),
            dma((3,)),
            dma,
            dma,
            dma((rings,)),
            dma((rings,)),
            dma((UNITS,)),
            dma((UNITS,)),
            dma((UNITS,)),
            dma((UNITS,)),
            dma((UNITS,)),
            dma((UNITS,)),
            dma((UNITS,)),
            dma((UNITS,)),
            pltpu.SemaphoreType.REGULAR,
        ],
        compiler_params=pltpu.CompilerParams(
            has_side_effects=True, vmem_limit_bytes=60 * 1024 * 1024
        ),
        name="blocks",
    )(
        x_in.reshape(VIDS, places, D),
        x_tan.reshape(VIDS, places, D),
        w_qkv[0],
        w_out[0],
        qk_gain[0],
        t_index,
        *waves,
    )
    return (out[None, :, None], tan[None, :, None])


def solution(mesh):
    count = mesh.shape["seq"]
    sizes = (count // 8, 2, 4)
    placed = (
        P(None, "seq", None, None),
        P(None, "seq", None, None),
        P(),
        P("section", "seq", None),
        P("section", "seq", None),
        P("section", None, None),
        P("section", None, None),
        P("section", None, None),
        P("section", None, None),
    )
    return jax.shard_map(
        functools.partial(shards, sizes),
        mesh=mesh,
        in_specs=placed,
        out_specs=(P("section", None, "seq", None, None), P("section", None, "seq", None, None)),
        check_vma=False,
    )
```

```python
import functools
import math

import jax
import jax.numpy as jnp
from jax import lax
from jax.experimental import pallas as pl
from jax.experimental.pallas import tpu as pltpu
from jax.sharding import PartitionSpec as P

HEADS = 8
HEAD = 128
T_STEPS = 1000
D = 2048
KT = D // HEAD
HD = HEADS * HEAD
F = 64
NP = 2
VIDS = 2
UNITS = VIDS * NP
ROWS = 2 * F
HALF = F
HOP_PARTS = 4
STRIDE = 27
EPS = 1e-06
F32 = jnp.float32
BF16 = jnp.bfloat16
MESH = pl.DeviceIdType.MESH
ROWS_OUT = 16
PACKED = 2 * 3 * HD + D
Z_LAST, Y_LAST = 2816, 5632


def timing(amp, freq, phase, time_value):
    angle = freq * time_value + phase
    return (amp * jnp.sin(angle), amp * freq * jnp.cos(angle))


class Gather:
    def __init__(self, sizes, section, coords, weights, send, recv):
        self.sizes, self.section, self.coords = sizes, section, coords
        self.weights, self.send, self.recv = weights, send, recv
        self.live = []
        self.sems = 0
        self.rings = {}

    def peer(self, axis, by):
        z, xl, y = self.coords
        nz, nx, ny = self.sizes
        if axis == "z":
            z = lax.rem(z + by + nz, nz)
        elif axis == "y":
            y = lax.rem(y + by + ny, ny)
        else:
            xl = nx - 1 - xl
        return (self.section, (z * nx + xl) * ny + y)

    def copy(self, ref, sem, peer):
        return pltpu.make_async_remote_copy(
            src_ref=ref,
            dst_ref=ref,
            send_sem=self.send.at[sem],
            recv_sem=self.recv.at[sem],
            device_id=peer,
            device_id_type=MESH,
        )

    def start(self, piece, begin, width, sem, peer):
        copy = self.copy(piece(pl.ds(begin, width)), sem, peer)
        copy.start()
        self.live.append(copy)

    def ring(self, axis, first, stop, fixed, single=False):
        size = self.sizes[0] if axis == "z" else self.sizes[2]
        me = self.coords[0] if axis == "z" else self.coords[2]
        last = size // 2
        first_sem = self.sems
        self.sems += 2 * last

        def arguments(way, step, index):
            z, y = (index, fixed) if axis == "z" else (fixed, index)
            begin, width = first, stop - first
            xl = self.coords[1] if single else slice(None)
            if step == last - 1:
                if single:
                    width = width // 2
                    begin = begin + way * width
                else:
                    xl = way

            def piece(columns):
                return self.weights.at[z, xl, y, :, columns]

            return piece, begin, width, first_sem + 2 * step + way, self.peer(axis, 1 - 2 * way)

        def at(way, step):
            return lax.rem(me - (1 - 2 * way) * step + size, size)

        for step in range(last):
            for way in (0, 1):
                self.start(*arguments(way, step, at(way, step)))
            yield
            for way in (0, 1):
                piece, begin, width, sem, peer = arguments(way, step, at(way, step + 1))
                self.copy(piece(pl.ds(begin, width)), sem, peer).wait_recv()

    def beside(self, fixed):
        sem = self.sems
        self.sems += 1
        _, xl, _ = self.coords
        nx = self.sizes[1]
        peer = self.peer("x", 0)
        self.start(
            lambda columns: self.weights.at[fixed, xl, :, :, columns],
            Y_LAST,
            PACKED - Y_LAST,
            sem,
            peer,
        )
        yield
        columns = pl.ds(Y_LAST, PACKED - Y_LAST)
        self.copy(self.weights.at[fixed, nx - 1 - xl, :, :, columns], sem, peer).wait_recv()

    def build(self):
        z, _, y = self.coords
        nz, _, ny = self.sizes
        rings = self.rings
        rings["a"] = self.ring("y", 0, Z_LAST, z)
        rings["b"] = self.ring("z", Z_LAST, Y_LAST, y)
        rings["c"] = self.ring("z", Y_LAST, PACKED, y, True)
        for by in range(ny):
            rings["az", by] = self.ring("z", 0, Z_LAST, lax.rem(y + by, ny))
        for by in range(nz):
            there = lax.rem(z + by, nz)
            rings["by", by] = self.ring("y", Z_LAST, Y_LAST, there)
            rings["cy", by] = self.ring("y", Y_LAST, PACKED, there, True)
            rings["cx", by] = self.beside(there)

    def go(self, *names):
        for name in names:
            next(self.rings[name], None)

    def finish(self):
        for copy in self.live:
            copy.wait_send()


def spread(source, tall, start):
    count = source.shape[0]
    for k in range(KT):
        tall[pl.ds(start + k, count, stride=KT), :] = source[:, k * HEAD : (k + 1) * HEAD].astype(
            F32
        )


def normalize(values, tangents, gain):
    inverse = lax.rsqrt(jnp.mean(values * values, axis=-1, keepdims=True) + EPS)
    cross = jnp.mean(values * tangents, axis=-1, keepdims=True)
    scaled = values * inverse
    return (
        (scaled * gain).astype(BF16),
        ((inverse * tangents - values * inverse**3 * cross) * gain).astype(BF16),
    )


def attend(q2, k2, v2, gains_ref):
    factor = 1.0 / math.sqrt(HEAD)
    qn, dqn = normalize(q2[:HALF], q2[HALF:], gains_ref[0:1, :])
    kn, dkn = normalize(k2[:HALF], k2[HALF:], gains_ref[1:2, :])
    value, dvalue = v2[:HALF].astype(BF16), v2[HALF:].astype(BF16)

    def against(rows, columns):
        return lax.dot_general(
            rows, columns, (((1,), (1,)), ((), ())), preferred_element_type=F32
        )

    scores = against(jnp.concatenate([qn, dqn], axis=0), kn)
    score = scores[:HALF] * factor
    dscore = (scores[HALF:] + against(qn, dkn)) * factor
    expo = jnp.exp(score)
    prob = expo * (1.0 / jnp.sum(expo, axis=-1, keepdims=True))
    growth = prob * dscore
    dprob = growth - prob * jnp.sum(growth, axis=-1, keepdims=True)
    prob, dprob = prob.astype(BF16), dprob.astype(BF16)
    mixed = jnp.dot(
        jnp.concatenate([prob, dprob], axis=0), value, preferred_element_type=F32
    )
    return mixed[:HALF], mixed[HALF:] + jnp.dot(prob, dvalue, preferred_element_type=F32)


def block_step(
    unit, entering, leaving, weights, gains_ref, mods_ref, dmods_ref, tall, flat, att
):
    group = 8
    vid, pos = unit // NP, unit % NP

    @pl.loop(0, F // group, unroll=4)
    def _(i):
        first = pl.multiple_of(i * group, group)
        hidden = entering[unit, pl.ds(first, group), 0].astype(F32)
        tangent = entering[unit, pl.ds(first, group), 1].astype(F32)

        def mean(values):
            return jnp.sum(
                jnp.sum(values, axis=1, keepdims=True), axis=2, keepdims=True
            ) * (1.0 / D)

        inverse = lax.rsqrt(mean(hidden * hidden) + EPS)
        cross = mean(hidden * tangent)
        normed = hidden * inverse
        dnormed = inverse * tangent - hidden * inverse**3 * cross
        scale = 1.0 + mods_ref[vid, 1][None]
        modulated = normed * scale + mods_ref[vid, 0][None]
        dmodulated = dnormed * scale + normed * dmods_ref[vid, 1][None] + dmods_ref[vid, 0][None]
        row = pl.multiple_of(first * KT, group * KT)
        tall[pl.ds(row, group * KT), :] = modulated.reshape(group * KT, HEAD)
        tall[pl.ds(row + HALF * KT, group * KT), :] = dmodulated.reshape(group * KT, HEAD)

    for k in range(KT):
        flat[:, k * HEAD : (k + 1) * HEAD] = tall[pl.ds(k, ROWS, stride=KT), :].astype(BF16)

    def third(number, pair):
        column = number * HD + pair * 2 * HEAD
        halves = [
            weights[
                :, :, :, :, column + lower * 3 * HD : column + lower * 3 * HD + 2 * HEAD
            ].reshape(F, 1, ROWS_OUT, 2 * HEAD)
            for lower in range(2)
        ]
        matrix = jnp.concatenate(halves, axis=1).reshape(D, 2 * HEAD)
        return jnp.dot(flat[...], matrix, preferred_element_type=F32)

    ahead = [third(number, 0) for number in range(3)]
    for pair in range(HEADS // 2):
        q2, k2, v2 = ahead
        if pair + 1 < HEADS // 2:
            ahead = [third(number, pair + 1) for number in range(3)]
        for one in range(2):
            lanes = slice(one * HEAD, (one + 1) * HEAD)
            output, doutput = attend(q2[:, lanes], k2[:, lanes], v2[:, lanes], gains_ref)
            column = (pair * 2 + one) * HEAD
            att[:HALF, column : column + HEAD] = output.astype(BF16)
            att[HALF:, column : column + HEAD] = doutput.astype(BF16)

    for n in range(KT // 2):
        column = 2 * 3 * HD + n * 2 * HEAD
        matrix = weights[:, :, :, :, column : column + 2 * HEAD].reshape(HD, 2 * HEAD)
        y = jnp.dot(att[...], matrix, preferred_element_type=F32)
        tall[pl.ds(2 * n, ROWS, stride=KT), :] = y[:, :HEAD]
        tall[pl.ds(2 * n + 1, ROWS, stride=KT), :] = y[:, HEAD:]

    @pl.loop(0, F // group, unroll=4)
    def _(i):
        first = pl.multiple_of(i * group, group)
        row = pl.multiple_of(first * KT, group * KT)
        y = tall[pl.ds(row, group * KT), :].reshape(group, KT, HEAD)
        dy = tall[pl.ds(row + HALF * KT, group * KT), :].reshape(group, KT, HEAD)
        hidden = entering[unit, pl.ds(first, group), 0].astype(F32)
        tangent = entering[unit, pl.ds(first, group), 1].astype(F32)
        gate = mods_ref[vid, 2][None]
        dgate = dmods_ref[vid, 2][None]
        leaving[vid, pl.ds(first, group), pos, 0] = (hidden + gate * y).astype(BF16)
        leaving[vid, pl.ds(first, group), pos, 1] = (tangent + dgate * y + gate * dy).astype(BF16)


def kernel(
    sizes,
    sections,
    x_ref,
    t_ref,
    wqkv_ref,
    wout_ref,
    gains_ref,
    index_ref,
    amp_ref,
    freq_ref,
    phase_ref,
    out_ref,
    tan_ref,
    weights,
    mods_ref,
    dmods_ref,
    plain,
    staged,
    relay,
    entering,
    leaving,
    returned,
    tall,
    flat,
    att,
    load_sem,
    own_sem,
    swap_send,
    swap_recv,
    ring_send,
    ring_recv,
    x_send,
    x_recv,
    relay_send,
    relay_recv,
    pass_send,
    pass_recv,
    out_send,
    out_recv,
    turn_sem,
):
    nz, nx, ny = sizes
    count = nz * nx * ny
    section = lax.axis_index("section")
    me = lax.axis_index("seq")
    coords = (me // (nx * ny), (me // ny) % nx, me % ny)
    z, xl, y = coords
    first_half = section < 2

    def flip(index):
        return index + ny - 2 * ny * ((index // ny) % nx)

    across = flip(me)
    slot = jnp.where(first_half, me, across)
    neighbour = (section, lax.rem(me + 1, count))
    group = 8

    def exchange(source, row_of, target, place, send, recv):
        pltpu.make_async_copy(source.at[row_of(me)], target.at[place], recv).start()

        @pl.loop(1, count, unroll=21)
        def _(by):
            to = lax.rem(me + by * STRIDE, count)
            pltpu.make_async_remote_copy(
                src_ref=source.at[row_of(to)],
                dst_ref=target.at[place],
                send_sem=send,
                recv_sem=recv,
                device_id=(section, to),
                device_id_type=MESH,
            ).start()

    def exchange_came(source, target, recv):
        pltpu.make_async_copy(source, target, recv).wait()

    def exchange_sent(source, target, send, recv):
        pltpu.make_async_remote_copy(
            src_ref=source.at[pl.ds(0, count - 1)],
            dst_ref=target.at[pl.ds(0, count - 1)],
            send_sem=send,
            recv_sem=recv,
            device_id=neighbour,
            device_id_type=MESH,
        ).wait_send()

    leads = lax.rem(section, 2) == 0
    loads = [
        pltpu.make_async_copy(ref, plain.at[tan], load_sem.at[tan])
        for tan, ref in enumerate((x_ref, t_ref))
    ]

    @pl.when(leads)
    def _():
        for load in loads:
            load.start()

    own = []
    for part, (ref, first, width) in enumerate(
        (
            (wqkv_ref.at[pl.ds(0, ROWS_OUT)], 0, 3 * HD),
            (wqkv_ref.at[pl.ds(ROWS_OUT, ROWS_OUT)], 3 * HD, 3 * HD),
            (wout_ref, 6 * HD, D),
        )
    ):
        home = weights.at[z, xl, y, :, pl.ds(first, width)]
        own.append(pltpu.make_async_copy(ref, home, own_sem.at[part]))
        own[-1].start()
    for copy in own:
        copy.wait()

    @pl.when(jnp.logical_not(leads))
    def _():
        pl.semaphore_wait(turn_sem, 1)

    gather = Gather(sizes, section, coords, weights, ring_send, ring_recv)
    gather.build()
    go = gather.go
    mine = weights.at[z, xl, y, :, pl.ds(0, Y_LAST)]
    swap = pltpu.make_async_remote_copy(
        src_ref=mine,
        dst_ref=mine,
        send_sem=swap_send,
        recv_sem=swap_recv,
        device_id=(section, across),
        device_id_type=MESH,
    )
    theirs = weights.at[z, nx - 1 - xl, y, :, pl.ds(0, Y_LAST)]
    swapped = pltpu.make_async_remote_copy(
        src_ref=theirs,
        dst_ref=theirs,
        send_sem=swap_send,
        recv_sem=swap_recv,
        device_id=(section, across),
        device_id_type=MESH,
    )
    swap.start()
    go("c", ("cy", 0))

    def prepare(vid):
        for tan in range(2):
            spread(plain.at[tan, vid], tall, 0)

            @pl.loop(0, count // group)
            def _(i):
                first = pl.multiple_of(i * group, group)
                row = pl.multiple_of(first * NP * KT, group * NP * KT)
                tiles = (
                    tall[pl.ds(row, group * NP * KT), :]
                    .astype(BF16)
                    .reshape(group, NP, KT, HEAD)
                )
                for pos in range(NP):
                    staged[vid * NP + pos, pl.ds(first, group), tan] = tiles[:, pos]

    @pl.when(leads)
    def _():
        for load in loads:
            load.wait()
        prepare(0)

    @pl.when(section == 0)
    def _():
        exchange(
            staged.at[0], lambda f: f, entering.at[0], me, x_send.at[0], x_recv.at[0]
        )

    def second_round(unit):
        exchange(
            staged.at[unit], flip, relay.at[unit], me, x_send.at[unit], x_recv.at[unit]
        )

    @pl.when(section == 2)
    def _():
        second_round(1)
        prepare(1)
        second_round(2)
        second_round(3)

    def relayed(unit):
        return pltpu.make_async_remote_copy(
            src_ref=relay.at[unit],
            dst_ref=entering.at[unit],
            send_sem=relay_send.at[unit],
            recv_sem=relay_recv.at[unit],
            device_id=(0, across),
            device_id_type=MESH,
        )

    def pass_to_first(unit):
        @pl.when(section == 2)
        def _():
            exchange_came(staged.at[unit], relay.at[unit], x_recv.at[unit])
            relayed(unit).start()

    for vid in range(VIDS):
        time_value = (index_ref[vid].astype(F32) + 0.5) * (math.pi / (2.0 * T_STEPS))
        mods_ref[vid], dmods_ref[vid] = timing(
            amp_ref[...], freq_ref[...], phase_ref[...], time_value
        )

    swapped.wait_recv()
    go("b", "a", ("by", 0), ("az", 0))
    go("c", ("cy", 1), ("cy", 7))
    go("a", ("az", 1), ("az", 3))
    go(("cy", 0),)
    go("b", ("by", 1), ("by", 7))
    go("c", ("cy", 2), ("cy", 6))

    @pl.when(leads)
    def _():
        pl.semaphore_signal(
            turn_sem, inc=1, device_id=(section + 1, me), device_id_type=MESH
        )

    go("a", ("az", 2))
    go(("cy", 0), ("cx", 0), ("cy", 1), ("cy", 7))
    go(("az", 0), ("by", 0))
    go("c", ("cy", 3), ("cy", 5))
    go(("cy", 1), ("cx", 1), ("cy", 7), ("cx", 7), ("cy", 2), ("cy", 6))
    go("b", ("by", 2), ("by", 6))
    go("c", ("cy", 4))
    pass_to_first(1)
    go(("az", 1), ("az", 3), ("by", 1), ("by", 7), ("az", 2))
    go(("cy", 2), ("cx", 2), ("cy", 6), ("cx", 6), ("cy", 3), ("cy", 5), ("cy", 4))
    go("b", ("by", 3), ("by", 5))
    go(("az", 0), ("by", 0), ("az", 1), ("az", 3))
    go(("cy", 3), ("cx", 3), ("cy", 5), ("cx", 5), ("cy", 4), ("cx", 4))
    pass_to_first(2)

    go("b", ("by", 4))
    go(("by", 2), ("by", 6), ("az", 2), ("by", 1), ("by", 7), ("az", 0))
    pass_to_first(3)
    go(("by", 3), ("by", 5), ("az", 1), ("az", 3), ("by", 4), ("az", 2))
    go(("by", 2), ("by", 6), ("az", 0), ("by", 3), ("by", 5))
    go(("az", 1), ("az", 3), ("by", 4), ("az", 2))
    go(*(("cx", by) for by in range(nz)))

    @pl.when(section == 1)
    def _():
        pl.semaphore_signal(turn_sem, inc=1, device_id=(0, me), device_id_type=MESH)

    def onward(unit, first=0, frames=F):
        return pltpu.make_async_remote_copy(
            src_ref=leaving.at[unit // NP, pl.ds(first, frames), unit % NP],
            dst_ref=entering.at[unit, pl.ds(first, frames)],
            send_sem=pass_send.at[unit],
            recv_sem=pass_recv.at[unit],
            device_id=(
                lax.rem(section + 1, sections),
                jnp.where(section == 1, across, me),
            ),
            device_id_type=MESH,
        )

    def send_back(vid):
        exchange(
            leaving.at[vid],
            lambda f: f,
            returned.at[vid],
            slot,
            out_send.at[vid],
            out_recv.at[vid],
        )

    @pl.loop(0, UNITS)
    def _(unit):
        @pl.when(jnp.logical_and(section == 0, unit == 0))
        def _():
            exchange_came(staged.at[0], entering.at[0], x_recv.at[0])

        @pl.when(jnp.logical_and(section == 0, unit > 0))
        def _():
            relayed(unit).wait_recv()

        @pl.when(section > 0)
        def _():
            onward(unit).wait_recv()

        block_step(
            unit, entering, leaving, weights, gains_ref, mods_ref, dmods_ref, tall, flat, att
        )

        @pl.when(section < sections - 1)
        def _():
            for part in range(HOP_PARTS):
                onward(unit, part * (F // HOP_PARTS), F // HOP_PARTS).start()

        @pl.when(jnp.logical_and(section > 1, unit % NP == NP - 1))
        def _():
            send_back(unit // NP)

    @pl.when(section == 0)
    def _():
        pl.semaphore_wait(turn_sem, 1)

    @pl.when(section < 2)
    def _():
        @pl.loop(0, VIDS)
        def _(vid):
            send_back(vid)

    gather.finish()
    swap.wait_send()

    @pl.loop(0, VIDS)
    def _(vid):
        exchange_came(leaving.at[vid], returned.at[vid], out_recv.at[vid])

        @pl.loop(0, count // group)
        def _(i):
            first = pl.multiple_of(i * group, group)
            for tan in range(2):
                row = pl.multiple_of((tan * count + first) * NP * KT, group * NP * KT)
                tall[pl.ds(row, group * NP * KT), :] = (
                    returned[vid, pl.ds(first, group), :, tan]
                    .reshape(group * NP * KT, HEAD)
                    .astype(F32)
                )

        for tan, result in enumerate((out_ref, tan_ref)):
            for k in range(KT):
                result[vid, :, k * HEAD : (k + 1) * HEAD] = tall[
                    pl.ds(tan * count * NP * KT + k, count * NP, stride=KT), :
                ].astype(BF16)

    @pl.loop(0, VIDS)
    def _(vid):
        exchange_sent(
            leaving.at[vid], returned.at[vid], out_send.at[vid], out_recv.at[vid]
        )

    @pl.loop(0, UNITS)
    def _(unit):
        @pl.when(section < sections - 1)
        def _():
            onward(unit).wait_send()

        @pl.when(
            jnp.logical_or(
                jnp.logical_and(section == 0, unit == 0),
                jnp.logical_and(section == 2, unit > 0),
            )
        )
        def _():
            exchange_sent(
                staged.at[unit], relay.at[unit], x_send.at[unit], x_recv.at[unit]
            )

        @pl.when(jnp.logical_and(section == 2, unit > 0))
        def _():
            relayed(unit).wait_send()


def shards(sizes, x_in, x_tan, t_index, w_qkv, w_out, qk_gain, mod_amp, mod_freq, mod_phase):
    nz, nx, ny = sizes
    count = nz * nx * ny
    sections = lax.axis_size("section")
    places = x_in.shape[2]
    waves = [wave.reshape(3, KT, HEAD) for wave in (mod_amp, mod_freq, mod_phase)]
    outside = pl.BlockSpec(memory_space=pl.ANY)
    inside = pl.BlockSpec(memory_space=pltpu.VMEM)
    result = jax.ShapeDtypeStruct((VIDS, places, D), BF16)
    units = (UNITS, F, 2, KT, HEAD)
    rings = 2 * (ny // 2) * (1 + 2 * nz) + 2 * (nz // 2) * (2 + ny) + nz
    dma = pltpu.SemaphoreType.DMA
    out, tan = pl.pallas_call(
        functools.partial(kernel, sizes, sections),
        out_shape=(result, result),
        in_specs=[outside] * 4
        + [inside, pl.BlockSpec(memory_space=pltpu.SMEM)]
        + [inside] * 3,
        out_specs=(inside, inside),
        scratch_shapes=[
            pltpu.VMEM((nz, nx, ny, ROWS_OUT, PACKED), BF16),
            pltpu.VMEM((VIDS, 3, KT, HEAD), F32),
            pltpu.VMEM((VIDS, 3, KT, HEAD), F32),
            pltpu.VMEM((2, VIDS, places, D), BF16),
            pltpu.VMEM(units, BF16),
            pltpu.VMEM(units, BF16),
            pltpu.VMEM(units, BF16),
            pltpu.VMEM((VIDS, F, NP, 2, KT, HEAD), BF16),
            pltpu.VMEM((VIDS, F, NP, 2, KT, HEAD), BF16),
            pltpu.VMEM((2 * places * KT, HEAD), F32),
            pltpu.VMEM((ROWS, D), BF16),
            pltpu.VMEM((ROWS, HD), BF16),
            dma((2,)),
            dma((3,)),
            dma,
            dma,
            dma((rings,)),
            dma((rings,)),
            dma((UNITS,)),
            dma((UNITS,)),
            dma((UNITS,)),
            dma((UNITS,)),
            dma((UNITS,)),
            dma((UNITS,)),
            dma((VIDS,)),
            dma((VIDS,)),
            pltpu.SemaphoreType.REGULAR,
        ],
        compiler_params=pltpu.CompilerParams(
            has_side_effects=True, vmem_limit_bytes=60 * 1024 * 1024
        ),
        name="blocks",
    )(
        x_in.reshape(VIDS, places, D),
        x_tan.reshape(VIDS, places, D),
        w_qkv[0],
        w_out[0],
        qk_gain[0],
        t_index,
        *waves,
    )
    return (out[None, :, None], tan[None, :, None])


def solution(mesh):
    count = mesh.shape["seq"]
    sizes = (count // 8, 2, 4)
    placed = (
        P(None, "seq", None, None),
        P(None, "seq", None, None),
        P(),
        P("section", "seq", None),
        P("section", "seq", None),
        P("section", None, None),
        P("section", None, None),
        P("section", None, None),
        P("section", None, None),
    )
    return jax.shard_map(
        functools.partial(shards, sizes),
        mesh=mesh,
        in_specs=placed,
        out_specs=(P("section", None, "seq", None, None), P("section", None, "seq", None, None)),
        check_vma=False,
    )
```

```python
import functools
import math

import jax
import jax.numpy as jnp
from jax import lax
from jax.experimental import pallas as pl
from jax.experimental.pallas import tpu as pltpu
from jax.sharding import PartitionSpec as P

HEADS = 8
HEAD = 128
T_STEPS = 1000
D = 2048
KT = D // HEAD
HD = HEADS * HEAD
F = 64
NP = 2
VIDS = 2
UNITS = VIDS * NP
ROWS = 2 * F
HALF = F
HOP_PARTS = 4
STRIDE = 27
EPS = 1e-06
F32 = jnp.float32
BF16 = jnp.bfloat16
MESH = pl.DeviceIdType.MESH
ROWS_OUT = 16
PACKED = 2 * 3 * HD + D
Z_LAST, Y_LAST = 2816, 5632


def timing(amp, freq, phase, time_value):
    angle = freq * time_value + phase
    return (amp * jnp.sin(angle), amp * freq * jnp.cos(angle))


class Gather:
    def __init__(self, sizes, section, coords, weights, send, recv):
        self.sizes, self.section, self.coords = sizes, section, coords
        self.weights, self.send, self.recv = weights, send, recv
        self.live = []
        self.sems = 0
        self.rings = {}

    def peer(self, axis, by):
        z, xl, y = self.coords
        nz, nx, ny = self.sizes
        if axis == "z":
            z = lax.rem(z + by + nz, nz)
        elif axis == "y":
            y = lax.rem(y + by + ny, ny)
        else:
            xl = nx - 1 - xl
        return (self.section, (z * nx + xl) * ny + y)

    def copy(self, ref, sem, peer):
        return pltpu.make_async_remote_copy(
            src_ref=ref,
            dst_ref=ref,
            send_sem=self.send.at[sem],
            recv_sem=self.recv.at[sem],
            device_id=peer,
            device_id_type=MESH,
        )

    def start(self, piece, begin, width, sem, peer):
        copy = self.copy(piece(pl.ds(begin, width)), sem, peer)
        copy.start()
        self.live.append(copy)

    def ring(self, axis, first, stop, fixed, single=False):
        size = self.sizes[0] if axis == "z" else self.sizes[2]
        me = self.coords[0] if axis == "z" else self.coords[2]
        last = size // 2
        first_sem = self.sems
        self.sems += 2 * last

        def arguments(way, step, index):
            z, y = (index, fixed) if axis == "z" else (fixed, index)
            begin, width = first, stop - first
            xl = self.coords[1] if single else slice(None)
            if step == last - 1:
                if single:
                    width = width // 2
                    begin = begin + way * width
                else:
                    xl = way

            def piece(columns):
                return self.weights.at[z, xl, y, :, columns]

            return piece, begin, width, first_sem + 2 * step + way, self.peer(axis, 1 - 2 * way)

        def at(way, step):
            return lax.rem(me - (1 - 2 * way) * step + size, size)

        for step in range(last):
            for way in (0, 1):
                self.start(*arguments(way, step, at(way, step)))
            yield
            for way in (0, 1):
                piece, begin, width, sem, peer = arguments(way, step, at(way, step + 1))
                self.copy(piece(pl.ds(begin, width)), sem, peer).wait_recv()

    def beside(self, fixed):
        sem = self.sems
        self.sems += 1
        _, xl, _ = self.coords
        nx = self.sizes[1]
        peer = self.peer("x", 0)
        self.start(
            lambda columns: self.weights.at[fixed, xl, :, :, columns],
            Y_LAST,
            PACKED - Y_LAST,
            sem,
            peer,
        )
        yield
        columns = pl.ds(Y_LAST, PACKED - Y_LAST)
        self.copy(self.weights.at[fixed, nx - 1 - xl, :, :, columns], sem, peer).wait_recv()

    def build(self):
        z, _, y = self.coords
        nz, _, ny = self.sizes
        rings = self.rings
        rings["a"] = self.ring("y", 0, Z_LAST, z)
        rings["b"] = self.ring("z", Z_LAST, Y_LAST, y)
        rings["c"] = self.ring("z", Y_LAST, PACKED, y, True)
        for by in range(ny):
            rings["az", by] = self.ring("z", 0, Z_LAST, lax.rem(y + by, ny))
        for by in range(nz):
            there = lax.rem(z + by, nz)
            rings["by", by] = self.ring("y", Z_LAST, Y_LAST, there)
            rings["cy", by] = self.ring("y", Y_LAST, PACKED, there, True)
            rings["cx", by] = self.beside(there)

    def go(self, *names):
        for name in names:
            next(self.rings[name], None)

    def finish(self):
        for copy in self.live:
            copy.wait_send()


def spread(source, tall, start):
    count = source.shape[0]
    for k in range(KT):
        tall[pl.ds(start + k, count, stride=KT), :] = source[:, k * HEAD : (k + 1) * HEAD].astype(
            F32
        )


def normalize(values, tangents, gain):
    inverse = lax.rsqrt(jnp.mean(values * values, axis=-1, keepdims=True) + EPS)
    cross = jnp.mean(values * tangents, axis=-1, keepdims=True)
    scaled = values * inverse
    return (
        (scaled * gain).astype(BF16),
        ((inverse * tangents - values * inverse**3 * cross) * gain).astype(BF16),
    )


def attend(q2, k2, v2, gains_ref):
    factor = 1.0 / math.sqrt(HEAD)
    qn, dqn = normalize(q2[:HALF], q2[HALF:], gains_ref[0:1, :])
    kn, dkn = normalize(k2[:HALF], k2[HALF:], gains_ref[1:2, :])
    value, dvalue = v2[:HALF].astype(BF16), v2[HALF:].astype(BF16)

    def against(rows, columns):
        return lax.dot_general(
            rows, columns, (((1,), (1,)), ((), ())), preferred_element_type=F32
        )

    scores = against(jnp.concatenate([qn, dqn], axis=0), kn)
    score = scores[:HALF] * factor
    dscore = (scores[HALF:] + against(qn, dkn)) * factor
    expo = jnp.exp(score)
    prob = expo * (1.0 / jnp.sum(expo, axis=-1, keepdims=True))
    growth = prob * dscore
    dprob = growth - prob * jnp.sum(growth, axis=-1, keepdims=True)
    prob, dprob = prob.astype(BF16), dprob.astype(BF16)
    mixed = jnp.dot(
        jnp.concatenate([prob, dprob], axis=0), value, preferred_element_type=F32
    )
    return mixed[:HALF], mixed[HALF:] + jnp.dot(prob, dvalue, preferred_element_type=F32)


def block_step(
    unit, entering, leaving, weights, gains_ref, mods_ref, dmods_ref, tall, flat, att
):
    group = 8
    vid = unit // NP

    @pl.loop(0, F // group, unroll=4)
    def _(i):
        first = pl.multiple_of(i * group, group)
        hidden = entering[unit, pl.ds(first, group), 0].astype(F32)
        tangent = entering[unit, pl.ds(first, group), 1].astype(F32)

        def mean(values):
            return jnp.sum(
                jnp.sum(values, axis=1, keepdims=True), axis=2, keepdims=True
            ) * (1.0 / D)

        inverse = lax.rsqrt(mean(hidden * hidden) + EPS)
        cross = mean(hidden * tangent)
        normed = hidden * inverse
        dnormed = inverse * tangent - hidden * inverse**3 * cross
        scale = 1.0 + mods_ref[vid, 1][None]
        modulated = normed * scale + mods_ref[vid, 0][None]
        dmodulated = dnormed * scale + normed * dmods_ref[vid, 1][None] + dmods_ref[vid, 0][None]
        row = pl.multiple_of(first * KT, group * KT)
        tall[pl.ds(row, group * KT), :] = modulated.reshape(group * KT, HEAD)
        tall[pl.ds(row + HALF * KT, group * KT), :] = dmodulated.reshape(group * KT, HEAD)

    for k in range(KT):
        flat[:, k * HEAD : (k + 1) * HEAD] = tall[pl.ds(k, ROWS, stride=KT), :].astype(BF16)

    def third(number, pair):
        column = number * HD + pair * 2 * HEAD
        halves = [
            weights[
                :, :, :, :, column + lower * 3 * HD : column + lower * 3 * HD + 2 * HEAD
            ].reshape(F, 1, ROWS_OUT, 2 * HEAD)
            for lower in range(2)
        ]
        matrix = jnp.concatenate(halves, axis=1).reshape(D, 2 * HEAD)
        return jnp.dot(flat[...], matrix, preferred_element_type=F32)

    ahead = [third(number, 0) for number in range(3)]
    for pair in range(HEADS // 2):
        q2, k2, v2 = ahead
        if pair + 1 < HEADS // 2:
            ahead = [third(number, pair + 1) for number in range(3)]
        for one in range(2):
            lanes = slice(one * HEAD, (one + 1) * HEAD)
            output, doutput = attend(q2[:, lanes], k2[:, lanes], v2[:, lanes], gains_ref)
            column = (pair * 2 + one) * HEAD
            att[:HALF, column : column + HEAD] = output.astype(BF16)
            att[HALF:, column : column + HEAD] = doutput.astype(BF16)

    for n in range(KT // 2):
        column = 2 * 3 * HD + n * 2 * HEAD
        matrix = weights[:, :, :, :, column : column + 2 * HEAD].reshape(HD, 2 * HEAD)
        y = jnp.dot(att[...], matrix, preferred_element_type=F32)
        tall[pl.ds(2 * n, ROWS, stride=KT), :] = y[:, :HEAD]
        tall[pl.ds(2 * n + 1, ROWS, stride=KT), :] = y[:, HEAD:]

    @pl.loop(0, F // group, unroll=4)
    def _(i):
        first = pl.multiple_of(i * group, group)
        row = pl.multiple_of(first * KT, group * KT)
        y = tall[pl.ds(row, group * KT), :].reshape(group, KT, HEAD)
        dy = tall[pl.ds(row + HALF * KT, group * KT), :].reshape(group, KT, HEAD)
        hidden = entering[unit, pl.ds(first, group), 0].astype(F32)
        tangent = entering[unit, pl.ds(first, group), 1].astype(F32)
        gate = mods_ref[vid, 2][None]
        dgate = dmods_ref[vid, 2][None]
        leaving[unit, pl.ds(first, group), 0] = (hidden + gate * y).astype(BF16)
        leaving[unit, pl.ds(first, group), 1] = (tangent + dgate * y + gate * dy).astype(BF16)


def kernel(
    sizes,
    sections,
    x_ref,
    t_ref,
    wqkv_ref,
    wout_ref,
    gains_ref,
    index_ref,
    amp_ref,
    freq_ref,
    phase_ref,
    out_ref,
    tan_ref,
    weights,
    mods_ref,
    dmods_ref,
    plain,
    staged,
    relay,
    entering,
    leaving,
    returned,
    tall,
    flat,
    att,
    load_sem,
    own_sem,
    swap_send,
    swap_recv,
    ring_send,
    ring_recv,
    x_send,
    x_recv,
    relay_send,
    relay_recv,
    pass_send,
    pass_recv,
    out_send,
    out_recv,
    turn_sem,
):
    nz, nx, ny = sizes
    count = nz * nx * ny
    section = lax.axis_index("section")
    me = lax.axis_index("seq")
    coords = (me // (nx * ny), (me // ny) % nx, me % ny)
    z, xl, y = coords
    first_half = section < 2

    def flip(index):
        return index + ny - 2 * ny * ((index // ny) % nx)

    across = flip(me)
    slot = jnp.where(first_half, me, across)
    neighbour = (section, lax.rem(me + 1, count))
    group = 8

    def exchange(source, row_of, target, place, send, recv):
        pltpu.make_async_copy(source.at[row_of(me)], target.at[place], recv).start()

        @pl.loop(1, count, unroll=21)
        def _(by):
            to = lax.rem(me + by * STRIDE, count)
            pltpu.make_async_remote_copy(
                src_ref=source.at[row_of(to)],
                dst_ref=target.at[place],
                send_sem=send,
                recv_sem=recv,
                device_id=(section, to),
                device_id_type=MESH,
            ).start()

    def exchange_came(source, target, recv):
        pltpu.make_async_copy(source, target, recv).wait()

    def exchange_sent(source, target, send, recv):
        pltpu.make_async_remote_copy(
            src_ref=source.at[pl.ds(0, count - 1)],
            dst_ref=target.at[pl.ds(0, count - 1)],
            send_sem=send,
            recv_sem=recv,
            device_id=neighbour,
            device_id_type=MESH,
        ).wait_send()

    leads = lax.rem(section, 2) == 0
    loads = [
        pltpu.make_async_copy(ref, plain.at[tan], load_sem.at[tan])
        for tan, ref in enumerate((x_ref, t_ref))
    ]

    @pl.when(section == 2)
    def _():
        for load in loads:
            load.start()

    own = []
    for part, (ref, first, width) in enumerate(
        (
            (wqkv_ref.at[pl.ds(0, ROWS_OUT)], 0, 3 * HD),
            (wqkv_ref.at[pl.ds(ROWS_OUT, ROWS_OUT)], 3 * HD, 3 * HD),
            (wout_ref, 6 * HD, D),
        )
    ):
        home = weights.at[z, xl, y, :, pl.ds(first, width)]
        own.append(pltpu.make_async_copy(ref, home, own_sem.at[part]))
        own[-1].start()
    for copy in own:
        copy.wait()

    @pl.when(jnp.logical_not(leads))
    def _():
        pl.semaphore_wait(turn_sem, 1)

    gather = Gather(sizes, section, coords, weights, ring_send, ring_recv)
    gather.build()
    go = gather.go
    mine = weights.at[z, xl, y, :, pl.ds(0, Y_LAST)]
    swap = pltpu.make_async_remote_copy(
        src_ref=mine,
        dst_ref=mine,
        send_sem=swap_send,
        recv_sem=swap_recv,
        device_id=(section, across),
        device_id_type=MESH,
    )
    theirs = weights.at[z, nx - 1 - xl, y, :, pl.ds(0, Y_LAST)]
    swapped = pltpu.make_async_remote_copy(
        src_ref=theirs,
        dst_ref=theirs,
        send_sem=swap_send,
        recv_sem=swap_recv,
        device_id=(section, across),
        device_id_type=MESH,
    )
    swap.start()
    go("c", ("cy", 0))

    def prepare(vid):
        for tan in range(2):
            spread(plain.at[tan, vid], tall, 0)

            @pl.loop(0, count // group)
            def _(i):
                first = pl.multiple_of(i * group, group)
                row = pl.multiple_of(first * NP * KT, group * NP * KT)
                tiles = (
                    tall[pl.ds(row, group * NP * KT), :]
                    .astype(BF16)
                    .reshape(group, NP, KT, HEAD)
                )
                for pos in range(NP):
                    staged[vid * NP + pos, pl.ds(first, group), tan] = tiles[:, pos]

    @pl.when(section == 2)
    def _():
        for load in loads:
            load.wait()
        for vid in range(VIDS):
            prepare(vid)
            for unit in range(vid * NP, vid * NP + NP):
                exchange(
                    staged.at[unit],
                    flip,
                    relay.at[unit],
                    me,
                    x_send.at[unit],
                    x_recv.at[unit],
                )

    def relayed(unit):
        return pltpu.make_async_remote_copy(
            src_ref=relay.at[unit],
            dst_ref=entering.at[unit],
            send_sem=relay_send.at[unit],
            recv_sem=relay_recv.at[unit],
            device_id=(0, across),
            device_id_type=MESH,
        )

    def pass_to_first(unit):
        @pl.when(section == 2)
        def _():
            exchange_came(staged.at[unit], relay.at[unit], x_recv.at[unit])
            relayed(unit).start()

    for vid in range(VIDS):
        time_value = (index_ref[vid].astype(F32) + 0.5) * (math.pi / (2.0 * T_STEPS))
        mods_ref[vid], dmods_ref[vid] = timing(
            amp_ref[...], freq_ref[...], phase_ref[...], time_value
        )

    swapped.wait_recv()
    go("b", "a", ("by", 0), ("az", 0))
    go("c", ("cy", 1), ("cy", 7))
    go("a", ("az", 1), ("az", 3))
    go(("cy", 0),)
    go("b", ("by", 1), ("by", 7))
    go("c", ("cy", 2), ("cy", 6))

    @pl.when(leads)
    def _():
        pl.semaphore_signal(
            turn_sem, inc=1, device_id=(section + 1, me), device_id_type=MESH
        )

    go("a", ("az", 2))
    go(("cy", 0), ("cx", 0), ("cy", 1), ("cy", 7))
    go(("az", 0), ("by", 0))
    go("c", ("cy", 3), ("cy", 5))
    go(("cy", 1), ("cx", 1), ("cy", 7), ("cx", 7), ("cy", 2), ("cy", 6))
    go("b", ("by", 2), ("by", 6))
    go("c", ("cy", 4))
    pass_to_first(0)
    pass_to_first(1)
    go(("az", 1), ("az", 3), ("by", 1), ("by", 7), ("az", 2))
    go(("cy", 2), ("cx", 2), ("cy", 6), ("cx", 6), ("cy", 3), ("cy", 5), ("cy", 4))
    go("b", ("by", 3), ("by", 5))
    go(("az", 0), ("by", 0), ("az", 1), ("az", 3))
    go(("cy", 3), ("cx", 3), ("cy", 5), ("cx", 5), ("cy", 4), ("cx", 4))
    pass_to_first(2)

    go("b", ("by", 4))
    go(("by", 2), ("by", 6), ("az", 2), ("by", 1), ("by", 7), ("az", 0))
    pass_to_first(3)
    go(("by", 3), ("by", 5), ("az", 1), ("az", 3), ("by", 4), ("az", 2))
    go(("by", 2), ("by", 6), ("az", 0), ("by", 3), ("by", 5))
    go(("az", 1), ("az", 3), ("by", 4), ("az", 2))
    go(*(("cx", by) for by in range(nz)))

    @pl.when(section == 1)
    def _():
        pl.semaphore_signal(turn_sem, inc=1, device_id=(0, me), device_id_type=MESH)

    def onward(unit, first=0, frames=F):
        return pltpu.make_async_remote_copy(
            src_ref=leaving.at[unit, pl.ds(first, frames)],
            dst_ref=entering.at[unit, pl.ds(first, frames)],
            send_sem=pass_send.at[unit],
            recv_sem=pass_recv.at[unit],
            device_id=(
                lax.rem(section + 1, sections),
                jnp.where(section == 1, across, me),
            ),
            device_id_type=MESH,
        )

    def send_back(unit):
        exchange(
            leaving.at[unit],
            lambda f: f,
            returned.at[unit],
            slot,
            out_send.at[unit],
            out_recv.at[unit],
        )

    @pl.loop(0, UNITS)
    def _(unit):
        @pl.when(section == 0)
        def _():
            relayed(unit).wait_recv()

        @pl.when(section > 0)
        def _():
            onward(unit).wait_recv()

        block_step(
            unit, entering, leaving, weights, gains_ref, mods_ref, dmods_ref, tall, flat, att
        )

        @pl.when(section < sections - 1)
        def _():
            for part in range(HOP_PARTS):
                onward(unit, part * (F // HOP_PARTS), F // HOP_PARTS).start()

        @pl.when(section > 1)
        def _():
            send_back(unit)

    @pl.when(section == 0)
    def _():
        pl.semaphore_wait(turn_sem, 1)

    @pl.when(section < 2)
    def _():
        @pl.loop(0, UNITS)
        def _(unit):
            send_back(unit)

    gather.finish()
    swap.wait_send()

    @pl.loop(0, VIDS)
    def _(vid):
        for pos in range(NP):
            unit = vid * NP + pos
            exchange_came(leaving.at[unit], returned.at[unit], out_recv.at[unit])

            @pl.loop(0, count // group)
            def _(i):
                first = pl.multiple_of(i * group, group)
                for tan in range(2):
                    tiles = returned[unit, pl.ds(first, group), tan].astype(F32)
                    for one in range(group):
                        row = pl.multiple_of(
                            ((tan * count + first + one) * NP + pos) * KT, KT
                        )
                        tall[pl.ds(row, KT), :] = tiles[one]

        for tan, result in enumerate((out_ref, tan_ref)):
            for k in range(KT):
                result[vid, :, k * HEAD : (k + 1) * HEAD] = tall[
                    pl.ds(tan * count * NP * KT + k, count * NP, stride=KT), :
                ].astype(BF16)

    @pl.loop(0, UNITS)
    def _(unit):
        exchange_sent(
            leaving.at[unit], returned.at[unit], out_send.at[unit], out_recv.at[unit]
        )

        @pl.when(section < sections - 1)
        def _():
            onward(unit).wait_send()

        @pl.when(section == 2)
        def _():
            exchange_sent(
                staged.at[unit], relay.at[unit], x_send.at[unit], x_recv.at[unit]
            )
            relayed(unit).wait_send()


def shards(sizes, x_in, x_tan, t_index, w_qkv, w_out, qk_gain, mod_amp, mod_freq, mod_phase):
    nz, nx, ny = sizes
    count = nz * nx * ny
    sections = lax.axis_size("section")
    places = x_in.shape[2]
    waves = [wave.reshape(3, KT, HEAD) for wave in (mod_amp, mod_freq, mod_phase)]
    outside = pl.BlockSpec(memory_space=pl.ANY)
    inside = pl.BlockSpec(memory_space=pltpu.VMEM)
    result = jax.ShapeDtypeStruct((VIDS, places, D), BF16)
    units = (UNITS, F, 2, KT, HEAD)
    rings = 2 * (ny // 2) * (1 + 2 * nz) + 2 * (nz // 2) * (2 + ny) + nz
    dma = pltpu.SemaphoreType.DMA
    out, tan = pl.pallas_call(
        functools.partial(kernel, sizes, sections),
        out_shape=(result, result),
        in_specs=[outside] * 4
        + [inside, pl.BlockSpec(memory_space=pltpu.SMEM)]
        + [inside] * 3,
        out_specs=(inside, inside),
        scratch_shapes=[
            pltpu.VMEM((nz, nx, ny, ROWS_OUT, PACKED), BF16),
            pltpu.VMEM((VIDS, 3, KT, HEAD), F32),
            pltpu.VMEM((VIDS, 3, KT, HEAD), F32),
            pltpu.VMEM((2, VIDS, places, D), BF16),
            pltpu.VMEM(units, BF16),
            pltpu.VMEM(units, BF16),
            pltpu.VMEM(units, BF16),
            pltpu.VMEM(units, BF16),
            pltpu.VMEM(units, BF16),
            pltpu.VMEM((2 * places * KT, HEAD), F32),
            pltpu.VMEM((ROWS, D), BF16),
            pltpu.VMEM((ROWS, HD), BF16),
            dma((2,)),
            dma((3,)),
            dma,
            dma,
            dma((rings,)),
            dma((rings,)),
            dma((UNITS,)),
            dma((UNITS,)),
            dma((UNITS,)),
            dma((UNITS,)),
            dma((UNITS,)),
            dma((UNITS,)),
            dma((UNITS,)),
            dma((UNITS,)),
            pltpu.SemaphoreType.REGULAR,
        ],
        compiler_params=pltpu.CompilerParams(
            has_side_effects=True, vmem_limit_bytes=60 * 1024 * 1024
        ),
        name="blocks",
    )(
        x_in.reshape(VIDS, places, D),
        x_tan.reshape(VIDS, places, D),
        w_qkv[0],
        w_out[0],
        qk_gain[0],
        t_index,
        *waves,
    )
    return (out[None, :, None], tan[None, :, None])


def solution(mesh):
    count = mesh.shape["seq"]
    sizes = (count // 8, 2, 4)
    placed = (
        P(None, "seq", None, None),
        P(None, "seq", None, None),
        P(),
        P("section", "seq", None),
        P("section", "seq", None),
        P("section", None, None),
        P("section", None, None),
        P("section", None, None),
        P("section", None, None),
    )
    return jax.shard_map(
        functools.partial(shards, sizes),
        mesh=mesh,
        in_specs=placed,
        out_specs=(P("section", None, "seq", None, None), P("section", None, "seq", None, None)),
        check_vma=False,
    )
```

```python
import functools
import math

import jax
import jax.numpy as jnp
from jax import lax
from jax.experimental import pallas as pl
from jax.experimental.pallas import tpu as pltpu
from jax.sharding import PartitionSpec as P

HEADS = 8
HEAD = 128
T_STEPS = 1000
D = 2048
KT = D // HEAD
HD = HEADS * HEAD
F = 64
NP = 2
VIDS = 2
UNITS = VIDS * NP
ROWS = 2 * F
HALF = F
HOP_PARTS = 4
STRIDE = 27
EPS = 1e-06
F32 = jnp.float32
BF16 = jnp.bfloat16
MESH = pl.DeviceIdType.MESH
ROWS_OUT = 16
PACKED = 2 * 3 * HD + D
Z_LAST, Y_LAST = 2816, 5632


def timing(amp, freq, phase, time_value):
    angle = freq * time_value + phase
    return (amp * jnp.sin(angle), amp * freq * jnp.cos(angle))


class Gather:
    def __init__(self, sizes, section, coords, weights, send, recv):
        self.sizes, self.section, self.coords = sizes, section, coords
        self.weights, self.send, self.recv = weights, send, recv
        self.live = []
        self.sems = 0
        self.rings = {}

    def peer(self, axis, by):
        z, xl, y = self.coords
        nz, nx, ny = self.sizes
        if axis == "z":
            z = lax.rem(z + by + nz, nz)
        elif axis == "y":
            y = lax.rem(y + by + ny, ny)
        else:
            xl = nx - 1 - xl
        return (self.section, (z * nx + xl) * ny + y)

    def copy(self, ref, sem, peer):
        return pltpu.make_async_remote_copy(
            src_ref=ref,
            dst_ref=ref,
            send_sem=self.send.at[sem],
            recv_sem=self.recv.at[sem],
            device_id=peer,
            device_id_type=MESH,
        )

    def start(self, piece, begin, width, sem, peer):
        copy = self.copy(piece(pl.ds(begin, width)), sem, peer)
        copy.start()
        self.live.append(copy)

    def ring(self, axis, first, stop, fixed, single=False):
        size = self.sizes[0] if axis == "z" else self.sizes[2]
        me = self.coords[0] if axis == "z" else self.coords[2]
        last = size // 2
        first_sem = self.sems
        self.sems += 2 * last

        def arguments(way, step, index):
            z, y = (index, fixed) if axis == "z" else (fixed, index)
            begin, width = first, stop - first
            xl = self.coords[1] if single else slice(None)
            if step == last - 1:
                if single:
                    width = width // 2
                    begin = begin + way * width
                else:
                    xl = way

            def piece(columns):
                return self.weights.at[z, xl, y, :, columns]

            return piece, begin, width, first_sem + 2 * step + way, self.peer(axis, 1 - 2 * way)

        def at(way, step):
            return lax.rem(me - (1 - 2 * way) * step + size, size)

        for step in range(last):
            for way in (0, 1):
                self.start(*arguments(way, step, at(way, step)))
            yield
            for way in (0, 1):
                piece, begin, width, sem, peer = arguments(way, step, at(way, step + 1))
                self.copy(piece(pl.ds(begin, width)), sem, peer).wait_recv()

    def beside(self, fixed):
        sem = self.sems
        self.sems += 1
        _, xl, _ = self.coords
        nx = self.sizes[1]
        peer = self.peer("x", 0)
        self.start(
            lambda columns: self.weights.at[fixed, xl, :, :, columns],
            Y_LAST,
            PACKED - Y_LAST,
            sem,
            peer,
        )
        yield
        columns = pl.ds(Y_LAST, PACKED - Y_LAST)
        self.copy(self.weights.at[fixed, nx - 1 - xl, :, :, columns], sem, peer).wait_recv()

    def build(self):
        z, _, y = self.coords
        nz, _, ny = self.sizes
        rings = self.rings
        rings["a"] = self.ring("y", 0, Z_LAST, z)
        rings["b"] = self.ring("z", Z_LAST, Y_LAST, y)
        rings["c"] = self.ring("z", Y_LAST, PACKED, y, True)
        for by in range(ny):
            rings["az", by] = self.ring("z", 0, Z_LAST, lax.rem(y + by, ny))
        for by in range(nz):
            there = lax.rem(z + by, nz)
            rings["by", by] = self.ring("y", Z_LAST, Y_LAST, there)
            rings["cy", by] = self.ring("y", Y_LAST, PACKED, there, True)
            rings["cx", by] = self.beside(there)

    def go(self, *names):
        for name in names:
            next(self.rings[name], None)

    def finish(self):
        for copy in self.live:
            copy.wait_send()


def spread(source, tall, start):
    count = source.shape[0]
    for k in range(KT):
        tall[pl.ds(start + k, count, stride=KT), :] = source[:, k * HEAD : (k + 1) * HEAD].astype(
            F32
        )


def normalize(values, tangents, gain):
    inverse = lax.rsqrt(jnp.mean(values * values, axis=-1, keepdims=True) + EPS)
    cross = jnp.mean(values * tangents, axis=-1, keepdims=True)
    scaled = values * inverse
    return (
        (scaled * gain).astype(BF16),
        ((inverse * tangents - values * inverse**3 * cross) * gain).astype(BF16),
    )


def attend(q2, k2, v2, gains_ref):
    factor = 1.0 / math.sqrt(HEAD)
    qn, dqn = normalize(q2[:HALF], q2[HALF:], gains_ref[0:1, :])
    kn, dkn = normalize(k2[:HALF], k2[HALF:], gains_ref[1:2, :])
    value, dvalue = v2[:HALF].astype(BF16), v2[HALF:].astype(BF16)

    def against(rows, columns):
        return lax.dot_general(
            rows, columns, (((1,), (1,)), ((), ())), preferred_element_type=F32
        )

    scores = against(jnp.concatenate([qn, dqn], axis=0), kn)
    score = scores[:HALF] * factor
    dscore = (scores[HALF:] + against(qn, dkn)) * factor
    expo = jnp.exp(score)
    prob = expo * (1.0 / jnp.sum(expo, axis=-1, keepdims=True))
    growth = prob * dscore
    dprob = growth - prob * jnp.sum(growth, axis=-1, keepdims=True)
    prob, dprob = prob.astype(BF16), dprob.astype(BF16)
    mixed = jnp.dot(
        jnp.concatenate([prob, dprob], axis=0), value, preferred_element_type=F32
    )
    return mixed[:HALF], mixed[HALF:] + jnp.dot(prob, dvalue, preferred_element_type=F32)


def block_step(
    unit, entering, leaving, weights, gains_ref, mods_ref, dmods_ref, tall, flat, att
):
    group = 8
    vid = unit // NP

    @pl.loop(0, F // group, unroll=8)
    def _(i):
        first = pl.multiple_of(i * group, group)
        hidden = entering[unit, pl.ds(first, group), 0].astype(F32)
        tangent = entering[unit, pl.ds(first, group), 1].astype(F32)

        def mean(values):
            return jnp.sum(
                jnp.sum(values, axis=1, keepdims=True), axis=2, keepdims=True
            ) * (1.0 / D)

        inverse = lax.rsqrt(mean(hidden * hidden) + EPS)
        cross = mean(hidden * tangent)
        normed = hidden * inverse
        dnormed = inverse * tangent - hidden * inverse**3 * cross
        scale = 1.0 + mods_ref[vid, 1][None]
        modulated = normed * scale + mods_ref[vid, 0][None]
        dmodulated = dnormed * scale + normed * dmods_ref[vid, 1][None] + dmods_ref[vid, 0][None]
        row = pl.multiple_of(first * KT, group * KT)
        tall[pl.ds(row, group * KT), :] = modulated.reshape(group * KT, HEAD)
        tall[pl.ds(row + HALF * KT, group * KT), :] = dmodulated.reshape(group * KT, HEAD)

    for k in range(KT):
        flat[:, k * HEAD : (k + 1) * HEAD] = tall[pl.ds(k, ROWS, stride=KT), :].astype(BF16)

    def third(number, pair):
        column = number * HD + pair * 2 * HEAD
        halves = [
            weights[
                :, :, :, :, column + lower * 3 * HD : column + lower * 3 * HD + 2 * HEAD
            ].reshape(F, 1, ROWS_OUT, 2 * HEAD)
            for lower in range(2)
        ]
        matrix = jnp.concatenate(halves, axis=1).reshape(D, 2 * HEAD)
        return jnp.dot(flat[...], matrix, preferred_element_type=F32)

    ahead = [third(number, 0) for number in range(3)]
    for pair in range(HEADS // 2):
        q2, k2, v2 = ahead
        if pair + 1 < HEADS // 2:
            ahead = [third(number, pair + 1) for number in range(3)]
        for one in range(2):
            lanes = slice(one * HEAD, (one + 1) * HEAD)
            output, doutput = attend(q2[:, lanes], k2[:, lanes], v2[:, lanes], gains_ref)
            column = (pair * 2 + one) * HEAD
            att[:HALF, column : column + HEAD] = output.astype(BF16)
            att[HALF:, column : column + HEAD] = doutput.astype(BF16)

    for n in range(KT // 2):
        column = 2 * 3 * HD + n * 2 * HEAD
        matrix = weights[:, :, :, :, column : column + 2 * HEAD].reshape(HD, 2 * HEAD)
        y = jnp.dot(att[...], matrix, preferred_element_type=F32)
        tall[pl.ds(2 * n, ROWS, stride=KT), :] = y[:, :HEAD]
        tall[pl.ds(2 * n + 1, ROWS, stride=KT), :] = y[:, HEAD:]

    @pl.loop(0, F // group, unroll=8)
    def _(i):
        first = pl.multiple_of(i * group, group)
        row = pl.multiple_of(first * KT, group * KT)
        y = tall[pl.ds(row, group * KT), :].reshape(group, KT, HEAD)
        dy = tall[pl.ds(row + HALF * KT, group * KT), :].reshape(group, KT, HEAD)
        hidden = entering[unit, pl.ds(first, group), 0].astype(F32)
        tangent = entering[unit, pl.ds(first, group), 1].astype(F32)
        gate = mods_ref[vid, 2][None]
        dgate = dmods_ref[vid, 2][None]
        leaving[unit, pl.ds(first, group), 0] = (hidden + gate * y).astype(BF16)
        leaving[unit, pl.ds(first, group), 1] = (tangent + dgate * y + gate * dy).astype(BF16)


def kernel(
    sizes,
    sections,
    x_ref,
    t_ref,
    wqkv_ref,
    wout_ref,
    gains_ref,
    index_ref,
    amp_ref,
    freq_ref,
    phase_ref,
    out_ref,
    tan_ref,
    weights,
    mods_ref,
    dmods_ref,
    plain,
    staged,
    relay,
    entering,
    leaving,
    returned,
    tall,
    flat,
    att,
    load_sem,
    own_sem,
    swap_send,
    swap_recv,
    ring_send,
    ring_recv,
    x_send,
    x_recv,
    relay_send,
    relay_recv,
    pass_send,
    pass_recv,
    out_send,
    out_recv,
    turn_sem,
):
    nz, nx, ny = sizes
    count = nz * nx * ny
    section = lax.axis_index("section")
    me = lax.axis_index("seq")
    coords = (me // (nx * ny), (me // ny) % nx, me % ny)
    z, xl, y = coords
    first_half = section < 2

    def flip(index):
        return index + ny - 2 * ny * ((index // ny) % nx)

    across = flip(me)
    slot = jnp.where(first_half, me, across)
    neighbour = (section, lax.rem(me + 1, count))
    group = 8

    def exchange(source, row_of, target, place, send, recv):
        pltpu.make_async_copy(source.at[row_of(me)], target.at[place], recv).start()

        @pl.loop(1, count, unroll=21)
        def _(by):
            to = lax.rem(me + by * STRIDE, count)
            pltpu.make_async_remote_copy(
                src_ref=source.at[row_of(to)],
                dst_ref=target.at[place],
                send_sem=send,
                recv_sem=recv,
                device_id=(section, to),
                device_id_type=MESH,
            ).start()

    def exchange_came(source, target, recv):
        pltpu.make_async_copy(source, target, recv).wait()

    def exchange_sent(source, target, send, recv):
        pltpu.make_async_remote_copy(
            src_ref=source.at[pl.ds(0, count - 1)],
            dst_ref=target.at[pl.ds(0, count - 1)],
            send_sem=send,
            recv_sem=recv,
            device_id=neighbour,
            device_id_type=MESH,
        ).wait_send()

    leads = lax.rem(section, 2) == 0
    loads = [
        pltpu.make_async_copy(ref, plain.at[tan], load_sem.at[tan])
        for tan, ref in enumerate((x_ref, t_ref))
    ]

    @pl.when(section == 2)
    def _():
        for load in loads:
            load.start()

    own = []
    for part, (ref, first, width) in enumerate(
        (
            (wqkv_ref.at[pl.ds(0, ROWS_OUT)], 0, 3 * HD),
            (wqkv_ref.at[pl.ds(ROWS_OUT, ROWS_OUT)], 3 * HD, 3 * HD),
            (wout_ref, 6 * HD, D),
        )
    ):
        home = weights.at[z, xl, y, :, pl.ds(first, width)]
        own.append(pltpu.make_async_copy(ref, home, own_sem.at[part]))
        own[-1].start()
    for copy in own:
        copy.wait()

    @pl.when(jnp.logical_not(leads))
    def _():
        pl.semaphore_wait(turn_sem, 1)

    gather = Gather(sizes, section, coords, weights, ring_send, ring_recv)
    gather.build()
    go = gather.go
    mine = weights.at[z, xl, y, :, pl.ds(0, Y_LAST)]
    swap = pltpu.make_async_remote_copy(
        src_ref=mine,
        dst_ref=mine,
        send_sem=swap_send,
        recv_sem=swap_recv,
        device_id=(section, across),
        device_id_type=MESH,
    )
    theirs = weights.at[z, nx - 1 - xl, y, :, pl.ds(0, Y_LAST)]
    swapped = pltpu.make_async_remote_copy(
        src_ref=theirs,
        dst_ref=theirs,
        send_sem=swap_send,
        recv_sem=swap_recv,
        device_id=(section, across),
        device_id_type=MESH,
    )
    swap.start()
    go("c", ("cy", 0))

    def prepare(vid):
        for tan in range(2):
            spread(plain.at[tan, vid], tall, 0)

            @pl.loop(0, count // group)
            def _(i):
                first = pl.multiple_of(i * group, group)
                row = pl.multiple_of(first * NP * KT, group * NP * KT)
                tiles = (
                    tall[pl.ds(row, group * NP * KT), :]
                    .astype(BF16)
                    .reshape(group, NP, KT, HEAD)
                )
                for pos in range(NP):
                    staged[vid * NP + pos, pl.ds(first, group), tan] = tiles[:, pos]

    @pl.when(section == 2)
    def _():
        for load in loads:
            load.wait()
        for vid in range(VIDS):
            prepare(vid)
            for unit in range(vid * NP, vid * NP + NP):
                exchange(
                    staged.at[unit],
                    flip,
                    relay.at[unit],
                    me,
                    x_send.at[unit],
                    x_recv.at[unit],
                )

    def relayed(unit):
        return pltpu.make_async_remote_copy(
            src_ref=relay.at[unit],
            dst_ref=entering.at[unit],
            send_sem=relay_send.at[unit],
            recv_sem=relay_recv.at[unit],
            device_id=(0, across),
            device_id_type=MESH,
        )

    def pass_to_first(unit):
        @pl.when(section == 2)
        def _():
            exchange_came(staged.at[unit], relay.at[unit], x_recv.at[unit])
            relayed(unit).start()

    for vid in range(VIDS):
        time_value = (index_ref[vid].astype(F32) + 0.5) * (math.pi / (2.0 * T_STEPS))
        mods_ref[vid], dmods_ref[vid] = timing(
            amp_ref[...], freq_ref[...], phase_ref[...], time_value
        )

    swapped.wait_recv()
    go("b", "a", ("by", 0), ("az", 0))
    go("c", ("cy", 1), ("cy", 7))
    go("a", ("az", 1), ("az", 3))
    go(("cy", 0),)
    go("b", ("by", 1), ("by", 7))
    go("c", ("cy", 2), ("cy", 6))

    @pl.when(leads)
    def _():
        pl.semaphore_signal(
            turn_sem, inc=1, device_id=(section + 1, me), device_id_type=MESH
        )

    go("a", ("az", 2))
    go(("cy", 0), ("cx", 0), ("cy", 1), ("cy", 7))
    go(("az", 0), ("by", 0))
    go("c", ("cy", 3), ("cy", 5))
    go(("cy", 1), ("cx", 1), ("cy", 7), ("cx", 7), ("cy", 2), ("cy", 6))
    go("b", ("by", 2), ("by", 6))
    go("c", ("cy", 4))
    pass_to_first(0)
    pass_to_first(1)
    go(("az", 1), ("az", 3), ("by", 1), ("by", 7), ("az", 2))
    go(("cy", 2), ("cx", 2), ("cy", 6), ("cx", 6), ("cy", 3), ("cy", 5), ("cy", 4))
    go("b", ("by", 3), ("by", 5))
    go(("az", 0), ("by", 0), ("az", 1), ("az", 3))
    go(("cy", 3), ("cx", 3), ("cy", 5), ("cx", 5), ("cy", 4), ("cx", 4))
    pass_to_first(2)

    go("b", ("by", 4))
    go(("by", 2), ("by", 6), ("az", 2), ("by", 1), ("by", 7), ("az", 0))
    pass_to_first(3)
    go(("by", 3), ("by", 5), ("az", 1), ("az", 3), ("by", 4), ("az", 2))
    go(("by", 2), ("by", 6), ("az", 0), ("by", 3), ("by", 5))
    go(("az", 1), ("az", 3), ("by", 4), ("az", 2))
    go(*(("cx", by) for by in range(nz)))

    @pl.when(section == 1)
    def _():
        pl.semaphore_signal(turn_sem, inc=1, device_id=(0, me), device_id_type=MESH)

    def onward(unit, first=0, frames=F):
        return pltpu.make_async_remote_copy(
            src_ref=leaving.at[unit, pl.ds(first, frames)],
            dst_ref=entering.at[unit, pl.ds(first, frames)],
            send_sem=pass_send.at[unit],
            recv_sem=pass_recv.at[unit],
            device_id=(
                lax.rem(section + 1, sections),
                jnp.where(section == 1, across, me),
            ),
            device_id_type=MESH,
        )

    def send_back(unit):
        exchange(
            leaving.at[unit],
            lambda f: f,
            returned.at[unit],
            slot,
            out_send.at[unit],
            out_recv.at[unit],
        )

    @pl.loop(0, UNITS)
    def _(unit):
        @pl.when(section == 0)
        def _():
            relayed(unit).wait_recv()

        @pl.when(section > 0)
        def _():
            onward(unit).wait_recv()

        block_step(
            unit, entering, leaving, weights, gains_ref, mods_ref, dmods_ref, tall, flat, att
        )

        @pl.when(section < sections - 1)
        def _():
            for part in range(HOP_PARTS):
                onward(unit, part * (F // HOP_PARTS), F // HOP_PARTS).start()

        @pl.when(section > 1)
        def _():
            send_back(unit)

    @pl.when(section == 0)
    def _():
        pl.semaphore_wait(turn_sem, 1)

    @pl.when(section < 2)
    def _():
        @pl.loop(0, UNITS)
        def _(unit):
            send_back(unit)

    gather.finish()
    swap.wait_send()

    @pl.loop(0, VIDS)
    def _(vid):
        for pos in range(NP):
            unit = vid * NP + pos
            exchange_came(leaving.at[unit], returned.at[unit], out_recv.at[unit])

            @pl.loop(0, count // group, unroll=4)
            def _(i):
                first = pl.multiple_of(i * group, group)
                for tan in range(2):
                    tiles = returned[unit, pl.ds(first, group), tan].astype(F32)
                    for one in range(group):
                        row = pl.multiple_of(
                            ((tan * count + first + one) * NP + pos) * KT, KT
                        )
                        tall[pl.ds(row, KT), :] = tiles[one]

        for tan, result in enumerate((out_ref, tan_ref)):
            for k in range(KT):
                result[vid, :, k * HEAD : (k + 1) * HEAD] = tall[
                    pl.ds(tan * count * NP * KT + k, count * NP, stride=KT), :
                ].astype(BF16)

    @pl.loop(0, UNITS)
    def _(unit):
        exchange_sent(
            leaving.at[unit], returned.at[unit], out_send.at[unit], out_recv.at[unit]
        )

        @pl.when(section < sections - 1)
        def _():
            onward(unit).wait_send()

        @pl.when(section == 2)
        def _():
            exchange_sent(
                staged.at[unit], relay.at[unit], x_send.at[unit], x_recv.at[unit]
            )
            relayed(unit).wait_send()


def shards(sizes, x_in, x_tan, t_index, w_qkv, w_out, qk_gain, mod_amp, mod_freq, mod_phase):
    nz, nx, ny = sizes
    count = nz * nx * ny
    sections = lax.axis_size("section")
    places = x_in.shape[2]
    waves = [wave.reshape(3, KT, HEAD) for wave in (mod_amp, mod_freq, mod_phase)]
    outside = pl.BlockSpec(memory_space=pl.ANY)
    inside = pl.BlockSpec(memory_space=pltpu.VMEM)
    result = jax.ShapeDtypeStruct((VIDS, places, D), BF16)
    units = (UNITS, F, 2, KT, HEAD)
    rings = 2 * (ny // 2) * (1 + 2 * nz) + 2 * (nz // 2) * (2 + ny) + nz
    dma = pltpu.SemaphoreType.DMA
    out, tan = pl.pallas_call(
        functools.partial(kernel, sizes, sections),
        out_shape=(result, result),
        in_specs=[outside] * 4
        + [inside, pl.BlockSpec(memory_space=pltpu.SMEM)]
        + [inside] * 3,
        out_specs=(inside, inside),
        scratch_shapes=[
            pltpu.VMEM((nz, nx, ny, ROWS_OUT, PACKED), BF16),
            pltpu.VMEM((VIDS, 3, KT, HEAD), F32),
            pltpu.VMEM((VIDS, 3, KT, HEAD), F32),
            pltpu.VMEM((2, VIDS, places, D), BF16),
            pltpu.VMEM(units, BF16),
            pltpu.VMEM(units, BF16),
            pltpu.VMEM(units, BF16),
            pltpu.VMEM(units, BF16),
            pltpu.VMEM(units, BF16),
            pltpu.VMEM((2 * places * KT, HEAD), F32),
            pltpu.VMEM((ROWS, D), BF16),
            pltpu.VMEM((ROWS, HD), BF16),
            dma((2,)),
            dma((3,)),
            dma,
            dma,
            dma((rings,)),
            dma((rings,)),
            dma((UNITS,)),
            dma((UNITS,)),
            dma((UNITS,)),
            dma((UNITS,)),
            dma((UNITS,)),
            dma((UNITS,)),
            dma((UNITS,)),
            dma((UNITS,)),
            pltpu.SemaphoreType.REGULAR,
        ],
        compiler_params=pltpu.CompilerParams(
            has_side_effects=True, vmem_limit_bytes=60 * 1024 * 1024
        ),
        name="blocks",
    )(
        x_in.reshape(VIDS, places, D),
        x_tan.reshape(VIDS, places, D),
        w_qkv[0],
        w_out[0],
        qk_gain[0],
        t_index,
        *waves,
    )
    return (out[None, :, None], tan[None, :, None])


def solution(mesh):
    count = mesh.shape["seq"]
    sizes = (count // 8, 2, 4)
    placed = (
        P(None, "seq", None, None),
        P(None, "seq", None, None),
        P(),
        P("section", "seq", None),
        P("section", "seq", None),
        P("section", None, None),
        P("section", None, None),
        P("section", None, None),
        P("section", None, None),
    )
    return jax.shard_map(
        functools.partial(shards, sizes),
        mesh=mesh,
        in_specs=placed,
        out_specs=(P("section", None, "seq", None, None), P("section", None, "seq", None, None)),
        check_vma=False,
    )
```

```python
import functools
import math

import jax
import jax.numpy as jnp
from jax import lax
from jax.experimental import pallas as pl
from jax.experimental.pallas import tpu as pltpu
from jax.sharding import PartitionSpec as P

HEADS = 8
HEAD = 128
T_STEPS = 1000
D = 2048
KT = D // HEAD
HD = HEADS * HEAD
F = 64
NP = 2
VIDS = 2
UNITS = VIDS * NP
ROWS = 2 * F
HALF = F
HOP_PARTS = 4
STRIDE = 27
EPS = 1e-06
F32 = jnp.float32
BF16 = jnp.bfloat16
MESH = pl.DeviceIdType.MESH
ROWS_OUT = 16
PACKED = 2 * 3 * HD + D
Z_LAST, Y_LAST = 2816, 5632


def timing(amp, freq, phase, time_value):
    angle = freq * time_value + phase
    return (amp * jnp.sin(angle), amp * freq * jnp.cos(angle))


class Gather:
    def __init__(self, sizes, section, coords, weights, send, recv):
        self.sizes, self.section, self.coords = sizes, section, coords
        self.weights, self.send, self.recv = weights, send, recv
        self.live = []
        self.sems = 0
        self.rings = {}

    def peer(self, axis, by):
        z, xl, y = self.coords
        nz, nx, ny = self.sizes
        if axis == "z":
            z = lax.rem(z + by + nz, nz)
        elif axis == "y":
            y = lax.rem(y + by + ny, ny)
        else:
            xl = nx - 1 - xl
        return (self.section, (z * nx + xl) * ny + y)

    def copy(self, ref, sem, peer):
        return pltpu.make_async_remote_copy(
            src_ref=ref,
            dst_ref=ref,
            send_sem=self.send.at[sem],
            recv_sem=self.recv.at[sem],
            device_id=peer,
            device_id_type=MESH,
        )

    def start(self, piece, begin, width, sem, peer):
        copy = self.copy(piece(pl.ds(begin, width)), sem, peer)
        copy.start()
        self.live.append(copy)

    def ring(self, axis, first, stop, fixed, single=False):
        size = self.sizes[0] if axis == "z" else self.sizes[2]
        me = self.coords[0] if axis == "z" else self.coords[2]
        last = size // 2
        first_sem = self.sems
        self.sems += 2 * last

        def arguments(way, step, index):
            z, y = (index, fixed) if axis == "z" else (fixed, index)
            begin, width = first, stop - first
            xl = self.coords[1] if single else slice(None)
            if step == last - 1:
                if single:
                    width = width // 2
                    begin = begin + way * width
                else:
                    xl = way

            def piece(columns):
                return self.weights.at[z, xl, y, :, columns]

            return piece, begin, width, first_sem + 2 * step + way, self.peer(axis, 1 - 2 * way)

        def at(way, step):
            return lax.rem(me - (1 - 2 * way) * step + size, size)

        for step in range(last):
            for way in (0, 1):
                self.start(*arguments(way, step, at(way, step)))
            yield
            for way in (0, 1):
                piece, begin, width, sem, peer = arguments(way, step, at(way, step + 1))
                self.copy(piece(pl.ds(begin, width)), sem, peer).wait_recv()

    def beside(self, fixed):
        sem = self.sems
        self.sems += 1
        _, xl, _ = self.coords
        nx = self.sizes[1]
        peer = self.peer("x", 0)
        self.start(
            lambda columns: self.weights.at[fixed, xl, :, :, columns],
            Y_LAST,
            PACKED - Y_LAST,
            sem,
            peer,
        )
        yield
        columns = pl.ds(Y_LAST, PACKED - Y_LAST)
        self.copy(self.weights.at[fixed, nx - 1 - xl, :, :, columns], sem, peer).wait_recv()

    def build(self):
        z, _, y = self.coords
        nz, _, ny = self.sizes
        rings = self.rings
        rings["a"] = self.ring("y", 0, Z_LAST, z)
        rings["b"] = self.ring("z", Z_LAST, Y_LAST, y)
        rings["c"] = self.ring("z", Y_LAST, PACKED, y, True)
        for by in range(ny):
            rings["az", by] = self.ring("z", 0, Z_LAST, lax.rem(y + by, ny))
        for by in range(nz):
            there = lax.rem(z + by, nz)
            rings["by", by] = self.ring("y", Z_LAST, Y_LAST, there)
            rings["cy", by] = self.ring("y", Y_LAST, PACKED, there, True)
            rings["cx", by] = self.beside(there)

    def go(self, *names):
        for name in names:
            next(self.rings[name], None)

    def finish(self):
        for copy in self.live:
            copy.wait_send()


def spread(source, tall, start):
    count = source.shape[0]
    for k in range(KT):
        tall[pl.ds(start + k, count, stride=KT), :] = source[:, k * HEAD : (k + 1) * HEAD].astype(
            F32
        )


def normalize(values, tangents, gain):
    inverse = lax.rsqrt(jnp.mean(values * values, axis=-1, keepdims=True) + EPS)
    cross = jnp.mean(values * tangents, axis=-1, keepdims=True)
    scaled = values * inverse
    return (
        (scaled * gain).astype(BF16),
        ((inverse * tangents - values * inverse**3 * cross) * gain).astype(BF16),
    )


def attend(q2, k2, v2, gains_ref):
    factor = 1.0 / math.sqrt(HEAD)
    qn, dqn = normalize(q2[:HALF], q2[HALF:], gains_ref[0:1, :])
    kn, dkn = normalize(k2[:HALF], k2[HALF:], gains_ref[1:2, :])
    value, dvalue = v2[:HALF].astype(BF16), v2[HALF:].astype(BF16)

    def against(rows, columns):
        return lax.dot_general(
            rows, columns, (((1,), (1,)), ((), ())), preferred_element_type=F32
        )

    scores = against(jnp.concatenate([qn, dqn], axis=0), kn)
    score = scores[:HALF] * factor
    dscore = (scores[HALF:] + against(qn, dkn)) * factor
    expo = jnp.exp(score)
    prob = expo * (1.0 / jnp.sum(expo, axis=-1, keepdims=True))
    growth = prob * dscore
    dprob = growth - prob * jnp.sum(growth, axis=-1, keepdims=True)
    prob, dprob = prob.astype(BF16), dprob.astype(BF16)
    mixed = jnp.dot(
        jnp.concatenate([prob, dprob], axis=0), value, preferred_element_type=F32
    )
    return mixed[:HALF], mixed[HALF:] + jnp.dot(prob, dvalue, preferred_element_type=F32)


def block_step(
    unit, entering, leaving, weights, gains_ref, mods_ref, dmods_ref, tall, flat, att
):
    group = 8
    vid = unit // NP

    @pl.loop(0, F // group, unroll=4)
    def _(i):
        first = pl.multiple_of(i * group, group)
        hidden = entering[unit, pl.ds(first, group), 0].astype(F32)
        tangent = entering[unit, pl.ds(first, group), 1].astype(F32)

        def mean(values):
            return jnp.sum(
                jnp.sum(values, axis=1, keepdims=True), axis=2, keepdims=True
            ) * (1.0 / D)

        inverse = lax.rsqrt(mean(hidden * hidden) + EPS)
        cross = mean(hidden * tangent)
        normed = hidden * inverse
        dnormed = inverse * tangent - hidden * inverse**3 * cross
        scale = 1.0 + mods_ref[vid, 1][None]
        modulated = normed * scale + mods_ref[vid, 0][None]
        dmodulated = dnormed * scale + normed * dmods_ref[vid, 1][None] + dmods_ref[vid, 0][None]
        row = pl.multiple_of(first * KT, group * KT)
        tall[pl.ds(row, group * KT), :] = modulated.reshape(group * KT, HEAD)
        tall[pl.ds(row + HALF * KT, group * KT), :] = dmodulated.reshape(group * KT, HEAD)

    for k in range(KT):
        flat[:, k * HEAD : (k + 1) * HEAD] = tall[pl.ds(k, ROWS, stride=KT), :].astype(BF16)

    def third(number, pair):
        column = number * HD + pair * 2 * HEAD
        halves = [
            weights[
                :, :, :, :, column + lower * 3 * HD : column + lower * 3 * HD + 2 * HEAD
            ].reshape(F, 1, ROWS_OUT, 2 * HEAD)
            for lower in range(2)
        ]
        matrix = jnp.concatenate(halves, axis=1).reshape(D, 2 * HEAD)
        return jnp.dot(flat[...], matrix, preferred_element_type=F32)

    ahead = [third(number, 0) for number in range(3)]
    for pair in range(HEADS // 2):
        q2, k2, v2 = ahead
        if pair + 1 < HEADS // 2:
            ahead = [third(number, pair + 1) for number in range(3)]
        for one in range(2):
            lanes = slice(one * HEAD, (one + 1) * HEAD)
            output, doutput = attend(q2[:, lanes], k2[:, lanes], v2[:, lanes], gains_ref)
            column = (pair * 2 + one) * HEAD
            att[:HALF, column : column + HEAD] = output.astype(BF16)
            att[HALF:, column : column + HEAD] = doutput.astype(BF16)

    for n in range(KT // 2):
        column = 2 * 3 * HD + n * 2 * HEAD
        matrix = weights[:, :, :, :, column : column + 2 * HEAD].reshape(HD, 2 * HEAD)
        y = jnp.dot(att[...], matrix, preferred_element_type=F32)
        tall[pl.ds(2 * n, ROWS, stride=KT), :] = y[:, :HEAD]
        tall[pl.ds(2 * n + 1, ROWS, stride=KT), :] = y[:, HEAD:]

    @pl.loop(0, F // group, unroll=4)
    def _(i):
        first = pl.multiple_of(i * group, group)
        row = pl.multiple_of(first * KT, group * KT)
        y = tall[pl.ds(row, group * KT), :].reshape(group, KT, HEAD)
        dy = tall[pl.ds(row + HALF * KT, group * KT), :].reshape(group, KT, HEAD)
        hidden = entering[unit, pl.ds(first, group), 0].astype(F32)
        tangent = entering[unit, pl.ds(first, group), 1].astype(F32)
        gate = mods_ref[vid, 2][None]
        dgate = dmods_ref[vid, 2][None]
        leaving[unit, pl.ds(first, group), 0] = (hidden + gate * y).astype(BF16)
        leaving[unit, pl.ds(first, group), 1] = (tangent + dgate * y + gate * dy).astype(BF16)


def kernel(
    sizes,
    sections,
    x_ref,
    t_ref,
    wqkv_ref,
    wout_ref,
    gains_ref,
    index_ref,
    amp_ref,
    freq_ref,
    phase_ref,
    out_ref,
    tan_ref,
    weights,
    mods_ref,
    dmods_ref,
    plain,
    staged,
    relay,
    entering,
    leaving,
    returned,
    tall,
    flat,
    att,
    load_sem,
    own_sem,
    swap_send,
    swap_recv,
    ring_send,
    ring_recv,
    x_send,
    x_recv,
    relay_send,
    relay_recv,
    pass_send,
    pass_recv,
    out_send,
    out_recv,
    turn_sem,
):
    nz, nx, ny = sizes
    count = nz * nx * ny
    section = lax.axis_index("section")
    me = lax.axis_index("seq")
    coords = (me // (nx * ny), (me // ny) % nx, me % ny)
    z, xl, y = coords
    first_half = section < 2

    def flip(index):
        return index + ny - 2 * ny * ((index // ny) % nx)

    across = flip(me)
    slot = jnp.where(first_half, me, across)
    neighbour = (section, lax.rem(me + 1, count))
    group = 8

    def exchange(source, row_of, target, place, send, recv):
        pltpu.make_async_copy(source.at[row_of(me)], target.at[place], recv).start()

        @pl.loop(1, count, unroll=21)
        def _(by):
            to = lax.rem(me + by * STRIDE, count)
            pltpu.make_async_remote_copy(
                src_ref=source.at[row_of(to)],
                dst_ref=target.at[place],
                send_sem=send,
                recv_sem=recv,
                device_id=(section, to),
                device_id_type=MESH,
            ).start()

    def exchange_came(source, target, recv):
        pltpu.make_async_copy(source, target, recv).wait()

    def exchange_sent(source, target, send, recv):
        pltpu.make_async_remote_copy(
            src_ref=source.at[pl.ds(0, count - 1)],
            dst_ref=target.at[pl.ds(0, count - 1)],
            send_sem=send,
            recv_sem=recv,
            device_id=neighbour,
            device_id_type=MESH,
        ).wait_send()

    leads = lax.rem(section, 2) == 0
    loads = [
        pltpu.make_async_copy(ref, plain.at[tan], load_sem.at[tan])
        for tan, ref in enumerate((x_ref, t_ref))
    ]

    @pl.when(section == 3)
    def _():
        for load in loads:
            load.start()

    own = []
    for part, (ref, first, width) in enumerate(
        (
            (wqkv_ref.at[pl.ds(0, ROWS_OUT)], 0, 3 * HD),
            (wqkv_ref.at[pl.ds(ROWS_OUT, ROWS_OUT)], 3 * HD, 3 * HD),
            (wout_ref, 6 * HD, D),
        )
    ):
        home = weights.at[z, xl, y, :, pl.ds(first, width)]
        own.append(pltpu.make_async_copy(ref, home, own_sem.at[part]))
        own[-1].start()
    for copy in own:
        copy.wait()

    def prepare(vid):
        for tan in range(2):
            spread(plain.at[tan, vid], tall, 0)

            @pl.loop(0, count // group)
            def _(i):
                first = pl.multiple_of(i * group, group)
                row = pl.multiple_of(first * NP * KT, group * NP * KT)
                tiles = (
                    tall[pl.ds(row, group * NP * KT), :]
                    .astype(BF16)
                    .reshape(group, NP, KT, HEAD)
                )
                for pos in range(NP):
                    staged[vid * NP + pos, pl.ds(first, group), tan] = tiles[:, pos]

    @pl.when(section == 3)
    def _():
        for load in loads:
            load.wait()
        for vid in range(VIDS):
            prepare(vid)
            for unit in range(vid * NP, vid * NP + NP):
                exchange(
                    staged.at[unit],
                    flip,
                    relay.at[unit],
                    me,
                    x_send.at[unit],
                    x_recv.at[unit],
                )

    @pl.when(jnp.logical_not(leads))
    def _():
        pl.semaphore_wait(turn_sem, 1)

    gather = Gather(sizes, section, coords, weights, ring_send, ring_recv)
    gather.build()
    go = gather.go
    mine = weights.at[z, xl, y, :, pl.ds(0, Y_LAST)]
    swap = pltpu.make_async_remote_copy(
        src_ref=mine,
        dst_ref=mine,
        send_sem=swap_send,
        recv_sem=swap_recv,
        device_id=(section, across),
        device_id_type=MESH,
    )
    theirs = weights.at[z, nx - 1 - xl, y, :, pl.ds(0, Y_LAST)]
    swapped = pltpu.make_async_remote_copy(
        src_ref=theirs,
        dst_ref=theirs,
        send_sem=swap_send,
        recv_sem=swap_recv,
        device_id=(section, across),
        device_id_type=MESH,
    )
    swap.start()
    go("c", ("cy", 0))

    def relayed(unit):
        return pltpu.make_async_remote_copy(
            src_ref=relay.at[unit],
            dst_ref=entering.at[unit],
            send_sem=relay_send.at[unit],
            recv_sem=relay_recv.at[unit],
            device_id=(0, across),
            device_id_type=MESH,
        )

    def pass_to_first(unit):
        @pl.when(section == 3)
        def _():
            exchange_came(staged.at[unit], relay.at[unit], x_recv.at[unit])
            relayed(unit).start()

    for vid in range(VIDS):
        time_value = (index_ref[vid].astype(F32) + 0.5) * (math.pi / (2.0 * T_STEPS))
        mods_ref[vid], dmods_ref[vid] = timing(
            amp_ref[...], freq_ref[...], phase_ref[...], time_value
        )

    swapped.wait_recv()
    go("b", "a", ("by", 0), ("az", 0))
    go("c", ("cy", 1), ("cy", 7))
    go("a", ("az", 1), ("az", 3))
    go(("cy", 0),)
    go("b", ("by", 1), ("by", 7))
    go("c", ("cy", 2), ("cy", 6))

    @pl.when(leads)
    def _():
        pl.semaphore_signal(
            turn_sem, inc=1, device_id=(section + 1, me), device_id_type=MESH
        )

    go("a", ("az", 2))
    go(("cy", 0), ("cx", 0), ("cy", 1), ("cy", 7))
    go(("az", 0), ("by", 0))
    go("c", ("cy", 3), ("cy", 5))
    go(("cy", 1), ("cx", 1), ("cy", 7), ("cx", 7), ("cy", 2), ("cy", 6))
    go("b", ("by", 2), ("by", 6))
    go("c", ("cy", 4))
    pass_to_first(0)
    pass_to_first(1)
    go(("az", 1), ("az", 3), ("by", 1), ("by", 7), ("az", 2))
    go(("cy", 2), ("cx", 2), ("cy", 6), ("cx", 6), ("cy", 3), ("cy", 5), ("cy", 4))
    go("b", ("by", 3), ("by", 5))
    go(("az", 0), ("by", 0), ("az", 1), ("az", 3))
    go(("cy", 3), ("cx", 3), ("cy", 5), ("cx", 5), ("cy", 4), ("cx", 4))
    pass_to_first(2)

    go("b", ("by", 4))
    go(("by", 2), ("by", 6), ("az", 2), ("by", 1), ("by", 7), ("az", 0))
    pass_to_first(3)
    go(("by", 3), ("by", 5), ("az", 1), ("az", 3), ("by", 4), ("az", 2))
    go(("by", 2), ("by", 6), ("az", 0), ("by", 3), ("by", 5))
    go(("az", 1), ("az", 3), ("by", 4), ("az", 2))
    go(*(("cx", by) for by in range(nz)))

    @pl.when(section == 1)
    def _():
        pl.semaphore_signal(turn_sem, inc=1, device_id=(0, me), device_id_type=MESH)

    def onward(unit, first=0, frames=F):
        return pltpu.make_async_remote_copy(
            src_ref=leaving.at[unit, pl.ds(first, frames)],
            dst_ref=entering.at[unit, pl.ds(first, frames)],
            send_sem=pass_send.at[unit],
            recv_sem=pass_recv.at[unit],
            device_id=(
                lax.rem(section + 1, sections),
                jnp.where(section == 1, across, me),
            ),
            device_id_type=MESH,
        )

    def send_back(unit):
        exchange(
            leaving.at[unit],
            lambda f: f,
            returned.at[unit],
            slot,
            out_send.at[unit],
            out_recv.at[unit],
        )

    @pl.loop(0, UNITS)
    def _(unit):
        @pl.when(section == 0)
        def _():
            relayed(unit).wait_recv()

        @pl.when(section > 0)
        def _():
            onward(unit).wait_recv()

        block_step(
            unit, entering, leaving, weights, gains_ref, mods_ref, dmods_ref, tall, flat, att
        )

        @pl.when(section < sections - 1)
        def _():
            for part in range(HOP_PARTS):
                onward(unit, part * (F // HOP_PARTS), F // HOP_PARTS).start()

        @pl.when(section > 1)
        def _():
            send_back(unit)

    @pl.when(section == 0)
    def _():
        pl.semaphore_wait(turn_sem, 1)

    @pl.when(section < 2)
    def _():
        @pl.loop(0, UNITS)
        def _(unit):
            send_back(unit)

    gather.finish()
    swap.wait_send()

    @pl.loop(0, VIDS)
    def _(vid):
        for pos in range(NP):
            unit = vid * NP + pos
            exchange_came(leaving.at[unit], returned.at[unit], out_recv.at[unit])

            @pl.loop(0, count // group)
            def _(i):
                first = pl.multiple_of(i * group, group)
                for tan in range(2):
                    tiles = returned[unit, pl.ds(first, group), tan].astype(F32)
                    for one in range(group):
                        row = pl.multiple_of(
                            ((tan * count + first + one) * NP + pos) * KT, KT
                        )
                        tall[pl.ds(row, KT), :] = tiles[one]

        for tan, result in enumerate((out_ref, tan_ref)):
            for k in range(KT):
                result[vid, :, k * HEAD : (k + 1) * HEAD] = tall[
                    pl.ds(tan * count * NP * KT + k, count * NP, stride=KT), :
                ].astype(BF16)

    @pl.loop(0, UNITS)
    def _(unit):
        exchange_sent(
            leaving.at[unit], returned.at[unit], out_send.at[unit], out_recv.at[unit]
        )

        @pl.when(section < sections - 1)
        def _():
            onward(unit).wait_send()

        @pl.when(section == 3)
        def _():
            exchange_sent(
                staged.at[unit], relay.at[unit], x_send.at[unit], x_recv.at[unit]
            )
            relayed(unit).wait_send()


def shards(sizes, x_in, x_tan, t_index, w_qkv, w_out, qk_gain, mod_amp, mod_freq, mod_phase):
    nz, nx, ny = sizes
    count = nz * nx * ny
    sections = lax.axis_size("section")
    places = x_in.shape[2]
    waves = [wave.reshape(3, KT, HEAD) for wave in (mod_amp, mod_freq, mod_phase)]
    outside = pl.BlockSpec(memory_space=pl.ANY)
    inside = pl.BlockSpec(memory_space=pltpu.VMEM)
    result = jax.ShapeDtypeStruct((VIDS, places, D), BF16)
    units = (UNITS, F, 2, KT, HEAD)
    rings = 2 * (ny // 2) * (1 + 2 * nz) + 2 * (nz // 2) * (2 + ny) + nz
    dma = pltpu.SemaphoreType.DMA
    out, tan = pl.pallas_call(
        functools.partial(kernel, sizes, sections),
        out_shape=(result, result),
        in_specs=[outside] * 4
        + [inside, pl.BlockSpec(memory_space=pltpu.SMEM)]
        + [inside] * 3,
        out_specs=(inside, inside),
        scratch_shapes=[
            pltpu.VMEM((nz, nx, ny, ROWS_OUT, PACKED), BF16),
            pltpu.VMEM((VIDS, 3, KT, HEAD), F32),
            pltpu.VMEM((VIDS, 3, KT, HEAD), F32),
            pltpu.VMEM((2, VIDS, places, D), BF16),
            pltpu.VMEM(units, BF16),
            pltpu.VMEM(units, BF16),
            pltpu.VMEM(units, BF16),
            pltpu.VMEM(units, BF16),
            pltpu.VMEM(units, BF16),
            pltpu.VMEM((2 * places * KT, HEAD), F32),
            pltpu.VMEM((ROWS, D), BF16),
            pltpu.VMEM((ROWS, HD), BF16),
            dma((2,)),
            dma((3,)),
            dma,
            dma,
            dma((rings,)),
            dma((rings,)),
            dma((UNITS,)),
            dma((UNITS,)),
            dma((UNITS,)),
            dma((UNITS,)),
            dma((UNITS,)),
            dma((UNITS,)),
            dma((UNITS,)),
            dma((UNITS,)),
            pltpu.SemaphoreType.REGULAR,
        ],
        compiler_params=pltpu.CompilerParams(
            has_side_effects=True, vmem_limit_bytes=60 * 1024 * 1024
        ),
        name="blocks",
    )(
        x_in.reshape(VIDS, places, D),
        x_tan.reshape(VIDS, places, D),
        w_qkv[0],
        w_out[0],
        qk_gain[0],
        t_index,
        *waves,
    )
    return (out[None, :, None], tan[None, :, None])


def solution(mesh):
    count = mesh.shape["seq"]
    sizes = (count // 8, 2, 4)
    placed = (
        P(None, "seq", None, None),
        P(None, "seq", None, None),
        P(),
        P("section", "seq", None),
        P("section", "seq", None),
        P("section", None, None),
        P("section", None, None),
        P("section", None, None),
        P("section", None, None),
    )
    return jax.shard_map(
        functools.partial(shards, sizes),
        mesh=mesh,
        in_specs=placed,
        out_specs=(P("section", None, "seq", None, None), P("section", None, "seq", None, None)),
        check_vma=False,
    )
```
